32 devices in a mesh: dp: 16 (over z, x, core), tensor: 2 (over y).
Axes of the slice: x: 2, y: 2, z: 4, core: 2. Of those that a mesh axis runs over, the one named last changes fastest.
Arguments:
- frames: bfloat16 [19200, 512], P('dp', 'tensor'), may hold values from -6 to 6
- resets: int32 [19200], P('dp'), may hold values 0 or 1
- first_gain: float32 [512], replicated, may hold values from 0.5 to 1.5
- first_shift: float32 [512], replicated, may hold values from -1 to 1
- qkv_weight: bfloat16 [3, 512, 512], P(None, None, 'tensor'), may hold values from -0.375 to 0.375
- out_weight: bfloat16 [512, 512], P('tensor'), may hold values from -0.75 to 0.75
- out_bias: float32 [512], replicated, may hold values from -1 to 1
- second_gain: float32 [512], replicated, may hold values from 0.5 to 1.5
- second_shift: float32 [512], replicated, may hold values from -1 to 1
- up_weight: bfloat16 [512, 2048], P(None, 'tensor'), may hold values from -0.25 to 0.25
- up_bias: float32 [2048], P('tensor'), may hold values from -1 to 1
- down_weight: bfloat16 [2048, 512], P('tensor'), may hold values from -0.125 to 0.125
- down_bias: float32 [512], replicated, may hold values from -1 to 1
- prior_gain: float32 [512], replicated, may hold values from 0.5 to 1.5
- prior_shift: float32 [512], replicated, may hold values from -1 to 1
- prior_weight: bfloat16 [512, 1024], P(None, 'tensor'), may hold values from -0.25 to 0.25
- prior_bias: float32 [1024], P('tensor'), may hold values from -2.5 to 2.5
- out_cotangent: bfloat16 [19200, 512], P('dp', 'tensor'), may hold values from -6 to 6
- logit_cotangent: bfloat16 [19200, 1024], P('dp', 'tensor'), may hold values from -6 to 6
Outputs:
- block_out: bfloat16 [19200, 512], P('dp', 'tensor')
- logits: float32 [19200, 1024], P('dp', 'tensor')
- grad_frames: float32 [19200, 512], P('dp', 'tensor')
- grad_first_gain: float32 [512], replicated
- grad_first_shift: float32 [512], replicated
- grad_qkv: float32 [3, 512, 512], P(None, None, 'tensor')
- grad_out_weight: float32 [512, 512], P('tensor')
- grad_out_bias: float32 [512], replicated
- grad_second_gain: float32 [512], replicated
- grad_second_shift: float32 [512], replicated
- grad_up_weight: float32 [512, 2048], P(None, 'tensor')
- grad_up_bias: float32 [2048], P('tensor')
- grad_down_weight: float32 [2048, 512], P('tensor')
- grad_down_bias: float32 [512], replicated
- grad_prior_gain: float32 [512], replicated
- grad_prior_shift: float32 [512], replicated
- grad_prior_weight: float32 [512, 1024], P(None, 'tensor')
- grad_prior_bias: float32 [1024], P('tensor')
The draws below stay inside these ranges and needn't reach their ends.
All inputs are finite; a program needn't handle non-finite values. No bound on the sum of `resets` on one device may be relied on, other than what follows from the above.
Results may differ from the reference program's by a relative error of at most 0.012.
The reference program's roundings to bfloat16 on the way count: a program that leaves them out, or rounds other values in their place, can miss the bound.
Values may be sent and summed in bfloat16 or wider, within the bound.
No kernel may reach another device: no remote copies, remote signals or barrier semaphores. Data moves between devices by JAX's collectives and lax.ppermute only.
A program may use at most 128 MiB of HBM per device.

```python
import jax
import jax.numpy as jnp
from jax import lax

HEADS = 8
HEAD_DIM = 64
D = 512
FF = 2048
PRIOR = 1024
SEQ_LEN = 50
ROWS = 1200
TOKENS = 19200
N_DP = 16


def place_ends(entries, key, low, top_value):
    longest = entries.shape.index(max(entries.shape))
    spots = []
    for shift in (0, 1):
        where = [jax.random.randint(jax.random.fold_in(key, axis), (), 0, length) for axis, length in enumerate(entries.shape)]
        where[longest] = (where[longest] + shift) % entries.shape[longest]
        spots.append(tuple(where))
    return entries.at[spots[0]].set(low).at[spots[1]].set(top_value)


def block_levels(own_key, extent, pieces, low, high):
    def one(dim, shards_of):
        steps = jax.random.uniform(jax.random.fold_in(jax.random.fold_in(own_key, 6), dim), (shards_of,), jnp.float32, low / len(pieces), high / len(pieces))
        return jnp.repeat(jnp.exp(steps), extent[dim] // shards_of).reshape((-1,) + (1,) * (len(extent) - dim - 1))

    level = one(*pieces[0])
    for cut in pieces[1:]:
        level = level * one(*cut)
    return level


def scatter_about(rng, shape, scale, reach, shards=(), held_as=jnp.bfloat16):
    drawn = scale * jax.random.normal(rng, shape, jnp.float32)
    if shards:
        drawn = drawn * block_levels(rng, shape, shards, -0.22, 0.18)
    return jnp.clip(drawn, -reach, reach).astype(held_as)


def setup_inputs(seed: int = 0) -> dict:
    seeds = jax.random.split(jax.random.key(seed), 20)
    frames = scatter_about(seeds[0], (TOKENS, D), 1.0, 6.0, ((0, 16), (1, 2)))
    resets = place_ends((jax.random.randint(seeds[1], (TOKENS,), 0, 16) < 1).astype(jnp.int32), jax.random.fold_in(seeds[1], 1), 0, 1)
    first_gain = jnp.clip(1.0 + 0.1 * jax.random.normal(seeds[2], (D,), jnp.float32), 0.5, 1.5)
    first_shift = scatter_about(seeds[3], (D,), 0.2, 1.0, (), jnp.float32)
    qkv_weight = scatter_about(seeds[4], (3, D, D), (D // 2) ** -0.5, 0.375, ((2, 2),))
    out_weight = scatter_about(seeds[5], (D, D), (D // 8) ** -0.5, 0.75, ((0, 2),))
    out_bias = scatter_about(seeds[6], (D,), 0.2, 1.0, (), jnp.float32)
    second_gain = jnp.clip(1.0 + 0.1 * jax.random.normal(seeds[7], (D,), jnp.float32), 0.5, 1.5)
    second_shift = scatter_about(seeds[8], (D,), 0.2, 1.0, (), jnp.float32)
    up_weight = scatter_about(seeds[9], (D, FF), D ** -0.5, 0.25, ((1, 2),))
    up_bias = scatter_about(seeds[10], (FF,), 0.2, 1.0, ((0, 2),), jnp.float32)
    down_weight = scatter_about(seeds[11], (FF, D), FF ** -0.5, 0.125, ((0, 2),))
    down_bias = scatter_about(seeds[12], (D,), 0.2, 1.0, (), jnp.float32)
    prior_gain = jnp.clip(1.0 + 0.1 * jax.random.normal(seeds[13], (D,), jnp.float32), 0.5, 1.5)
    prior_shift = scatter_about(seeds[14], (D,), 0.2, 1.0, (), jnp.float32)
    prior_weight = scatter_about(seeds[15], (D, PRIOR), D ** -0.5, 0.25, ((1, 2),))
    prior_bias = scatter_about(seeds[16], (PRIOR,), 0.5, 2.5, ((0, 2),), jnp.float32)
    out_cotangent = scatter_about(seeds[17], (TOKENS, D), 1.0, 6.0, ((0, 16), (1, 2)))
    logit_cotangent = scatter_about(seeds[18], (TOKENS, PRIOR), 1.0, 6.0, ((0, 16), (1, 2)))
    return dict(frames=frames, resets=resets, first_gain=first_gain, first_shift=first_shift, qkv_weight=qkv_weight, out_weight=out_weight, out_bias=out_bias, second_gain=second_gain, second_shift=second_shift, up_weight=up_weight, up_bias=up_bias, down_weight=down_weight, down_bias=down_bias, prior_gain=prior_gain, prior_shift=prior_shift, prior_weight=prior_weight, prior_bias=prior_bias, out_cotangent=out_cotangent, logit_cotangent=logit_cotangent)


EPS = 1e-05
NEG = -1e+30

@jax.custom_vjp
def low(v):
    return lax.optimization_barrier(v.astype(jnp.bfloat16)).astype(jnp.float32)

@jax.custom_vjp
def low_back(v):
    return v

def low_keep(v):
    return (low(v), None)

def low_pass(kept, grad):
    return (grad,)

def back_keep(v):
    return (v, None)

def back_low(kept, grad):
    return (low(grad),)
low.defvjp(low_keep, low_pass)
low_back.defvjp(back_keep, back_low)

def normalize(value, gain, shift):
    centre = value - lax.optimization_barrier(jnp.mean(value, axis=-1, keepdims=True))
    spread = lax.optimization_barrier(jnp.mean(centre * centre, axis=-1, keepdims=True))
    return centre * lax.rsqrt(spread + EPS) * gain + shift

def matmul(left, right):
    return jnp.dot(left, right, precision=lax.Precision.HIGHEST)

def episodes(resets):
    places = jnp.arange(resets.shape[0], dtype=jnp.int32)
    starts = jnp.where((places % SEQ_LEN == 0) | (resets == 1), 1, 0).astype(jnp.int32)
    return jnp.cumsum(starts).astype(jnp.int32)

def attend(queries, keys, values, labels):
    raw = jnp.einsum('qhd,khd->hqk', queries, keys, precision=lax.Precision.HIGHEST)
    scores = low_back(raw * HEAD_DIM ** (-0.5))
    places = jnp.arange(labels.shape[0], dtype=jnp.int32)
    allowed = (labels[:, None] == labels[None, :]) & (places[:, None] >= places[None, :])
    scores = jnp.where(allowed[None], scores, NEG)
    top = lax.optimization_barrier(jnp.max(scores, axis=-1, keepdims=True))
    expo = jnp.exp(scores - top)
    weights = expo / lax.optimization_barrier(jnp.sum(expo, axis=-1, keepdims=True))
    return jnp.einsum('hqk,khd->qhd', low(weights), values, precision=lax.Precision.HIGHEST)

def smooth(value):
    return jax.nn.gelu(value, approximate=True)

def forward(frames, first_gain, first_shift, qkv_weight, out_weight, out_bias, second_gain, second_shift, up_weight, up_bias, down_weight, down_bias, prior_gain, prior_shift, prior_weight, prior_bias, labels):
    first = low(normalize(frames, first_gain, first_shift))
    projected = [low(low_back(matmul(first, qkv_weight[index]))) for index in range(3)]
    shaped = [item.reshape(N_DP, ROWS, HEADS, HEAD_DIM) for item in projected]
    blocked = jax.checkpoint(attend)

    def one_block(block):
        return blocked(block[0], block[1], block[2], block[3])
    mixed = lax.map(one_block, (shaped[0], shaped[1], shaped[2], labels.reshape(N_DP, ROWS)))
    mixed = low(low_back(mixed.reshape(TOKENS, D)))
    middle = frames + low_back(matmul(mixed, out_weight)) + out_bias
    second = low(normalize(middle, second_gain, second_shift))
    hidden = low_back(matmul(second, up_weight) + up_bias)
    activated = low(smooth(hidden))
    ending = middle + low_back(matmul(activated, down_weight)) + down_bias
    prior_in = low(normalize(ending, prior_gain, prior_shift))
    logits = matmul(prior_in, prior_weight) + prior_bias
    return (ending, logits)

def reference(frames, resets, first_gain, first_shift, qkv_weight, out_weight, out_bias, second_gain, second_shift, up_weight, up_bias, down_weight, down_bias, prior_gain, prior_shift, prior_weight, prior_bias, out_cotangent, logit_cotangent):
    labels = episodes(resets)
    params = tuple((item.astype(jnp.float32) for item in (frames, first_gain, first_shift, qkv_weight, out_weight, out_bias, second_gain, second_shift, up_weight, up_bias, down_weight, down_bias, prior_gain, prior_shift, prior_weight, prior_bias)))

    def run(*values):
        return forward(*values, labels)
    outputs, pull = jax.vjp(run, *params)
    grads = pull((out_cotangent.astype(jnp.float32), logit_cotangent.astype(jnp.float32)))
    return (outputs[0].astype(jnp.bfloat16), outputs[1], grads[0], grads[1], grads[2], grads[3], grads[4], grads[5], grads[6], grads[7], grads[8], grads[9], grads[10], grads[11], grads[12], grads[13], grads[14], grads[15])
```

```python
import functools

import jax
import jax.numpy as jnp
from jax import lax
from jax.experimental import pallas as pl
from jax.experimental.pallas import tpu as pltpu
from jax.sharding import PartitionSpec as P

HEAD_DIM = 64
SEQ_LEN = 50
BLOCK = 4 * SEQ_LEN
PAD = -(-BLOCK // 16) * 16
EPS = 1e-05
NEG = -1e30
GELU_C = 0.7978845608028654
GELU_A = 0.044715
VMEM = 48 * 1024 * 1024
BF = jnp.bfloat16
F32 = jnp.float32


def mm(a, b):
    return lax.dot_general(a, b, (((1,), (0,)), ((), ())), preferred_element_type=F32)


def mm_bt(a, b):
    return lax.dot_general(a, b, (((1,), (1,)), ((), ())), preferred_element_type=F32)


def mm_at(a, b):
    return lax.dot_general(a, b, (((0,), (0,)), ((), ())), preferred_element_type=F32)


def norm_of(value):
    centre = value - jnp.mean(value, axis=-1, keepdims=True)
    factor = lax.rsqrt(jnp.mean(centre * centre, axis=-1, keepdims=True) + EPS)
    return centre * factor, factor


def norm_back(grad, unit, factor, gain):
    scaled = grad * gain
    first = jnp.mean(scaled, axis=-1, keepdims=True)
    second = jnp.mean(scaled * unit, axis=-1, keepdims=True)
    return factor * (scaled - first - unit * second)


def col_sum(value):
    return jnp.sum(value, axis=0, keepdims=True)


def whole_row(here, own, other):
    low = jnp.where(here == 0, own, other)
    high = jnp.where(here == 0, other, own)
    return jnp.concatenate([low, high], axis=1).astype(F32)


def allowed_pairs(seg):
    seg2 = jnp.concatenate([seg, seg], axis=0)
    row = lax.broadcasted_iota(jnp.int32, (2 * PAD, PAD), 0)
    row = jnp.where(row >= PAD, row - PAD, row)
    col = lax.broadcasted_iota(jnp.int32, (2 * PAD, PAD), 1)
    return (col <= row) & (col >= seg2)


def two_heads(value):
    first = lax.broadcasted_iota(jnp.int32, value.shape, 1) < HEAD_DIM
    none = jnp.zeros_like(value)
    return jnp.concatenate([jnp.where(first, value, none), jnp.where(first, none, value)], axis=0)


def one_pair(value):
    first = lax.broadcasted_iota(jnp.int32, (PAD, 2 * HEAD_DIM), 1) < HEAD_DIM
    return jnp.where(first, value[:PAD], value[PAD:])


def softmax_of(query2, key, allowed):
    scores = jnp.where(allowed, mm_bt(query2, key) * HEAD_DIM ** (-0.5), NEG)
    expo = jnp.exp(scores - jnp.max(scores, axis=-1, keepdims=True))
    return expo / jnp.sum(expo, axis=-1, keepdims=True)


def accumulate(step, ref, index, value):
    @pl.when(step == 0)
    def _():
        ref[index] = value

    @pl.when(step != 0)
    def _():
        ref[index] += value


def attend_kernel(
    s, own, other, seg, gain, shift, qkv, qkv_o, out, out_o, out_bias, gain2, shift2,
    first_ref, triple_ref, mixed_ref, middle_ref, second_ref,
):
    frames = whole_row(s[0], own[0], other[0])
    unit, _ = norm_of(frames)
    first = (unit * gain[...] + shift[...]).astype(BF)
    first_ref[0] = first
    allowed = allowed_pairs(seg[0])
    total = frames + out_bias[...]
    for half, (weight, weight_out) in enumerate(((qkv, out), (qkv_o, out_o))):
        triple = [mm(first, weight[c]).astype(BF) for c in range(3)]
        mixed = []
        for pair in range(2):
            at = slice(pair * 128, pair * 128 + 128)
            query, key, value = (item[:, at] for item in triple)
            weights = softmax_of(two_heads(query), key, allowed).astype(BF)
            mixed.append(one_pair(mm(weights, value)).astype(BF))
        mixed = jnp.concatenate(mixed, axis=1)
        for c in range(3):
            triple_ref[0, :, (half * 3 + c) * 256 : (half * 3 + c + 1) * 256] = triple[c]
        mixed_ref[0, :, half * 256 : half * 256 + 256] = mixed
        total = total + mm(mixed, weight_out[...])
    middle_ref[0] = total
    unit2, _ = norm_of(total)
    second_ref[0] = (unit2 * gain2[...] + shift2[...]).astype(BF)


def feed_kernel(
    s, second, middle, up, u0, u1, u2, u3, up_bias, down, d0, d1, d2, d3, down_bias, gain, shift,
    act_ref, slope_ref, ending_ref, prior_in_ref, block_own_ref, block_other_ref,
):
    x = second[0]
    total = middle[0] + down_bias[...]
    ups = [up[:, i * 256 : i * 256 + 256] for i in range(4)] + [u[...] for u in (u0, u1, u2, u3)]
    downs = [down[i * 256 : i * 256 + 256, :] for i in range(4)] + [d[...] for d in (d0, d1, d2, d3)]
    half = up.shape[1]
    for i in range(8):
        if i < 4:
            at = pl.ds(i * 256, 256)
        else:
            at = pl.ds(pl.multiple_of(half + (s[1] ^ (i - 4)) * 256, 256), 256)
        hidden = mm(x, ups[i]) + up_bias[:, at]
        square = hidden * hidden
        bent = jnp.tanh(GELU_C * (hidden + GELU_A * hidden * square))
        act = (0.5 * hidden * (1.0 + bent)).astype(BF)
        slope = 0.5 * (1.0 + bent) + (0.5 * GELU_C) * hidden * (1.0 - bent * bent) * (
            1.0 + (3.0 * GELU_A) * square
        )
        act_ref[0, :, at] = act
        slope_ref[0, :, at] = slope
        total = total + mm(act, downs[i])
    ending_ref[0] = total
    unit, _ = norm_of(total)
    prior_in_ref[0] = (unit * gain[...] + shift[...]).astype(BF)
    low, high = total[:, :256].astype(BF), total[:, 256:].astype(BF)
    block_own_ref[0] = jnp.where(s[0] == 0, low, high)
    block_other_ref[0] = jnp.where(s[0] == 0, high, low)


def prior_kernel(
    s, prior_in, ending, prior, p0, p1, p2, p3, bias, logit_own, logit_other, out_own, out_other, gain,
    logits_ref, logits_other_ref, grad_ending_ref, ending_grad_ref, vec_ref, bias_ref,
):
    step = pl.program_id(0)
    half = prior.shape[1]
    x = prior_in[0]
    cot = logit_own[0]
    logits_ref[0] = mm(x, prior[...]) + bias[:, :half]
    back = mm_bt(cot, prior[...])
    accumulate(step, bias_ref, (slice(None), slice(0, half)), col_sum(cot.astype(F32)))
    cot_o = logit_other[0]
    accumulate(step, bias_ref, (slice(None), slice(half, 2 * half)), col_sum(cot_o.astype(F32)))
    for j, piece in enumerate((p0, p1, p2, p3)):
        start = pl.multiple_of((s[1] ^ j) * 128, 128)
        at = pl.ds(start, 128)
        far = pl.ds(pl.multiple_of(half + start, 128), 128)
        logits_other_ref[0, :, at] = (mm(x, piece[...]) + bias[:, far]).astype(BF)
        back = back + mm_bt(logit_other[0, :, at], piece[...])
    unit, factor = norm_of(ending[0])
    grad = whole_row(s[0], out_own[0], out_other[0]) + norm_back(back, unit, factor, gain[...])
    grad_ending_ref[0] = grad
    ending_grad_ref[0] = grad.astype(BF)
    rows = jnp.concatenate([col_sum(back * unit), col_sum(back), col_sum(grad)], axis=0)
    accumulate(step, vec_ref, (slice(0, 3), slice(None)), rows)


def piece_targets(s, step, last, keep, sums, send):
    def put(h, j, rows, value):
        if j < 2:
            accumulate(step, keep, (2 * h + j, rows), value)
        else:
            accumulate(step, sums, (2 * h + j - 2, rows), value)

    def finish():
        @pl.when(step == last)
        def _():
            send[...] = sums[...].astype(BF)

    return put, finish


def late_grads_kernel(
    s, prior_in, logit_own, logit_other, act, ending_grad, keep, send, sums,
):
    step = pl.program_id(0)
    put, finish = piece_targets(s, step, pl.num_programs(0) - 1, keep, sums, send)
    x = prior_in[0]
    grad = ending_grad[0]
    half = act.shape[2] // 2
    n = x.shape[1]
    for h in range(2):
        for j in range(4):
            place = s[1] ^ j
            cot = (logit_own, logit_other)[h][0, :, pl.ds(pl.multiple_of(place * 128, 128), 128)]
            put(h, j, slice(0, n), mm_at(x, cot))
            part = act[0, :, pl.ds(pl.multiple_of(h * half + place * 256, 256), 256)]
            value = mm_at(part, grad)
            for t in range(4):
                put(h, j, slice(n + t * 256, n + t * 256 + 256), value[:, t * 128 : t * 128 + 128])
    finish()


def feed_back_kernel(
    s, ending_grad, slope, second, middle, grad_ending, up, u0, u1, u2, u3, down, d0, d1, d2, d3, gain,
    grad_middle_ref, middle_grad_ref, vec_ref, bias_ref, keep, send, sums,
):
    step = pl.program_id(0)
    put, finish = piece_targets(s, step, pl.num_programs(0) - 1, keep, sums, send)
    grad = ending_grad[0]
    x = second[0]
    half = up.shape[1]
    n = x.shape[1]
    back = jnp.zeros((PAD, n), F32)
    for h in range(2):
        for j in range(4):
            place = pl.multiple_of((s[1] ^ j) * 256, 256)
            at = pl.ds(pl.multiple_of(h * half + place, 256), 256)
            if h == 0:
                w_up, w_down = up[:, pl.ds(place, 256)], down[pl.ds(place, 256), :]
            else:
                w_up, w_down = (u0, u1, u2, u3)[j][...], (d0, d1, d2, d3)[j][...]
            low = (mm_bt(grad, w_down) * slope[0, :, at]).astype(BF)
            accumulate(step, bias_ref, (slice(None), at), col_sum(low.astype(F32)))
            value = mm_at(x, low)
            for t in range(2):
                put(h, j, slice(t * n, t * n + n), value[:, t * 128 : t * 128 + 128])
            back = back + mm_bt(low, w_up)
    finish()
    unit, factor = norm_of(middle[0])
    total = grad_ending[0] + norm_back(back, unit, factor, gain[...])
    grad_middle_ref[0] = total
    middle_grad_ref[0] = total.astype(BF)
    rows = jnp.concatenate([col_sum(back * unit), col_sum(back), col_sum(total)], axis=0)
    accumulate(step, vec_ref, (slice(0, 3), slice(None)), rows)


def attend_back_kernel(
    s, middle_grad, grad_middle, own, other, first, triple, mixed, seg, qkv, qkv_o, out, out_o, gain,
    frames_own_ref, frames_other_ref, vec_ref, keep, send, sums,
):
    step = pl.program_id(0)
    put, finish = piece_targets(s, step, pl.num_programs(0) - 1, keep, sums, send)
    grad = middle_grad[0]
    allowed = allowed_pairs(seg[0])
    factor = HEAD_DIM ** (-0.5)
    back = jnp.zeros(grad.shape, F32)
    for h, (weight, weight_out) in enumerate(((qkv, out), (qkv_o, out_o))):
        for j in range(4):
            part = middle_grad[0, :, pl.ds(pl.multiple_of((s[1] ^ j) * 128, 128), 128)]
            put(h, j, slice(0, 256), mm_at(mixed[0, :, h * 256 : h * 256 + 256], part))
        mixed_grad = mm_bt(grad, weight_out[...]).astype(BF)
        thirds = ([], [], [])
        for pair in range(2):
            at = slice(pair * 128, pair * 128 + 128)
            query, key, value = (
                triple[0, :, (h * 3 + c) * 256 + pair * 128 : (h * 3 + c) * 256 + pair * 128 + 128]
                for c in range(3)
            )
            query2 = two_heads(query)
            mixed2 = two_heads(mixed_grad[:, at])
            again = softmax_of(query2, key, allowed)
            weight_grad = mm_bt(mixed2, value)
            inner = jnp.sum(again * weight_grad, axis=-1, keepdims=True)
            score_grad = (again * (weight_grad - inner)).astype(BF)
            thirds[0].append((one_pair(mm(score_grad, key)) * factor).astype(BF))
            thirds[1].append((mm_at(score_grad, query2) * factor).astype(BF))
            thirds[2].append(mm_at(again.astype(BF), mixed2).astype(BF))
        for c in range(3):
            part = jnp.concatenate(thirds[c], axis=1)
            back = back + mm_bt(part, weight[c])
            for j in range(4):
                x = first[0, :, pl.ds(pl.multiple_of((s[1] ^ j) * 128, 128), 128)]
                value = mm_at(x, part)
                for t in range(2):
                    start = 256 + (t * 3 + c) * 128
                    put(h, j, slice(start, start + 128), value[:, t * 128 : t * 128 + 128])
    finish()
    unit, scale = norm_of(whole_row(s[0], own[0], other[0]))
    total = grad_middle[0] + norm_back(back, unit, scale, gain[...])
    low, high = total[:, :256], total[:, 256:]
    frames_own_ref[0] = jnp.where(s[0] == 0, low, high)
    frames_other_ref[0] = jnp.where(s[0] == 0, high, low).astype(BF)
    rows = jnp.concatenate([col_sum(back * unit), col_sum(back)], axis=0)
    accumulate(step, vec_ref, (slice(0, 2), slice(None)), rows)


def call(kernel, scalars, ins, outs, scratch=(), name=None, flops=0):
    steps = next(value.shape[0] for value, blocked in ins if blocked)

    def spec(shape, blocked):
        if blocked:
            return pl.BlockSpec((1,) + tuple(shape[1:]), lambda b, s: (b,) + (0,) * (len(shape) - 1))
        return pl.BlockSpec(tuple(shape), lambda b, s: (0,) * len(shape))

    moved = sum(v.size * v.dtype.itemsize for v, _ in ins) + sum(
        o.size * o.dtype.itemsize for o, _ in outs
    )
    return pl.pallas_call(
        kernel,
        grid_spec=pltpu.PrefetchScalarGridSpec(
            num_scalar_prefetch=1,
            grid=(steps,),
            in_specs=[spec(v.shape, blocked) for v, blocked in ins],
            out_specs=[spec(o.shape, blocked) for o, blocked in outs],
            scratch_shapes=list(scratch),
        ),
        out_shape=[o for o, _ in outs],
        compiler_params=pltpu.CompilerParams(vmem_limit_bytes=VMEM),
        cost_estimate=pl.CostEstimate(flops=flops, bytes_accessed=moved, transcendentals=0),
        name=name,
    )(scalars, *[v for v, _ in ins])


def swap(value, axes, sizes, mask):
    count = 1
    for size in sizes:
        count *= size
    return lax.ppermute(value, axes, [(i, i ^ mask) for i in range(count)])


class Moves:
    def __init__(self, n_dp, n_tensor):
        self.n_dp, self.n_tensor = n_dp, n_tensor
        self.dp = lax.axis_index("dp")
        self.here = lax.axis_index("tensor")

    def along(self, value, mask):
        return swap(value, "dp", (self.n_dp,), mask)

    def core(self, value):
        return self.along(value, 1)

    def side(self, value):
        return self.along(value, 2)

    def over(self, value):
        return swap(value, "tensor", (self.n_tensor,), 1)

    def cross(self, value):
        return swap(value, ("dp", "tensor"), (self.n_dp, self.n_tensor), 5)

    def groups(self):
        shift, rest = 2, self.n_dp // 4
        while rest > 1:
            size = 4 if rest % 4 == 0 else 2
            yield shift, size
            shift, rest = shift + (2 if size == 4 else 1), rest // size

    def reduce(self, keep, sent):
        total = keep + self.core(sent)
        parts = [total[i].astype(BF) for i in (1, 2, 3)]
        total = total[0] + self.side(parts[0]) + self.over(parts[1]) + self.cross(parts[2])
        for shift, size in self.groups():
            mine = (self.dp >> shift) & (size - 1)
            split = total.reshape(size, total.shape[0] // size, total.shape[1])
            total = lax.dynamic_index_in_dim(split, mine, 0, False)
            for k in range(1, size):
                part = lax.dynamic_index_in_dim(split, mine ^ k, 0, False).astype(BF)
                total = total + self.along(part, k << shift)
        return total

    def gather(self, total):
        total = total.astype(BF)
        for shift, size in reversed(list(self.groups())):
            mine = (self.dp >> shift) & (size - 1)
            parts = [total] + [self.along(total, k << shift) for k in range(1, size)]
            total = jnp.concatenate([pick(mine ^ i, parts) for i in range(size)], axis=0)
        near = self.side(total)
        far = self.core(jnp.stack([total, near]))
        parts = [total, near, far[0], far[1]]
        place = self.dp & 1, (self.dp >> 1) & 1
        place = place[0] * 2 + place[1]
        return jnp.stack([pick(place ^ i, parts) for i in range(4)])


def pick(which, parts):
    value = parts[-1]
    for i in range(len(parts) - 2, -1, -1):
        value = jnp.where(which == i, parts[i], value)
    return value


def blocks_of(value, start, count):
    rows = lax.dynamic_slice_in_dim(value, start, count, 0)
    rows = rows.reshape(count // BLOCK, BLOCK, value.shape[1])
    return jnp.pad(rows, ((0, 0), (0, PAD - BLOCK), (0, 0)))


def rows_of(here, own, other):
    cut = [v[:, :BLOCK].reshape(-1, v.shape[2]) for v in (own, other.astype(own.dtype))]
    return jnp.concatenate(
        [jnp.where(here == 0, cut[0], cut[1]), jnp.where(here == 0, cut[1], cut[0])], axis=0
    )


def episode_starts(resets):
    rows = resets.shape[0]
    inside = lax.broadcasted_iota(jnp.int32, (rows // SEQ_LEN, SEQ_LEN), 1)
    starts = jnp.where((inside == 0) | (resets.reshape(-1, SEQ_LEN) == 1), inside, 0)
    starts = lax.cummax(starts, axis=1).reshape(rows // BLOCK, BLOCK // SEQ_LEN, SEQ_LEN)
    starts = starts + SEQ_LEN * jnp.arange(BLOCK // SEQ_LEN, dtype=jnp.int32)[None, :, None]
    starts = starts.reshape(rows // BLOCK, BLOCK)
    tail = jnp.broadcast_to(jnp.arange(BLOCK, PAD, dtype=jnp.int32), (rows // BLOCK, PAD - BLOCK))
    return jnp.concatenate([starts, tail], axis=1)[:, :, None]


def local(
    n_dp, n_tensor, frames, resets, first_gain, first_shift, qkv_weight, out_weight, out_bias, second_gain,
    second_shift, up_weight, up_bias, down_weight, down_bias, prior_gain, prior_shift, prior_weight,
    prior_bias, out_cotangent, logit_cotangent,
):
    move = Moves(n_dp, n_tensor)
    here = move.here
    core, side = move.dp & 1, (move.dp >> 1) & 1
    place = core * 2 + side
    scalars = jnp.stack([here, place]).astype(jnp.int32)
    rows, half = frames.shape
    width = 2 * half
    mine = rows // 2
    blocks = mine // BLOCK
    row = lambda v: v.reshape(1, -1)

    def both(value):
        sent = blocks_of(value, (1 - here) * mine, mine)
        return blocks_of(value, here * mine, mine), move.over(sent)

    def part(value, index, size, dim):
        return lax.dynamic_slice_in_dim(value, index * size, size, dim)

    def half_pieces(value, dim):
        size = value.shape[dim] // 2
        got = move.over(part(value, core, size, dim))
        near = move.core(got)
        return jnp.concatenate(
            [jnp.where(core == 0, got, near), jnp.where(core == 0, near, got)], axis=dim
        )

    def quarter_pieces(value, dim):
        got = move.over(part(value, place, value.shape[dim] // 4, dim))
        beside = move.side(got)
        return [got, beside, move.core(got), move.core(beside)]

    qkv_other = half_pieces(qkv_weight, 2)
    frames_own, frames_other = both(frames)
    out_other = half_pieces(out_weight, 0)
    bias_other = move.over(jnp.concatenate([up_bias, prior_bias]))
    up_pieces = quarter_pieces(up_weight, 1)
    down_pieces = quarter_pieces(down_weight, 0)
    prior_pieces = quarter_pieces(prior_weight, 1)
    logit_own, logit_other = both(logit_cotangent)
    out_own, out_other_cot = both(out_cotangent)
    hidden_width = up_bias.shape[0]
    up_bias_all = row(jnp.concatenate([up_bias, bias_other[:hidden_width]]))
    prior_bias_all = row(jnp.concatenate([prior_bias, bias_other[hidden_width:]]))
    seg = lax.dynamic_slice_in_dim(episode_starts(resets), here * blocks, blocks, 0)

    def blocked(n, dtype):
        return (jax.ShapeDtypeStruct((blocks, PAD, n), dtype), True)

    def fixed(shape, dtype):
        return (jax.ShapeDtypeStruct(shape, dtype), False)

    def b(*values):
        return [(v, True) for v in values]

    def w(*values):
        return [(v, False) for v in values]

    first, triple, mixed, middle, second = call(
        attend_kernel,
        scalars,
        b(frames_own, frames_other, seg)
        + w(row(first_gain), row(first_shift), qkv_weight, qkv_other, out_weight, out_other)
        + w(row(out_bias), row(second_gain), row(second_shift)),
        [blocked(width, BF), blocked(3 * width, BF), blocked(width, BF), blocked(width, F32), blocked(width, BF)],
        name="attend",
        flops=2 * mine * width * width * 4,
    )
    act, slope, ending, prior_in, block_own, block_send = call(
        feed_kernel,
        scalars,
        b(second, middle)
        + w(up_weight, *up_pieces, up_bias_all, down_weight, *down_pieces, row(down_bias))
        + w(row(prior_gain), row(prior_shift)),
        [blocked(2 * hidden_width, BF), blocked(2 * hidden_width, F32), blocked(width, F32)]
        + [blocked(width, BF), blocked(half, BF), blocked(half, BF)],
        name="feed",
        flops=2 * mine * width * hidden_width * 4,
    )
    block_got = move.over(block_send)
    n_logits = prior_bias.shape[0]
    logits_own, logits_send, grad_ending, ending_grad, vec_three, prior_bias_sum = call(
        prior_kernel,
        scalars,
        b(prior_in, ending)
        + w(prior_weight, *prior_pieces, prior_bias_all)
        + b(logit_own, logit_other, out_own, out_other_cot)
        + w(row(prior_gain)),
        [blocked(n_logits, F32), blocked(n_logits, BF), blocked(width, F32), blocked(width, BF)]
        + [fixed((3, width), F32), fixed((1, 2 * n_logits), F32)],
        name="prior",
        flops=2 * mine * width * n_logits * 4,
    )
    logits_got = move.over(logits_send)

    def pieces(n):
        return [fixed((4, n, 128), F32), fixed((4, n, 128), BF)], [pltpu.VMEM((4, n, 128), F32)]

    n_late = width + hidden_width
    outs, scratch = pieces(n_late)
    keep, send = call(
        late_grads_kernel,
        scalars,
        b(prior_in, logit_own, logit_other, act, ending_grad),
        outs,
        scratch,
        name="late_grads",
        flops=2 * mine * width * (2 * n_logits + 2 * hidden_width),
    )
    late = move.gather(move.reduce(keep, send))
    n_up = width * hidden_width // 512
    outs, scratch = pieces(n_up)
    grad_middle, middle_grad, vec_two, up_bias_sum, keep, send = call(
        feed_back_kernel,
        scalars,
        b(ending_grad, slope, second, middle, grad_ending)
        + w(up_weight, *up_pieces, down_weight, *down_pieces, row(second_gain)),
        [blocked(width, F32), blocked(width, BF), fixed((3, width), F32), fixed((1, 2 * hidden_width), F32)] + outs,
        scratch,
        name="feed_back",
        flops=2 * mine * width * hidden_width * 6,
    )
    middle_part = move.gather(move.reduce(keep, send))
    n_early = 256 + 768
    outs, scratch = pieces(n_early)
    frames_grad, frames_send, vec_one, keep, send = call(
        attend_back_kernel,
        scalars,
        b(middle_grad, grad_middle, frames_own, frames_other, first, triple, mixed, seg)
        + w(qkv_weight, qkv_other, out_weight, out_other, row(first_gain)),
        [blocked(half, F32), blocked(half, BF), fixed((2, width), F32)] + outs,
        scratch,
        name="attend_back",
        flops=2 * mine * width * width * 8,
    )
    frames_got = move.over(frames_send)
    early = move.gather(move.reduce(keep, send))

    def in_order(value):
        n = value.shape[1] // 2
        return jnp.where(here == 0, value[0], jnp.concatenate([value[0, n:], value[0, :n]]))

    vectors = jnp.concatenate(
        [vec_one.reshape(-1), vec_two.reshape(-1), vec_three.reshape(-1)]
        + [in_order(up_bias_sum), in_order(prior_bias_sum)]
    ).reshape(-1, 128)
    vectors = vectors + move.over(vectors)
    shift = 1
    while shift < n_dp:
        vectors = vectors + move.along(vectors, shift)
        shift *= 2
    vectors = vectors.reshape(-1)
    named = vectors[: 8 * width].reshape(8, width)
    rest = vectors[8 * width :]
    up_bias_grad = lax.dynamic_slice_in_dim(rest, here * hidden_width, hidden_width, 0)
    prior_bias_grad = lax.dynamic_slice_in_dim(rest, 2 * hidden_width + here * n_logits, n_logits, 0)

    prior_grad = late[:, :width].transpose(1, 0, 2).reshape(width, n_logits).astype(F32)
    down_grad = (
        late[:, width:].reshape(4, width // 128, -1, 128).transpose(0, 2, 1, 3).reshape(hidden_width, width)
    ).astype(F32)
    up_grad = (
        middle_part.reshape(4, -1, width, 128).transpose(2, 0, 1, 3).reshape(width, hidden_width).astype(F32)
    )
    out_grad = early[:, :256].transpose(1, 0, 2).reshape(half, width).astype(F32)
    qkv_grad = (
        early[:, 256:].reshape(4, 2, 3, 128, 128).transpose(2, 0, 3, 1, 4).reshape(3, width, half).astype(F32)
    )
    return (
        rows_of(here, block_own, block_got),
        rows_of(here, logits_own, logits_got),
        rows_of(here, frames_grad, frames_got),
        named[0],
        named[1],
        qkv_grad,
        out_grad,
        named[4],
        named[2],
        named[3],
        up_grad,
        up_bias_grad,
        down_grad,
        named[7],
        named[5],
        named[6],
        prior_grad,
        prior_bias_grad,
    )


def solution(mesh):
    rows, cols = P("dp", "tensor"), P(None, "tensor")
    placed = (
        rows, P("dp"), P(), P(), P(None, None, "tensor"), P("tensor", None), P(), P(), P(), cols, P("tensor"),
        P("tensor", None), P(), P(), P(), cols, P("tensor"), rows, rows,
    )
    given = (
        rows, rows, rows, P(), P(), P(None, None, "tensor"), P("tensor", None), P(), P(), P(), cols,
        P("tensor"), P("tensor", None), P(), P(), P(), cols, P("tensor"),
    )
    return jax.shard_map(
        functools.partial(local, mesh.shape["dp"], mesh.shape["tensor"]),
        mesh=mesh,
        in_specs=placed,
        out_specs=given,
        check_vma=False,
    )
```

```python
import functools

import jax
import jax.numpy as jnp
from jax import lax
from jax.experimental import pallas as pl
from jax.experimental.pallas import tpu as pltpu
from jax.sharding import PartitionSpec as P

HEAD_DIM = 64
SEQ_LEN = 50
BLOCK = 4 * SEQ_LEN
PAD = -(-BLOCK // 16) * 16
EPS = 1e-05
NEG = -1e30
GELU_C = 0.7978845608028654
GELU_A = 0.044715
VMEM = 48 * 1024 * 1024
BF = jnp.bfloat16
F32 = jnp.float32


def mm(a, b):
    return lax.dot_general(a, b, (((1,), (0,)), ((), ())), preferred_element_type=F32)


def mm_bt(a, b):
    return lax.dot_general(a, b, (((1,), (1,)), ((), ())), preferred_element_type=F32)


def mm_at(a, b):
    return lax.dot_general(a, b, (((0,), (0,)), ((), ())), preferred_element_type=F32)


def norm_of(value):
    centre = value - jnp.mean(value, axis=-1, keepdims=True)
    factor = lax.rsqrt(jnp.mean(centre * centre, axis=-1, keepdims=True) + EPS)
    return centre * factor, factor


def norm_back(grad, unit, factor, gain):
    scaled = grad * gain
    first = jnp.mean(scaled, axis=-1, keepdims=True)
    second = jnp.mean(scaled * unit, axis=-1, keepdims=True)
    return factor * (scaled - first - unit * second)


def col_sum(value):
    return jnp.sum(value, axis=0, keepdims=True)


def whole_row(here, own, other):
    low = jnp.where(here == 0, own, other)
    high = jnp.where(here == 0, other, own)
    return jnp.concatenate([low, high], axis=1).astype(F32)


def allowed_pairs(seg):
    seg2 = jnp.concatenate([seg, seg], axis=0)
    row = lax.broadcasted_iota(jnp.int32, (2 * PAD, PAD), 0)
    row = jnp.where(row >= PAD, row - PAD, row)
    col = lax.broadcasted_iota(jnp.int32, (2 * PAD, PAD), 1)
    return (col <= row) & (col >= seg2)


def two_heads(value):
    first = lax.broadcasted_iota(jnp.int32, value.shape, 1) < HEAD_DIM
    none = jnp.zeros_like(value)
    return jnp.concatenate([jnp.where(first, value, none), jnp.where(first, none, value)], axis=0)


def one_pair(value):
    first = lax.broadcasted_iota(jnp.int32, (PAD, 2 * HEAD_DIM), 1) < HEAD_DIM
    return jnp.where(first, value[:PAD], value[PAD:])


def softmax_of(query2, key, allowed):
    scores = jnp.where(allowed, mm_bt(query2, key) * HEAD_DIM ** (-0.5), NEG)
    expo = jnp.exp(scores - jnp.max(scores, axis=-1, keepdims=True))
    return expo / jnp.sum(expo, axis=-1, keepdims=True)


def accumulate(step, ref, index, value):
    @pl.when(step == 0)
    def _():
        ref[index] = value

    @pl.when(step != 0)
    def _():
        ref[index] += value


def attend_kernel(
    s, own, other, seg, gain, shift, qkv, qkv_o, out, out_o, out_bias, gain2, shift2,
    first_ref, triple_ref, mixed_ref, middle_ref, second_ref,
):
    frames = whole_row(s[0], own[0], other[0])
    unit, _ = norm_of(frames)
    first = (unit * gain[...] + shift[...]).astype(BF)
    first_ref[0] = first
    allowed = allowed_pairs(seg[0])
    total = frames + out_bias[...]
    for half, (weight, weight_out) in enumerate(((qkv, out), (qkv_o, out_o))):
        triple = [mm(first, weight[c]).astype(BF) for c in range(3)]
        mixed = []
        for pair in range(2):
            at = slice(pair * 128, pair * 128 + 128)
            query, key, value = (item[:, at] for item in triple)
            weights = softmax_of(two_heads(query), key, allowed).astype(BF)
            mixed.append(one_pair(mm(weights, value)).astype(BF))
        mixed = jnp.concatenate(mixed, axis=1)
        for c in range(3):
            triple_ref[0, :, (half * 3 + c) * 256 : (half * 3 + c + 1) * 256] = triple[c]
        mixed_ref[0, :, half * 256 : half * 256 + 256] = mixed
        total = total + mm(mixed, weight_out[...])
    middle_ref[0] = total
    unit2, _ = norm_of(total)
    second_ref[0] = (unit2 * gain2[...] + shift2[...]).astype(BF)


def feed_kernel(
    s, second, middle, up, u0, u1, u2, u3, up_bias, down, d0, d1, d2, d3, down_bias, gain, shift,
    act_ref, slope_ref, ending_ref, prior_in_ref, block_own_ref, block_other_ref,
):
    x = second[0]
    total = middle[0] + down_bias[...]
    ups = [up[:, i * 256 : i * 256 + 256] for i in range(4)] + [u[...] for u in (u0, u1, u2, u3)]
    downs = [down[i * 256 : i * 256 + 256, :] for i in range(4)] + [d[...] for d in (d0, d1, d2, d3)]
    half = up.shape[1]
    for i in range(8):
        if i < 4:
            at = pl.ds(i * 256, 256)
        else:
            at = pl.ds(pl.multiple_of(half + (s[1] ^ (i - 4)) * 256, 256), 256)
        hidden = mm(x, ups[i]) + up_bias[:, at]
        square = hidden * hidden
        bent = jnp.tanh(GELU_C * (hidden + GELU_A * hidden * square))
        act = (0.5 * hidden * (1.0 + bent)).astype(BF)
        slope = 0.5 * (1.0 + bent) + (0.5 * GELU_C) * hidden * (1.0 - bent * bent) * (
            1.0 + (3.0 * GELU_A) * square
        )
        act_ref[0, :, at] = act
        slope_ref[0, :, at] = slope
        total = total + mm(act, downs[i])
    ending_ref[0] = total
    unit, _ = norm_of(total)
    prior_in_ref[0] = (unit * gain[...] + shift[...]).astype(BF)
    low, high = total[:, :256].astype(BF), total[:, 256:].astype(BF)
    block_own_ref[0] = jnp.where(s[0] == 0, low, high)
    block_other_ref[0] = jnp.where(s[0] == 0, high, low)


def prior_kernel(
    s, prior_in, ending, prior, p0, p1, p2, p3, bias, logit_own, logit_other, out_own, out_other, gain,
    logits_ref, logits_other_ref, grad_ending_ref, ending_grad_ref, vec_ref, bias_ref,
):
    step = pl.program_id(0)
    half = prior.shape[1]
    x = prior_in[0]
    cot = logit_own[0]
    logits_ref[0] = mm(x, prior[...]) + bias[:, :half]
    back = mm_bt(cot, prior[...])
    accumulate(step, bias_ref, (slice(None), slice(0, half)), col_sum(cot.astype(F32)))
    cot_o = logit_other[0]
    accumulate(step, bias_ref, (slice(None), slice(half, 2 * half)), col_sum(cot_o.astype(F32)))
    for j, piece in enumerate((p0, p1, p2, p3)):
        start = pl.multiple_of((s[1] ^ j) * 128, 128)
        at = pl.ds(start, 128)
        far = pl.ds(pl.multiple_of(half + start, 128), 128)
        logits_other_ref[0, :, at] = (mm(x, piece[...]) + bias[:, far]).astype(BF)
        back = back + mm_bt(logit_other[0, :, at], piece[...])
    unit, factor = norm_of(ending[0])
    grad = whole_row(s[0], out_own[0], out_other[0]) + norm_back(back, unit, factor, gain[...])
    grad_ending_ref[0] = grad
    ending_grad_ref[0] = grad.astype(BF)
    rows = jnp.concatenate([col_sum(back * unit), col_sum(back), col_sum(grad)], axis=0)
    accumulate(step, vec_ref, (slice(0, 3), slice(None)), rows)


def piece_of(step):
    return step // 4, step % 4


def store_piece(step, keep, send, rows, value):
    place = step % 4

    @pl.when(place < 2)
    def _():
        keep[0, rows] = value

    @pl.when(place >= 2)
    def _():
        send[0, rows] = value.astype(BF)


def flat(ref):
    return ref[...].reshape(-1, ref.shape[-1])


def late_grads_kernel(s, prior_in, logit_own, logit_other, act, ending_grad, keep, send, turned):
    step = pl.program_id(0)

    @pl.when(step == 0)
    def _():
        turned[...] = flat(prior_in).T

    cot = jnp.where(step < 4, flat(logit_own), flat(logit_other))
    n = turned.shape[0]
    store_piece(step, keep, send, slice(0, n), mm(turned[...], cot))
    value = mm_at(flat(act), flat(ending_grad))
    m = value.shape[0]
    for t in range(value.shape[1] // 128):
        store_piece(step, keep, send, slice(n + t * m, n + t * m + m), value[:, t * 128 : t * 128 + 128])


def up_grads_kernel(s, second, hidden_grad, keep, send, turned):
    step = pl.program_id(0)

    @pl.when(step == 0)
    def _():
        turned[...] = flat(second).T

    value = mm(turned[...], flat(hidden_grad))
    n = value.shape[0]
    for t in range(value.shape[1] // 128):
        store_piece(step, keep, send, slice(t * n, t * n + n), value[:, t * 128 : t * 128 + 128])


def early_grads_kernel(s, mixed, middle_grad, first, triple_grad, keep, send, turned, turned_mixed):
    step = pl.program_id(0)

    @pl.when(step == 0)
    def _():
        turned[...] = flat(first).T

    @pl.when(step % 4 == 0)
    def _():
        turned_mixed[...] = flat(mixed).T

    n = turned_mixed.shape[0]
    store_piece(step, keep, send, slice(0, n), mm(turned_mixed[...], flat(middle_grad)))
    at = pl.ds(pl.multiple_of((s[1] ^ (step % 4)) * 128, 128), 128)
    value = mm(turned[at, :], flat(triple_grad))
    for c in range(3):
        for t in range(2):
            start = n + (t * 3 + c) * 128
            piece = value[:, c * 256 + t * 128 : c * 256 + t * 128 + 128]
            store_piece(step, keep, send, slice(start, start + 128), piece)


def feed_back_kernel(
    s, ending_grad, slope, second, middle, grad_ending, up, u0, u1, u2, u3, down, d0, d1, d2, d3, gain,
    hidden_grad_ref, grad_middle_ref, middle_grad_ref, vec_ref, bias_ref,
):
    step = pl.program_id(0)
    grad = ending_grad[0]
    half, n = up.shape[1], up.shape[0]
    back = jnp.zeros((PAD, n), F32)
    for i in range(8):
        if i < 4:
            at = slice(i * 256, i * 256 + 256)
            w_up, w_down = up[:, at], down[at, :]
        else:
            at = pl.ds(pl.multiple_of(half + (s[1] ^ (i - 4)) * 256, 256), 256)
            w_up, w_down = (u0, u1, u2, u3)[i - 4][...], (d0, d1, d2, d3)[i - 4][...]
        low = (mm_bt(grad, w_down) * slope[0, :, at]).astype(BF)
        hidden_grad_ref[0, :, at] = low
        accumulate(step, bias_ref, (slice(None), at), col_sum(low.astype(F32)))
        back = back + mm_bt(low, w_up)
    unit, factor = norm_of(middle[0])
    total = grad_ending[0] + norm_back(back, unit, factor, gain[...])
    grad_middle_ref[0] = total
    middle_grad_ref[0] = total.astype(BF)
    rows = jnp.concatenate([col_sum(back * unit), col_sum(back), col_sum(total)], axis=0)
    accumulate(step, vec_ref, (slice(0, 3), slice(None)), rows)


def attend_back_kernel(
    s, middle_grad, grad_middle, own, other, triple, seg, qkv, qkv_o, out, out_o, gain,
    triple_grad_ref, frames_own_ref, frames_other_ref, vec_ref,
):
    step = pl.program_id(0)
    grad = middle_grad[0]
    allowed = allowed_pairs(seg[0])
    factor = HEAD_DIM ** (-0.5)
    back = jnp.zeros(grad.shape, F32)
    for h, (weight, weight_out) in enumerate(((qkv, out), (qkv_o, out_o))):
        mixed_grad = mm_bt(grad, weight_out[...]).astype(BF)
        thirds = ([], [], [])
        for pair in range(2):
            at = slice(pair * 128, pair * 128 + 128)
            query, key, value = (
                triple[0, :, (h * 3 + c) * 256 + pair * 128 : (h * 3 + c) * 256 + pair * 128 + 128]
                for c in range(3)
            )
            query2 = two_heads(query)
            mixed2 = two_heads(mixed_grad[:, at])
            again = softmax_of(query2, key, allowed)
            weight_grad = mm_bt(mixed2, value)
            inner = jnp.sum(again * weight_grad, axis=-1, keepdims=True)
            score_grad = (again * (weight_grad - inner)).astype(BF)
            thirds[0].append((one_pair(mm(score_grad, key)) * factor).astype(BF))
            thirds[1].append((mm_at(score_grad, query2) * factor).astype(BF))
            thirds[2].append(mm_at(again.astype(BF), mixed2).astype(BF))
        for c in range(3):
            part = jnp.concatenate(thirds[c], axis=1)
            triple_grad_ref[0, :, (h * 3 + c) * 256 : (h * 3 + c) * 256 + 256] = part
            back = back + mm_bt(part, weight[c])
    unit, scale = norm_of(whole_row(s[0], own[0], other[0]))
    total = grad_middle[0] + norm_back(back, unit, scale, gain[...])
    low, high = total[:, :256], total[:, 256:]
    frames_own_ref[0] = jnp.where(s[0] == 0, low, high)
    frames_other_ref[0] = jnp.where(s[0] == 0, high, low).astype(BF)
    rows = jnp.concatenate([col_sum(back * unit), col_sum(back)], axis=0)
    accumulate(step, vec_ref, (slice(0, 2), slice(None)), rows)


def pieces_call(kernel, scalars, ins, n, scratch, name, flops):
    def spec(value, width, at):
        if width is None:
            return pl.BlockSpec(value.shape, lambda i, s: (0, 0, 0))
        return pl.BlockSpec((*value.shape[:2], width), lambda i, s: (0, 0, at(i, s)))

    moved = sum(v.size * v.dtype.itemsize for v, _, _ in ins) + 24 * n * 128
    return pl.pallas_call(
        kernel,
        grid_spec=pltpu.PrefetchScalarGridSpec(
            num_scalar_prefetch=1,
            grid=(8,),
            in_specs=[spec(*entry) for entry in ins],
            out_specs=[
                pl.BlockSpec((1, n, 128), lambda i, s: ((i // 4) * 2 + jnp.minimum(i % 4, 1), 0, 0)),
                pl.BlockSpec(
                    (1, n, 128), lambda i, s: (jnp.maximum((i // 4) * 2 + jnp.maximum(i % 4, 1) - 2, 0), 0, 0)
                ),
            ],
            scratch_shapes=list(scratch),
        ),
        out_shape=[jax.ShapeDtypeStruct((4, n, 128), F32), jax.ShapeDtypeStruct((4, n, 128), BF)],
        compiler_params=pltpu.CompilerParams(vmem_limit_bytes=VMEM),
        cost_estimate=pl.CostEstimate(flops=flops, bytes_accessed=moved, transcendentals=0),
        name=name,
    )(scalars, *[v for v, _, _ in ins])


def call(kernel, scalars, ins, outs, scratch=(), name=None, flops=0):
    steps = next(value.shape[0] for value, blocked in ins if blocked)

    def spec(shape, blocked):
        if blocked:
            return pl.BlockSpec((1,) + tuple(shape[1:]), lambda b, s: (b,) + (0,) * (len(shape) - 1))
        return pl.BlockSpec(tuple(shape), lambda b, s: (0,) * len(shape))

    moved = sum(v.size * v.dtype.itemsize for v, _ in ins) + sum(
        o.size * o.dtype.itemsize for o, _ in outs
    )
    return pl.pallas_call(
        kernel,
        grid_spec=pltpu.PrefetchScalarGridSpec(
            num_scalar_prefetch=1,
            grid=(steps,),
            in_specs=[spec(v.shape, blocked) for v, blocked in ins],
            out_specs=[spec(o.shape, blocked) for o, blocked in outs],
            scratch_shapes=list(scratch),
        ),
        out_shape=[o for o, _ in outs],
        compiler_params=pltpu.CompilerParams(vmem_limit_bytes=VMEM),
        cost_estimate=pl.CostEstimate(flops=flops, bytes_accessed=moved, transcendentals=0),
        name=name,
    )(scalars, *[v for v, _ in ins])


def swap(value, axes, sizes, mask):
    count = 1
    for size in sizes:
        count *= size
    return lax.ppermute(value, axes, [(i, i ^ mask) for i in range(count)])


class Moves:
    def __init__(self, n_dp, n_tensor):
        self.n_dp, self.n_tensor = n_dp, n_tensor
        self.dp = lax.axis_index("dp")
        self.here = lax.axis_index("tensor")

    def along(self, value, mask):
        return swap(value, "dp", (self.n_dp,), mask)

    def core(self, value):
        return self.along(value, 1)

    def side(self, value):
        return self.along(value, 2)

    def over(self, value):
        return swap(value, "tensor", (self.n_tensor,), 1)

    def cross(self, value):
        return swap(value, ("dp", "tensor"), (self.n_dp, self.n_tensor), 5)

    def groups(self):
        shift, rest = 2, self.n_dp // 4
        while rest > 1:
            size = 4 if rest % 4 == 0 else 2
            yield shift, size
            shift, rest = shift + (2 if size == 4 else 1), rest // size

    def reduce(self, keep, sent):
        total = keep + self.core(sent)
        parts = [total[i].astype(BF) for i in (1, 2, 3)]
        total = total[0] + self.side(parts[0]) + self.over(parts[1]) + self.cross(parts[2])
        for shift, size in self.groups():
            mine = (self.dp >> shift) & (size - 1)
            split = total.reshape(size, total.shape[0] // size, total.shape[1])
            total = lax.dynamic_index_in_dim(split, mine, 0, False)
            for k in range(1, size):
                part = lax.dynamic_index_in_dim(split, mine ^ k, 0, False).astype(BF)
                total = total + self.along(part, k << shift)
        return total

    def gather(self, total):
        total = total.astype(BF)
        for shift, size in reversed(list(self.groups())):
            mine = (self.dp >> shift) & (size - 1)
            parts = [total] + [self.along(total, k << shift) for k in range(1, size)]
            total = jnp.concatenate([pick(mine ^ i, parts) for i in range(size)], axis=0)
        near = self.side(total)
        far = self.core(jnp.stack([total, near]))
        parts = [total, near, far[0], far[1]]
        place = self.dp & 1, (self.dp >> 1) & 1
        place = place[0] * 2 + place[1]
        return jnp.stack([pick(place ^ i, parts) for i in range(4)])


def pick(which, parts):
    value = parts[-1]
    for i in range(len(parts) - 2, -1, -1):
        value = jnp.where(which == i, parts[i], value)
    return value


def blocks_of(value, start, count):
    rows = lax.dynamic_slice_in_dim(value, start, count, 0)
    rows = rows.reshape(count // BLOCK, BLOCK, value.shape[1])
    return jnp.pad(rows, ((0, 0), (0, PAD - BLOCK), (0, 0)))


def rows_of(here, own, other):
    cut = [v[:, :BLOCK].reshape(-1, v.shape[2]) for v in (own, other.astype(own.dtype))]
    return jnp.concatenate(
        [jnp.where(here == 0, cut[0], cut[1]), jnp.where(here == 0, cut[1], cut[0])], axis=0
    )


def episode_starts(resets):
    rows = resets.shape[0]
    inside = lax.broadcasted_iota(jnp.int32, (rows // SEQ_LEN, SEQ_LEN), 1)
    starts = jnp.where((inside == 0) | (resets.reshape(-1, SEQ_LEN) == 1), inside, 0)
    starts = lax.cummax(starts, axis=1).reshape(rows // BLOCK, BLOCK // SEQ_LEN, SEQ_LEN)
    starts = starts + SEQ_LEN * jnp.arange(BLOCK // SEQ_LEN, dtype=jnp.int32)[None, :, None]
    starts = starts.reshape(rows // BLOCK, BLOCK)
    tail = jnp.broadcast_to(jnp.arange(BLOCK, PAD, dtype=jnp.int32), (rows // BLOCK, PAD - BLOCK))
    return jnp.concatenate([starts, tail], axis=1)[:, :, None]


def local(
    n_dp, n_tensor, frames, resets, first_gain, first_shift, qkv_weight, out_weight, out_bias, second_gain,
    second_shift, up_weight, up_bias, down_weight, down_bias, prior_gain, prior_shift, prior_weight,
    prior_bias, out_cotangent, logit_cotangent,
):
    move = Moves(n_dp, n_tensor)
    here = move.here
    core, side = move.dp & 1, (move.dp >> 1) & 1
    place = core * 2 + side
    scalars = jnp.stack([here, place]).astype(jnp.int32)
    rows, half = frames.shape
    width = 2 * half
    mine = rows // 2
    blocks = mine // BLOCK
    row = lambda v: v.reshape(1, -1)

    def both(value):
        sent = blocks_of(value, (1 - here) * mine, mine)
        return blocks_of(value, here * mine, mine), move.over(sent)

    def part(value, index, size, dim):
        return lax.dynamic_slice_in_dim(value, index * size, size, dim)

    def half_pieces(value, dim):
        size = value.shape[dim] // 2
        got = move.over(part(value, core, size, dim))
        near = move.core(got)
        return jnp.concatenate(
            [jnp.where(core == 0, got, near), jnp.where(core == 0, near, got)], axis=dim
        )

    def quarter_pieces(value, dim):
        got = move.over(part(value, place, value.shape[dim] // 4, dim))
        beside = move.side(got)
        return [got, beside, move.core(got), move.core(beside)]

    qkv_other = half_pieces(qkv_weight, 2)
    frames_own, frames_other = both(frames)
    out_other = half_pieces(out_weight, 0)
    bias_other = move.over(jnp.concatenate([up_bias, prior_bias]))
    up_pieces = quarter_pieces(up_weight, 1)
    down_pieces = quarter_pieces(down_weight, 0)
    prior_pieces = quarter_pieces(prior_weight, 1)
    logit_own, logit_other = both(logit_cotangent)
    out_own, out_other_cot = both(out_cotangent)
    hidden_width = up_bias.shape[0]
    up_bias_all = row(jnp.concatenate([up_bias, bias_other[:hidden_width]]))
    prior_bias_all = row(jnp.concatenate([prior_bias, bias_other[hidden_width:]]))
    seg = lax.dynamic_slice_in_dim(episode_starts(resets), here * blocks, blocks, 0)

    def blocked(n, dtype):
        return (jax.ShapeDtypeStruct((blocks, PAD, n), dtype), True)

    def fixed(shape, dtype):
        return (jax.ShapeDtypeStruct(shape, dtype), False)

    def b(*values):
        return [(v, True) for v in values]

    def w(*values):
        return [(v, False) for v in values]

    first, triple, mixed, middle, second = call(
        attend_kernel,
        scalars,
        b(frames_own, frames_other, seg)
        + w(row(first_gain), row(first_shift), qkv_weight, qkv_other, out_weight, out_other)
        + w(row(out_bias), row(second_gain), row(second_shift)),
        [blocked(width, BF), blocked(3 * width, BF), blocked(width, BF), blocked(width, F32), blocked(width, BF)],
        name="attend",
        flops=2 * mine * width * width * 4,
    )
    act, slope, ending, prior_in, block_own, block_send = call(
        feed_kernel,
        scalars,
        b(second, middle)
        + w(up_weight, *up_pieces, up_bias_all, down_weight, *down_pieces, row(down_bias))
        + w(row(prior_gain), row(prior_shift)),
        [blocked(2 * hidden_width, BF), blocked(2 * hidden_width, F32), blocked(width, F32)]
        + [blocked(width, BF), blocked(half, BF), blocked(half, BF)],
        name="feed",
        flops=2 * mine * width * hidden_width * 4,
    )
    block_got = move.over(block_send)
    n_logits = prior_bias.shape[0]
    logits_own, logits_send, grad_ending, ending_grad, vec_three, prior_bias_sum = call(
        prior_kernel,
        scalars,
        b(prior_in, ending)
        + w(prior_weight, *prior_pieces, prior_bias_all)
        + b(logit_own, logit_other, out_own, out_other_cot)
        + w(row(prior_gain)),
        [blocked(n_logits, F32), blocked(n_logits, BF), blocked(width, F32), blocked(width, BF)]
        + [fixed((3, width), F32), fixed((1, 2 * n_logits), F32)],
        name="prior",
        flops=2 * mine * width * n_logits * 4,
    )
    logits_got = move.over(logits_send)

    turned = pltpu.VMEM((width, blocks * PAD), BF)
    n_late = width + hidden_width
    keep, send = pieces_call(
        late_grads_kernel,
        scalars,
        [
            (prior_in, None, None),
            (logit_own, 128, lambda i, s: s[1] ^ jnp.minimum(i, 3)),
            (logit_other, 128, lambda i, s: s[1] ^ jnp.maximum(i - 4, 0)),
            (act, 256, lambda i, s: (i // 4) * 4 + (s[1] ^ (i % 4))),
            (ending_grad, None, None),
        ],
        n_late,
        [turned],
        "late_grads",
        2 * mine * width * (2 * n_logits + 2 * hidden_width),
    )
    late = move.gather(move.reduce(keep, send))
    hidden_grad, grad_middle, middle_grad, vec_two, up_bias_sum = call(
        feed_back_kernel,
        scalars,
        b(ending_grad, slope, second, middle, grad_ending)
        + w(up_weight, *up_pieces, down_weight, *down_pieces, row(second_gain)),
        [blocked(2 * hidden_width, BF), blocked(width, F32), blocked(width, BF)]
        + [fixed((3, width), F32), fixed((1, 2 * hidden_width), F32)],
        name="feed_back",
        flops=2 * mine * width * hidden_width * 4,
    )
    n_up = width * hidden_width // 512
    keep, send = pieces_call(
        up_grads_kernel,
        scalars,
        [(second, None, None), (hidden_grad, 256, lambda i, s: (i // 4) * 4 + (s[1] ^ (i % 4)))],
        n_up,
        [turned],
        "up_grads",
        2 * mine * width * hidden_width * 2,
    )
    middle_part = move.gather(move.reduce(keep, send))
    triple_grad, frames_grad, frames_send, vec_one = call(
        attend_back_kernel,
        scalars,
        b(middle_grad, grad_middle, frames_own, frames_other, triple, seg)
        + w(qkv_weight, qkv_other, out_weight, out_other, row(first_gain)),
        [blocked(3 * width, BF), blocked(half, F32), blocked(half, BF), fixed((2, width), F32)],
        name="attend_back",
        flops=2 * mine * width * width * 4,
    )
    n_early = 256 + 768
    keep, send = pieces_call(
        early_grads_kernel,
        scalars,
        [
            (mixed, 256, lambda i, s: i // 4),
            (middle_grad, 128, lambda i, s: s[1] ^ (i % 4)),
            (first, None, None),
            (triple_grad, 768, lambda i, s: i // 4),
        ],
        n_early,
        [turned, pltpu.VMEM((256, blocks * PAD), BF)],
        "early_grads",
        2 * mine * width * width * 4,
    )
    frames_got = move.over(frames_send)
    early = move.gather(move.reduce(keep, send))

    def in_order(value):
        n = value.shape[1] // 2
        return jnp.where(here == 0, value[0], jnp.concatenate([value[0, n:], value[0, :n]]))

    vectors = jnp.concatenate(
        [vec_one.reshape(-1), vec_two.reshape(-1), vec_three.reshape(-1)]
        + [in_order(up_bias_sum), in_order(prior_bias_sum)]
    ).reshape(-1, 128)
    vectors = vectors + move.over(vectors)
    shift = 1
    while shift < n_dp:
        vectors = vectors + move.along(vectors, shift)
        shift *= 2
    vectors = vectors.reshape(-1)
    named = vectors[: 8 * width].reshape(8, width)
    rest = vectors[8 * width :]
    up_bias_grad = lax.dynamic_slice_in_dim(rest, here * hidden_width, hidden_width, 0)
    prior_bias_grad = lax.dynamic_slice_in_dim(rest, 2 * hidden_width + here * n_logits, n_logits, 0)

    prior_grad = late[:, :width].transpose(1, 0, 2).reshape(width, n_logits).astype(F32)
    down_grad = (
        late[:, width:].reshape(4, width // 128, -1, 128).transpose(0, 2, 1, 3).reshape(hidden_width, width)
    ).astype(F32)
    up_grad = (
        middle_part.reshape(4, -1, width, 128).transpose(2, 0, 1, 3).reshape(width, hidden_width).astype(F32)
    )
    out_grad = early[:, :256].transpose(1, 0, 2).reshape(half, width).astype(F32)
    qkv_grad = (
        early[:, 256:].reshape(4, 2, 3, 128, 128).transpose(2, 0, 3, 1, 4).reshape(3, width, half).astype(F32)
    )
    return (
        rows_of(here, block_own, block_got),
        rows_of(here, logits_own, logits_got),
        rows_of(here, frames_grad, frames_got),
        named[0],
        named[1],
        qkv_grad,
        out_grad,
        named[4],
        named[2],
        named[3],
        up_grad,
        up_bias_grad,
        down_grad,
        named[7],
        named[5],
        named[6],
        prior_grad,
        prior_bias_grad,
    )


def solution(mesh):
    rows, cols = P("dp", "tensor"), P(None, "tensor")
    placed = (
        rows, P("dp"), P(), P(), P(None, None, "tensor"), P("tensor", None), P(), P(), P(), cols, P("tensor"),
        P("tensor", None), P(), P(), P(), cols, P("tensor"), rows, rows,
    )
    given = (
        rows, rows, rows, P(), P(), P(None, None, "tensor"), P("tensor", None), P(), P(), P(), cols,
        P("tensor"), P("tensor", None), P(), P(), P(), cols, P("tensor"),
    )
    return jax.shard_map(
        functools.partial(local, mesh.shape["dp"], mesh.shape["tensor"]),
        mesh=mesh,
        in_specs=placed,
        out_specs=given,
        check_vma=False,
    )
```

```python
import functools
import math

import jax
import jax.numpy as jnp
from jax import lax
from jax.experimental import pallas as pl
from jax.experimental.pallas import tpu as pltpu
from jax.sharding import PartitionSpec as P

HEAD_DIM = 64
SEQ_LEN = 50
BLOCK = 4 * SEQ_LEN
PAD = -(-BLOCK // 16) * 16
EPS = 1e-05
NEG = -1e30
GELU_C = 0.7978845608028654
GELU_A = 0.044715
SPILL = 8 * 1024 * 1024
BF = jnp.bfloat16
F32 = jnp.float32
FIRST_GAIN, FIRST_SHIFT, OUT_BIAS, SECOND_GAIN, SECOND_SHIFT, DOWN_BIAS, PRIOR_GAIN, PRIOR_SHIFT, UP_BIAS, PRIOR_BIAS = range(10)


def mm(a, b):
    return lax.dot_general(a, b, (((1,), (0,)), ((), ())), preferred_element_type=F32)


def mm_bt(a, b):
    return lax.dot_general(a, b, (((1,), (1,)), ((), ())), preferred_element_type=F32)


def mm_at(a, b):
    return lax.dot_general(a, b, (((0,), (0,)), ((), ())), preferred_element_type=F32)


def norm_of(value):
    centre = value - jnp.mean(value, axis=-1, keepdims=True)
    factor = lax.rsqrt(jnp.mean(centre * centre, axis=-1, keepdims=True) + EPS)
    return centre * factor, factor


def norm_back(grad, unit, factor, gain):
    scaled = grad * gain
    first = jnp.mean(scaled, axis=-1, keepdims=True)
    second = jnp.mean(scaled * unit, axis=-1, keepdims=True)
    return factor * (scaled - first - unit * second)


def col_sum(value):
    return jnp.sum(value, axis=0, keepdims=True)


def whole_rows(here, own, other):
    low = jnp.where(here == 0, own[...], other[...])
    high = jnp.where(here == 0, other[...], own[...])
    return jnp.concatenate([low, high], axis=1).astype(F32)


def in_order(core, got, near, axis):
    low = jnp.where(core == 0, got, near)
    high = jnp.where(core == 0, near, got)
    return jnp.concatenate([low, high], axis=axis)


def allowed_pairs(seg):
    seg2 = jnp.concatenate([seg, seg], axis=0)
    row = lax.broadcasted_iota(jnp.int32, (2 * PAD, PAD), 0)
    row = jnp.where(row >= PAD, row - PAD, row)
    col = lax.broadcasted_iota(jnp.int32, (2 * PAD, PAD), 1)
    return (col <= row) & (col >= seg2)


def two_heads(value):
    first = lax.broadcasted_iota(jnp.int32, value.shape, 1) < HEAD_DIM
    none = jnp.zeros_like(value)
    return jnp.concatenate([jnp.where(first, value, none), jnp.where(first, none, value)], axis=0)


def one_pair(value):
    first = lax.broadcasted_iota(jnp.int32, (PAD, 2 * HEAD_DIM), 1) < HEAD_DIM
    return jnp.where(first, value[:PAD], value[PAD:])


def softmax_of(query2, key, allowed):
    scores = jnp.where(allowed, mm_bt(query2, key), NEG)
    expo = jnp.exp(scores - jnp.max(scores, axis=-1, keepdims=True))
    return expo * (1.0 / jnp.sum(expo, axis=-1, keepdims=True))


def vector(small, index, n):
    return small[index : index + 1, :n]


def blocks_in(ref):
    return [slice(i * PAD, i * PAD + PAD) for i in range(ref.shape[0] // PAD)]


def add_up(sums, values):
    return [v if s is None else s + v for s, v in zip(sums, values, strict=True)]


def split_rows(half, source, own, sent, wide_rows):
    rows, n = source.shape
    wide_rows[0:rows, 0:n] = source[...].astype(F32)
    for which, target in ((half, own), (1 - half, sent)):
        for block, at in enumerate(blocks_in(target)):
            start = pl.multiple_of(which * (rows // 2) + block * BLOCK, 8)
            part = wide_rows[pl.ds(start, PAD), 0:n]
            inside = lax.broadcasted_iota(jnp.int32, part.shape, 0) < BLOCK
            target[at, :] = jnp.where(inside, part, 0.0).astype(BF)


def first_kernel(s, frames, qkv, up, prior, down, out, *refs):
    smalls, (qkv_ref, sent_ref, wide_ref, tall_ref, bias_ref, own_ref, small_ref, wide_rows) = refs[:-8], refs[-8:]
    qkv_ref[...] = qkv[...]
    split_rows(s[0], frames, own_ref, sent_ref, wide_rows)
    n, m = up.shape[1], down.shape[0]
    wide_ref[:, :n] = up[...]
    wide_ref[:, n:] = prior[...]
    tall_ref[:m, :] = down[...]
    tall_ref[m:, :] = out[...]
    for i, ref in enumerate(smalls):
        small_ref[i : i + 1, : ref.shape[1]] = ref[...]
    n = smalls[UP_BIAS].shape[1]
    bias_ref[:, :n] = smalls[UP_BIAS][...]
    bias_ref[:, n:] = smalls[PRIOR_BIAS][...]


def cotangents_kernel(s, logit, out, logit_sent, out_sent, logit_own, out_own, wide_rows):
    split_rows(s[0], logit, logit_own, logit_sent, wide_rows)
    split_rows(s[0], out, out_own, out_sent, wide_rows)


def gate(values, after, name=None):
    def run(*refs):
        pass

    near = pl.BlockSpec(memory_space=pltpu.VMEM)
    return pl.pallas_call(
        run,
        in_specs=[near] * (len(values) + len(after)),
        out_specs=[near] * len(values),
        out_shape=[pltpu.VMEM(v.shape, v.dtype) for v in values],
        input_output_aliases={i: i for i in range(len(values))},
        name=name,
    )(*[pin(v) for v in values], *[pin(v) for v in after])


def attend_kernel(
    s, own, other, seg, small, qkv, got, near,
    first_ref, triple_ref, mixed_ref, qkv_other_ref,
):
    unit, _ = norm_of(whole_rows(s[0], own, other))
    n = first_ref.shape[1]
    first_ref[...] = (unit * vector(small, FIRST_GAIN, n) + vector(small, FIRST_SHIFT, n)).astype(BF)
    for c in range(3):
        qkv_other_ref[c] = in_order(s[2], got[c], near[c], 1)
        for half, weight in enumerate((qkv, qkv_other_ref)):
            value = mm(first_ref[...], weight[c]).astype(BF)
            triple_ref[:, (half * 3 + c) * 256 : (half * 3 + c + 1) * 256] = value
    for at in blocks_in(own):
        allowed = allowed_pairs(seg[at, :])
        for pair in range(4):
            start = (pair // 2) * 768 + (pair % 2) * 128
            query, key, value = (
                triple_ref[at, start + c * 256 : start + c * 256 + 128] for c in range(3)
            )
            query2 = two_heads(query * HEAD_DIM ** (-0.5))
            weights = softmax_of(query2, key, allowed).astype(BF)
            mixed_ref[at, pair * 128 : pair * 128 + 128] = one_pair(mm(weights, value)).astype(BF)


def feed_kernel(
    s, own, other, mixed, small, out, t0, t1, t2, t3, up, down, w0, w1, w2, w3, bias_other,
    block_other_ref, block_own_ref, middle_ref, second_ref, act_ref, slope_ref, ending_ref, prior_in_ref,
    out_other_ref,
):
    n, half = out.shape[0], up.shape[1]
    for j, piece in enumerate((t0, t1, t2, t3)):
        size = n // 4
        out_other_ref[pl.ds(pl.multiple_of((s[1] ^ j) * size, 16), size), :] = piece[256:, :]
    middle_ref[...] = (
        whole_rows(s[0], own, other)
        + vector(small, OUT_BIAS, middle_ref.shape[1])
        + mm(mixed[:, :n], out[...])
        + mm(mixed[:, n:], out_other_ref[...])
    )
    unit, _ = norm_of(middle_ref[...])
    wide = middle_ref.shape[1]
    second_ref[...] = (unit * vector(small, SECOND_GAIN, wide) + vector(small, SECOND_SHIFT, wide)).astype(BF)
    ending_ref[...] = middle_ref[...] + vector(small, DOWN_BIAS, wide)
    for i in range(8):
        if i < 4:
            at = slice(i * 256, i * 256 + 256)
            w_up, w_down, bias = up[:, at], down[at, :], small[UP_BIAS : UP_BIAS + 1, at]
        else:
            place = pl.multiple_of((s[1] ^ (i - 4)) * 256, 256)
            at = pl.ds(pl.multiple_of(half + place, 256), 256)
            w_up, w_down = (w0, w1, w2, w3)[i - 4][:, :256], (t0, t1, t2, t3)[i - 4][:256, :]
            bias = bias_other[:, pl.ds(place, 256)]
        for rows in blocks_in(own):
            hidden = mm(second_ref[rows, :], w_up) + bias
            square = hidden * hidden
            bent = jnp.tanh(GELU_C * (hidden + GELU_A * hidden * square))
            act = (0.5 * hidden * (1.0 + bent)).astype(BF)
            slope = 0.5 * (1.0 + bent) + (0.5 * GELU_C) * hidden * (1.0 - bent * bent) * (
                1.0 + (3.0 * GELU_A) * square
            )
            act_ref[rows, at] = act
            slope_ref[rows, at] = slope
            ending_ref[rows, :] += mm(act, w_down)
    total = ending_ref[...]
    unit, _ = norm_of(total)
    prior_in_ref[...] = (unit * vector(small, PRIOR_GAIN, wide) + vector(small, PRIOR_SHIFT, wide)).astype(BF)
    low, high = total[:, :256].astype(BF), total[:, 256:].astype(BF)
    block_own_ref[...] = jnp.where(s[0] == 0, low, high)
    block_other_ref[...] = jnp.where(s[0] == 0, high, low)


def prior_kernel(
    s, prior_in, ending, small, logit_own, out_own, prior, w0, w1, w2, w3, logit_other, out_other, bias_other,
    logits_other_ref, logits_ref, grad_ending_ref, ending_grad_ref, vec_ref, bias_ref, weight,
):
    half = prior.shape[1]
    for j, piece in enumerate((w0, w1, w2, w3)):
        weight[:, pl.ds(pl.multiple_of((s[1] ^ j) * 128, 128), 128)] = piece[:, 256:]
    logits_other_ref[...] = (mm(prior_in[...], weight[...]) + bias_other[:, -half:]).astype(BF)
    logits_ref[...] = mm(prior_in[...], prior[...]) + vector(small, PRIOR_BIAS, half)
    logits_ref.send()
    back = mm_bt(logit_own[...], prior[...]) + mm_bt(logit_other[...], weight[...])
    unit, factor = norm_of(ending[...])
    gain = vector(small, PRIOR_GAIN, unit.shape[1])
    grad = whole_rows(s[0], out_own, out_other) + norm_back(back, unit, factor, gain)
    grad_ending_ref[...] = grad
    ending_grad_ref[...] = grad.astype(BF)
    vec_ref[...] = jnp.concatenate([col_sum(back * unit), col_sum(back), col_sum(grad)], axis=0)
    bias_ref[:, :half] = col_sum(logit_own[...].astype(F32))
    bias_ref[:, half:] = col_sum(logit_other[...].astype(F32))


def store_piece(keep, send, h, j, start, value):
    at = slice(start, start + value.shape[0])
    if j < 2:
        keep[h * 2 + j, at, :] = value
    else:
        send[h * 2 + j - 2, at, :] = value.astype(BF)


def late_grads_kernel(s, prior_in, logit_own, logit_other, act, ending_grad, keep, send, wide):
    half = act.shape[1] // 2
    n = prior_in.shape[1]
    for h in range(2):
        wide[...] = mm_at(prior_in[...], (logit_own, logit_other)[h][...])
        for j in (2, 3, 0, 1):
            place = s[1] ^ j
            store_piece(keep, send, h, j, 0, wide[:, pl.ds(pl.multiple_of(place * 128, 128), 128)])
            part = act[:, pl.ds(pl.multiple_of(h * half + place * 256, 256), 256)]
            value = mm_at(part, ending_grad[...])
            for t in range(n // 128):
                store_piece(keep, send, h, j, n + t * 256, value[:, t * 128 : t * 128 + 128])


def up_grads_kernel(s, second, hidden_grad, keep, send, turned):
    turned[...] = second[...].T
    half = hidden_grad.shape[1] // 2
    n = second.shape[1]
    for h in range(2):
        for j in (2, 3, 0, 1):
            at = pl.ds(pl.multiple_of(h * half + (s[1] ^ j) * 256, 256), 256)
            value = mm(turned[...], hidden_grad[:, at])
            for t in range(2):
                store_piece(keep, send, h, j, t * n, value[:, t * 128 : t * 128 + 128])


def early_grads_kernel(
    s, mixed, middle_grad, first, triple_grad, vec_one, vec_two, vec_three, bias_up, bias_prior,
    keep, send, wide, vectors,
):
    row = 0
    for ref in (vec_one, vec_two, vec_three):
        for i in range(ref.shape[0]):
            for t in range(ref.shape[1] // 128):
                vectors[row : row + 1, :] = ref[i : i + 1, t * 128 : t * 128 + 128]
                row += 1
    for ref in (bias_up, bias_prior):
        tiles = ref.shape[1] // 128
        for t in range(tiles):
            place = row + lax.rem(t + s[0] * (tiles // 2), tiles)
            vectors[pl.ds(place, 1), :] = ref[:, t * 128 : t * 128 + 128]
        row += tiles
    vectors[row:, :] = jnp.zeros((vectors.shape[0] - row, 128), F32)
    m = mixed.shape[1] // 2
    for h in range(2):
        wide[...] = mm_at(mixed[:, h * m : h * m + m], middle_grad[...])
        for j in (2, 3, 0, 1):
            place = pl.multiple_of((s[1] ^ j) * 128, 128)
            store_piece(keep, send, h, j, 0, wide[:, pl.ds(place, 128)])
            value = mm_at(first[:, pl.ds(place, 128)], triple_grad[:, h * 768 : h * 768 + 768])
            for c in range(3):
                for t in range(2):
                    at = slice(c * 256 + t * 128, c * 256 + t * 128 + 128)
                    store_piece(keep, send, h, j, m + (t * 3 + c) * 128, value[:, at])
            part = vectors[(h * 2 + j % 2) * 16 : (h * 2 + j % 2) * 16 + 16, :]
            store_piece(keep, send, h, j, m + 768, part)


def feed_back_kernel(
    s, ending_grad, slope, middle, grad_ending, small, down, up, t0, w0, t1, w1, t2, w2, t3, w3,
    hidden_grad_ref, grad_middle_ref, middle_grad_ref, vec_ref, bias_ref, back,
):
    half = up.shape[1]
    for i in range(8):
        if i < 4:
            at = slice(i * 256, i * 256 + 256)
            w_up, w_down = up[:, at], down[at, :]
        else:
            at = pl.ds(pl.multiple_of(half + (s[1] ^ (i - 4)) * 256, 256), 256)
            w_up, w_down = (w0, w1, w2, w3)[i - 4][:, :256], (t0, t1, t2, t3)[i - 4][:256, :]
        sums = [None]
        for rows in blocks_in(ending_grad):
            low = (mm_bt(ending_grad[rows, :], w_down) * slope[rows, at]).astype(BF)
            hidden_grad_ref[rows, at] = low
            sums = add_up(sums, [col_sum(low.astype(F32))])
            value = mm_bt(low, w_up)
            if i == 0:
                back[rows, :] = value
            else:
                back[rows, :] += value
        bias_ref[:, at] = sums[0]
    unit, factor = norm_of(middle[...])
    value = back[...]
    gain = vector(small, SECOND_GAIN, unit.shape[1])
    total = grad_ending[...] + norm_back(value, unit, factor, gain)
    grad_middle_ref[...] = total
    middle_grad_ref[...] = total.astype(BF)
    vec_ref[...] = jnp.concatenate([col_sum(value * unit), col_sum(value), col_sum(total)], axis=0)


def attend_back_kernel(
    s, middle_grad, grad_middle, own, triple, qkv_other, out_other, small, out, seg, other, qkv,
    triple_grad_ref, frames_other_ref, frames_own_ref, vec_ref, mixed_grad,
):
    n = out.shape[0]
    mixed_grad[:, :n] = mm_bt(middle_grad[...], out[...]).astype(BF)
    mixed_grad[:, n:] = mm_bt(middle_grad[...], out_other[...]).astype(BF)
    factor = HEAD_DIM ** (-0.5)
    for at in blocks_in(own):
        allowed = allowed_pairs(seg[at, :])
        for pair in range(4):
            start = (pair // 2) * 768 + (pair % 2) * 128
            query, key, value = (triple[at, start + c * 256 : start + c * 256 + 128] for c in range(3))
            query2 = two_heads(query * factor)
            mixed2 = two_heads(mixed_grad[at, pair * 128 : pair * 128 + 128])
            again = softmax_of(query2, key, allowed)
            weight_grad = mm_bt(mixed2, value)
            inner = jnp.sum(again * weight_grad, axis=-1, keepdims=True)
            score_grad = (again * (weight_grad - inner)).astype(BF)
            thirds = (
                (one_pair(mm(score_grad, key)) * factor).astype(BF),
                mm_at(score_grad, query2).astype(BF),
                mm_at(again.astype(BF), mixed2).astype(BF),
            )
            for c in range(3):
                triple_grad_ref[at, start + c * 256 : start + c * 256 + 128] = thirds[c]
    back = None
    for half, weight in enumerate((qkv, qkv_other)):
        for c in range(3):
            value = mm_bt(triple_grad_ref[:, (half * 3 + c) * 256 : (half * 3 + c + 1) * 256], weight[c])
            back = value if back is None else back + value
    unit, scale = norm_of(whole_rows(s[0], own, other))
    total = grad_middle[...] + norm_back(back, unit, scale, vector(small, FIRST_GAIN, unit.shape[1]))
    low, high = total[:, :256], total[:, 256:]
    frames_own_ref[...] = jnp.where(s[0] == 0, low, high)
    frames_other_ref[...] = jnp.where(s[0] == 0, high, low).astype(BF)
    vec_ref[...] = jnp.concatenate([col_sum(back * unit), col_sum(back)], axis=0)


def late_place_kernel(s, mine, near, far, farther, prior_ref, down_ref):
    n = prior_ref.shape[0]
    for j, piece in enumerate((mine, near, far, farther)):
        place = s[1] ^ j
        prior_ref[:, pl.ds(pl.multiple_of(place * 128, 128), 128)] = piece[:n, :].astype(F32)
        rows = pl.ds(pl.multiple_of(place * 256, 256), 256)
        for t in range(down_ref.shape[1] // 128):
            down_ref[rows, t * 128 : t * 128 + 128] = piece[n + t * 256 : n + t * 256 + 256, :].astype(F32)


def up_place_kernel(s, mine, near, far, farther, up_ref):
    n = up_ref.shape[0]
    for j, piece in enumerate((mine, near, far, farther)):
        for t in range(2):
            start = pl.multiple_of((s[1] ^ j) * 256 + t * 128, 128)
            up_ref[:, pl.ds(start, 128)] = piece[t * n : t * n + n, :].astype(F32)


def early_place_kernel(s, mine, near, far, farther, sums, out_ref, qkv_ref, *vecs):
    n = out_ref.shape[0]
    for j, piece in enumerate((mine, near, far, farther)):
        at = pl.ds(pl.multiple_of((s[1] ^ j) * 128, 128), 128)
        out_ref[:, at] = piece[0:n, :].astype(F32)
        for c in range(3):
            for t in range(2):
                start = n + (t * 3 + c) * 128
                qkv_ref[c, at, t * 128 : t * 128 + 128] = piece[start : start + 128, :].astype(F32)
    row = 0
    for ref in vecs[:8]:
        for t in range(ref.shape[1] // 128):
            ref[:, t * 128 : t * 128 + 128] = sums[row : row + 1, :]
            row += 1
    for ref in vecs[8:]:
        tiles = ref.shape[1] // 128
        for t in range(tiles):
            ref[:, t * 128 : t * 128 + 128] = sums[pl.ds(row + s[0] * tiles + t, 1), :]
        row += 2 * tiles


def core_kernel(lows, rests, s, keep, got, *outs):
    for places, low in zip(lows, outs):
        for k, i in enumerate(places):
            value = (keep[i] + got[i].astype(F32)).astype(BF)
            if len(places) == 1:
                low[...] = value
            else:
                low[k] = value
    for k, i in enumerate(rests):
        outs[-1][k] = keep[i] + got[i].astype(F32)


def early_core_kernel(extra, s, keep, got, *outs):
    n = keep.shape[1] - extra // 4
    for i in (3, 2, 1, 0):
        out = outs[i - 1] if i else outs[3]
        dtype = BF if i else F32
        out[:n, :] = (keep[i, :n] + got[i, :n].astype(F32)).astype(dtype)
        for k in range(4):
            start = n + k * (extra // 4)
            out[start : start + extra // 4, :] = (keep[k, n:] + got[k, n:].astype(F32)).astype(dtype)


def fold_two_kernel(s, rest, got, low, out):
    low[...] = (rest[1] + got[1].astype(F32)).astype(BF)
    out[...] = rest[0] + got[0].astype(F32)


def fold_kernel(size, which, extra, n_got, s, rest, *refs):
    got, outs, total = refs[:n_got], refs[n_got:-1], refs[-1]
    total[...] = functools.reduce(lambda x, y: x + y[...].astype(F32), got, rest[...])
    n = (total.shape[0] - extra) // size
    for k in list(range(1, size)) + [0]:
        target = outs[k]
        start = pl.multiple_of((s[which] ^ k) * n if size > 1 else 0, 16)
        target[:n, :] = total[pl.ds(start, n), :].astype(BF if k else F32)
        if extra:
            target[n:, :] = total[n * size :, :].astype(BF if k else F32)


def last_fold_kernel(extra, n_got, s, rest, *refs):
    got, outs = refs[:n_got], refs[n_got:]
    total = functools.reduce(lambda x, y: x + y[...].astype(F32), got, rest[...])
    n = total.shape[0] - extra
    outs[0][...] = total[:n].astype(BF)
    if extra:
        outs[1][...] = total[n:]


def join_kernel(which, s, *refs):
    parts, out = refs[:-1], refs[-1]
    n = parts[0].shape[0]
    for k, part in enumerate(parts):
        out[pl.ds(pl.multiple_of((s[which] ^ k) * n, 16), n), :] = part[...]


class Loaded:
    def __init__(self, ref, copy):
        self.ref, self.copy, self.shape = ref, copy, ref.shape

    def get(self):
        if self.copy is not None:
            self.copy.wait()
            self.copy = None
        return self.ref

    def __getitem__(self, index):
        return self.get()[index]


class Leaving:
    def __init__(self, ref, copy):
        self.ref, self.copy, self.shape, self.sent = ref, copy, ref.shape, False

    def __getitem__(self, index):
        return self.ref[index]

    def __setitem__(self, index, value):
        self.ref[index] = value

    def send(self):
        if not self.sent:
            self.copy.start()
            self.sent = True


class Far:
    def __init__(self, value, shape=None, cut=None):
        self.value, self.shape, self.cut = value, shape or value.shape, cut or (lambda s, ref: ref)


def call(kernel, scalars, ins, outs, scratch=(), name=None, after=()):
    n_in, n_out, n_after = len(ins), len(outs), len(after)
    far_in = [i for i, v in enumerate(ins) if isinstance(v, Far)]
    far_out = [i for i, o in enumerate(outs) if not o[2]]
    room = [pltpu.VMEM(ins[i].shape, ins[i].value.dtype) for i in far_in]
    room += [pltpu.VMEM(outs[i][0], outs[i][1]) for i in far_out]
    need = sum(math.prod(r.shape) * jnp.dtype(r.dtype).itemsize for r in room + list(scratch))

    def run(s, *refs):
        given, refs = list(refs[:n_in]), refs[n_in + n_after :]
        made, refs = list(refs[:n_out]), refs[n_out:]
        own, refs = refs[: len(scratch)], refs[len(scratch) :]
        rooms, sems = refs[:-1], refs[-1]
        for k, i in enumerate(far_in):
            copy = pltpu.make_async_copy(ins[i].cut(s, given[i]), rooms[k], sems.at[k])
            copy.start()
            given[i] = Loaded(rooms[k], copy)
        leaving = []
        for k, i in enumerate(far_out, len(far_in)):
            made[i] = Leaving(rooms[k], pltpu.make_async_copy(rooms[k], made[i], sems.at[k]))
            leaving.append(made[i])
        kernel(s, *given, *made, *own)
        for value in given:
            if isinstance(value, Loaded):
                value.get()
        for value in leaving:
            value.send()
        for value in leaving:
            value.copy.wait()

    near, far = pl.BlockSpec(memory_space=pltpu.VMEM), pl.BlockSpec(memory_space=pltpu.HBM)
    return pl.pallas_call(
        run,
        in_specs=[pl.BlockSpec(memory_space=pltpu.SMEM)]
        + [far if isinstance(v, Far) else near for v in ins]
        + [near] * n_after,
        out_specs=[near if stays else far for _, _, stays in outs],
        out_shape=[(pltpu.VMEM if stays else pltpu.HBM)(shape, dtype) for shape, dtype, stays in outs],
        scratch_shapes=list(scratch) + room + [pltpu.SemaphoreType.DMA((max(1, len(room)),))],
        compiler_params=pltpu.CompilerParams(vmem_limit_bytes=need + SPILL),
        cost_estimate=pl.CostEstimate(flops=0, bytes_accessed=0, transcendentals=0),
        name=name,
    )(scalars, *[pin(v) for v in ins], *[pin(v) for v in after])


def pin(value):
    if isinstance(value, Far):
        return pltpu.with_memory_space_constraint(value.value, pltpu.HBM)
    return pltpu.with_memory_space_constraint(value, pltpu.VMEM)


def swap(value, axes, sizes, mask):
    count = 1
    for size in sizes:
        count *= size
    return lax.ppermute(value, axes, [(i, i ^ mask) for i in range(count)])


class Moves:
    def __init__(self, n_dp, n_tensor):
        self.n_dp, self.n_tensor = n_dp, n_tensor
        self.dp = lax.axis_index("dp")
        self.here = lax.axis_index("tensor")

    def along(self, value, mask):
        return swap(value, "dp", (self.n_dp,), mask)

    def core(self, value):
        return self.along(value, 1)

    def side(self, value):
        return self.along(value, 2)

    def over(self, value):
        return swap(value, "tensor", (self.n_tensor,), 1)

    def cross(self, value):
        return swap(value, ("dp", "tensor"), (self.n_dp, self.n_tensor), 5)

    def groups(self):
        shift, rest = 2, self.n_dp // 4
        while rest > 1:
            size = 4 if rest % 4 == 0 else 2
            yield shift, size
            shift, rest = shift + (2 if size == 4 else 1), rest // size


    def reduce_core(self, scalars, keep, sent, lows, rests, name, after=()):
        n = sent.shape[1]
        outs = [(((len(p), n, 128) if len(p) > 1 else (n, 128)), BF, True) for p in lows]
        got = self.core(sent)
        return call(
            functools.partial(core_kernel, lows, rests),
            scalars,
            [keep, got],
            outs + [((len(rests), n, 128), F32, True)],
            name=name,
            after=after,
        )

    def fold_two(self, scalars, rest, got, name, after=()):
        n = got.shape[1]
        return call(
            fold_two_kernel, scalars, [rest, got], [((n, 128), BF, True), ((n, 128), F32, True)], name=name, after=after
        )

    def fold_rest(self, scalars, rest, got, name, extra=0, after=()):
        n = got[0].shape[0] - extra
        which = 3
        for shift, size in self.groups():
            m = n // size + extra
            outs = [((m, 128), F32, True)] + [((m, 128), BF, True)] * (size - 1)
            rest, *sent = call(
                functools.partial(fold_kernel, size, which, extra, len(got)),
                scalars,
                [rest, *got],
                outs,
                [pltpu.VMEM((n + extra, 128), F32)],
                name=name + "_fold",
                after=after,
            )
            got = [self.along(v, k << shift) for k, v in enumerate(sent, 1)]
            n, which, after = n // size, which + 1, ()
        outs = [((n, 128), BF, True)] + ([((extra, 128), F32, True)] if extra else [])
        return call(functools.partial(last_fold_kernel, extra, len(got)), scalars, [rest, *got], outs, name=name + "_last")

    def gather(self, scalars, total, name):
        groups = list(self.groups())
        for i in reversed(range(len(groups))):
            shift, size = groups[i]
            parts = [total] + [self.along(total, k << shift) for k in range(1, size)]
            (total,) = call(
                functools.partial(join_kernel, 3 + i),
                scalars,
                parts,
                [((total.shape[0] * size, 128), BF, True)],
                name=name + "_join",
            )
        near = self.side(total)
        return total, near, self.core(total), self.core(near)


def rows_of(here, own, other):
    cut = [
        v.reshape(-1, PAD, v.shape[1])[:, :BLOCK].reshape(-1, v.shape[1]) for v in (own, other.astype(own.dtype))
    ]
    return jnp.concatenate(
        [jnp.where(here == 0, cut[0], cut[1]), jnp.where(here == 0, cut[1], cut[0])], axis=0
    )


def episode_starts(resets):
    rows = resets.shape[0]
    inside = lax.broadcasted_iota(jnp.int32, (rows // SEQ_LEN, SEQ_LEN), 1)
    starts = jnp.where((inside == 0) | (resets.reshape(-1, SEQ_LEN) == 1), inside, 0)
    starts = lax.cummax(starts, axis=1).reshape(rows // BLOCK, BLOCK // SEQ_LEN, SEQ_LEN)
    starts = starts + SEQ_LEN * jnp.arange(BLOCK // SEQ_LEN, dtype=jnp.int32)[None, :, None]
    starts = starts.reshape(rows // BLOCK, BLOCK)
    tail = jnp.broadcast_to(jnp.arange(BLOCK, PAD, dtype=jnp.int32), (rows // BLOCK, PAD - BLOCK))
    return jnp.concatenate([starts, tail], axis=1)


def local(
    n_dp, n_tensor, frames, resets, first_gain, first_shift, qkv_weight, out_weight, out_bias, second_gain,
    second_shift, up_weight, up_bias, down_weight, down_bias, prior_gain, prior_shift, prior_weight,
    prior_bias, out_cotangent, logit_cotangent,
):
    move = Moves(n_dp, n_tensor)
    rows, half = frames.shape
    width = 2 * half
    mine = rows // 2
    blocks = mine // BLOCK
    hidden_width, n_logits = up_bias.shape[0], prior_bias.shape[0]
    row = lambda v: v.reshape(1, -1)
    core, side = move.dp & 1, (move.dp >> 1) & 1
    groups = [(move.dp >> shift) & (size - 1) for shift, size in move.groups()]
    scalars = jnp.stack([move.here, core * 2 + side, core, *groups]).astype(jnp.int32)
    here = move.here
    total_rows = blocks * PAD
    quarter = hidden_width // 4

    def near_rows(*entries):
        return [((total_rows, n), dtype, True) for n, dtype in entries]

    def pieces(n):
        return [((4, n, 128), F32, True), ((4, n, 128), BF, True)]

    def columns(value, size, which):
        cut = lambda s, ref: ref.at[..., pl.ds(pl.multiple_of(s[which] * size, 128), size)]
        return Far(value, (*value.shape[:-1], size), cut)

    def some_rows(value, size, which):
        cut = lambda s, ref: ref.at[pl.ds(pl.multiple_of(s[which] * size, 16), size), :]
        return Far(value, (size, value.shape[1]), cut)

    vectors = [first_gain, first_shift, out_bias, second_gain, second_shift, down_bias, prior_gain, prior_shift]
    vectors = [row(v) for v in vectors + [up_bias, prior_bias]]
    qkv_part, frames_sent, wide_part, tall_part, bias_sent, frames_own, small = call(
        first_kernel,
        scalars,
        [
            Far(frames),
            columns(qkv_weight, half // 2, 2),
            columns(up_weight, quarter, 1),
            columns(prior_weight, n_logits // 4, 1),
            some_rows(down_weight, quarter, 1),
            some_rows(out_weight, half // 4, 1),
            *[Far(v) for v in vectors],
        ],
        [((3, width, half // 2), BF, True)]
        + near_rows((half, BF))
        + [((width, quarter + n_logits // 4), BF, True), ((quarter + half // 4, width), BF, True)]
        + [((1, hidden_width + n_logits), F32, True)]
        + near_rows((half, BF))
        + [((16, hidden_width), F32, True)],
        [pltpu.VMEM((rows + 16, half), F32)],
        "first_parts",
    )
    qkv_got = move.over(qkv_part)
    frames_other = move.over(frames_sent)
    qkv_near = move.core(qkv_got)
    wide_part, tall_part, bias_sent = gate([wide_part, tall_part, bias_sent], [qkv_got], "after_first")
    wide_got = move.over(wide_part)
    tall_got = move.over(tall_part)
    bias_other = move.over(bias_sent)
    seg = lax.dynamic_slice_in_dim(episode_starts(resets), here * blocks, blocks, 0).reshape(-1, 1)
    first, triple, mixed, qkv_other = call(
        attend_kernel,
        scalars,
        [frames_own, frames_other, seg, small, Far(qkv_weight), qkv_got, qkv_near],
        near_rows((width, BF), (3 * width, BF), (width, BF)) + [(qkv_weight.shape, BF, True)],
        name="attend",
    )
    wide_got, tall_got = gate([wide_got, tall_got], [mixed], "after_attend")

    def all_quarters(got):
        beside = move.side(got)
        return [got, beside, move.core(got), move.core(beside)]

    wide_pieces = all_quarters(wide_got)
    tall_pieces = all_quarters(tall_got)
    logit_sent, out_sent, logit_own, out_own = call(
        cotangents_kernel,
        scalars,
        [Far(logit_cotangent), Far(out_cotangent)],
        near_rows((n_logits, BF), (half, BF)) + near_rows((n_logits, BF), (half, BF)),
        [pltpu.VMEM((rows + 16, n_logits), F32)],
        name="cotangents",
        after=(tall_got,),
    )
    logit_other = move.over(logit_sent)
    out_other = move.over(out_sent)
    block_send, block_own, middle, second, act, slope, ending, prior_in, out_weight_other = call(
        feed_kernel,
        scalars,
        [frames_own, frames_other, mixed, small, Far(out_weight), *tall_pieces, Far(up_weight), Far(down_weight)]
        + [*wide_pieces, bias_other],
        near_rows((half, BF), (half, BF))
        + near_rows((width, F32), (width, BF), (2 * hidden_width, BF), (2 * hidden_width, F32))
        + near_rows((width, F32), (width, BF))
        + [(out_weight.shape, BF, True)],
        name="feed",
    )
    block_got = move.over(block_send)
    logits_send, logits_own, grad_ending, ending_grad, vec_three, prior_bias_sum = call(
        prior_kernel,
        scalars,
        [prior_in, ending, small, logit_own, out_own, Far(prior_weight), *wide_pieces, logit_other, out_other, bias_other],
        near_rows((n_logits, BF)) + [((total_rows, n_logits), F32, False)]
        + near_rows((width, F32), (width, BF))
        + [((3, width), F32, True), ((1, 2 * n_logits), F32, True)],
        [pltpu.VMEM(prior_weight.shape, BF)],
        name="prior",
    )
    logits_got = move.over(logits_send)
    late_keep, late_send = call(
        late_grads_kernel,
        scalars,
        [prior_in, logit_own, logit_other, act, ending_grad],
        pieces(width + hidden_width),
        [pltpu.VMEM((width, n_logits), F32)],
        name="late_grads",
        after=(block_got,),
    )
    late_low, late_rest = move.reduce_core(scalars, late_keep, late_send, ((2, 3),), (0, 1), "late_core")
    hidden_grad, grad_middle, middle_grad, vec_two, up_bias_sum = call(
        feed_back_kernel,
        scalars,
        [ending_grad, slope, middle, grad_ending, small, Far(down_weight), Far(up_weight)]
        + [v for both in zip(tall_pieces, wide_pieces) for v in both],
        near_rows((2 * hidden_width, BF), (width, F32), (width, BF))
        + [((3, width), F32, True), ((1, 2 * hidden_width), F32, True)],
        [pltpu.VMEM((total_rows, width), F32)],
        name="feed_back",
        after=(late_send,),
    )
    up_keep, up_send = call(
        up_grads_kernel,
        scalars,
        [second, hidden_grad],
        pieces(width * hidden_width // 512),
        [pltpu.VMEM((width, total_rows), BF)],
        name="up_grads",
        after=(late_low,),
    )
    up_low, up_rest = move.reduce_core(scalars, up_keep, up_send, ((1, 3),), (0, 2), "up_core")
    late_low2, late_rest = move.fold_two(scalars, late_rest, move.over(late_low), "late_over")
    triple_grad, frames_send, frames_grad, vec_one = call(
        attend_back_kernel,
        scalars,
        [middle_grad, grad_middle, frames_own, triple, qkv_other, out_weight_other, small, Far(out_weight), seg, frames_other]
        + [Far(qkv_weight)],
        near_rows((3 * width, BF), (half, BF)) + [((total_rows, half), F32, False)] + [((2, width), F32, True)],
        [pltpu.VMEM((total_rows, width), BF)],
        name="attend_back",
        after=(up_send, logits_got),
    )
    spare = 64
    keep, send = call(
        early_grads_kernel,
        scalars,
        [mixed, middle_grad, first, triple_grad, vec_one, vec_two, vec_three, up_bias_sum, prior_bias_sum],
        pieces(half + 768 + spare // 4),
        [pltpu.VMEM((half, width), F32), pltpu.VMEM((spare, 128), F32)],
        name="early_grads",
        after=(up_low,),
    )
    up_low2, up_rest = move.fold_two(scalars, up_rest, move.side(up_low), "up_side")
    (late,) = move.fold_rest(scalars, late_rest, [move.side(late_low2)], "late")
    (up_sums,) = move.fold_rest(scalars, up_rest, [move.over(up_low2)], "up")
    late = move.gather(scalars, late, "late")
    up_sums = move.gather(scalars, up_sums, "up")
    frames_got = move.over(frames_send)
    *lows, rest = call(
        functools.partial(early_core_kernel, spare),
        scalars,
        [keep, move.core(send)],
        [((half + 768 + spare, 128), BF, True)] * 3 + [((half + 768 + spare, 128), F32, True)],
        name="early_core",
    )
    total, sums = move.fold_rest(
        scalars, rest, [move.side(lows[0]), move.over(lows[1]), move.cross(lows[2])], "early", spare
    )
    placed = call(
        early_place_kernel,
        scalars,
        [*move.gather(scalars, total, "early"), sums],
        [((half, width), F32, False), ((3, width, half), F32, False)]
        + [((1, n), F32, False) for n in [width] * 8 + [hidden_width, n_logits]],
        name="early_place",
    )
    out_grad, qkv_grad = placed[:2]
    named = [v.reshape(-1) for v in placed[2:]]
    prior_grad, down_grad = call(
        late_place_kernel,
        scalars,
        list(late),
        [((width, n_logits), F32, False), ((hidden_width, width), F32, False)],
        name="late_place",
    )
    (up_grad,) = call(
        up_place_kernel, scalars, list(up_sums), [((width, hidden_width), F32, False)], name="up_place"
    )
    return (
        rows_of(here, block_own, block_got),
        rows_of(here, logits_own, logits_got),
        rows_of(here, frames_grad, frames_got),
        named[0],
        named[1],
        qkv_grad,
        out_grad,
        named[4],
        named[2],
        named[3],
        up_grad,
        named[8],
        down_grad,
        named[7],
        named[5],
        named[6],
        prior_grad,
        named[9],
    )


def solution(mesh):
    rows, cols = P("dp", "tensor"), P(None, "tensor")
    placed = (
        rows, P("dp"), P(), P(), P(None, None, "tensor"), P("tensor", None), P(), P(), P(), cols, P("tensor"),
        P("tensor", None), P(), P(), P(), cols, P("tensor"), rows, rows,
    )
    given = (
        rows, rows, rows, P(), P(), P(None, None, "tensor"), P("tensor", None), P(), P(), P(), cols,
        P("tensor"), P("tensor", None), P(), P(), P(), cols, P("tensor"),
    )
    return jax.shard_map(
        functools.partial(local, mesh.shape["dp"], mesh.shape["tensor"]),
        mesh=mesh,
        in_specs=placed,
        out_specs=given,
        check_vma=False,
    )
```

```python
import functools
import math

import jax
import jax.numpy as jnp
from jax import lax
from jax.experimental import pallas as pl
from jax.experimental.pallas import tpu as pltpu
from jax.sharding import PartitionSpec as P

HEAD_DIM = 64
SEQ_LEN = 50
BLOCK = 4 * SEQ_LEN
PAD = -(-BLOCK // 16) * 16
EPS = 1e-05
NEG = -1e30
GELU_C = 0.7978845608028654
GELU_A = 0.044715
SPILL = 4 * 1024 * 1024
COST = 3e8
BF = jnp.bfloat16
F32 = jnp.float32
FIRST_GAIN, FIRST_SHIFT, OUT_BIAS, SECOND_GAIN, SECOND_SHIFT, DOWN_BIAS, PRIOR_GAIN, PRIOR_SHIFT, UP_BIAS, PRIOR_BIAS = range(10)


def mm(a, b):
    return lax.dot_general(a, b, (((1,), (0,)), ((), ())), preferred_element_type=F32)


def mm_bt(a, b):
    return lax.dot_general(a, b, (((1,), (1,)), ((), ())), preferred_element_type=F32)


def mm_at(a, b):
    return lax.dot_general(a, b, (((0,), (0,)), ((), ())), preferred_element_type=F32)


def norm_of(value):
    centre = value - jnp.mean(value, axis=-1, keepdims=True)
    factor = lax.rsqrt(jnp.mean(centre * centre, axis=-1, keepdims=True) + EPS)
    return centre * factor, factor


def norm_back(grad, unit, factor, gain):
    scaled = grad * gain
    first = jnp.mean(scaled, axis=-1, keepdims=True)
    second = jnp.mean(scaled * unit, axis=-1, keepdims=True)
    return factor * (scaled - first - unit * second)


def col_sum(value):
    return jnp.sum(value, axis=0, keepdims=True)


def whole_rows(here, own, other):
    low = jnp.where(here == 0, own[...], other[...])
    high = jnp.where(here == 0, other[...], own[...])
    return jnp.concatenate([low, high], axis=1).astype(F32)


def allowed_pairs(resets):
    place = lax.broadcasted_iota(jnp.int32, (1, PAD), 1)
    starts = jnp.where((resets == 1) | (lax.rem(place, SEQ_LEN) == 0) | (place >= BLOCK), place, 0)
    row = lax.broadcasted_iota(jnp.int32, (PAD, PAD), 0)
    col = lax.broadcasted_iota(jnp.int32, (PAD, PAD), 1)
    seg = jnp.max(jnp.where(col <= row, starts, 0).astype(F32), axis=-1, keepdims=True).astype(jnp.int32)
    seg2 = jnp.concatenate([seg, seg], axis=0)
    row = lax.broadcasted_iota(jnp.int32, (2 * PAD, PAD), 0)
    row = jnp.where(row >= PAD, row - PAD, row)
    col = lax.broadcasted_iota(jnp.int32, (2 * PAD, PAD), 1)
    return (col <= row) & (col >= seg2)


def two_heads(value):
    first = lax.broadcasted_iota(jnp.int32, value.shape, 1) < HEAD_DIM
    none = jnp.zeros_like(value)
    return jnp.concatenate([jnp.where(first, value, none), jnp.where(first, none, value)], axis=0)


def one_pair(value):
    first = lax.broadcasted_iota(jnp.int32, (PAD, 2 * HEAD_DIM), 1) < HEAD_DIM
    return jnp.where(first, value[:PAD], value[PAD:])


def softmax_of(query2, key, allowed):
    scores = jnp.where(allowed, mm_bt(query2, key), NEG)
    expo = jnp.exp(scores - jnp.max(scores, axis=-1, keepdims=True))
    return expo * (1.0 / jnp.sum(expo, axis=-1, keepdims=True))


def vector(small, index, n):
    return small[index : index + 1, :n]


def blocks_in(ref):
    return [slice(i * PAD, i * PAD + PAD) for i in range(ref.shape[0] // PAD)]


def add_up(sums, values):
    return [v if s is None else s + v for s, v in zip(sums, values, strict=True)]


def split_rows(half, source, own, sent, wide_rows):
    rows, n = source.shape
    wide_rows[0:rows, 0:n] = source[...].astype(F32)
    for which, target in ((half, own), (1 - half, sent)):
        for block, at in enumerate(blocks_in(target)):
            start = pl.multiple_of(which * (rows // 2) + block * BLOCK, 8)
            part = wide_rows[pl.ds(start, PAD), 0:n]
            inside = lax.broadcasted_iota(jnp.int32, part.shape, 0) < BLOCK
            target[at, :] = jnp.where(inside, part, 0.0).astype(BF)


def tiles_of(ref, start, n, count):
    return jnp.concatenate([ref[start + t * n : start + t * n + n, :] for t in range(count)], axis=1)


class Packed:
    def __init__(self, refs, n, q, o):
        self.one, self.two = refs
        self.n, self.q, self.o = n, q, o

    def up(self):
        return tiles_of(self.one, 0, self.n, 2)

    def out(self):
        return tiles_of(self.one, 2 * self.n, self.o, 4)

    def bias(self):
        start = 2 * self.n + 4 * self.o
        parts = [self.one[start + 16 * k : start + 16 * k + 16, :].astype(F32) for k in range(3)]
        return (parts[2] + parts[1] + parts[0])[:3]

    def down(self):
        return tiles_of(self.two, 0, self.q, 4)

    def prior(self):
        return self.two[4 * self.q : 4 * self.q + self.n, :]


def put_tiles(target, start, part):
    for t in range(part.shape[-1] // 128):
        target[start : start + part.shape[0], :] = part[:, t * 128 : t * 128 + 128]
        start += part.shape[0]
    return start


def first_kernel(s, frames, qkv, up, out, down, prior, *refs):
    smalls, (sent_ref, one_ref, two_ref, own_ref, small_ref, wide_rows, rows, other) = refs[:-8], refs[-8:]
    split_rows(s[0], frames, own_ref, other, wide_rows)
    start = put_tiles(sent_ref, 0, other)
    for c in range(3):
        start = put_tiles(sent_ref, start, qkv.get().at[c])
    start = put_tiles(one_ref, put_tiles(one_ref, 0, up), out)
    for i, ref in enumerate(smalls):
        small_ref[i : i + 1, : ref.shape[1]] = ref[...]
    rows[...] = jnp.zeros_like(rows)
    for t in range(2):
        rows[t : t + 1, :] = smalls[UP_BIAS][:, pl.ds(pl.multiple_of(s[1] * 256 + t * 128, 128), 128)]
    rows[2:3, :] = smalls[PRIOR_BIAS][:, pl.ds(pl.multiple_of(s[1] * 128, 128), 128)]
    left = rows[...]
    for k in range(3):
        term = left.astype(BF)
        one_ref[start : start + 16, :] = term
        left = left - term.astype(F32)
        start += 16
    put_tiles(two_ref, put_tiles(two_ref, 0, down), prior)


def cut_kernel(s, got, qkv_ref):
    qkv_ref[...] = got[got.shape[0] - qkv_ref.shape[0] :, :]


def cotangents_kernel(s, logit, out, sent, logit_own, out_own, wide_rows, logit_sent, out_sent):
    split_rows(s[0], logit, logit_own, logit_sent, wide_rows)
    split_rows(s[0], out, out_own, out_sent, wide_rows)
    n = logit_sent.shape[1]
    sent[:, :n] = logit_sent[...]
    sent[:, n:] = out_sent[...]


def gate(values, after, name=None):
    def run(*refs):
        pass

    near = pl.BlockSpec(memory_space=pltpu.VMEM)
    return pl.pallas_call(
        run,
        in_specs=[near] * (len(values) + len(after)),
        out_specs=[near] * len(values),
        out_shape=[pltpu.VMEM(v.shape, v.dtype) for v in values],
        input_output_aliases={i: i for i in range(len(values))},
        compiler_params=pltpu.CompilerParams(vmem_limit_bytes=1024 * 1024),
        cost_estimate=pl.CostEstimate(flops=0, bytes_accessed=0, transcendentals=0),
        name=name,
    )(*[pin(v) for v in values], *[pin(v) for v in after])


def attend_kernel(
    s, own, got, resets, small, q0, q1, q2, q3, qkv,
    first_ref, triple_ref, mixed_ref, qkv_other_ref, other,
):
    other[...] = tiles_of(got, 0, own.shape[0], 2)
    unit, _ = norm_of(whole_rows(s[0], own, other))
    n = first_ref.shape[1]
    first_ref[...] = (unit * vector(small, FIRST_GAIN, n) + vector(small, FIRST_SHIFT, n)).astype(BF)
    for j, piece in enumerate((q0, q1, q2, q3)):
        size = qkv.shape[1] // 4
        rows = pl.ds(pl.multiple_of((s[1] ^ j) * size, 16), size)
        for c in range(3):
            qkv_other_ref[c, rows, :] = tiles_of(piece, c * 2 * size, size, 2)
    for half, weight in enumerate((qkv, qkv_other_ref)):
        for c in range(3):
            value = mm(first_ref[...], weight[c]).astype(BF)
            triple_ref[:, (half * 3 + c) * 256 : (half * 3 + c + 1) * 256] = value
    for block, at in enumerate(blocks_in(own)):
        allowed = allowed_pairs(resets[pl.ds(s[0] * len(blocks_in(own)) + block, 1), :PAD])
        for pair in range(4):
            start = (pair // 2) * 768 + (pair % 2) * 128
            query, key, value = (
                triple_ref[at, start + c * 256 : start + c * 256 + 128] for c in range(3)
            )
            query2 = two_heads(query * HEAD_DIM ** (-0.5))
            weights = softmax_of(query2, key, allowed).astype(BF)
            mixed_ref[at, pair * 128 : pair * 128 + 128] = one_pair(mm(weights, value)).astype(BF)


def feed_kernel(
    s, own, other, mixed, small, out, up, down, *refs,
):
    packs, refs = refs[:8], refs[8:]
    block_other_ref, block_own_ref, middle_ref, second_ref, act_ref, slope_ref, ending_ref, prior_in_ref = refs[:-1]
    out_other_ref = refs[-1]
    n, half = out.shape[0], up.shape[1]
    packed = [Packed(p, up.shape[0], half // 4, n // 4) for p in zip(packs[:4], packs[4:])]
    for j, piece in enumerate(packed):
        out_other_ref[pl.ds(pl.multiple_of((s[1] ^ j) * (n // 4), 16), n // 4), :] = piece.out()
    middle_ref[...] = (
        whole_rows(s[0], own, other)
        + vector(small, OUT_BIAS, middle_ref.shape[1])
        + mm(mixed[:, :n], out[...])
        + mm(mixed[:, n:], out_other_ref[...])
    )
    unit, _ = norm_of(middle_ref[...])
    wide = middle_ref.shape[1]
    second_ref[...] = (unit * vector(small, SECOND_GAIN, wide) + vector(small, SECOND_SHIFT, wide)).astype(BF)
    ending_ref[...] = middle_ref[...] + vector(small, DOWN_BIAS, wide)
    for i in range(8):
        if i < 4:
            at = slice(i * 256, i * 256 + 256)
            w_up, w_down, bias = up[:, at], down[at, :], small[UP_BIAS : UP_BIAS + 1, at]
        else:
            place = pl.multiple_of((s[1] ^ (i - 4)) * 256, 256)
            at = pl.ds(pl.multiple_of(half + place, 256), 256)
            w_up, w_down = packed[i - 4].up(), packed[i - 4].down()
            bias = packed[i - 4].bias()
            bias = jnp.concatenate([bias[0:1], bias[1:2]], axis=1)
        for rows in blocks_in(own):
            hidden = mm(second_ref[rows, :], w_up) + bias
            square = hidden * hidden
            bent = jnp.tanh(GELU_C * (hidden + GELU_A * hidden * square))
            act = (0.5 * hidden * (1.0 + bent)).astype(BF)
            slope = 0.5 * (1.0 + bent) + (0.5 * GELU_C) * hidden * (1.0 - bent * bent) * (
                1.0 + (3.0 * GELU_A) * square
            )
            act_ref[rows, at] = act
            slope_ref[rows, at] = slope
            ending_ref[rows, :] += mm(act, w_down)
    total = ending_ref[...]
    unit, _ = norm_of(total)
    prior_in_ref[...] = (unit * vector(small, PRIOR_GAIN, wide) + vector(small, PRIOR_SHIFT, wide)).astype(BF)
    low, high = total[:, :256].astype(BF), total[:, 256:].astype(BF)
    block_own_ref[...] = jnp.where(s[0] == 0, low, high)
    block_other_ref[...] = jnp.where(s[0] == 0, high, low)


def prior_kernel(
    s, prior_in, ending, small, logit_own, out_own, block_other, a0, a1, a2, a3, b0, b1, b2, b3, cotangents, prior,
    sent_ref, logits_ref, grad_ending_ref, ending_grad_ref, vec_ref, bias_ref, weight, bias,
):
    half, n = prior.shape[1], prior.shape[0]
    for j, piece in enumerate(zip((a0, a1, a2, a3), (b0, b1, b2, b3))):
        at = pl.ds(pl.multiple_of((s[1] ^ j) * 128, 128), 128)
        piece = Packed(piece, n, n // 2, n // 8)
        weight[:, at] = piece.prior()
        bias[:, at] = piece.bias()[2:3]
    logit_other = cotangents.at[:, :half]
    sent_ref[:, :half] = (mm(prior_in[...], weight[...]) + bias[...]).astype(BF)
    sent_ref[:, half:] = block_other[...]
    logits_ref[...] = mm(prior_in[...], prior[...]) + vector(small, PRIOR_BIAS, half)
    back = mm_bt(logit_own[...], prior[...]) + mm_bt(logit_other[...], weight[...])
    unit, factor = norm_of(ending[...])
    gain = vector(small, PRIOR_GAIN, unit.shape[1])
    grad = whole_rows(s[0], out_own, cotangents.at[:, half:]) + norm_back(back, unit, factor, gain)
    grad_ending_ref[...] = grad
    ending_grad_ref[...] = grad.astype(BF)
    vec_ref[...] = jnp.concatenate([col_sum(back * unit), col_sum(back), col_sum(grad)], axis=0)
    bias_ref[:, :half] = col_sum(logit_own[...].astype(F32))
    bias_ref[:, half:] = col_sum(logit_other[...].astype(F32))


def store_piece(keep, send, h, j, start, value):
    at = slice(start, start + value.shape[0])
    if j < 2:
        keep[h * 2 + j, at, :] = value
    else:
        send[h * 2 + j - 2, at, :] = value.astype(BF)


def late_grads_kernel(s, prior_in, logit_own, cotangents, act, ending_grad, keep, send, wide):
    half = act.shape[1] // 2
    logit_other = cotangents.at[:, : logit_own.shape[1]]
    n = prior_in.shape[1]
    for h in range(2):
        wide[...] = mm_at(prior_in[...], (logit_own, logit_other)[h][...])
        for j in (2, 3, 0, 1):
            place = s[1] ^ j
            store_piece(keep, send, h, j, 0, wide[:, pl.ds(pl.multiple_of(place * 128, 128), 128)])
            part = act[:, pl.ds(pl.multiple_of(h * half + place * 256, 256), 256)]
            value = mm_at(part, ending_grad[...])
            for t in range(n // 128):
                store_piece(keep, send, h, j, n + t * 256, value[:, t * 128 : t * 128 + 128])


def up_grads_kernel(s, second, hidden_grad, mixed, middle_grad, keep, send, turned, wide):
    turned[...] = second[...].T
    half = hidden_grad.shape[1] // 2
    n, m = second.shape[1], mixed.shape[1] // 2
    for h in range(2):
        wide[...] = mm_at(mixed[:, h * m : h * m + m], middle_grad[...])
        for j in (2, 3, 0, 1):
            place = s[1] ^ j
            value = mm(turned[...], hidden_grad[:, pl.ds(pl.multiple_of(h * half + place * 256, 256), 256)])
            for t in range(2):
                store_piece(keep, send, h, j, t * n, value[:, t * 128 : t * 128 + 128])
            store_piece(keep, send, h, j, 2 * n, wide[:, pl.ds(pl.multiple_of(place * 128, 128), 128)])


def early_grads_kernel(
    s, first, triple_grad, vec_one, vec_two, vec_three, bias_up, bias_prior, keep, send, vectors,
):
    row = 0
    for ref in (vec_one, vec_two, vec_three):
        for i in range(ref.shape[0]):
            for t in range(ref.shape[1] // 128):
                vectors[row : row + 1, :] = ref[i : i + 1, t * 128 : t * 128 + 128]
                row += 1
    for ref in (bias_up, bias_prior):
        tiles = ref.shape[1] // 128
        for t in range(tiles):
            place = row + lax.rem(t + s[0] * (tiles // 2), tiles)
            vectors[pl.ds(place, 1), :] = ref[:, t * 128 : t * 128 + 128]
        row += tiles
    vectors[row:, :] = jnp.zeros((vectors.shape[0] - row, 128), F32)
    for h in range(2):
        for j in (2, 3, 0, 1):
            place = pl.multiple_of((s[1] ^ j) * 128, 128)
            value = mm_at(first[:, pl.ds(place, 128)], triple_grad[:, h * 768 : h * 768 + 768])
            for c in range(3):
                for t in range(2):
                    at = slice(c * 256 + t * 128, c * 256 + t * 128 + 128)
                    store_piece(keep, send, h, j, (t * 3 + c) * 128, value[:, at])
            part = vectors[(h * 2 + j % 2) * 16 : (h * 2 + j % 2) * 16 + 16, :]
            store_piece(keep, send, h, j, 768, part)


def feed_back_kernel(
    s, ending_grad, slope, middle, grad_ending, small, a0, a1, a2, a3, b0, b1, b2, b3, down, up,
    hidden_grad_ref, grad_middle_ref, middle_grad_ref, vec_ref, bias_ref, back,
):
    half, n = up.shape[1], up.shape[0]
    packed = [Packed(p, n, half // 4, n // 8) for p in zip((a0, a1, a2, a3), (b0, b1, b2, b3))]
    for i in range(8):
        if i < 4:
            at = slice(i * 256, i * 256 + 256)
            w_up, w_down = up[:, at], down[at, :]
        else:
            at = pl.ds(pl.multiple_of(half + (s[1] ^ (i - 4)) * 256, 256), 256)
            w_up, w_down = packed[i - 4].up(), packed[i - 4].down()
        sums = [None]
        for rows in blocks_in(ending_grad):
            low = (mm_bt(ending_grad[rows, :], w_down) * slope[rows, at]).astype(BF)
            hidden_grad_ref[rows, at] = low
            sums = add_up(sums, [col_sum(low.astype(F32))])
            value = mm_bt(low, w_up)
            if i == 0:
                back[rows, :] = value
            else:
                back[rows, :] += value
        bias_ref[:, at] = sums[0]
    unit, factor = norm_of(middle[...])
    value = back[...]
    gain = vector(small, SECOND_GAIN, unit.shape[1])
    total = grad_ending[...] + norm_back(value, unit, factor, gain)
    grad_middle_ref[...] = total
    middle_grad_ref[...] = total.astype(BF)
    vec_ref[...] = jnp.concatenate([col_sum(value * unit), col_sum(value), col_sum(total)], axis=0)


def attend_back_kernel(
    s, middle_grad, grad_middle, own, triple, qkv_other, out_other, small, out, resets, other, qkv,
    triple_grad_ref, frames_other_ref, frames_own_ref, vec_ref, mixed_grad,
):
    n = out.shape[0]
    mixed_grad[:, :n] = mm_bt(middle_grad[...], out[...]).astype(BF)
    mixed_grad[:, n:] = mm_bt(middle_grad[...], out_other[...]).astype(BF)
    factor = HEAD_DIM ** (-0.5)
    for block, at in enumerate(blocks_in(own)):
        allowed = allowed_pairs(resets[pl.ds(s[0] * len(blocks_in(own)) + block, 1), :PAD])
        for pair in range(4):
            start = (pair // 2) * 768 + (pair % 2) * 128
            query, key, value = (triple[at, start + c * 256 : start + c * 256 + 128] for c in range(3))
            query2 = two_heads(query * factor)
            mixed2 = two_heads(mixed_grad[at, pair * 128 : pair * 128 + 128])
            again = softmax_of(query2, key, allowed)
            weight_grad = mm_bt(mixed2, value)
            inner = jnp.sum(again * weight_grad, axis=-1, keepdims=True)
            score_grad = (again * (weight_grad - inner)).astype(BF)
            thirds = (
                (one_pair(mm(score_grad, key)) * factor).astype(BF),
                mm_at(score_grad, query2).astype(BF),
                mm_at(again.astype(BF), mixed2).astype(BF),
            )
            for c in range(3):
                triple_grad_ref[at, start + c * 256 : start + c * 256 + 128] = thirds[c]
    back = None
    for half, weight in enumerate((qkv, qkv_other)):
        for c in range(3):
            value = mm_bt(triple_grad_ref[:, (half * 3 + c) * 256 : (half * 3 + c + 1) * 256], weight[c])
            back = value if back is None else back + value
    unit, scale = norm_of(whole_rows(s[0], own, other))
    total = grad_middle[...] + norm_back(back, unit, scale, vector(small, FIRST_GAIN, unit.shape[1]))
    low, high = total[:, :256], total[:, 256:]
    frames_own_ref[...] = jnp.where(s[0] == 0, low, high)
    frames_other_ref[...] = jnp.where(s[0] == 0, high, low).astype(BF)
    vec_ref[...] = jnp.concatenate([col_sum(back * unit), col_sum(back)], axis=0)


def late_place_kernel(s, mine, near, far, farther, down_ref, prior_ref):
    n, q = prior_ref.shape[0], down_ref.shape[0] // 4
    for j, piece in enumerate((mine, near, far, farther)):
        place = s[1] ^ j
        rows = pl.ds(pl.multiple_of(place * q, 8), q)
        for t in range(down_ref.shape[1] // 128):
            down_ref[rows, t * 128 : t * 128 + 128] = piece[n + t * q : n + t * q + q, :].astype(F32)
        prior_ref[:, pl.ds(pl.multiple_of(place * 128, 128), 128)] = piece[:n, :].astype(F32)


def up_place_kernel(s, mine, near, far, farther, up_ref, out_ref):
    n, m = up_ref.shape[0], out_ref.shape[0]
    for j, piece in enumerate((mine, near, far, farther)):
        place = s[1] ^ j
        for t in range(2):
            columns = pl.ds(pl.multiple_of(place * 256 + t * 128, 128), 128)
            up_ref[:, columns] = piece[t * n : t * n + n, :].astype(F32)
        out_ref[:, pl.ds(pl.multiple_of(place * 128, 128), 128)] = piece[2 * n : 2 * n + m, :].astype(F32)


def early_place_kernel(s, mine, near, far, farther, qkv_ref, *vecs):
    vecs, sums = vecs[:-1], vecs[-1]
    sums[...] = mine[6 * 128 :, :].astype(F32)
    for j, piece in enumerate((mine, near, far, farther)):
        at = pl.ds(pl.multiple_of((s[1] ^ j) * 128, 128), 128)
        for c in range(3):
            for t in range(2):
                start = (t * 3 + c) * 128
                qkv_ref[c, at, t * 128 : t * 128 + 128] = piece[start : start + 128, :].astype(F32)
    qkv_ref.send()
    row = 0
    for ref in vecs[:8]:
        for t in range(ref.shape[1] // 128):
            ref[:, t * 128 : t * 128 + 128] = sums[row : row + 1, :]
            row += 1
    for ref in vecs[8:]:
        tiles = ref.shape[1] // 128
        for t in range(tiles):
            ref[:, t * 128 : t * 128 + 128] = sums[pl.ds(row + s[0] * tiles + t, 1), :]
        row += 2 * tiles


def core_kernel(extra, s, keep, got, *outs):
    n = keep.shape[1] - extra // 4
    for i in (3, 2, 1, 0):
        out = outs[i - 1] if i else outs[3]
        dtype = BF if i else F32
        out[:n, :] = (keep[i, :n] + got[i, :n].astype(F32)).astype(dtype)
        for k in range(4 if extra else 0):
            start = n + k * (extra // 4)
            out[start : start + extra // 4, :] = (keep[k, n:] + got[k, n:].astype(F32)).astype(dtype)


def total_kernel(s, *refs):
    refs[-1][...] = functools.reduce(lambda x, y: x + y, [r[...].astype(F32) for r in refs[:-1]]).astype(BF)


def rows_kernel(entries, s, *refs):
    count = len(entries)
    given, outs, rooms = refs[: 2 * count], refs[2 * count : 3 * count], refs[3 * count :]
    for i, columns in enumerate(entries):
        own, got, out, room = given[2 * i], given[2 * i + 1], outs[i], rooms[i]
        rows = out.shape[0] // 2
        for block, at in enumerate(blocks_in(own)):
            for which, ref, cut in ((s[0], own, slice(None)), (1 - s[0], got, columns)):
                start = pl.multiple_of(which * rows + block * BLOCK, 8)
                room[pl.ds(start, BLOCK), :] = ref[at, cut].astype(F32)[:BLOCK]
        out[...] = room[...].astype(out.ref.dtype)
        out.send()


class Loaded:
    def __init__(self, ref, copy):
        self.ref, self.copy, self.shape = ref, copy, ref.shape

    def get(self):
        if self.copy is not None:
            self.copy.wait()
            self.copy = None
        return self.ref

    def __getitem__(self, index):
        return self.get()[index]


class Leaving:
    def __init__(self, ref, copy):
        self.ref, self.copy, self.shape, self.sent = ref, copy, ref.shape, False

    def __getitem__(self, index):
        return self.ref[index]

    def __setitem__(self, index, value):
        self.ref[index] = value

    def send(self):
        if not self.sent:
            self.copy.start()
            self.sent = True


class Far:
    def __init__(self, value, shape=None, cut=None):
        self.value, self.shape, self.cut = value, shape or value.shape, cut or (lambda s, ref: ref)


def call(kernel, scalars, ins, outs, scratch=(), name=None, after=(), cost=1.0):
    n_in, n_out, n_after = len(ins), len(outs), len(after)
    far_in = [i for i, v in enumerate(ins) if isinstance(v, Far)]
    far_out = [i for i, o in enumerate(outs) if not o[2]]
    room = [pltpu.VMEM(ins[i].shape, ins[i].value.dtype) for i in far_in]
    room += [pltpu.VMEM(outs[i][0], outs[i][1]) for i in far_out]
    need = sum(math.prod(r.shape) * jnp.dtype(r.dtype).itemsize for r in room + list(scratch))

    def run(s, *refs):
        given, refs = list(refs[:n_in]), refs[n_in + n_after :]
        made, refs = list(refs[:n_out]), refs[n_out:]
        own, refs = refs[: len(scratch)], refs[len(scratch) :]
        rooms, sems = refs[:-1], refs[-1]
        for k, i in enumerate(far_in):
            copy = pltpu.make_async_copy(ins[i].cut(s, given[i]), rooms[k], sems.at[k])
            copy.start()
            given[i] = Loaded(rooms[k], copy)
        leaving = []
        for k, i in enumerate(far_out, len(far_in)):
            made[i] = Leaving(rooms[k], pltpu.make_async_copy(rooms[k], made[i], sems.at[k]))
            leaving.append(made[i])
        kernel(s, *given, *made, *own)
        for value in given:
            if isinstance(value, Loaded):
                value.get()
        for value in leaving:
            value.send()
        for value in leaving:
            value.copy.wait()

    near, far = pl.BlockSpec(memory_space=pltpu.VMEM), pl.BlockSpec(memory_space=pltpu.HBM)
    return pl.pallas_call(
        run,
        in_specs=[pl.BlockSpec(memory_space=pltpu.SMEM)]
        + [far if isinstance(v, Far) else near for v in ins]
        + [near] * n_after,
        out_specs=[near if stays else far for _, _, stays in outs],
        out_shape=[(pltpu.VMEM if stays else pltpu.HBM)(shape, dtype) for shape, dtype, stays in outs],
        scratch_shapes=list(scratch) + room + [pltpu.SemaphoreType.DMA((max(1, len(room)),))],
        compiler_params=pltpu.CompilerParams(vmem_limit_bytes=need + SPILL),
        cost_estimate=pl.CostEstimate(flops=int(cost * COST), bytes_accessed=0, transcendentals=0),
        name=name,
    )(scalars, *[pin(v) for v in ins], *[pin(v) for v in after])


def pin(value):
    if isinstance(value, Far):
        return pltpu.with_memory_space_constraint(value.value, pltpu.HBM)
    return pltpu.with_memory_space_constraint(value, pltpu.VMEM)


def swap(value, axes, sizes, mask):
    count = 1
    for size in sizes:
        count *= size
    return lax.ppermute(value, axes, [(i, i ^ mask) for i in range(count)])


class Moves:
    def __init__(self, n_dp, n_tensor):
        self.n_dp, self.n_tensor = n_dp, n_tensor
        self.dp = lax.axis_index("dp")
        self.here = lax.axis_index("tensor")

    def along(self, value, mask):
        return swap(value, "dp", (self.n_dp,), mask)

    def core(self, value):
        return self.along(value, 1)

    def side(self, value):
        return self.along(value, 2)

    def over(self, value):
        return swap(value, "tensor", (self.n_tensor,), 1)

    def cross(self, value):
        return swap(value, ("dp", "tensor"), (self.n_dp, self.n_tensor), 5)


    def reduce_core(self, scalars, keep, sent, name, extra=0, after=()):
        n = sent.shape[1] + extra // 4 * 3
        return call(
            functools.partial(core_kernel, extra),
            scalars,
            [keep, self.core(sent)],
            [((n, 128), BF, True)] * 3 + [((n, 128), F32, True)],
            name=name,
            after=after,
        )

    def sides(self, lows):
        return [self.side(lows[0]), self.over(lows[1]), self.cross(lows[2])]

    def total(self, scalars, values, name, after=()):
        shape = values[0].shape
        return call(total_kernel, scalars, values, [(shape, BF, True)], name=name, after=after, cost=0.7)[0]

    def bits(self):
        return [1 << i for i in range(2, self.n_dp.bit_length() - 1)]

    def gather(self, total):
        near = self.side(total)
        return total, near, self.core(total), self.core(near)


def local(
    n_dp, n_tensor, frames, resets, first_gain, first_shift, qkv_weight, out_weight, out_bias, second_gain,
    second_shift, up_weight, up_bias, down_weight, down_bias, prior_gain, prior_shift, prior_weight,
    prior_bias, out_cotangent, logit_cotangent,
):
    move = Moves(n_dp, n_tensor)
    rows, half = frames.shape
    width = 2 * half
    mine = rows // 2
    blocks = mine // BLOCK
    hidden_width, n_logits = up_bias.shape[0], prior_bias.shape[0]
    row = lambda v: v.reshape(1, -1)
    core, side = move.dp & 1, (move.dp >> 1) & 1
    reset_rows = jnp.pad(resets.reshape(-1, BLOCK), ((0, -(2 * blocks) % 8), (0, -BLOCK % 128)))
    scalars = jnp.stack([move.here, core * 2 + side]).astype(jnp.int32)
    total_rows = blocks * PAD
    quarter = hidden_width // 4

    def near_rows(*entries):
        return [((total_rows, n), dtype, True) for n, dtype in entries]

    def pieces(n):
        return [((4, n, 128), F32, True), ((4, n, 128), BF, True)]

    def columns(value, size, which):
        cut = lambda s, ref: ref.at[..., pl.ds(pl.multiple_of(s[which] * size, 128), size)]
        return Far(value, (*value.shape[:-1], size), cut)

    def some_rows(value, size, which):
        cut = lambda s, ref: ref.at[pl.ds(pl.multiple_of(s[which] * size, 16), size), :]
        return Far(value, (size, value.shape[1]), cut)

    vectors = [first_gain, first_shift, out_bias, second_gain, second_shift, down_bias, prior_gain, prior_shift]
    vectors = [row(v) for v in vectors + [up_bias, prior_bias]]
    qkv_rows = 3 * (width // 4) * (half // 128)
    sent_first, sent_one, sent_two, frames_own, small = call(
        first_kernel,
        scalars,
        [
            Far(frames),
            Far(
                qkv_weight,
                (3, width // 4, half),
                lambda s, ref: ref.at[:, pl.ds(pl.multiple_of(s[1] * (width // 4), 16), width // 4), :],
            ),
            columns(up_weight, quarter, 1),
            some_rows(out_weight, half // 4, 1),
            some_rows(down_weight, quarter, 1),
            columns(prior_weight, n_logits // 4, 1),
            *[Far(v) for v in vectors],
        ],
        [((total_rows * (half // 128) + qkv_rows, 128), BF, True)]
        + [((width * 2 + half + 48, 128), BF, True), ((quarter * 4 + width, 128), BF, True)]
        + near_rows((half, BF))
        + [((16, hidden_width), F32, True)],
        [pltpu.VMEM((rows + 16, half), F32), pltpu.VMEM((16, 128), F32), pltpu.VMEM((total_rows, half), BF)],
        "first_parts",
        cost=2.0,
    )

    def all_quarters(got):
        beside = move.side(got)
        return [got, beside, move.core(got), move.core(beside)]

    got_first = move.over(sent_first)
    (qkv_got,) = call(cut_kernel, scalars, [got_first], [((qkv_rows, 128), BF, True)], name="cut", cost=0.7)
    (sent_one,) = gate([sent_one], [got_first], "after_first")
    got_one = move.over(sent_one)
    (sent_two,) = gate([sent_two], [qkv_got, sent_one], "after_cut")
    got_two = move.over(sent_two)
    cot_sent, logit_own, out_own = call(
        cotangents_kernel,
        scalars,
        [Far(logit_cotangent), Far(out_cotangent)],
        near_rows((n_logits + half, BF), (n_logits, BF), (half, BF)),
        [pltpu.VMEM((rows + 16, n_logits), F32)]
        + [pltpu.VMEM((total_rows, n), BF) for n in (n_logits, half)],
        name="cotangents",
        after=(sent_first,),
        cost=2.3,
    )
    first, triple, mixed, qkv_other, frames_other = call(
        attend_kernel,
        scalars,
        [frames_own, got_first, Far(reset_rows), small, *all_quarters(qkv_got), Far(qkv_weight)],
        near_rows((width, BF), (3 * width, BF), (width, BF)) + [(qkv_weight.shape, BF, True)] + near_rows((half, BF)),
        name="attend",
        cost=5.5,
    )
    got_two, cot_sent = gate([got_two, cot_sent], [mixed], "after_attend")
    packed = all_quarters(got_one) + all_quarters(got_two)
    cotangents = move.over(cot_sent)
    block_send, block_own, middle, second, act, slope, ending, prior_in, out_weight_other = call(
        feed_kernel,
        scalars,
        [frames_own, frames_other, mixed, small, Far(out_weight), Far(up_weight), Far(down_weight), *packed],
        near_rows((half, BF))
        + near_rows((half, BF))
        + near_rows((width, F32), (width, BF), (2 * hidden_width, BF), (2 * hidden_width, F32))
        + near_rows((width, F32), (width, BF))
        + [(out_weight.shape, BF, True)],
        name="feed",
        cost=7.2,
    )
    made_send, logits_own, grad_ending, ending_grad, vec_three, prior_bias_sum = call(
        prior_kernel,
        scalars,
        [prior_in, ending, small, logit_own, out_own, block_send, *packed, cotangents, Far(prior_weight)],
        near_rows((n_logits + half, BF), (n_logits, F32), (width, F32), (width, BF))
        + [((3, width), F32, True), ((1, 2 * n_logits), F32, True)],
        [pltpu.VMEM(prior_weight.shape, BF), pltpu.VMEM((1, n_logits), F32)],
        name="prior",
        cost=3.7,
    )
    late_keep, late_send = call(
        late_grads_kernel,
        scalars,
        [prior_in, logit_own, cotangents, act, ending_grad],
        pieces(width + hidden_width),
        [pltpu.VMEM((width, n_logits), F32)],
        name="late_grads",
        cost=3.5,
    )
    hidden_grad, grad_middle, middle_grad, vec_two, up_bias_sum = call(
        feed_back_kernel,
        scalars,
        [ending_grad, slope, middle, grad_ending, small, *packed, Far(down_weight), Far(up_weight)],
        near_rows((2 * hidden_width, BF), (width, F32), (width, BF))
        + [((3, width), F32, True), ((1, 2 * hidden_width), F32, True)],
        [pltpu.VMEM((total_rows, width), F32)],
        name="feed_back",
        cost=6.5,
        after=(late_send,),
    )
    *late_low, late_rest = move.reduce_core(scalars, late_keep, late_send, "late_core", after=(hidden_grad,))
    up_keep, up_send = call(
        up_grads_kernel,
        scalars,
        [second, hidden_grad, mixed, middle_grad],
        pieces(width * hidden_width // 512 + half),
        [pltpu.VMEM((width, total_rows), BF), pltpu.VMEM((half, width), F32)],
        name="up_grads",
        after=(late_low[0],),
        cost=3.0,
    )
    triple_grad, frames_send, frames_grad, vec_one = call(
        attend_back_kernel,
        scalars,
        [middle_grad, grad_middle, frames_own, triple, qkv_other, out_weight_other, small, Far(out_weight), Far(reset_rows), frames_other]
        + [Far(qkv_weight)],
        near_rows((3 * width, BF), (half, BF), (half, F32)) + [((2, width), F32, True)],
        [pltpu.VMEM((total_rows, width), BF)],
        name="attend_back",
        after=(up_send,),
        cost=12.0,
    )
    *up_low, up_rest = move.reduce_core(scalars, up_keep, up_send, "up_core", after=(triple_grad,))
    late = move.total(scalars, [late_rest, *move.sides(late_low)], "late_1", after=(up_low[0],))
    spare = 64
    keep, send = call(
        early_grads_kernel,
        scalars,
        [first, triple_grad, vec_one, vec_two, vec_three, up_bias_sum, prior_bias_sum],
        pieces(768 + spare // 4),
        [pltpu.VMEM((spare, 128), F32)],
        name="early_grads",
        after=(late,),
        cost=2.0,
    )
    *lows, rest = move.reduce_core(scalars, keep, send, "early_core", spare)
    chains = {"late": late, "up": None, "early": None}
    done = lows[0]
    order = [("late", 0), ("up", None), ("early", None), ("up", 0), ("early", 0)]
    for bit in range(1, len(move.bits())):
        order += [("late", bit), ("up", bit), ("early", bit)]
    for name, bit in order:
        if bit is None:
            own, sent = (up_rest, up_low) if name == "up" else (rest, lows)
            values = [own, *move.sides(sent)]
        else:
            values = [chains[name], move.along(chains[name], move.bits()[bit])]
        done = chains[name] = move.total(scalars, values, f"{name}_{2 if bit is not None else 1}", after=(done,))
        if name == "early" and bit is None:
            frames_send, made_send = gate([frames_send, made_send], [done], "after_sides")
    frames_got = move.over(frames_send)
    made_got = move.over(made_send)
    late, up, early = (move.gather(chains[name]) for name in ("late", "up", "early"))
    qkv_grad, *named = call(
        early_place_kernel,
        scalars,
        list(early),
        [((3, width, half), F32, False)]
        + [((1, n), F32, False) for n in [width] * 8 + [hidden_width, n_logits]],
        [pltpu.VMEM((spare, 128), F32)],
        name="early_place",
        cost=2.0,
    )
    named = [v.reshape(-1) for v in named]
    down_grad, prior_grad = call(
        late_place_kernel,
        scalars,
        list(late),
        [((hidden_width, width), F32, False), ((width, n_logits), F32, False)],
        name="late_place",
        cost=2.5,
    )
    up_grad, out_grad = call(
        up_place_kernel,
        scalars,
        list(up),
        [((width, hidden_width), F32, False), ((half, width), F32, False)],
        name="up_place",
        cost=2.0,
    )
    block_out, logits = call(
        functools.partial(rows_kernel, [slice(n_logits, n_logits + half), slice(0, n_logits)]),
        scalars,
        [block_own, made_got, logits_own, made_got],
        [((rows, half), BF, False), ((rows, n_logits), F32, False)],
        [pltpu.VMEM((rows, half), F32), pltpu.VMEM((rows, n_logits), F32)],
        name="rows_made",
        cost=3.0,
    )
    (grad_frames,) = call(
        functools.partial(rows_kernel, [slice(None)]),
        scalars,
        [frames_grad, frames_got],
        [((rows, half), F32, False)],
        [pltpu.VMEM((rows, half), F32)],
        name="rows_frames",
        cost=2.0,
    )
    return (
        block_out,
        logits,
        grad_frames,
        named[0],
        named[1],
        qkv_grad,
        out_grad,
        named[4],
        named[2],
        named[3],
        up_grad,
        named[8],
        down_grad,
        named[7],
        named[5],
        named[6],
        prior_grad,
        named[9],
    )


def solution(mesh):
    rows, cols = P("dp", "tensor"), P(None, "tensor")
    placed = (
        rows, P("dp"), P(), P(), P(None, None, "tensor"), P("tensor", None), P(), P(), P(), cols, P("tensor"),
        P("tensor", None), P(), P(), P(), cols, P("tensor"), rows, rows,
    )
    given = (
        rows, rows, rows, P(), P(), P(None, None, "tensor"), P("tensor", None), P(), P(), P(), cols,
        P("tensor"), P("tensor", None), P(), P(), P(), cols, P("tensor"),
    )
    return jax.shard_map(
        functools.partial(local, mesh.shape["dp"], mesh.shape["tensor"]),
        mesh=mesh,
        in_specs=placed,
        out_specs=given,
        check_vma=False,
    )
```

```python
import functools
import math

import jax
import jax.numpy as jnp
from jax import lax
from jax.experimental import pallas as pl
from jax.experimental.pallas import tpu as pltpu
from jax.sharding import PartitionSpec as P

HEAD_DIM = 64
SEQ_LEN = 50
BLOCK = 4 * SEQ_LEN
PAD = -(-BLOCK // 16) * 16
EPS = 1e-05
NEG = -1e30
GELU_C = 0.7978845608028654
GELU_A = 0.044715
SPILL = 4 * 1024 * 1024
COST = 1e8
FOLD = 100.0
BF = jnp.bfloat16
F32 = jnp.float32
FIRST_GAIN, FIRST_SHIFT, OUT_BIAS, SECOND_GAIN, SECOND_SHIFT, DOWN_BIAS, PRIOR_GAIN, PRIOR_SHIFT, UP_BIAS, PRIOR_BIAS = range(10)


def mm(a, b):
    return lax.dot_general(a, b, (((1,), (0,)), ((), ())), preferred_element_type=F32)


def mm_bt(a, b):
    return lax.dot_general(a, b, (((1,), (1,)), ((), ())), preferred_element_type=F32)


def mm_at(a, b):
    return lax.dot_general(a, b, (((0,), (0,)), ((), ())), preferred_element_type=F32)


def norm_of(value):
    centre = value - jnp.mean(value, axis=-1, keepdims=True)
    factor = lax.rsqrt(jnp.mean(centre * centre, axis=-1, keepdims=True) + EPS)
    return centre * factor, factor


def norm_back(grad, unit, factor, gain):
    scaled = grad * gain
    first = jnp.mean(scaled, axis=-1, keepdims=True)
    second = jnp.mean(scaled * unit, axis=-1, keepdims=True)
    return factor * (scaled - first - unit * second)


def col_sum(value):
    return jnp.sum(value, axis=0, keepdims=True)


def whole_rows(here, own, other):
    low = jnp.where(here == 0, own[...], other[...])
    high = jnp.where(here == 0, other[...], own[...])
    return jnp.concatenate([low, high], axis=1).astype(F32)


def allowed_pairs(resets):
    place = lax.broadcasted_iota(jnp.int32, (1, PAD), 1)
    starts = jnp.where((resets == 1) | (lax.rem(place, SEQ_LEN) == 0) | (place >= BLOCK), place, 0)
    row = lax.broadcasted_iota(jnp.int32, (PAD, PAD), 0)
    col = lax.broadcasted_iota(jnp.int32, (PAD, PAD), 1)
    seg = jnp.max(jnp.where(col <= row, starts, 0).astype(F32), axis=-1, keepdims=True).astype(jnp.int32)
    seg2 = jnp.concatenate([seg, seg], axis=0)
    row = lax.broadcasted_iota(jnp.int32, (2 * PAD, PAD), 0)
    row = jnp.where(row >= PAD, row - PAD, row)
    col = lax.broadcasted_iota(jnp.int32, (2 * PAD, PAD), 1)
    return (col <= row) & (col >= seg2)


def two_heads(value):
    first = lax.broadcasted_iota(jnp.int32, value.shape, 1) < HEAD_DIM
    none = jnp.zeros_like(value)
    return jnp.concatenate([jnp.where(first, value, none), jnp.where(first, none, value)], axis=0)


def one_pair(value):
    first = lax.broadcasted_iota(jnp.int32, (PAD, 2 * HEAD_DIM), 1) < HEAD_DIM
    return jnp.where(first, value[:PAD], value[PAD:])


def softmax_of(query2, key, allowed):
    scores = jnp.where(allowed, mm_bt(query2, key), NEG)
    expo = jnp.exp(scores - jnp.max(scores, axis=-1, keepdims=True))
    return expo * (1.0 / jnp.sum(expo, axis=-1, keepdims=True))


def vector(small, index, n):
    return small[index : index + 1, :n]


def blocks_in(ref):
    return [slice(i * PAD, i * PAD + PAD) for i in range(ref.shape[0] // PAD)]


def add_up(sums, values):
    return [v if s is None else s + v for s, v in zip(sums, values, strict=True)]


def split_rows(half, source, own, sent, wide_rows):
    rows, n = source.shape
    wide_rows[0:rows, 0:n] = source[...].astype(F32)
    for which, target in ((half, own), (1 - half, sent)):
        for block, at in enumerate(blocks_in(target)):
            start = pl.multiple_of(which * (rows // 2) + block * BLOCK, 8)
            part = wide_rows[pl.ds(start, PAD), 0:n]
            inside = lax.broadcasted_iota(jnp.int32, part.shape, 0) < BLOCK
            target[at, :] = jnp.where(inside, part, 0.0).astype(BF)


def tiles_of(ref, start, n, count):
    return jnp.concatenate([ref[start + t * n : start + t * n + n, :] for t in range(count)], axis=1)


class Packed:
    def __init__(self, refs, n, q, o):
        self.one, self.two = refs
        self.n, self.q, self.o = n, q, o

    def up(self):
        return tiles_of(self.one, 0, self.n, 2)

    def out(self):
        return tiles_of(self.one, 2 * self.n, self.o, 4)

    def bias(self):
        start = 2 * self.n + 4 * self.o
        parts = [self.one[start + 16 * k : start + 16 * k + 16, :].astype(F32) for k in range(3)]
        return (parts[2] + parts[1] + parts[0])[:3]

    def down(self):
        return tiles_of(self.two, 0, self.q, 4)

    def prior(self):
        return self.two[4 * self.q : 4 * self.q + self.n, :]


def put_tiles(target, start, part):
    for t in range(part.shape[-1] // 128):
        target[start : start + part.shape[0], :] = part[:, t * 128 : t * 128 + 128]
        start += part.shape[0]
    return start


def first_kernel(s, frames, qkv, up, out, down, prior, *refs):
    smalls, (sent_ref, one_ref, two_ref, own_ref, small_ref, wide_rows, rows, other) = refs[:-8], refs[-8:]
    split_rows(s[0], frames, own_ref, other, wide_rows)
    start = put_tiles(sent_ref, 0, other)
    for c in range(3):
        start = put_tiles(sent_ref, start, qkv.get().at[c])
    start = put_tiles(one_ref, put_tiles(one_ref, 0, up), out)
    for i, ref in enumerate(smalls):
        small_ref[i : i + 1, : ref.shape[1]] = ref[...]
    rows[...] = jnp.zeros_like(rows)
    for t in range(2):
        rows[t : t + 1, :] = smalls[UP_BIAS][:, pl.ds(pl.multiple_of(s[1] * 256 + t * 128, 128), 128)]
    rows[2:3, :] = smalls[PRIOR_BIAS][:, pl.ds(pl.multiple_of(s[1] * 128, 128), 128)]
    left = rows[...]
    for k in range(3):
        term = left.astype(BF)
        one_ref[start : start + 16, :] = term
        left = left - term.astype(F32)
        start += 16
    put_tiles(two_ref, put_tiles(two_ref, 0, down), prior)


def cut_kernel(s, got, qkv_ref):
    qkv_ref[...] = got[got.shape[0] - qkv_ref.shape[0] :, :]


def cotangents_kernel(s, logit, out, sent, logit_own, out_own, wide_rows, logit_sent, out_sent):
    split_rows(s[0], logit, logit_own, logit_sent, wide_rows)
    split_rows(s[0], out, out_own, out_sent, wide_rows)
    n = logit_sent.shape[1]
    sent[:, :n] = logit_sent[...]
    sent[:, n:] = out_sent[...]


def gate(values, after, name=None):
    def run(*refs):
        pass

    near = pl.BlockSpec(memory_space=pltpu.VMEM)
    return pl.pallas_call(
        run,
        in_specs=[near] * (len(values) + len(after)),
        out_specs=[near] * len(values),
        out_shape=[pltpu.VMEM(v.shape, v.dtype) for v in values],
        input_output_aliases={i: i for i in range(len(values))},
        compiler_params=pltpu.CompilerParams(vmem_limit_bytes=1024 * 1024),
        cost_estimate=pl.CostEstimate(flops=0, bytes_accessed=0, transcendentals=0),
        name=name,
    )(*[pin(v) for v in values], *[pin(v) for v in after])


def attend_kernel(
    s, own, got, resets, small, q0, q1, q2, q3, qkv,
    first_ref, triple_ref, mixed_ref, qkv_other_ref, other,
):
    other[...] = tiles_of(got, 0, own.shape[0], 2)
    unit, _ = norm_of(whole_rows(s[0], own, other))
    n = first_ref.shape[1]
    first_ref[...] = (unit * vector(small, FIRST_GAIN, n) + vector(small, FIRST_SHIFT, n)).astype(BF)
    for j, piece in enumerate((q0, q1, q2, q3)):
        size = qkv.shape[1] // 4
        rows = pl.ds(pl.multiple_of((s[1] ^ j) * size, 16), size)
        for c in range(3):
            qkv_other_ref[c, rows, :] = tiles_of(piece, c * 2 * size, size, 2)
    for half, weight in enumerate((qkv, qkv_other_ref)):
        for c in range(3):
            value = mm(first_ref[...], weight[c]).astype(BF)
            triple_ref[:, (half * 3 + c) * 256 : (half * 3 + c + 1) * 256] = value
    for block, at in enumerate(blocks_in(own)):
        allowed = allowed_pairs(resets[pl.ds(s[0] * len(blocks_in(own)) + block, 1), :PAD])
        for pair in range(4):
            start = (pair // 2) * 768 + (pair % 2) * 128
            query, key, value = (
                triple_ref[at, start + c * 256 : start + c * 256 + 128] for c in range(3)
            )
            query2 = two_heads(query * HEAD_DIM ** (-0.5))
            weights = softmax_of(query2, key, allowed).astype(BF)
            mixed_ref[at, pair * 128 : pair * 128 + 128] = one_pair(mm(weights, value)).astype(BF)


def feed_kernel(
    s, own, other, mixed, small, out, up, down, *refs,
):
    packs, refs = refs[:8], refs[8:]
    block_other_ref, block_own_ref, middle_ref, second_ref, act_ref, slope_ref, ending_ref, prior_in_ref = refs[:-1]
    out_other_ref = refs[-1]
    n, half = out.shape[0], up.shape[1]
    packed = [Packed(p, up.shape[0], half // 4, n // 4) for p in zip(packs[:4], packs[4:])]
    for j, piece in enumerate(packed):
        out_other_ref[pl.ds(pl.multiple_of((s[1] ^ j) * (n // 4), 16), n // 4), :] = piece.out()
    middle_ref[...] = (
        whole_rows(s[0], own, other)
        + vector(small, OUT_BIAS, middle_ref.shape[1])
        + mm(mixed[:, :n], out[...])
        + mm(mixed[:, n:], out_other_ref[...])
    )
    unit, _ = norm_of(middle_ref[...])
    wide = middle_ref.shape[1]
    second_ref[...] = (unit * vector(small, SECOND_GAIN, wide) + vector(small, SECOND_SHIFT, wide)).astype(BF)
    ending_ref[...] = middle_ref[...] + vector(small, DOWN_BIAS, wide)
    for i in range(8):
        if i < 4:
            at = slice(i * 256, i * 256 + 256)
            w_up, w_down, bias = up[:, at], down[at, :], small[UP_BIAS : UP_BIAS + 1, at]
        else:
            place = pl.multiple_of((s[1] ^ (i - 4)) * 256, 256)
            at = pl.ds(pl.multiple_of(half + place, 256), 256)
            w_up, w_down = packed[i - 4].up(), packed[i - 4].down()
            bias = packed[i - 4].bias()
            bias = jnp.concatenate([bias[0:1], bias[1:2]], axis=1)
        for rows in blocks_in(own):
            hidden = mm(second_ref[rows, :], w_up) + bias
            square = hidden * hidden
            bent = jnp.tanh(GELU_C * (hidden + GELU_A * hidden * square))
            act = (0.5 * hidden * (1.0 + bent)).astype(BF)
            slope = 0.5 * (1.0 + bent) + (0.5 * GELU_C) * hidden * (1.0 - bent * bent) * (
                1.0 + (3.0 * GELU_A) * square
            )
            act_ref[rows, at] = act
            slope_ref[rows, at] = slope
            ending_ref[rows, :] += mm(act, w_down)
    total = ending_ref[...]
    unit, _ = norm_of(total)
    prior_in_ref[...] = (unit * vector(small, PRIOR_GAIN, wide) + vector(small, PRIOR_SHIFT, wide)).astype(BF)
    low, high = total[:, :256].astype(BF), total[:, 256:].astype(BF)
    block_own_ref[...] = jnp.where(s[0] == 0, low, high)
    block_other_ref[...] = jnp.where(s[0] == 0, high, low)


def prior_kernel(
    s, prior_in, ending, small, logit_own, out_own, block_other, a0, a1, a2, a3, b0, b1, b2, b3, cotangents, prior,
    sent_ref, logits_ref, grad_ending_ref, ending_grad_ref, vec_ref, bias_ref, weight, bias,
):
    half, n = prior.shape[1], prior.shape[0]
    for j, piece in enumerate(zip((a0, a1, a2, a3), (b0, b1, b2, b3))):
        at = pl.ds(pl.multiple_of((s[1] ^ j) * 128, 128), 128)
        piece = Packed(piece, n, n // 2, n // 8)
        weight[:, at] = piece.prior()
        bias[:, at] = piece.bias()[2:3]
    logit_other = cotangents.at[:, :half]
    sent_ref[:, :half] = (mm(prior_in[...], weight[...]) + bias[...]).astype(BF)
    sent_ref[:, half:] = block_other[...]
    logits_ref[...] = mm(prior_in[...], prior[...]) + vector(small, PRIOR_BIAS, half)
    back = mm_bt(logit_own[...], prior[...]) + mm_bt(logit_other[...], weight[...])
    unit, factor = norm_of(ending[...])
    gain = vector(small, PRIOR_GAIN, unit.shape[1])
    grad = whole_rows(s[0], out_own, cotangents.at[:, half:]) + norm_back(back, unit, factor, gain)
    grad_ending_ref[...] = grad
    ending_grad_ref[...] = grad.astype(BF)
    vec_ref[...] = jnp.concatenate([col_sum(back * unit), col_sum(back), col_sum(grad)], axis=0)
    bias_ref[:, :half] = col_sum(logit_own[...].astype(F32))
    bias_ref[:, half:] = col_sum(logit_other[...].astype(F32))


def store_piece(keep, send, h, j, start, value):
    at = slice(start, start + value.shape[0])
    if j < 2:
        keep[h * 2 + j, at, :] = value
    else:
        send[h * 2 + j - 2, at, :] = value.astype(BF)


def late_grads_kernel(s, prior_in, logit_own, cotangents, act, ending_grad, keep, send, wide):
    half = act.shape[1] // 2
    logit_other = cotangents.at[:, : logit_own.shape[1]]
    n = prior_in.shape[1]
    for h in range(2):
        wide[...] = mm_at(prior_in[...], (logit_own, logit_other)[h][...])
        for j in (2, 3, 0, 1):
            place = s[1] ^ j
            store_piece(keep, send, h, j, 0, wide[:, pl.ds(pl.multiple_of(place * 128, 128), 128)])
            part = act[:, pl.ds(pl.multiple_of(h * half + place * 256, 256), 256)]
            value = mm_at(part, ending_grad[...])
            for t in range(n // 128):
                store_piece(keep, send, h, j, n + t * 256, value[:, t * 128 : t * 128 + 128])


def up_grads_kernel(s, second, hidden_grad, mixed, middle_grad, keep, send, turned, wide):
    turned[...] = second[...].T
    half = hidden_grad.shape[1] // 2
    n, m = second.shape[1], mixed.shape[1] // 2
    for h in range(2):
        wide[...] = mm_at(mixed[:, h * m : h * m + m], middle_grad[...])
        for j in (2, 3, 0, 1):
            place = s[1] ^ j
            value = mm(turned[...], hidden_grad[:, pl.ds(pl.multiple_of(h * half + place * 256, 256), 256)])
            for t in range(2):
                store_piece(keep, send, h, j, t * n, value[:, t * 128 : t * 128 + 128])
            store_piece(keep, send, h, j, 2 * n, wide[:, pl.ds(pl.multiple_of(place * 128, 128), 128)])


def early_grads_kernel(s, first, grad_own, grad_other, keep, send):
    for h in range(2):
        for j in (2, 3, 0, 1):
            place = pl.multiple_of((s[1] ^ j) * 128, 128)
            value = mm_at(first[:, pl.ds(place, 128)], (grad_own, grad_other)[h][...])
            for c in range(3):
                for t in range(2):
                    at = slice(c * 256 + t * 128, c * 256 + t * 128 + 128)
                    store_piece(keep, send, h, j, (t * 3 + c) * 128, value[:, at])


def feed_back_kernel(
    s, ending_grad, slope, middle, grad_ending, small, a0, a1, a2, a3, b0, b1, b2, b3, down, up,
    hidden_grad_ref, grad_middle_ref, middle_grad_ref, vec_ref, bias_ref, back,
):
    half, n = up.shape[1], up.shape[0]
    packed = [Packed(p, n, half // 4, n // 8) for p in zip((a0, a1, a2, a3), (b0, b1, b2, b3))]
    for i in range(8):
        if i < 4:
            at = slice(i * 256, i * 256 + 256)
            w_up, w_down = up[:, at], down[at, :]
        else:
            at = pl.ds(pl.multiple_of(half + (s[1] ^ (i - 4)) * 256, 256), 256)
            w_up, w_down = packed[i - 4].up(), packed[i - 4].down()
        sums = [None]
        for rows in blocks_in(ending_grad):
            low = (mm_bt(ending_grad[rows, :], w_down) * slope[rows, at]).astype(BF)
            hidden_grad_ref[rows, at] = low
            sums = add_up(sums, [col_sum(low.astype(F32))])
            value = mm_bt(low, w_up)
            if i == 0:
                back[rows, :] = value
            else:
                back[rows, :] += value
        bias_ref[:, at] = sums[0]
    unit, factor = norm_of(middle[...])
    value = back[...]
    gain = vector(small, SECOND_GAIN, unit.shape[1])
    total = grad_ending[...] + norm_back(value, unit, factor, gain)
    grad_middle_ref[...] = total
    middle_grad_ref[...] = total.astype(BF)
    vec_ref[...] = jnp.concatenate([col_sum(value * unit), col_sum(value), col_sum(total)], axis=0)


def attend_back_kernel(
    half, s, middle_grad, triple, out, resets,
    triple_grad_ref, mixed_grad,
):
    mixed_grad[...] = mm_bt(middle_grad[...], out[...]).astype(BF)
    factor = HEAD_DIM ** (-0.5)
    for block, at in enumerate(blocks_in(triple)):
        allowed = allowed_pairs(resets[pl.ds(s[0] * len(blocks_in(triple)) + block, 1), :PAD])
        for pair in range(2):
            start = half * 768 + pair * 128
            query, key, value = (triple[at, start + c * 256 : start + c * 256 + 128] for c in range(3))
            query2 = two_heads(query * factor)
            mixed2 = two_heads(mixed_grad[at, pair * 128 : pair * 128 + 128])
            again = softmax_of(query2, key, allowed)
            weight_grad = mm_bt(mixed2, value)
            inner = jnp.sum(again * weight_grad, axis=-1, keepdims=True)
            score_grad = (again * (weight_grad - inner)).astype(BF)
            thirds = (
                (one_pair(mm(score_grad, key)) * factor).astype(BF),
                mm_at(score_grad, query2).astype(BF),
                mm_at(again.astype(BF), mixed2).astype(BF),
            )
            for c in range(3):
                triple_grad_ref[at, c * 256 + pair * 128 : c * 256 + pair * 128 + 128] = thirds[c]


def frames_back_kernel(
    s, grad_own, grad_other, grad_middle, own, other, qkv_other, small, made, qkv,
    sent_ref, frames_own_ref, vec_ref,
):
    back = None
    for part, weight in ((grad_own, qkv), (grad_other, qkv_other)):
        for c in range(3):
            value = mm_bt(part[:, c * 256 : c * 256 + 256], weight[c])
            back = value if back is None else back + value
    unit, scale = norm_of(whole_rows(s[0], own, other))
    total = grad_middle[...] + norm_back(back, unit, scale, vector(small, FIRST_GAIN, unit.shape[1]))
    low, high = total[:, :256], total[:, 256:]
    frames_own_ref[...] = jnp.where(s[0] == 0, low, high)
    n = made.shape[1]
    sent_ref[:, :n] = made[...]
    sent_ref[:, n:] = jnp.where(s[0] == 0, high, low).astype(BF)
    vec_ref[...] = jnp.concatenate([col_sum(back * unit), col_sum(back)], axis=0)


def late_place_kernel(s, mine, near, far, farther, down_ref, prior_ref):
    n, q = prior_ref.shape[0], down_ref.shape[0] // 4
    for j, piece in enumerate((mine, near, far, farther)):
        place = s[1] ^ j
        rows = pl.ds(pl.multiple_of(place * q, 8), q)
        for t in range(down_ref.shape[1] // 128):
            down_ref[rows, t * 128 : t * 128 + 128] = piece[n + t * q : n + t * q + q, :].astype(F32)
        prior_ref[:, pl.ds(pl.multiple_of(place * 128, 128), 128)] = piece[:n, :].astype(F32)


def up_place_kernel(s, mine, near, far, farther, up_ref, out_ref):
    n, m = up_ref.shape[0], out_ref.shape[0]
    for j, piece in enumerate((mine, near, far, farther)):
        place = s[1] ^ j
        for t in range(2):
            columns = pl.ds(pl.multiple_of(place * 256 + t * 128, 128), 128)
            up_ref[:, columns] = piece[t * n : t * n + n, :].astype(F32)
        out_ref[:, pl.ds(pl.multiple_of(place * 128, 128), 128)] = piece[2 * n : 2 * n + m, :].astype(F32)


def early_place_kernel(s, mine, near, far, farther, qkv_ref, *vecs):
    vecs, sums = vecs[:-1], vecs[-1]
    sums[...] = mine[6 * 128 :, :].astype(F32) + far[6 * 128 :, :].astype(F32)
    for j, piece in enumerate((mine, near, far, farther)):
        at = pl.ds(pl.multiple_of((s[1] ^ j) * 128, 128), 128)
        for c in range(3):
            for t in range(2):
                start = (t * 3 + c) * 128
                qkv_ref[c, at, t * 128 : t * 128 + 128] = piece[start : start + 128, :].astype(F32)
    qkv_ref.send()
    row = 0
    for ref in vecs[:8]:
        for t in range(ref.shape[1] // 128):
            ref[:, t * 128 : t * 128 + 128] = sums[row : row + 1, :]
            row += 1
    for ref in vecs[8:]:
        tiles = ref.shape[1] // 128
        for t in range(tiles):
            ref[:, t * 128 : t * 128 + 128] = sums[pl.ds(row + s[0] * tiles + t, 1), :]
        row += 2 * tiles


def core_kernel(s, keep, got, low, rest):
    n = keep.shape[1]
    for out, places, dtype in ((low, (2, 3), BF), (rest, (0, 1), F32)):
        for k, i in enumerate(places):
            out[k * n : k * n + n, :] = (keep[i] + got[i].astype(F32)).astype(dtype)


def core_all_kernel(s, keep, got, *refs):
    vectors, lows, rest = refs[:-4], refs[-4:-1], refs[-1]
    n = keep.shape[1]
    for i in (1, 2, 3):
        lows[i - 1][:n, :] = (keep[i] + got[i].astype(F32)).astype(BF)
    rest[:n, :] = keep[0] + got[0].astype(F32)
    if vectors:
        put_vectors(s, vectors, rest, n)
        for low in lows:
            low[n:, :] = rest[n:, :].astype(BF)


def put_vectors(s, vectors, rest, row):
    for ref in vectors[:3]:
        for i in range(ref.shape[0]):
            for t in range(ref.shape[1] // 128):
                rest[row : row + 1, :] = ref[i : i + 1, t * 128 : t * 128 + 128]
                row += 1
    for ref in vectors[3:]:
        tiles = ref.shape[1] // 128
        for t in range(tiles):
            place = row + lax.rem(t + s[0] * (tiles // 2), tiles)
            rest[pl.ds(place, 1), :] = ref[:, t * 128 : t * 128 + 128]
        row += tiles
    rest[row:, :] = jnp.zeros((rest.shape[0] - row, 128), F32)


def over_kernel(s, rest, got, low, mine):
    n = low.shape[0]
    low[...] = (rest[n:, :] + got[n:, :].astype(F32)).astype(BF)
    mine[...] = rest[:n, :] + got[:n, :].astype(F32)


def halves_kernel(s, *refs):
    total, (keep, send) = refs[-1], refs[-3:-1]
    total[...] = functools.reduce(lambda x, y: x + y, [r[...].astype(F32) for r in refs[:-3]])
    n = keep.shape[0]
    send[...] = total[pl.ds(pl.multiple_of((1 - s[2]) * n, 16), n), :].astype(BF)
    keep[...] = total[pl.ds(pl.multiple_of(s[2] * n, 16), n), :].astype(BF)


def join_kernel(s, mine, got, out):
    n = mine.shape[0]
    out[pl.ds(pl.multiple_of(s[2] * n, 16), n), :] = mine[...]
    out[pl.ds(pl.multiple_of((1 - s[2]) * n, 16), n), :] = got[...]


def total_kernel(s, *refs):
    refs[-1][...] = functools.reduce(lambda x, y: x + y, [r[...].astype(F32) for r in refs[:-1]]).astype(BF)


def rows_kernel(entries, s, *refs):
    count = len(entries)
    given, outs, rooms = refs[: 2 * count], refs[2 * count : 3 * count], refs[3 * count :]
    for i, columns in enumerate(entries):
        own, got, out, room = given[2 * i], given[2 * i + 1], outs[i], rooms[i]
        rows = out.shape[0] // 2
        for block, at in enumerate(blocks_in(own)):
            for which, ref, cut in ((s[0], own, slice(None)), (1 - s[0], got, columns)):
                start = pl.multiple_of(which * rows + block * BLOCK, 8)
                room[pl.ds(start, BLOCK), :] = ref[at, cut].astype(F32)[:BLOCK]
        out[...] = room[...].astype(out.ref.dtype)
        out.send()


class Loaded:
    def __init__(self, ref, copy):
        self.ref, self.copy, self.shape = ref, copy, ref.shape

    def get(self):
        if self.copy is not None:
            self.copy.wait()
            self.copy = None
        return self.ref

    def __getitem__(self, index):
        return self.get()[index]


class Leaving:
    def __init__(self, ref, copy):
        self.ref, self.copy, self.shape, self.sent = ref, copy, ref.shape, False

    def __getitem__(self, index):
        return self.ref[index]

    def __setitem__(self, index, value):
        self.ref[index] = value

    def send(self):
        if not self.sent:
            self.copy.start()
            self.sent = True


class Far:
    def __init__(self, value, shape=None, cut=None):
        self.value, self.shape, self.cut = value, shape or value.shape, cut or (lambda s, ref: ref)


def call(kernel, scalars, ins, outs, scratch=(), name=None, after=(), cost=1.0):
    n_in, n_out, n_after = len(ins), len(outs), len(after)
    far_in = [i for i, v in enumerate(ins) if isinstance(v, Far)]
    far_out = [i for i, o in enumerate(outs) if not o[2]]
    room = [pltpu.VMEM(ins[i].shape, ins[i].value.dtype) for i in far_in]
    room += [pltpu.VMEM(outs[i][0], outs[i][1]) for i in far_out]
    need = sum(math.prod(r.shape) * jnp.dtype(r.dtype).itemsize for r in room + list(scratch))

    def run(s, *refs):
        given, refs = list(refs[:n_in]), refs[n_in + n_after :]
        made, refs = list(refs[:n_out]), refs[n_out:]
        own, refs = refs[: len(scratch)], refs[len(scratch) :]
        rooms, sems = refs[:-1], refs[-1]
        for k, i in enumerate(far_in):
            copy = pltpu.make_async_copy(ins[i].cut(s, given[i]), rooms[k], sems.at[k])
            copy.start()
            given[i] = Loaded(rooms[k], copy)
        leaving = []
        for k, i in enumerate(far_out, len(far_in)):
            made[i] = Leaving(rooms[k], pltpu.make_async_copy(rooms[k], made[i], sems.at[k]))
            leaving.append(made[i])
        kernel(s, *given, *made, *own)
        for value in given:
            if isinstance(value, Loaded):
                value.get()
        for value in leaving:
            value.send()
        for value in leaving:
            value.copy.wait()

    near, far = pl.BlockSpec(memory_space=pltpu.VMEM), pl.BlockSpec(memory_space=pltpu.HBM)
    return pl.pallas_call(
        run,
        in_specs=[pl.BlockSpec(memory_space=pltpu.SMEM)]
        + [far if isinstance(v, Far) else near for v in ins]
        + [far if isinstance(v, Far) else near for v in after],
        out_specs=[near if stays else far for _, _, stays in outs],
        out_shape=[(pltpu.VMEM if stays else pltpu.HBM)(shape, dtype) for shape, dtype, stays in outs],
        scratch_shapes=list(scratch) + room + [pltpu.SemaphoreType.DMA((max(1, len(room)),))],
        compiler_params=pltpu.CompilerParams(vmem_limit_bytes=need + SPILL),
        cost_estimate=pl.CostEstimate(flops=int(cost * COST), bytes_accessed=0, transcendentals=0),
        name=name,
    )(scalars, *[pin(v) for v in ins], *[pin(v) for v in after])


def pin(value):
    if isinstance(value, Far):
        return pltpu.with_memory_space_constraint(value.value, pltpu.HBM)
    return pltpu.with_memory_space_constraint(value, pltpu.VMEM)


def swap(value, axes, sizes, mask):
    count = 1
    for size in sizes:
        count *= size
    return lax.ppermute(value, axes, [(i, i ^ mask) for i in range(count)])


class Moves:
    def __init__(self, n_dp, n_tensor):
        self.n_dp, self.n_tensor = n_dp, n_tensor
        self.dp = lax.axis_index("dp")
        self.here = lax.axis_index("tensor")

    def along(self, value, mask):
        return swap(value, "dp", (self.n_dp,), mask)

    def core(self, value):
        return self.along(value, 1)

    def side(self, value):
        return self.along(value, 2)

    def over(self, value):
        return swap(value, "tensor", (self.n_tensor,), 1)

    def cross(self, value):
        return swap(value, ("dp", "tensor"), (self.n_dp, self.n_tensor), 5)


    def reduce_core(self, scalars, keep, sent, name, after=()):
        n = 2 * sent.shape[1]
        outs = [((n, 128), BF, True), ((n, 128), F32, True)]
        return call(core_kernel, scalars, [keep, self.core(sent)], outs, name=name, after=after, cost=FOLD)

    def reduce_over(self, scalars, low, rest, name, after=()):
        n = low.shape[0] // 2
        outs = [((n, 128), BF, True), ((n, 128), F32, True)]
        return call(over_kernel, scalars, [rest, self.over(low)], outs, name=name, after=after, cost=FOLD)

    def reduce_core_all(self, scalars, keep, sent, name, vectors=(), spare=0, after=()):
        n = sent.shape[1] + spare
        outs = [((n, 128), BF, True)] * 3 + [((n, 128), F32, True)]
        ins = [keep, self.core(sent), *vectors]
        return call(core_all_kernel, scalars, ins, outs, name=name, after=after, cost=FOLD)

    def sides(self, lows):
        return [self.side(lows[0]), self.over(lows[1]), self.cross(lows[2])]

    def total(self, scalars, values, name, after=()):
        shape = values[0].shape
        return call(total_kernel, scalars, values, [(shape, BF, True)], name=name, after=after, cost=FOLD)[0]

    def halves(self, scalars, values, name, after=()):
        n = values[0].shape[0]
        return call(
            halves_kernel,
            scalars,
            values,
            [((n // 2, 128), BF, True)] * 2,
            [pltpu.VMEM((n, 128), F32)],
            name=name,
            after=after,
            cost=FOLD,
        )

    def join(self, scalars, mine, got, name, after=()):
        shape = (mine.shape[0] * 2, 128)
        return call(join_kernel, scalars, [mine, got], [(shape, BF, True)], name=name, after=after, cost=FOLD)[0]

    def bits(self):
        return [1 << i for i in range(2, self.n_dp.bit_length() - 1)]

    def gather(self, total):
        near = self.side(total)
        return total, near, self.core(total), self.core(near)


def local(
    n_dp, n_tensor, frames, resets, first_gain, first_shift, qkv_weight, out_weight, out_bias, second_gain,
    second_shift, up_weight, up_bias, down_weight, down_bias, prior_gain, prior_shift, prior_weight,
    prior_bias, out_cotangent, logit_cotangent,
):
    move = Moves(n_dp, n_tensor)
    rows, half = frames.shape
    width = 2 * half
    mine = rows // 2
    blocks = mine // BLOCK
    hidden_width, n_logits = up_bias.shape[0], prior_bias.shape[0]
    row = lambda v: v.reshape(1, -1)
    core, side = move.dp & 1, (move.dp >> 1) & 1
    reset_rows = jnp.pad(resets.reshape(-1, BLOCK), ((0, -(2 * blocks) % 8), (0, -BLOCK % 128)))
    scalars = jnp.stack([move.here, core * 2 + side, (move.dp >> 2) & 1]).astype(jnp.int32)
    total_rows = blocks * PAD
    quarter = hidden_width // 4

    def near_rows(*entries):
        return [((total_rows, n), dtype, True) for n, dtype in entries]

    def pieces(n):
        return [((4, n, 128), F32, True), ((4, n, 128), BF, True)]

    def columns(value, size, which):
        cut = lambda s, ref: ref.at[..., pl.ds(pl.multiple_of(s[which] * size, 128), size)]
        return Far(value, (*value.shape[:-1], size), cut)

    def some_rows(value, size, which):
        cut = lambda s, ref: ref.at[pl.ds(pl.multiple_of(s[which] * size, 16), size), :]
        return Far(value, (size, value.shape[1]), cut)

    vectors = [first_gain, first_shift, out_bias, second_gain, second_shift, down_bias, prior_gain, prior_shift]
    vectors = [row(v) for v in vectors + [up_bias, prior_bias]]
    qkv_rows = 3 * (width // 4) * (half // 128)
    sent_first, sent_one, sent_two, frames_own, small = call(
        first_kernel,
        scalars,
        [
            Far(frames),
            Far(
                qkv_weight,
                (3, width // 4, half),
                lambda s, ref: ref.at[:, pl.ds(pl.multiple_of(s[1] * (width // 4), 16), width // 4), :],
            ),
            columns(up_weight, quarter, 1),
            some_rows(out_weight, half // 4, 1),
            some_rows(down_weight, quarter, 1),
            columns(prior_weight, n_logits // 4, 1),
            *[Far(v) for v in vectors],
        ],
        [((total_rows * (half // 128) + qkv_rows, 128), BF, True)]
        + [((width * 2 + half + 48, 128), BF, True), ((quarter * 4 + width, 128), BF, True)]
        + near_rows((half, BF))
        + [((16, hidden_width), F32, True)],
        [pltpu.VMEM((rows + 16, half), F32), pltpu.VMEM((16, 128), F32), pltpu.VMEM((total_rows, half), BF)],
        "first_parts",
        cost=2.0,
    )

    def all_quarters(got):
        beside = move.side(got)
        return [got, beside, move.core(got), move.core(beside)]

    got_first = move.over(sent_first)
    (qkv_got,) = call(cut_kernel, scalars, [got_first], [((qkv_rows, 128), BF, True)], name="cut", cost=100.0)
    (sent_one,) = gate([sent_one], [got_first], "after_first")
    got_one = move.over(sent_one)
    (sent_two,) = gate([sent_two], [qkv_got, sent_one], "after_cut")
    got_two = move.over(sent_two)
    cot_sent, logit_own, out_own = call(
        cotangents_kernel,
        scalars,
        [Far(logit_cotangent), Far(out_cotangent)],
        near_rows((n_logits + half, BF), (n_logits, BF), (half, BF)),
        [pltpu.VMEM((rows + 16, n_logits), F32)]
        + [pltpu.VMEM((total_rows, n), BF) for n in (n_logits, half)],
        name="cotangents",
        after=(sent_first,),
        cost=2.3,
    )
    first, triple, mixed, qkv_other, frames_other = call(
        attend_kernel,
        scalars,
        [frames_own, got_first, Far(reset_rows), small, *all_quarters(qkv_got), Far(qkv_weight)],
        near_rows((width, BF), (3 * width, BF), (width, BF)) + [(qkv_weight.shape, BF, True)] + near_rows((half, BF)),
        name="attend",
        cost=5.5,
    )
    beside_one = move.side(got_one)
    got_two, cot_sent = gate([got_two, cot_sent], [mixed, beside_one], "after_attend")
    beside_two = move.side(got_two)
    packed = [got_one, beside_one, move.core(got_one), move.core(beside_one)]
    packed += [got_two, beside_two, move.core(got_two), move.core(beside_two)]
    cotangents = move.over(cot_sent)
    block_send, block_own, middle, second, act, slope, ending, prior_in, out_weight_other = call(
        feed_kernel,
        scalars,
        [frames_own, frames_other, mixed, small, Far(out_weight), Far(up_weight), Far(down_weight), *packed],
        near_rows((half, BF))
        + near_rows((half, BF))
        + near_rows((width, F32), (width, BF), (2 * hidden_width, BF), (2 * hidden_width, F32))
        + near_rows((width, F32), (width, BF))
        + [(out_weight.shape, BF, True)],
        name="feed",
        cost=7.2,
    )
    made_send, logits_own, grad_ending, ending_grad, vec_three, prior_bias_sum = call(
        prior_kernel,
        scalars,
        [prior_in, ending, small, logit_own, out_own, block_send, *packed, cotangents, Far(prior_weight)],
        near_rows((n_logits + half, BF), (n_logits, F32), (width, F32), (width, BF))
        + [((3, width), F32, True), ((1, 2 * n_logits), F32, True)],
        [pltpu.VMEM(prior_weight.shape, BF), pltpu.VMEM((1, n_logits), F32)],
        name="prior",
        cost=3.7,
    )
    late_keep, late_send = call(
        late_grads_kernel,
        scalars,
        [prior_in, logit_own, cotangents, act, ending_grad],
        pieces(width + hidden_width),
        [pltpu.VMEM((width, n_logits), F32)],
        name="late_grads",
        cost=3.5,
    )
    hidden_grad, grad_middle, middle_grad, vec_two, up_bias_sum = call(
        feed_back_kernel,
        scalars,
        [ending_grad, slope, middle, grad_ending, small, *packed, Far(down_weight), Far(up_weight)],
        near_rows((2 * hidden_width, BF), (width, F32), (width, BF))
        + [((3, width), F32, True), ((1, 2 * hidden_width), F32, True)],
        [pltpu.VMEM((total_rows, width), F32)],
        name="feed_back",
        cost=6.5,
        after=(late_send,),
    )
    *late_low, late_rest = move.reduce_core_all(scalars, late_keep, late_send, "late_core", after=(hidden_grad,))
    up_keep, up_send = call(
        up_grads_kernel,
        scalars,
        [second, hidden_grad, mixed, middle_grad],
        pieces(width * hidden_width // 512 + half),
        [pltpu.VMEM((width, total_rows), BF), pltpu.VMEM((half, width), F32)],
        name="up_grads",
        after=(late_low[0],),
        cost=3.0,
    )
    def attend_back(half, out, after):
        return call(
            functools.partial(attend_back_kernel, half),
            scalars,
            [middle_grad, triple, out, Far(reset_rows)],
            near_rows((3 * width // 2, BF)),
            [pltpu.VMEM((total_rows, width // 2), BF)],
            name=f"attend_back_{half}",
            after=after,
            cost=4.5,
        )[0]

    grad_own = attend_back(0, Far(out_weight), (up_send,))
    up_low, up_rest = move.reduce_core(scalars, up_keep, up_send, "up_core", (grad_own,))
    grad_other = attend_back(1, out_weight_other, (up_low,))
    keep, send = call(
        early_grads_kernel,
        scalars,
        [first, grad_own, grad_other],
        pieces(768),
        name="early_grads",
        after=(),
        cost=2.0,
    )
    late, late_half = move.halves(scalars, [late_rest, *move.sides(late_low)], "late_1", (send,))
    back_send, frames_grad, vec_one = call(
        frames_back_kernel,
        scalars,
        [grad_own, grad_other, grad_middle, frames_own, frames_other, qkv_other, small, made_send]
        + [Far(qkv_weight)],
        near_rows((n_logits + 2 * half, BF), (half, F32)) + [((2, width), F32, True)],
        name="frames_back",
        after=(late,),
        cost=2.5,
    )
    bits = move.bits()
    spare = 64
    vectors = [vec_one, vec_two, vec_three, up_bias_sum, prior_bias_sum]
    *early_low, early_rest = move.reduce_core_all(scalars, keep, send, "early_core", vectors, spare)
    late = move.total(scalars, [late, move.along(late_half, bits[0])], "late_2", (early_low[0],))
    up_low, up_rest = move.reduce_over(scalars, up_low, up_rest, "up_over", (late,))
    done = up_low
    for bit in bits[1:]:
        done = late = move.total(scalars, [late, move.along(late, bit)], "late_3", (done,))
    done = early = move.total(scalars, [early_rest, *move.sides(early_low)], "early_1", (done,))
    up, up_half = move.halves(scalars, [up_rest, move.side(up_low)], "up_1", (done,))
    (back_send,) = gate([back_send], [up], "after_sides")
    done = late = move.join(scalars, late, move.along(late, bits[0]), "late_4", (up,))
    for bit in bits[:-1]:
        done = early = move.total(scalars, [early, move.along(early, bit)], "early_2", (done,))
    done = up = move.total(scalars, [up, move.along(up_half, bits[0])], "up_2", (done,))
    down_grad, prior_grad = call(
        late_place_kernel,
        scalars,
        list(move.gather(late)),
        [((hidden_width, width), F32, False), ((width, n_logits), F32, False)],
        name="late_place",
        after=(done,),
        cost=FOLD,
    )
    early = move.total(scalars, [early, move.along(early, bits[-1])], "early_3", (Far(down_grad),))
    done = early
    for bit in bits[1:]:
        done = up = move.total(scalars, [up, move.along(up, bit)], "up_3", (done,))
    up = move.join(scalars, up, move.along(up, bits[0]), "up_4", (done,))
    back_got = move.over(back_send)
    up, early_pieces = move.gather(up), move.gather(early)
    block_out, logits, grad_frames = call(
        functools.partial(
            rows_kernel,
            [slice(n_logits, n_logits + half), slice(0, n_logits), slice(n_logits + half, n_logits + 2 * half)],
        ),
        scalars,
        [v for own in (block_own, logits_own, frames_grad) for v in (own, back_got)],
        [((rows, half), BF, False), ((rows, n_logits), F32, False), ((rows, half), F32, False)],
        [pltpu.VMEM((rows, n), F32) for n in (half, n_logits, half)],
        name="rows_back",
        after=(up[0],),
        cost=FOLD,
    )
    qkv_grad, *named = call(
        early_place_kernel,
        scalars,
        list(early_pieces),
        [((3, width, half), F32, False)]
        + [((1, n), F32, False) for n in [width] * 8 + [hidden_width, n_logits]],
        [pltpu.VMEM((spare, 128), F32)],
        name="early_place",
        after=(Far(block_out),),
        cost=FOLD,
    )
    up_grad, out_grad = call(
        up_place_kernel,
        scalars,
        list(up),
        [((width, hidden_width), F32, False), ((half, width), F32, False)],
        name="up_place",
        after=(Far(qkv_grad),),
        cost=FOLD,
    )
    named = [v.reshape(-1) for v in named]
    return (
        block_out,
        logits,
        grad_frames,
        named[0],
        named[1],
        qkv_grad,
        out_grad,
        named[4],
        named[2],
        named[3],
        up_grad,
        named[8],
        down_grad,
        named[7],
        named[5],
        named[6],
        prior_grad,
        named[9],
    )


def solution(mesh):
    rows, cols = P("dp", "tensor"), P(None, "tensor")
    placed = (
        rows, P("dp"), P(), P(), P(None, None, "tensor"), P("tensor", None), P(), P(), P(), cols, P("tensor"),
        P("tensor", None), P(), P(), P(), cols, P("tensor"), rows, rows,
    )
    given = (
        rows, rows, rows, P(), P(), P(None, None, "tensor"), P("tensor", None), P(), P(), P(), cols,
        P("tensor"), P("tensor", None), P(), P(), P(), cols, P("tensor"),
    )
    return jax.shard_map(
        functools.partial(local, mesh.shape["dp"], mesh.shape["tensor"]),
        mesh=mesh,
        in_specs=placed,
        out_specs=given,
        check_vma=False,
    )
```

```python
import functools
import math

import jax
import jax.numpy as jnp
from jax import lax
from jax.experimental import pallas as pl
from jax.experimental.pallas import tpu as pltpu
from jax.sharding import PartitionSpec as P

HEAD_DIM = 64
SEQ_LEN = 50
BLOCK = 4 * SEQ_LEN
PAD = -(-BLOCK // 16) * 16
EPS = 1e-05
NEG = -1e30
GELU_C = 0.7978845608028654
GELU_A = 0.044715
SPILL = 8 * 1024 * 1024
GROUP, GROUP_BACK = 4, 6
COST = 1e8
FOLD = 100.0
BF = jnp.bfloat16
F32 = jnp.float32
FIRST_GAIN, FIRST_SHIFT, OUT_BIAS, SECOND_GAIN, SECOND_SHIFT, DOWN_BIAS, PRIOR_GAIN, PRIOR_SHIFT, UP_BIAS, PRIOR_BIAS = range(10)


def mm(a, b):
    return lax.dot_general(a, b, (((1,), (0,)), ((), ())), preferred_element_type=F32)


def mm_bt(a, b):
    return lax.dot_general(a, b, (((1,), (1,)), ((), ())), preferred_element_type=F32)


def mm_at(a, b):
    return lax.dot_general(a, b, (((0,), (0,)), ((), ())), preferred_element_type=F32)


def norm_of(value):
    centre = value - jnp.mean(value, axis=-1, keepdims=True)
    factor = lax.rsqrt(jnp.mean(centre * centre, axis=-1, keepdims=True) + EPS)
    return centre * factor, factor


def norm_back(grad, unit, factor, gain):
    scaled = grad * gain
    first = jnp.mean(scaled, axis=-1, keepdims=True)
    second = jnp.mean(scaled * unit, axis=-1, keepdims=True)
    return factor * (scaled - first - unit * second)


def col_sum(value):
    return jnp.sum(value, axis=0, keepdims=True)


def whole_rows(here, own, other):
    low = jnp.where(here == 0, own[...], other[...])
    high = jnp.where(here == 0, other[...], own[...])
    return jnp.concatenate([low, high], axis=1).astype(F32)


def allowed_pairs(resets):
    place = lax.broadcasted_iota(jnp.int32, (1, PAD), 1)
    starts = jnp.where((resets == 1) | (lax.rem(place, SEQ_LEN) == 0) | (place >= BLOCK), place, 0)
    row = lax.broadcasted_iota(jnp.int32, (PAD, PAD), 0)
    col = lax.broadcasted_iota(jnp.int32, (PAD, PAD), 1)
    seg = jnp.max(jnp.where(col <= row, starts, 0).astype(F32), axis=-1, keepdims=True).astype(jnp.int32)
    seg2 = jnp.concatenate([seg, seg], axis=0)
    row = lax.broadcasted_iota(jnp.int32, (2 * PAD, PAD), 0)
    row = jnp.where(row >= PAD, row - PAD, row)
    col = lax.broadcasted_iota(jnp.int32, (2 * PAD, PAD), 1)
    return (col <= row) & (col >= seg2)


def two_heads(value):
    first = lax.broadcasted_iota(jnp.int32, value.shape, 1) < HEAD_DIM
    none = jnp.zeros_like(value)
    return jnp.concatenate([jnp.where(first, value, none), jnp.where(first, none, value)], axis=0)


def one_pair(value):
    first = lax.broadcasted_iota(jnp.int32, (PAD, 2 * HEAD_DIM), 1) < HEAD_DIM
    return jnp.where(first, value[:PAD], value[PAD:])


def softmax_of(scores, allowed):
    scores = jnp.where(allowed, scores, NEG)
    expo = jnp.exp(scores - jnp.max(scores, axis=-1, keepdims=True))
    return expo * (1.0 / jnp.sum(expo, axis=-1, keepdims=True))


def vector(small, index, n):
    return small[index : index + 1, :n]


def blocks_in(ref):
    return [slice(i * PAD, i * PAD + PAD) for i in range(ref.shape[0] // PAD)]


def add_up(sums, values):
    return [v if s is None else s + v for s, v in zip(sums, values, strict=True)]


def split_rows(half, source, own, sent, wide_rows):
    rows, n = source.shape
    wide_rows[0:rows, 0:n] = source[...].astype(F32)
    for which, target in ((half, own), (1 - half, sent)):
        for block, at in enumerate(blocks_in(target)):
            start = pl.multiple_of(which * (rows // 2) + block * BLOCK, 8)
            part = wide_rows[pl.ds(start, PAD), 0:n]
            inside = lax.broadcasted_iota(jnp.int32, part.shape, 0) < BLOCK
            target[at, :] = jnp.where(inside, part, 0.0).astype(BF)


def tiles_of(ref, start, n, count):
    return jnp.concatenate([ref[start + t * n : start + t * n + n, :] for t in range(count)], axis=1)


class Packed:
    def __init__(self, refs, n, q, o):
        self.one, self.two = refs
        self.n, self.q, self.o = n, q, o

    def up(self):
        return tiles_of(self.one, 0, self.n, 2)

    def out(self):
        return tiles_of(self.one, 2 * self.n, self.o, 4)

    def bias(self):
        start = 2 * self.n + 4 * self.o
        parts = [self.one[start + 16 * k : start + 16 * k + 16, :].astype(F32) for k in range(3)]
        return (parts[2] + parts[1] + parts[0])[:3]

    def down(self):
        return tiles_of(self.two, 0, self.q, 4)

    def prior(self):
        return self.two[4 * self.q : 4 * self.q + self.n, :]


def put_tiles(target, start, part):
    for t in range(part.shape[-1] // 128):
        target[start : start + part.shape[0], :] = part[:, t * 128 : t * 128 + 128]
        start += part.shape[0]
    return start


def first_kernel(s, frames, qkv, up, out, down, prior, resets, *refs):
    smalls, refs = refs[:-9], refs[-9:]
    sent_ref, one_ref, two_ref, own_ref, small_ref, resets_ref, wide_rows, rows, other = refs
    resets_ref[...] = resets[...]
    split_rows(s[0], frames, own_ref, other, wide_rows)
    start = put_tiles(sent_ref, 0, other)
    for c in range(3):
        start = put_tiles(sent_ref, start, qkv.get().at[c])
    start = put_tiles(one_ref, put_tiles(one_ref, 0, up), out)
    for i, ref in enumerate(smalls):
        small_ref[i : i + 1, : ref.shape[1]] = ref[...]
    rows[...] = jnp.zeros_like(rows)
    for t in range(2):
        rows[t : t + 1, :] = smalls[UP_BIAS][:, pl.ds(pl.multiple_of(s[1] * 256 + t * 128, 128), 128)]
    rows[2:3, :] = smalls[PRIOR_BIAS][:, pl.ds(pl.multiple_of(s[1] * 128, 128), 128)]
    left = rows[...]
    for k in range(3):
        term = left.astype(BF)
        one_ref[start : start + 16, :] = term
        left = left - term.astype(F32)
        start += 16
    put_tiles(two_ref, put_tiles(two_ref, 0, down), prior)


def cut_kernel(s, got, qkv_ref):
    qkv_ref[...] = got[got.shape[0] - qkv_ref.shape[0] :, :]


def cotangents_kernel(s, logit, out, sent, logit_own, out_own, wide_rows, logit_sent, out_sent):
    split_rows(s[0], logit, logit_own, logit_sent, wide_rows)
    split_rows(s[0], out, out_own, out_sent, wide_rows)
    n = logit_sent.shape[1]
    sent[:, :n] = logit_sent[...]
    sent[:, n:] = out_sent[...]


def gate(values, after, name=None):
    count, total = len(values), len(values) + len(after)

    def run(*refs):
        for source, target in zip(refs[:count], refs[total:], strict=True):
            target[...] = source[...]

    near = pl.BlockSpec(memory_space=pltpu.VMEM)
    return pl.pallas_call(
        run,
        in_specs=[near] * total,
        out_specs=[near] * count,
        out_shape=[pltpu.VMEM(v.shape, v.dtype) for v in values],
        compiler_params=pltpu.CompilerParams(vmem_limit_bytes=SPILL),
        cost_estimate=pl.CostEstimate(flops=0, bytes_accessed=0, transcendentals=0),
        name=name,
    )(*[pin(v) for v in values], *[pin(v) for v in after])


def attend_kernel(
    s, own, got, resets, small, q0, q1, q2, q3, qkv,
    first_ref, triple_ref, mixed_ref, qkv_other_ref, other,
):
    other[...] = tiles_of(got, 0, own.shape[0], 2)
    unit, _ = norm_of(whole_rows(s[0], own, other))
    n = first_ref.shape[1]
    first_ref[...] = (unit * vector(small, FIRST_GAIN, n) + vector(small, FIRST_SHIFT, n)).astype(BF)
    for j, piece in enumerate((q0, q1, q2, q3)):
        size = qkv.shape[1] // 4
        rows = pl.ds(pl.multiple_of((s[1] ^ j) * size, 16), size)
        for c in range(3):
            qkv_other_ref[c, rows, :] = tiles_of(piece, c * 2 * size, size, 2)
    for half, weight in enumerate((qkv, qkv_other_ref)):
        for c in range(3):
            value = mm(first_ref[...], weight[c]).astype(BF)
            triple_ref[:, (half * 3 + c) * 256 : (half * 3 + c + 1) * 256] = value
    units = []
    for block, at in enumerate(blocks_in(own)):
        allowed = allowed_pairs(resets[pl.ds(s[0] * len(blocks_in(own)) + block, 1), :PAD])
        units += [(at, allowed, pair, (pair // 2) * 768 + (pair % 2) * 128) for pair in range(4)]
    for group in range(0, len(units), GROUP):
        some = units[group : group + GROUP]
        scores = [
            mm_bt(two_heads(triple_ref[at, start : start + 128] * HEAD_DIM ** (-0.5)), triple_ref[at, start + 256 : start + 384])
            for at, _, _, start in some
        ]
        weights = [softmax_of(score, allowed).astype(BF) for score, (_, allowed, _, _) in zip(scores, some, strict=True)]
        for weight, (at, _, pair, start) in zip(weights, some, strict=True):
            mixed = one_pair(mm(weight, triple_ref[at, start + 512 : start + 640])).astype(BF)
            mixed_ref[at, pair * 128 : pair * 128 + 128] = mixed


def feed_kernel(
    s, own, other, mixed, small, out, up, down, a0, a1, a2, a3, b0, b1, b2, b3,
    block_other_ref, block_own_ref, middle_ref, second_ref, act_ref, slope_ref, ending_ref, prior_in_ref,
    out_other_ref, up_other_ref, down_other_ref, bias_other,
):
    n, half, wide = out.shape[0], up.shape[1], up.shape[0]
    for j, piece in enumerate(zip((a0, a1, a2, a3), (b0, b1, b2, b3))):
        piece = Packed(piece, wide, half // 4, n // 4)
        place = s[1] ^ j
        out_other_ref[pl.ds(pl.multiple_of(place * (n // 4), 16), n // 4), :] = piece.out()
        at = pl.ds(pl.multiple_of(place * 256, 256), 256)
        up_other_ref[:, at] = piece.up()
        down_other_ref[at, :] = piece.down()
        bias = piece.bias()
        bias_other[:, at] = jnp.concatenate([bias[0:1], bias[1:2]], axis=1)
    middle_ref[...] = (
        whole_rows(s[0], own, other)
        + vector(small, OUT_BIAS, wide)
        + mm(mixed[:, :n], out[...])
        + mm(mixed[:, n:], out_other_ref[...])
    )
    unit, _ = norm_of(middle_ref[...])
    second_ref[...] = (unit * vector(small, SECOND_GAIN, wide) + vector(small, SECOND_SHIFT, wide)).astype(BF)
    total = middle_ref[...] + vector(small, DOWN_BIAS, wide)
    for h, (w_up, w_down) in enumerate(((up, down), (up_other_ref, down_other_ref))):
        for i in range(half // 256):
            at = slice(i * 256, i * 256 + 256)
            to = slice(h * half + i * 256, h * half + i * 256 + 256)
            bias = bias_other[:, at] if h else small[UP_BIAS : UP_BIAS + 1, at]
            for rows in blocks_in(own):
                hidden = mm(second_ref[rows, :], w_up[:, at]) + bias
                square = hidden * hidden
                bent = jnp.tanh(GELU_C * (hidden + GELU_A * hidden * square))
                act_ref[rows, to] = (0.5 * hidden * (1.0 + bent)).astype(BF)
                slope_ref[rows, to] = 0.5 * (1.0 + bent) + (0.5 * GELU_C) * hidden * (1.0 - bent * bent) * (
                    1.0 + (3.0 * GELU_A) * square
                )
        total = total + mm(act_ref[:, h * half : h * half + half], w_down[...])
    ending_ref[...] = total
    unit, _ = norm_of(total)
    prior_in_ref[...] = (unit * vector(small, PRIOR_GAIN, wide) + vector(small, PRIOR_SHIFT, wide)).astype(BF)
    low, high = total[:, :256].astype(BF), total[:, 256:].astype(BF)
    block_own_ref[...] = jnp.where(s[0] == 0, low, high)
    block_other_ref[...] = jnp.where(s[0] == 0, high, low)


def prior_kernel(
    s, ending, small, logit_own, out_own, a0, a1, a2, a3, b0, b1, b2, b3, cotangents, prior,
    grad_ending_ref, ending_grad_ref, vec_ref, bias_ref, weight, bias,
):
    half, n = prior.shape[1], prior.shape[0]
    for j, piece in enumerate(zip((a0, a1, a2, a3), (b0, b1, b2, b3))):
        at = pl.ds(pl.multiple_of((s[1] ^ j) * 128, 128), 128)
        piece = Packed(piece, n, n // 2, n // 8)
        weight[:, at] = piece.prior()
        bias[:, at] = piece.bias()[2:3]
    logit_other = cotangents.at[:, :half]
    back = mm_bt(logit_own[...], prior[...]) + mm_bt(logit_other[...], weight[...])
    unit, factor = norm_of(ending[...])
    gain = vector(small, PRIOR_GAIN, unit.shape[1])
    grad = whole_rows(s[0], out_own, cotangents.at[:, half:]) + norm_back(back, unit, factor, gain)
    grad_ending_ref[...] = grad
    ending_grad_ref[...] = grad.astype(BF)
    vec_ref[...] = jnp.concatenate([col_sum(back * unit), col_sum(back), col_sum(grad)], axis=0)
    bias_ref[:, :half] = col_sum(logit_own[...].astype(F32))
    bias_ref[:, half:] = col_sum(logit_other[...].astype(F32))


def logits_kernel(s, prior_in, small, prior, weight, bias, block_other, frames_other, sent_ref, logits_ref):
    half, n = prior.shape[1], block_other.shape[1]
    sent_ref[:, :half] = (mm(prior_in[...], weight[...]) + bias[...]).astype(BF)
    sent_ref[:, half : half + n] = block_other[...]
    sent_ref[:, half + n :] = frames_other[...]
    logits_ref[...] = mm(prior_in[...], prior[...]) + vector(small, PRIOR_BIAS, half)


def store_piece(keep, send, h, j, start, value):
    at = slice(start, start + value.shape[0])
    if j < 2:
        keep[h * 2 + j, at, :] = value
    else:
        send[h * 2 + j - 2, at, :] = value.astype(BF)


def late_grads_kernel(s, prior_in, logit_own, cotangents, act, ending_grad, keep, send, wide):
    half = act.shape[1] // 2
    logit_other = cotangents.at[:, : logit_own.shape[1]]
    n = prior_in.shape[1]
    for h in range(2):
        wide[...] = mm_at(prior_in[...], (logit_own, logit_other)[h][...])
        for j in (2, 3, 0, 1):
            place = s[1] ^ j
            store_piece(keep, send, h, j, 0, wide[:, pl.ds(pl.multiple_of(place * 128, 128), 128)])
            part = act[:, pl.ds(pl.multiple_of(h * half + place * 256, 256), 256)]
            value = mm_at(part, ending_grad[...])
            for t in range(n // 128):
                store_piece(keep, send, h, j, n + t * 256, value[:, t * 128 : t * 128 + 128])


def up_grads_kernel(s, second, hidden_grad, mixed, middle_grad, keep, send, turned, wide):
    turned[...] = second[...].T
    half = hidden_grad.shape[1] // 2
    n, m = second.shape[1], mixed.shape[1] // 2
    for h in range(2):
        wide[...] = mm_at(mixed[:, h * m : h * m + m], middle_grad[...])
        for j in (2, 3, 0, 1):
            place = s[1] ^ j
            value = mm(turned[...], hidden_grad[:, pl.ds(pl.multiple_of(h * half + place * 256, 256), 256)])
            for t in range(2):
                store_piece(keep, send, h, j, t * n, value[:, t * 128 : t * 128 + 128])
            store_piece(keep, send, h, j, 2 * n, wide[:, pl.ds(pl.multiple_of(place * 128, 128), 128)])


def early_grads_kernel(s, first, grad_own, grad_other, keep, send):
    for h in range(2):
        for j in (2, 3, 0, 1):
            place = pl.multiple_of((s[1] ^ j) * 128, 128)
            value = mm_at(first[:, pl.ds(place, 128)], (grad_own, grad_other)[h][...])
            for c in range(3):
                for t in range(2):
                    at = slice(c * 256 + t * 128, c * 256 + t * 128 + 128)
                    store_piece(keep, send, h, j, (t * 3 + c) * 128, value[:, at])


def feed_back_kernel(
    s, ending_grad, slope, middle, grad_ending, small, down, down_other, up, up_other,
    hidden_grad_ref, grad_middle_ref, middle_grad_ref, vec_ref, bias_ref,
):
    half = up.shape[1]
    back = None
    for h, (w_up, w_down) in enumerate(((up, down), (up_other, down_other))):
        for i in range(half // 256):
            at = slice(i * 256, i * 256 + 256)
            to = slice(h * half + i * 256, h * half + i * 256 + 256)
            sums = [None]
            for rows in blocks_in(ending_grad):
                low = (mm_bt(ending_grad[rows, :], w_down[at, :]) * slope[rows, to]).astype(BF)
                hidden_grad_ref[rows, to] = low
                sums = add_up(sums, [col_sum(low.astype(F32))])
            bias_ref[:, to] = sums[0]
        value = mm_bt(hidden_grad_ref[:, h * half : h * half + half], w_up[...])
        back = value if back is None else back + value
    unit, factor = norm_of(middle[...])
    gain = vector(small, SECOND_GAIN, unit.shape[1])
    total = grad_ending[...] + norm_back(back, unit, factor, gain)
    grad_middle_ref[...] = total
    middle_grad_ref[...] = total.astype(BF)
    vec_ref[...] = jnp.concatenate([col_sum(back * unit), col_sum(back), col_sum(total)], axis=0)


def attend_back_kernel(
    half, s, middle_grad, triple, out, resets,
    triple_grad_ref, mixed_grad,
):
    mixed_grad[...] = mm_bt(middle_grad[...], out[...]).astype(BF)
    factor = HEAD_DIM ** (-0.5)
    units = []
    for block, at in enumerate(blocks_in(triple)):
        allowed = allowed_pairs(resets[pl.ds(s[0] * len(blocks_in(triple)) + block, 1), :PAD])
        units += [(at, allowed, pair) for pair in range(2)]
    for group in range(0, len(units), GROUP_BACK):
        some = units[group : group + GROUP_BACK]
        loaded = []
        for at, _, pair in some:
            start = half * 768 + pair * 128
            query, key, value = (triple[at, start + c * 256 : start + c * 256 + 128] for c in range(3))
            mixed2 = two_heads(mixed_grad[at, pair * 128 : pair * 128 + 128])
            loaded.append((two_heads(query * factor), key, value, mixed2))
        scores = [mm_bt(query2, key) for query2, key, _, _ in loaded]
        weight_grads = [mm_bt(mixed2, value) for _, _, value, mixed2 in loaded]
        inner = []
        for score, weight_grad, (_, allowed, _) in zip(scores, weight_grads, some, strict=True):
            again = softmax_of(score, allowed)
            both = again * weight_grad
            total = jnp.sum(both, axis=-1, keepdims=True)
            inner.append((again.astype(BF), (both - again * total).astype(BF)))
        for (again, score_grad), (query2, key, _, mixed2), (at, _, pair) in zip(inner, loaded, some, strict=True):
            thirds = (
                (one_pair(mm(score_grad, key)) * factor).astype(BF),
                mm_at(score_grad, query2).astype(BF),
                mm_at(again, mixed2).astype(BF),
            )
            for c in range(3):
                triple_grad_ref[at, c * 256 + pair * 128 : c * 256 + pair * 128 + 128] = thirds[c]


def frames_back_kernel(
    s, grad_own, grad_other, grad_middle, own, other, qkv_other, small, qkv,
    sent_ref, frames_own_ref, vec_ref,
):
    back = None
    for part, weight in ((grad_own, qkv), (grad_other, qkv_other)):
        for c in range(3):
            value = mm_bt(part[:, c * 256 : c * 256 + 256], weight[c])
            back = value if back is None else back + value
    unit, scale = norm_of(whole_rows(s[0], own, other))
    total = grad_middle[...] + norm_back(back, unit, scale, vector(small, FIRST_GAIN, unit.shape[1]))
    low, high = total[:, :256], total[:, 256:]
    frames_own_ref[...] = jnp.where(s[0] == 0, low, high)
    sent_ref[...] = jnp.where(s[0] == 0, high, low).astype(BF)
    vec_ref[...] = jnp.concatenate([col_sum(back * unit), col_sum(back)], axis=0)


def late_place_kernel(s, mine, near, far, farther, down_ref, prior_ref):
    n, q = prior_ref.shape[0], down_ref.shape[0] // 4
    for j, piece in enumerate((mine, near, far, farther)):
        place = s[1] ^ j
        rows = pl.ds(pl.multiple_of(place * q, 8), q)
        for t in range(down_ref.shape[1] // 128):
            down_ref[rows, t * 128 : t * 128 + 128] = piece[n + t * q : n + t * q + q, :].astype(F32)
        prior_ref[:, pl.ds(pl.multiple_of(place * 128, 128), 128)] = piece[:n, :].astype(F32)


def up_place_kernel(s, mine, near, far, farther, up_ref, out_ref):
    n, m = up_ref.shape[0], out_ref.shape[0]
    for j, piece in enumerate((mine, near, far, farther)):
        place = s[1] ^ j
        for t in range(2):
            columns = pl.ds(pl.multiple_of(place * 256 + t * 128, 128), 128)
            up_ref[:, columns] = piece[t * n : t * n + n, :].astype(F32)
        out_ref[:, pl.ds(pl.multiple_of(place * 128, 128), 128)] = piece[2 * n : 2 * n + m, :].astype(F32)


def early_place_kernel(s, mine, near, far, farther, qkv_ref, *vecs):
    vecs, sums = vecs[:-1], vecs[-1]
    sums[...] = mine[6 * 128 :, :].astype(F32) + far[6 * 128 :, :].astype(F32)
    for j, piece in enumerate((mine, near, far, farther)):
        at = pl.ds(pl.multiple_of((s[1] ^ j) * 128, 128), 128)
        for c in range(3):
            for t in range(2):
                start = (t * 3 + c) * 128
                qkv_ref[c, at, t * 128 : t * 128 + 128] = piece[start : start + 128, :].astype(F32)
    qkv_ref.send()
    row = 0
    for ref in vecs[:8]:
        for t in range(ref.shape[1] // 128):
            ref[:, t * 128 : t * 128 + 128] = sums[row : row + 1, :]
            row += 1
    for ref in vecs[8:]:
        tiles = ref.shape[1] // 128
        for t in range(tiles):
            ref[:, t * 128 : t * 128 + 128] = sums[pl.ds(row + s[0] * tiles + t, 1), :]
        row += 2 * tiles


def core_kernel(s, keep, got, low, rest):
    n = keep.shape[1]
    for out, places, dtype in ((low, (2, 3), BF), (rest, (0, 1), F32)):
        for k, i in enumerate(places):
            out[k * n : k * n + n, :] = (keep[i] + got[i].astype(F32)).astype(dtype)


def core_all_kernel(s, keep, got, *refs):
    vectors, lows, rest = refs[:-4], refs[-4:-1], refs[-1]
    n = keep.shape[1]
    for i in (1, 2, 3):
        lows[i - 1][:n, :] = (keep[i] + got[i].astype(F32)).astype(BF)
    rest[:n, :] = keep[0] + got[0].astype(F32)
    if vectors:
        put_vectors(s, vectors, rest, n)
        for low in lows:
            low[n:, :] = rest[n:, :].astype(BF)


def put_vectors(s, vectors, rest, row):
    for ref in vectors[:3]:
        for i in range(ref.shape[0]):
            for t in range(ref.shape[1] // 128):
                rest[row : row + 1, :] = ref[i : i + 1, t * 128 : t * 128 + 128]
                row += 1
    for ref in vectors[3:]:
        tiles = ref.shape[1] // 128
        for t in range(tiles):
            place = row + lax.rem(t + s[0] * (tiles // 2), tiles)
            rest[pl.ds(place, 1), :] = ref[:, t * 128 : t * 128 + 128]
        row += tiles
    rest[row:, :] = jnp.zeros((rest.shape[0] - row, 128), F32)


def over_kernel(s, rest, got, low, mine):
    n = low.shape[0]
    low[...] = (rest[n:, :] + got[n:, :].astype(F32)).astype(BF)
    mine[...] = rest[:n, :] + got[:n, :].astype(F32)


def halves_kernel(s, *refs):
    total, (keep, send) = refs[-1], refs[-3:-1]
    total[...] = functools.reduce(lambda x, y: x + y, [r[...].astype(F32) for r in refs[:-3]])
    n = keep.shape[0]
    send[...] = total[pl.ds(pl.multiple_of((1 - s[2]) * n, 16), n), :].astype(BF)
    keep[...] = total[pl.ds(pl.multiple_of(s[2] * n, 16), n), :].astype(BF)


def join_kernel(s, mine, got, out):
    n = mine.shape[0]
    out[pl.ds(pl.multiple_of(s[2] * n, 16), n), :] = mine[...]
    out[pl.ds(pl.multiple_of((1 - s[2]) * n, 16), n), :] = got[...]


def total_kernel(s, *refs):
    refs[-1][...] = functools.reduce(lambda x, y: x + y, [r[...].astype(F32) for r in refs[:-1]]).astype(BF)


def rows_kernel(entries, s, *refs):
    count = len(entries)
    given, outs, rooms = refs[: 2 * count], refs[2 * count : 3 * count], refs[3 * count :]
    for i, columns in enumerate(entries):
        own, got, out, room = given[2 * i], given[2 * i + 1], outs[i], rooms[i]
        rows = out.shape[0] // 2
        for block, at in enumerate(blocks_in(own)):
            for which, ref, cut in ((s[0], own, slice(None)), (1 - s[0], got, columns)):
                start = pl.multiple_of(which * rows + block * BLOCK, 8)
                room[pl.ds(start, BLOCK), :] = ref[at, cut].astype(F32)[:BLOCK]
        out[...] = room[...].astype(out.ref.dtype)
        out.send()


class Loaded:
    def __init__(self, ref, copy):
        self.ref, self.copy, self.shape = ref, copy, ref.shape

    def get(self):
        if self.copy is not None:
            self.copy.wait()
            self.copy = None
        return self.ref

    def __getitem__(self, index):
        return self.get()[index]


class Leaving:
    def __init__(self, ref, copy):
        self.ref, self.copy, self.shape, self.sent = ref, copy, ref.shape, False

    def __getitem__(self, index):
        return self.ref[index]

    def __setitem__(self, index, value):
        self.ref[index] = value

    def send(self):
        if not self.sent:
            self.copy.start()
            self.sent = True


class Far:
    def __init__(self, value, shape=None, cut=None):
        self.value, self.shape, self.cut = value, shape or value.shape, cut or (lambda s, ref: ref)


def call(kernel, scalars, ins, outs, scratch=(), name=None, after=(), cost=1.0, loads=()):
    n_own, n_loads = len(ins), len(loads)
    ins, outs = [*ins, *[Far(v) for v in loads]], [*outs, *[(v.shape, v.dtype, True) for v in loads]]
    n_in, n_out, n_after = len(ins), len(outs), len(after)
    far_in = [i for i, v in enumerate(ins[:n_own]) if isinstance(v, Far)]
    far_out = [i for i, o in enumerate(outs) if not o[2]]
    room = [pltpu.VMEM(ins[i].shape, ins[i].value.dtype) for i in far_in]
    room += [pltpu.VMEM(outs[i][0], outs[i][1]) for i in far_out]
    need = sum(math.prod(r.shape) * jnp.dtype(r.dtype).itemsize for r in room + list(scratch))

    def run(s, *refs):
        given, refs = list(refs[:n_in]), refs[n_in + n_after :]
        made, refs = list(refs[:n_out]), refs[n_out:]
        own, refs = refs[: len(scratch)], refs[len(scratch) :]
        rooms, sems = refs[:-1], refs[-1]
        for k, i in enumerate(far_in):
            copy = pltpu.make_async_copy(ins[i].cut(s, given[i]), rooms[k], sems.at[k])
            copy.start()
            given[i] = Loaded(rooms[k], copy)
        bringing = []
        for k in range(n_loads):
            copy = pltpu.make_async_copy(given[n_own + k], made[n_out - n_loads + k], sems.at[len(rooms) + k])
            copy.start()
            bringing.append(copy)
        leaving = []
        for k, i in enumerate(far_out, len(far_in)):
            made[i] = Leaving(rooms[k], pltpu.make_async_copy(rooms[k], made[i], sems.at[k]))
            leaving.append(made[i])
        kernel(s, *given[:n_own], *made[: n_out - n_loads], *own)
        for copy in bringing:
            copy.wait()
        for value in given:
            if isinstance(value, Loaded):
                value.get()
        for value in leaving:
            value.send()
        for value in leaving:
            value.copy.wait()

    near, far = pl.BlockSpec(memory_space=pltpu.VMEM), pl.BlockSpec(memory_space=pltpu.HBM)
    return pl.pallas_call(
        run,
        in_specs=[pl.BlockSpec(memory_space=pltpu.SMEM)]
        + [far if isinstance(v, Far) else near for v in ins]
        + [far if isinstance(v, Far) else near for v in after],
        out_specs=[near if stays else far for _, _, stays in outs],
        out_shape=[(pltpu.VMEM if stays else pltpu.HBM)(shape, dtype) for shape, dtype, stays in outs],
        scratch_shapes=list(scratch) + room + [pltpu.SemaphoreType.DMA((max(1, len(room) + n_loads),))],
        compiler_params=pltpu.CompilerParams(vmem_limit_bytes=need + SPILL),
        cost_estimate=pl.CostEstimate(flops=int(cost * COST), bytes_accessed=0, transcendentals=0),
        name=name,
    )(scalars, *[pin(v) for v in ins], *[pin(v) for v in after])


def pin(value):
    if isinstance(value, Far):
        return pltpu.with_memory_space_constraint(value.value, pltpu.HBM)
    return pltpu.with_memory_space_constraint(value, pltpu.VMEM)


def swap(value, axes, sizes, mask):
    count = 1
    for size in sizes:
        count *= size
    return lax.ppermute(value, axes, [(i, i ^ mask) for i in range(count)])


class Moves:
    def __init__(self, n_dp, n_tensor):
        self.n_dp, self.n_tensor = n_dp, n_tensor
        self.dp = lax.axis_index("dp")
        self.here = lax.axis_index("tensor")

    def along(self, value, mask):
        return swap(value, "dp", (self.n_dp,), mask)

    def core(self, value):
        return self.along(value, 1)

    def side(self, value):
        return self.along(value, 2)

    def over(self, value):
        return swap(value, "tensor", (self.n_tensor,), 1)

    def cross(self, value):
        return swap(value, ("dp", "tensor"), (self.n_dp, self.n_tensor), 5)


    def reduce_core(self, scalars, keep, sent, name, after=()):
        n = 2 * sent.shape[1]
        outs = [((n, 128), BF, True), ((n, 128), F32, True)]
        return call(core_kernel, scalars, [keep, self.core(sent)], outs, name=name, after=after, cost=FOLD)

    def reduce_over(self, scalars, low, rest, name, after=()):
        n = low.shape[0] // 2
        outs = [((n, 128), BF, True), ((n, 128), F32, True)]
        return call(over_kernel, scalars, [rest, self.over(low)], outs, name=name, after=after, cost=FOLD)

    def reduce_core_all(self, scalars, keep, sent, name, vectors=(), spare=0, after=()):
        n = sent.shape[1] + spare
        outs = [((n, 128), BF, True)] * 3 + [((n, 128), F32, True)]
        ins = [keep, self.core(sent), *vectors]
        return call(core_all_kernel, scalars, ins, outs, name=name, after=after, cost=FOLD)

    def sides(self, lows):
        return [self.side(lows[0]), self.over(lows[1]), self.cross(lows[2])]

    def total(self, scalars, values, name, after=()):
        shape = values[0].shape
        return call(total_kernel, scalars, values, [(shape, BF, True)], name=name, after=after, cost=FOLD)[0]

    def halves(self, scalars, values, name, after=()):
        n = values[0].shape[0]
        return call(
            halves_kernel,
            scalars,
            values,
            [((n // 2, 128), BF, True)] * 2,
            [pltpu.VMEM((n, 128), F32)],
            name=name,
            after=after,
            cost=FOLD,
        )

    def join(self, scalars, mine, got, name, after=()):
        shape = (mine.shape[0] * 2, 128)
        return call(join_kernel, scalars, [mine, got], [(shape, BF, True)], name=name, after=after, cost=FOLD)[0]

    def bits(self):
        return [1 << i for i in range(2, self.n_dp.bit_length() - 1)]

    def gather(self, total):
        near = self.side(total)
        return total, near, self.core(total), self.core(near)


def local(
    n_dp, n_tensor, frames, resets, first_gain, first_shift, qkv_weight, out_weight, out_bias, second_gain,
    second_shift, up_weight, up_bias, down_weight, down_bias, prior_gain, prior_shift, prior_weight,
    prior_bias, out_cotangent, logit_cotangent,
):
    move = Moves(n_dp, n_tensor)
    rows, half = frames.shape
    width = 2 * half
    mine = rows // 2
    blocks = mine // BLOCK
    hidden_width, n_logits = up_bias.shape[0], prior_bias.shape[0]
    row = lambda v: v.reshape(1, -1)
    core, side = move.dp & 1, (move.dp >> 1) & 1
    reset_rows = jnp.pad(resets.reshape(-1, BLOCK), ((0, -(2 * blocks) % 8), (0, -BLOCK % 128)))
    scalars = jnp.stack([move.here, core * 2 + side, (move.dp >> 2) & 1]).astype(jnp.int32)
    total_rows = blocks * PAD
    quarter = hidden_width // 4

    def near_rows(*entries):
        return [((total_rows, n), dtype, True) for n, dtype in entries]

    def pieces(n):
        return [((4, n, 128), F32, True), ((4, n, 128), BF, True)]

    def columns(value, size, which):
        cut = lambda s, ref: ref.at[..., pl.ds(pl.multiple_of(s[which] * size, 128), size)]
        return Far(value, (*value.shape[:-1], size), cut)

    def some_rows(value, size, which):
        cut = lambda s, ref: ref.at[pl.ds(pl.multiple_of(s[which] * size, 16), size), :]
        return Far(value, (size, value.shape[1]), cut)

    vectors = [first_gain, first_shift, out_bias, second_gain, second_shift, down_bias, prior_gain, prior_shift]
    vectors = [row(v) for v in vectors + [up_bias, prior_bias]]
    qkv_rows = 3 * (width // 4) * (half // 128)
    sent_first, sent_one, sent_two, frames_own, small, resets_near = call(
        first_kernel,
        scalars,
        [
            Far(frames),
            Far(
                qkv_weight,
                (3, width // 4, half),
                lambda s, ref: ref.at[:, pl.ds(pl.multiple_of(s[1] * (width // 4), 16), width // 4), :],
            ),
            columns(up_weight, quarter, 1),
            some_rows(out_weight, half // 4, 1),
            some_rows(down_weight, quarter, 1),
            columns(prior_weight, n_logits // 4, 1),
            Far(reset_rows),
            *[Far(v) for v in vectors],
        ],
        [((total_rows * (half // 128) + qkv_rows, 128), BF, True)]
        + [((width * 2 + half + 48, 128), BF, True), ((quarter * 4 + width, 128), BF, True)]
        + near_rows((half, BF))
        + [((16, hidden_width), F32, True), (reset_rows.shape, jnp.int32, True)],
        [pltpu.VMEM((rows + 16, half), F32), pltpu.VMEM((16, 128), F32), pltpu.VMEM((total_rows, half), BF)],
        "first_parts",
        cost=2.0,
    )

    def all_quarters(got):
        beside = move.side(got)
        return [got, beside, move.core(got), move.core(beside)]

    got_first = move.over(sent_first)
    (qkv_got,) = call(cut_kernel, scalars, [got_first], [((qkv_rows, 128), BF, True)], name="cut", cost=100.0)
    (sent_one,) = gate([sent_one], [got_first], "after_first")
    got_one = move.over(sent_one)
    cot_sent, logit_own, out_own, qkv_near, out_near, up_near, down_near, prior_near = call(
        cotangents_kernel,
        scalars,
        [Far(logit_cotangent), Far(out_cotangent)],
        near_rows((n_logits + half, BF), (n_logits, BF), (half, BF)),
        [pltpu.VMEM((rows + 16, n_logits), F32)]
        + [pltpu.VMEM((total_rows, n), BF) for n in (n_logits, half)],
        name="cotangents",
        after=(sent_first,),
        cost=2.3,
        loads=(qkv_weight, out_weight, up_weight, down_weight, prior_weight),
    )
    (sent_two,) = gate([sent_two], [qkv_got, sent_one, cot_sent], "after_cut")
    got_two = move.over(sent_two)
    first, triple, mixed, qkv_other, frames_other = call(
        attend_kernel,
        scalars,
        [frames_own, got_first, resets_near, small, *all_quarters(qkv_got), qkv_near],
        near_rows((width, BF), (3 * width, BF), (width, BF)) + [(qkv_weight.shape, BF, True)] + near_rows((half, BF)),
        name="attend",
        cost=5.5,
    )
    beside_one = move.side(got_one)
    got_two, cot_sent = gate([got_two, cot_sent], [mixed, beside_one], "after_attend")
    beside_two = move.side(got_two)
    packed = [got_one, beside_one, move.core(got_one), move.core(beside_one)]
    packed += [got_two, beside_two, move.core(got_two), move.core(beside_two)]
    cotangents = move.over(cot_sent)
    block_send, block_own, middle, second, act, slope, ending, prior_in, out_other, up_other, down_other = call(
        feed_kernel,
        scalars,
        [frames_own, frames_other, mixed, small, out_near, up_near, down_near, *packed],
        near_rows((half, BF), (half, BF))
        + near_rows((width, F32), (width, BF), (2 * hidden_width, BF), (2 * hidden_width, F32))
        + near_rows((width, F32), (width, BF))
        + [(v.shape, BF, True) for v in (out_weight, up_weight, down_weight)],
        [pltpu.VMEM((1, hidden_width), F32)],
        name="feed",
        cost=7.2,
    )
    grad_ending, ending_grad, vec_three, prior_bias_sum, prior_other, prior_bias_other = call(
        prior_kernel,
        scalars,
        [ending, small, logit_own, out_own, *packed, cotangents, prior_near],
        near_rows((width, F32), (width, BF))
        + [((3, width), F32, True), ((1, 2 * n_logits), F32, True)]
        + [(prior_weight.shape, BF, True), ((1, n_logits), F32, True)],
        name="prior",
        cost=2.5,
    )
    late_keep, late_send = call(
        late_grads_kernel,
        scalars,
        [prior_in, logit_own, cotangents, act, ending_grad],
        pieces(width + hidden_width),
        [pltpu.VMEM((width, n_logits), F32)],
        name="late_grads",
        cost=3.5,
    )
    hidden_grad, grad_middle, middle_grad, vec_two, up_bias_sum = call(
        feed_back_kernel,
        scalars,
        [ending_grad, slope, middle, grad_ending, small, down_near, down_other, up_near, up_other],
        near_rows((2 * hidden_width, BF), (width, F32), (width, BF))
        + [((3, width), F32, True), ((1, 2 * hidden_width), F32, True)],
        name="feed_back",
        cost=6.5,
        after=(late_send,),
    )
    *late_low, late_rest = move.reduce_core_all(scalars, late_keep, late_send, "late_core", after=(hidden_grad,))
    up_keep, up_send = call(
        up_grads_kernel,
        scalars,
        [second, hidden_grad, mixed, middle_grad],
        pieces(width * hidden_width // 512 + half),
        [pltpu.VMEM((width, total_rows), BF), pltpu.VMEM((half, width), F32)],
        name="up_grads",
        after=(late_low[0],),
        cost=3.0,
    )
    def attend_back(half, out, after):
        return call(
            functools.partial(attend_back_kernel, half),
            scalars,
            [middle_grad, triple, out, resets_near],
            near_rows((3 * width // 2, BF)),
            [pltpu.VMEM((total_rows, width // 2), BF)],
            name=f"attend_back_{half}",
            after=after,
            cost=4.5,
        )[0]

    grad_own = attend_back(0, out_near, (up_send,))
    up_low, up_rest = move.reduce_core(scalars, up_keep, up_send, "up_core", (grad_own,))
    grad_other = attend_back(1, out_other, (up_low,))
    keep, send = call(
        early_grads_kernel,
        scalars,
        [first, grad_own, grad_other],
        pieces(768),
        name="early_grads",
        after=(),
        cost=2.0,
    )
    late, late_half = move.halves(scalars, [late_rest, *move.sides(late_low)], "late_1", (send,))
    frames_send, frames_grad, vec_one = call(
        frames_back_kernel,
        scalars,
        [grad_own, grad_other, grad_middle, frames_own, frames_other, qkv_other, small, qkv_near],
        near_rows((half, BF), (half, F32)) + [((2, width), F32, True)],
        name="frames_back",
        after=(late,),
        cost=2.5,
    )
    bits = move.bits()
    spare = 64
    vectors = [vec_one, vec_two, vec_three, up_bias_sum, prior_bias_sum]
    *early_low, early_rest = move.reduce_core_all(scalars, keep, send, "early_core", vectors, spare)
    late = move.total(scalars, [late, move.along(late_half, bits[0])], "late_2", (early_low[0],))
    up_low, up_rest = move.reduce_over(scalars, up_low, up_rest, "up_over", (late,))
    done = up_low
    for bit in bits[1:]:
        done = late = move.total(scalars, [late, move.along(late, bit)], "late_3", (done,))
    done = early = move.total(scalars, [early_rest, *move.sides(early_low)], "early_1", (done,))
    up, up_half = move.halves(scalars, [up_rest, move.side(up_low)], "up_1", (done,))
    back_send, logits_own = call(
        logits_kernel,
        scalars,
        [prior_in, small, prior_near, prior_other, prior_bias_other, block_send, frames_send],
        near_rows((n_logits + 2 * half, BF), (n_logits, F32)),
        name="logits",
        after=(up,),
        cost=2.0,
    )
    done = late = move.join(scalars, late, move.along(late, bits[0]), "late_4", (back_send,))
    for bit in bits[:-1]:
        done = early = move.total(scalars, [early, move.along(early, bit)], "early_2", (done,))
    done = up = move.total(scalars, [up, move.along(up_half, bits[0])], "up_2", (done,))
    down_grad, prior_grad = call(
        late_place_kernel,
        scalars,
        list(move.gather(late)),
        [((hidden_width, width), F32, False), ((width, n_logits), F32, False)],
        name="late_place",
        after=(done,),
        cost=FOLD,
    )
    early = move.total(scalars, [early, move.along(early, bits[-1])], "early_3", (Far(down_grad),))
    done = early
    for bit in bits[1:]:
        done = up = move.total(scalars, [up, move.along(up, bit)], "up_3", (done,))
    up = move.join(scalars, up, move.along(up, bits[0]), "up_4", (done,))
    back_got = move.over(back_send)
    up, early_pieces = move.gather(up), move.gather(early)
    block_out, logits, grad_frames = call(
        functools.partial(
            rows_kernel,
            [slice(n_logits, n_logits + half), slice(0, n_logits), slice(n_logits + half, n_logits + 2 * half)],
        ),
        scalars,
        [v for own in (block_own, logits_own, frames_grad) for v in (own, back_got)],
        [((rows, half), BF, False), ((rows, n_logits), F32, False), ((rows, half), F32, False)],
        [pltpu.VMEM((rows, n), F32) for n in (half, n_logits, half)],
        name="rows_back",
        after=(up[0],),
        cost=FOLD,
    )
    qkv_grad, *named = call(
        early_place_kernel,
        scalars,
        list(early_pieces),
        [((3, width, half), F32, False)]
        + [((1, n), F32, False) for n in [width] * 8 + [hidden_width, n_logits]],
        [pltpu.VMEM((spare, 128), F32)],
        name="early_place",
        after=(Far(block_out),),
        cost=FOLD,
    )
    up_grad, out_grad = call(
        up_place_kernel,
        scalars,
        list(up),
        [((width, hidden_width), F32, False), ((half, width), F32, False)],
        name="up_place",
        after=(Far(qkv_grad),),
        cost=FOLD,
    )
    named = [v.reshape(-1) for v in named]
    return (
        block_out,
        logits,
        grad_frames,
        named[0],
        named[1],
        qkv_grad,
        out_grad,
        named[4],
        named[2],
        named[3],
        up_grad,
        named[8],
        down_grad,
        named[7],
        named[5],
        named[6],
        prior_grad,
        named[9],
    )


def solution(mesh):
    rows, cols = P("dp", "tensor"), P(None, "tensor")
    placed = (
        rows, P("dp"), P(), P(), P(None, None, "tensor"), P("tensor", None), P(), P(), P(), cols, P("tensor"),
        P("tensor", None), P(), P(), P(), cols, P("tensor"), rows, rows,
    )
    given = (
        rows, rows, rows, P(), P(), P(None, None, "tensor"), P("tensor", None), P(), P(), P(), cols,
        P("tensor"), P("tensor", None), P(), P(), P(), cols, P("tensor"),
    )
    return jax.shard_map(
        functools.partial(local, mesh.shape["dp"], mesh.shape["tensor"]),
        mesh=mesh,
        in_specs=placed,
        out_specs=given,
        check_vma=False,
    )
```

```python
import functools
import math

import jax
import jax.numpy as jnp
from jax import lax
from jax.experimental import pallas as pl
from jax.experimental.pallas import tpu as pltpu
from jax.sharding import PartitionSpec as P

HEAD_DIM = 64
SEQ_LEN = 50
BLOCK = 4 * SEQ_LEN
PAD = -(-BLOCK // 16) * 16
EPS = 1e-05
NEG = -1e30
GELU_C = 0.7978845608028654
GELU_A = 0.044715
SPILL = 8 * 1024 * 1024
GROUP, GROUP_BACK = 4, 6
COST = 1e8
FOLD = 100.0
BF = jnp.bfloat16
F32 = jnp.float32
FIRST_GAIN, FIRST_SHIFT, OUT_BIAS, SECOND_GAIN, SECOND_SHIFT, DOWN_BIAS, PRIOR_GAIN, PRIOR_SHIFT, UP_BIAS, PRIOR_BIAS = range(10)


def mm(a, b):
    return lax.dot_general(a, b, (((1,), (0,)), ((), ())), preferred_element_type=F32)


def mm_bt(a, b):
    return lax.dot_general(a, b, (((1,), (1,)), ((), ())), preferred_element_type=F32)


def mm_at(a, b):
    return lax.dot_general(a, b, (((0,), (0,)), ((), ())), preferred_element_type=F32)


def norm_of(value):
    centre = value - jnp.mean(value, axis=-1, keepdims=True)
    factor = lax.rsqrt(jnp.mean(centre * centre, axis=-1, keepdims=True) + EPS)
    return centre * factor, factor


def norm_back(grad, unit, factor, gain):
    scaled = grad * gain
    first = jnp.mean(scaled, axis=-1, keepdims=True)
    second = jnp.mean(scaled * unit, axis=-1, keepdims=True)
    return factor * (scaled - first - unit * second)


def col_sum(value):
    return jnp.sum(value, axis=0, keepdims=True)


def whole_rows(here, own, other):
    low = jnp.where(here == 0, own[...], other[...])
    high = jnp.where(here == 0, other[...], own[...])
    return jnp.concatenate([low, high], axis=1).astype(F32)


def allowed_pairs(resets):
    place = lax.broadcasted_iota(jnp.int32, (1, PAD), 1)
    starts = jnp.where((resets == 1) | (lax.rem(place, SEQ_LEN) == 0) | (place >= BLOCK), place, 0)
    row = lax.broadcasted_iota(jnp.int32, (PAD, PAD), 0)
    col = lax.broadcasted_iota(jnp.int32, (PAD, PAD), 1)
    seg = jnp.max(jnp.where(col <= row, starts, 0).astype(F32), axis=-1, keepdims=True).astype(jnp.int32)
    seg2 = jnp.concatenate([seg, seg], axis=0)
    row = lax.broadcasted_iota(jnp.int32, (2 * PAD, PAD), 0)
    row = jnp.where(row >= PAD, row - PAD, row)
    col = lax.broadcasted_iota(jnp.int32, (2 * PAD, PAD), 1)
    return (col <= row) & (col >= seg2)


def two_heads(value):
    first = lax.broadcasted_iota(jnp.int32, value.shape, 1) < HEAD_DIM
    none = jnp.zeros_like(value)
    return jnp.concatenate([jnp.where(first, value, none), jnp.where(first, none, value)], axis=0)


def one_pair(value):
    first = lax.broadcasted_iota(jnp.int32, (PAD, 2 * HEAD_DIM), 1) < HEAD_DIM
    return jnp.where(first, value[:PAD], value[PAD:])


def softmax_of(scores, allowed):
    scores = jnp.where(allowed, scores, NEG)
    expo = jnp.exp(scores - jnp.max(scores, axis=-1, keepdims=True))
    return expo * (1.0 / jnp.sum(expo, axis=-1, keepdims=True))


def vector(small, index, n):
    return small[index : index + 1, :n]


def blocks_in(ref):
    return [slice(i * PAD, i * PAD + PAD) for i in range(ref.shape[0] // PAD)]


def add_up(sums, values):
    return [v if s is None else s + v for s, v in zip(sums, values, strict=True)]


def split_rows(half, source, own, sent, wide_rows):
    rows, n = source.shape
    wide_rows[0:rows, 0:n] = source[...].astype(F32)
    for which, target in ((half, own), (1 - half, sent)):
        for block, at in enumerate(blocks_in(target)):
            start = pl.multiple_of(which * (rows // 2) + block * BLOCK, 8)
            part = wide_rows[pl.ds(start, PAD), 0:n]
            inside = lax.broadcasted_iota(jnp.int32, part.shape, 0) < BLOCK
            target[at, :] = jnp.where(inside, part, 0.0).astype(BF)


def tiles_of(ref, start, n, count):
    return jnp.concatenate([ref[start + t * n : start + t * n + n, :] for t in range(count)], axis=1)


class Packed:
    def __init__(self, refs, n, q, o):
        self.one, self.two = refs
        self.n, self.q, self.o = n, q, o

    def up(self):
        return tiles_of(self.one, 0, self.n, 2)

    def out(self):
        return tiles_of(self.one, 2 * self.n, self.o, 4)

    def bias(self):
        start = 2 * self.n + 4 * self.o
        parts = [self.one[start + 16 * k : start + 16 * k + 16, :].astype(F32) for k in range(3)]
        return (parts[2] + parts[1] + parts[0])[:3]

    def down(self):
        return tiles_of(self.two, 0, self.q, 4)

    def prior(self):
        return self.two[4 * self.q : 4 * self.q + self.n, :]


def put_tiles(target, start, part):
    for t in range(part.shape[-1] // 128):
        target[start : start + part.shape[0], :] = part[:, t * 128 : t * 128 + 128]
        start += part.shape[0]
    return start


def first_kernel(s, frames, qkv, up, out, down, prior, resets, *refs):
    smalls, refs = refs[:-9], refs[-9:]
    sent_ref, one_ref, two_ref, own_ref, small_ref, resets_ref, wide_rows, rows, other = refs
    resets_ref[...] = resets[...]
    split_rows(s[0], frames, own_ref, other, wide_rows)
    start = put_tiles(sent_ref, 0, other)
    for c in range(3):
        start = put_tiles(sent_ref, start, qkv.get().at[c])
    start = put_tiles(one_ref, put_tiles(one_ref, 0, up), out)
    for i, ref in enumerate(smalls):
        small_ref[i : i + 1, : ref.shape[1]] = ref[...]
    rows[...] = jnp.zeros_like(rows)
    for t in range(2):
        rows[t : t + 1, :] = smalls[UP_BIAS][:, pl.ds(pl.multiple_of(s[1] * 256 + t * 128, 128), 128)]
    rows[2:3, :] = smalls[PRIOR_BIAS][:, pl.ds(pl.multiple_of(s[1] * 128, 128), 128)]
    left = rows[...]
    for k in range(3):
        term = left.astype(BF)
        one_ref[start : start + 16, :] = term
        left = left - term.astype(F32)
        start += 16
    put_tiles(two_ref, put_tiles(two_ref, 0, down), prior)


def cut_kernel(s, got, qkv_ref):
    qkv_ref[...] = got[got.shape[0] - qkv_ref.shape[0] :, :]


def cotangents_kernel(s, logit, out, sent, logit_own, out_own, wide_rows, logit_sent, out_sent):
    split_rows(s[0], logit, logit_own, logit_sent, wide_rows)
    split_rows(s[0], out, out_own, out_sent, wide_rows)
    n = logit_sent.shape[1]
    sent[:, :n] = logit_sent[...]
    sent[:, n:] = out_sent[...]


def gate(values, after, name=None):
    count, total = len(values), len(values) + len(after)

    def run(*refs):
        for source, target in zip(refs[:count], refs[total:], strict=True):
            target[...] = source[...]

    near = pl.BlockSpec(memory_space=pltpu.VMEM)
    return pl.pallas_call(
        run,
        in_specs=[near] * total,
        out_specs=[near] * count,
        out_shape=[pltpu.VMEM(v.shape, v.dtype) for v in values],
        compiler_params=pltpu.CompilerParams(vmem_limit_bytes=SPILL),
        cost_estimate=pl.CostEstimate(flops=0, bytes_accessed=0, transcendentals=0),
        name=name,
    )(*[pin(v) for v in values], *[pin(v) for v in after])


def attend_kernel(
    s, own, got, resets, small, q0, q1, q2, q3, qkv,
    first_ref, triple_ref, mixed_ref, qkv_other_ref, other,
):
    other[...] = tiles_of(got, 0, own.shape[0], 2)
    unit, _ = norm_of(whole_rows(s[0], own, other))
    n = first_ref.shape[1]
    first_ref[...] = (unit * vector(small, FIRST_GAIN, n) + vector(small, FIRST_SHIFT, n)).astype(BF)
    for j, piece in enumerate((q0, q1, q2, q3)):
        size = qkv.shape[1] // 4
        rows = pl.ds(pl.multiple_of((s[1] ^ j) * size, 16), size)
        for c in range(3):
            qkv_other_ref[c, rows, :] = tiles_of(piece, c * 2 * size, size, 2)
    for half, weight in enumerate((qkv, qkv_other_ref)):
        for c in range(3):
            value = mm(first_ref[...], weight[c]).astype(BF)
            triple_ref[:, (half * 3 + c) * 256 : (half * 3 + c + 1) * 256] = value
    units = []
    for block, at in enumerate(blocks_in(own)):
        allowed = allowed_pairs(resets[pl.ds(s[0] * len(blocks_in(own)) + block, 1), :PAD])
        units += [(at, allowed, pair, (pair // 2) * 768 + (pair % 2) * 128) for pair in range(4)]
    for group in range(0, len(units), GROUP):
        some = units[group : group + GROUP]
        scores = [
            mm_bt(two_heads(triple_ref[at, start : start + 128] * HEAD_DIM ** (-0.5)), triple_ref[at, start + 256 : start + 384])
            for at, _, _, start in some
        ]
        weights = [softmax_of(score, allowed).astype(BF) for score, (_, allowed, _, _) in zip(scores, some, strict=True)]
        for weight, (at, _, pair, start) in zip(weights, some, strict=True):
            mixed = one_pair(mm(weight, triple_ref[at, start + 512 : start + 640])).astype(BF)
            mixed_ref[at, pair * 128 : pair * 128 + 128] = mixed


def feed_kernel(
    s, own, other, mixed, small, out, up, down, a0, a1, a2, a3, b0, b1, b2, b3,
    block_other_ref, block_own_ref, middle_ref, second_ref, act_ref, slope_ref, ending_ref, prior_in_ref,
    out_other_ref, up_other_ref, down_other_ref, bias_other,
):
    n, half, wide = out.shape[0], up.shape[1], up.shape[0]
    for j, piece in enumerate(zip((a0, a1, a2, a3), (b0, b1, b2, b3))):
        piece = Packed(piece, wide, half // 4, n // 4)
        place = s[1] ^ j
        out_other_ref[pl.ds(pl.multiple_of(place * (n // 4), 16), n // 4), :] = piece.out()
        at = pl.ds(pl.multiple_of(place * 256, 256), 256)
        up_other_ref[:, at] = piece.up()
        down_other_ref[at, :] = piece.down()
        bias = piece.bias()
        bias_other[:, at] = jnp.concatenate([bias[0:1], bias[1:2]], axis=1)
    middle_ref[...] = (
        whole_rows(s[0], own, other)
        + vector(small, OUT_BIAS, wide)
        + mm(mixed[:, :n], out[...])
        + mm(mixed[:, n:], out_other_ref[...])
    )
    unit, _ = norm_of(middle_ref[...])
    second_ref[...] = (unit * vector(small, SECOND_GAIN, wide) + vector(small, SECOND_SHIFT, wide)).astype(BF)
    total = middle_ref[...] + vector(small, DOWN_BIAS, wide)
    for h, (w_up, w_down) in enumerate(((up, down), (up_other_ref, down_other_ref))):
        for i in range(half // 256):
            at = slice(i * 256, i * 256 + 256)
            to = slice(h * half + i * 256, h * half + i * 256 + 256)
            bias = bias_other[:, at] if h else small[UP_BIAS : UP_BIAS + 1, at]
            for rows in blocks_in(own):
                hidden = mm(second_ref[rows, :], w_up[:, at]) + bias
                square = hidden * hidden
                bent = jnp.tanh(GELU_C * (hidden + GELU_A * hidden * square))
                act_ref[rows, to] = (0.5 * hidden * (1.0 + bent)).astype(BF)
                slope_ref[rows, to] = 0.5 * (1.0 + bent) + (0.5 * GELU_C) * hidden * (1.0 - bent * bent) * (
                    1.0 + (3.0 * GELU_A) * square
                )
        total = total + mm(act_ref[:, h * half : h * half + half], w_down[...])
    ending_ref[...] = total
    unit, _ = norm_of(total)
    prior_in_ref[...] = (unit * vector(small, PRIOR_GAIN, wide) + vector(small, PRIOR_SHIFT, wide)).astype(BF)
    low, high = total[:, :256].astype(BF), total[:, 256:].astype(BF)
    block_own_ref[...] = jnp.where(s[0] == 0, low, high)
    block_other_ref[...] = jnp.where(s[0] == 0, high, low)


def prior_kernel(
    s, ending, small, logit_own, out_own, a0, a1, a2, a3, b0, b1, b2, b3, cotangents, prior,
    grad_ending_ref, ending_grad_ref, vec_ref, bias_ref, weight, bias,
):
    half, n = prior.shape[1], prior.shape[0]
    for j, piece in enumerate(zip((a0, a1, a2, a3), (b0, b1, b2, b3))):
        at = pl.ds(pl.multiple_of((s[1] ^ j) * 128, 128), 128)
        piece = Packed(piece, n, n // 2, n // 8)
        weight[:, at] = piece.prior()
        bias[:, at] = piece.bias()[2:3]
    logit_other = cotangents.at[:, :half]
    back = mm_bt(logit_own[...], prior[...]) + mm_bt(logit_other[...], weight[...])
    unit, factor = norm_of(ending[...])
    gain = vector(small, PRIOR_GAIN, unit.shape[1])
    grad = whole_rows(s[0], out_own, cotangents.at[:, half:]) + norm_back(back, unit, factor, gain)
    grad_ending_ref[...] = grad
    ending_grad_ref[...] = grad.astype(BF)
    vec_ref[...] = jnp.concatenate([col_sum(back * unit), col_sum(back), col_sum(grad)], axis=0)
    bias_ref[:, :half] = col_sum(logit_own[...].astype(F32))
    bias_ref[:, half:] = col_sum(logit_other[...].astype(F32))


def logits_kernel(s, prior_in, small, prior, weight, bias, block_other, frames_other, sent_ref, logits_ref):
    half, n = prior.shape[1], block_other.shape[1]
    sent_ref[:, :half] = (mm(prior_in[...], weight[...]) + bias[...]).astype(BF)
    sent_ref[:, half : half + n] = block_other[...]
    sent_ref[:, half + n :] = frames_other[...]
    logits_ref[...] = mm(prior_in[...], prior[...]) + vector(small, PRIOR_BIAS, half)


def store_piece(keep, send, h, j, start, value):
    at = slice(start, start + value.shape[0])
    if j < 2:
        keep[h * 2 + j, at, :] = value
    else:
        send[h * 2 + j - 2, at, :] = value.astype(BF)


def late_grads_kernel(s, act, ending_grad, keep, send):
    half = act.shape[1] // 2
    for h in range(2):
        for j in (2, 3, 0, 1):
            part = act[:, pl.ds(pl.multiple_of(h * half + (s[1] ^ j) * 256, 256), 256)]
            value = mm_at(part, ending_grad[...])
            for t in range(value.shape[1] // 128):
                store_piece(keep, send, h, j, t * 256, value[:, t * 128 : t * 128 + 128])


def up_grads_kernel(
    s, second, hidden_grad, mixed, middle_grad, prior_in, logit_own, cotangents, keep, send, turned, wide, tall,
):
    turned[...] = second[...].T
    half = hidden_grad.shape[1] // 2
    n, m = second.shape[1], mixed.shape[1] // 2
    logit_other = cotangents.at[:, : logit_own.shape[1]]
    for h in range(2):
        wide[...] = mm_at(mixed[:, h * m : h * m + m], middle_grad[...])
        tall[...] = mm_at(prior_in[...], (logit_own, logit_other)[h][...])
        for j in (2, 3, 0, 1):
            place = s[1] ^ j
            at = pl.ds(pl.multiple_of(place * 128, 128), 128)
            value = mm(turned[...], hidden_grad[:, pl.ds(pl.multiple_of(h * half + place * 256, 256), 256)])
            for t in range(2):
                store_piece(keep, send, h, j, t * n, value[:, t * 128 : t * 128 + 128])
            store_piece(keep, send, h, j, 2 * n, wide[:, at])
            store_piece(keep, send, h, j, 2 * n + m, tall[:, at])


def early_grads_kernel(s, first, grad_own, grad_other, keep, send):
    for h in range(2):
        for j in (2, 3, 0, 1):
            place = pl.multiple_of((s[1] ^ j) * 128, 128)
            value = mm_at(first[:, pl.ds(place, 128)], (grad_own, grad_other)[h][...])
            for c in range(3):
                for t in range(2):
                    at = slice(c * 256 + t * 128, c * 256 + t * 128 + 128)
                    store_piece(keep, send, h, j, (t * 3 + c) * 128, value[:, at])


def feed_back_kernel(
    s, ending_grad, slope, middle, grad_ending, small, down, down_other, up, up_other,
    hidden_grad_ref, grad_middle_ref, middle_grad_ref, vec_ref, bias_ref,
):
    half = up.shape[1]
    back = None
    for h, (w_up, w_down) in enumerate(((up, down), (up_other, down_other))):
        for i in range(half // 256):
            at = slice(i * 256, i * 256 + 256)
            to = slice(h * half + i * 256, h * half + i * 256 + 256)
            sums = [None]
            for rows in blocks_in(ending_grad):
                low = (mm_bt(ending_grad[rows, :], w_down[at, :]) * slope[rows, to]).astype(BF)
                hidden_grad_ref[rows, to] = low
                sums = add_up(sums, [col_sum(low.astype(F32))])
            bias_ref[:, to] = sums[0]
        value = mm_bt(hidden_grad_ref[:, h * half : h * half + half], w_up[...])
        back = value if back is None else back + value
    unit, factor = norm_of(middle[...])
    gain = vector(small, SECOND_GAIN, unit.shape[1])
    total = grad_ending[...] + norm_back(back, unit, factor, gain)
    grad_middle_ref[...] = total
    middle_grad_ref[...] = total.astype(BF)
    vec_ref[...] = jnp.concatenate([col_sum(back * unit), col_sum(back), col_sum(total)], axis=0)


def attend_back_kernel(
    half, s, middle_grad, triple, out, resets,
    triple_grad_ref, mixed_grad,
):
    mixed_grad[...] = mm_bt(middle_grad[...], out[...]).astype(BF)
    factor = HEAD_DIM ** (-0.5)
    units = []
    for block, at in enumerate(blocks_in(triple)):
        allowed = allowed_pairs(resets[pl.ds(s[0] * len(blocks_in(triple)) + block, 1), :PAD])
        units += [(at, allowed, pair) for pair in range(2)]
    for group in range(0, len(units), GROUP_BACK):
        some = units[group : group + GROUP_BACK]
        loaded = []
        for at, _, pair in some:
            start = half * 768 + pair * 128
            query, key, value = (triple[at, start + c * 256 : start + c * 256 + 128] for c in range(3))
            mixed2 = two_heads(mixed_grad[at, pair * 128 : pair * 128 + 128])
            loaded.append((two_heads(query * factor), key, value, mixed2))
        scores = [mm_bt(query2, key) for query2, key, _, _ in loaded]
        weight_grads = [mm_bt(mixed2, value) for _, _, value, mixed2 in loaded]
        inner = []
        for score, weight_grad, (_, allowed, _) in zip(scores, weight_grads, some, strict=True):
            again = softmax_of(score, allowed)
            both = again * weight_grad
            total = jnp.sum(both, axis=-1, keepdims=True)
            inner.append((again.astype(BF), (both - again * total).astype(BF)))
        for (again, score_grad), (query2, key, _, mixed2), (at, _, pair) in zip(inner, loaded, some, strict=True):
            thirds = (
                (one_pair(mm(score_grad, key)) * factor).astype(BF),
                mm_at(score_grad, query2).astype(BF),
                mm_at(again, mixed2).astype(BF),
            )
            for c in range(3):
                triple_grad_ref[at, c * 256 + pair * 128 : c * 256 + pair * 128 + 128] = thirds[c]


def frames_back_kernel(
    s, grad_own, grad_other, grad_middle, own, other, qkv_other, small, qkv,
    sent_ref, frames_own_ref, vec_ref,
):
    back = None
    for part, weight in ((grad_own, qkv), (grad_other, qkv_other)):
        for c in range(3):
            value = mm_bt(part[:, c * 256 : c * 256 + 256], weight[c])
            back = value if back is None else back + value
    unit, scale = norm_of(whole_rows(s[0], own, other))
    total = grad_middle[...] + norm_back(back, unit, scale, vector(small, FIRST_GAIN, unit.shape[1]))
    low, high = total[:, :256], total[:, 256:]
    frames_own_ref[...] = jnp.where(s[0] == 0, low, high)
    sent_ref[...] = jnp.where(s[0] == 0, high, low).astype(BF)
    vec_ref[...] = jnp.concatenate([col_sum(back * unit), col_sum(back)], axis=0)


def late_place_kernel(s, mine, near, far, farther, down_ref):
    q = down_ref.shape[0] // 4
    for j, piece in enumerate((mine, near, far, farther)):
        rows = pl.ds(pl.multiple_of((s[1] ^ j) * q, 8), q)
        for t in range(down_ref.shape[1] // 128):
            down_ref[rows, t * 128 : t * 128 + 128] = piece[t * q : t * q + q, :].astype(F32)


def up_place_kernel(s, mine, near, far, farther, up_ref, out_ref, prior_ref, token):
    token[...] = jnp.zeros_like(token)
    n, m = up_ref.shape[0], out_ref.shape[0]
    for j, piece in enumerate((mine, near, far, farther)):
        place = s[1] ^ j
        for t in range(2):
            columns = pl.ds(pl.multiple_of(place * 256 + t * 128, 128), 128)
            up_ref[:, columns] = piece[t * n : t * n + n, :].astype(F32)
        at = pl.ds(pl.multiple_of(place * 128, 128), 128)
        out_ref[:, at] = piece[2 * n : 2 * n + m, :].astype(F32)
        prior_ref[:, at] = piece[2 * n + m :, :].astype(F32)


def early_place_kernel(s, mine, near, far, farther, qkv_ref, *vecs):
    vecs, sums = vecs[:-1], vecs[-1]
    sums[...] = mine[6 * 128 :, :].astype(F32) + far[6 * 128 :, :].astype(F32)
    for j, piece in enumerate((mine, near, far, farther)):
        at = pl.ds(pl.multiple_of((s[1] ^ j) * 128, 128), 128)
        for c in range(3):
            for t in range(2):
                start = (t * 3 + c) * 128
                qkv_ref[c, at, t * 128 : t * 128 + 128] = piece[start : start + 128, :].astype(F32)
    qkv_ref.send()
    row = 0
    for ref in vecs[:8]:
        for t in range(ref.shape[1] // 128):
            ref[:, t * 128 : t * 128 + 128] = sums[row : row + 1, :]
            row += 1
    for ref in vecs[8:]:
        tiles = ref.shape[1] // 128
        for t in range(tiles):
            ref[:, t * 128 : t * 128 + 128] = sums[pl.ds(row + s[0] * tiles + t, 1), :]
        row += 2 * tiles


def core_kernel(s, keep, got, low, rest):
    n = keep.shape[1]
    for out, places, dtype in ((low, (2, 3), BF), (rest, (0, 1), F32)):
        for k, i in enumerate(places):
            out[k * n : k * n + n, :] = (keep[i] + got[i].astype(F32)).astype(dtype)


def core_all_kernel(s, keep, got, *refs):
    vectors, lows, rest = refs[:-4], refs[-4:-1], refs[-1]
    n = keep.shape[1]
    for i in (1, 2, 3):
        lows[i - 1][:n, :] = (keep[i] + got[i].astype(F32)).astype(BF)
    rest[:n, :] = keep[0] + got[0].astype(F32)
    if vectors:
        put_vectors(s, vectors, rest, n)
        for low in lows:
            low[n:, :] = rest[n:, :].astype(BF)


def put_vectors(s, vectors, rest, row):
    for ref in vectors[:3]:
        for i in range(ref.shape[0]):
            for t in range(ref.shape[1] // 128):
                rest[row : row + 1, :] = ref[i : i + 1, t * 128 : t * 128 + 128]
                row += 1
    for ref in vectors[3:]:
        tiles = ref.shape[1] // 128
        for t in range(tiles):
            place = row + lax.rem(t + s[0] * (tiles // 2), tiles)
            rest[pl.ds(place, 1), :] = ref[:, t * 128 : t * 128 + 128]
        row += tiles
    rest[row:, :] = jnp.zeros((rest.shape[0] - row, 128), F32)


def over_kernel(s, rest, got, low, mine):
    n = low.shape[0]
    low[...] = (rest[n:, :] + got[n:, :].astype(F32)).astype(BF)
    mine[...] = rest[:n, :] + got[:n, :].astype(F32)


def halves_kernel(s, *refs):
    total, (keep, send) = refs[-1], refs[-3:-1]
    total[...] = functools.reduce(lambda x, y: x + y, [r[...].astype(F32) for r in refs[:-3]])
    n = keep.shape[0]
    send[...] = total[pl.ds(pl.multiple_of((1 - s[2]) * n, 16), n), :].astype(BF)
    keep[...] = total[pl.ds(pl.multiple_of(s[2] * n, 16), n), :].astype(BF)


def join_kernel(s, mine, got, out):
    n = mine.shape[0]
    out[pl.ds(pl.multiple_of(s[2] * n, 16), n), :] = mine[...]
    out[pl.ds(pl.multiple_of((1 - s[2]) * n, 16), n), :] = got[...]


def total_kernel(s, *refs):
    refs[-1][...] = functools.reduce(lambda x, y: x + y, [r[...].astype(F32) for r in refs[:-1]]).astype(BF)


def rows_kernel(entries, s, *refs):
    count = len(entries)
    given, outs, token, rooms = refs[: 2 * count], refs[2 * count : 3 * count], refs[3 * count], refs[3 * count + 1 :]
    token[...] = jnp.zeros_like(token)
    for i, columns in enumerate(entries):
        own, got, out, room = given[2 * i], given[2 * i + 1], outs[i], rooms[i]
        rows = out.shape[0] // 2
        for block, at in enumerate(blocks_in(own)):
            for which, ref, cut in ((s[0], own, slice(None)), (1 - s[0], got, columns)):
                start = pl.multiple_of(which * rows + block * BLOCK, 8)
                room[pl.ds(start, BLOCK), :] = ref[at, cut].astype(F32)[:BLOCK]
        out[...] = room[...].astype(out.ref.dtype)
        out.send()


class Loaded:
    def __init__(self, ref, copy):
        self.ref, self.copy, self.shape = ref, copy, ref.shape

    def get(self):
        if self.copy is not None:
            self.copy.wait()
            self.copy = None
        return self.ref

    def __getitem__(self, index):
        return self.get()[index]


class Leaving:
    def __init__(self, ref, copy):
        self.ref, self.copy, self.shape, self.sent = ref, copy, ref.shape, False

    def __getitem__(self, index):
        return self.ref[index]

    def __setitem__(self, index, value):
        self.ref[index] = value

    def send(self):
        if not self.sent:
            self.copy.start()
            self.sent = True


class Far:
    def __init__(self, value, shape=None, cut=None):
        self.value, self.shape, self.cut = value, shape or value.shape, cut or (lambda s, ref: ref)


def call(kernel, scalars, ins, outs, scratch=(), name=None, after=(), cost=1.0, loads=()):
    n_own, n_loads = len(ins), len(loads)
    ins, outs = [*ins, *[Far(v) for v in loads]], [*outs, *[(v.shape, v.dtype, True) for v in loads]]
    n_in, n_out, n_after = len(ins), len(outs), len(after)
    far_in = [i for i, v in enumerate(ins[:n_own]) if isinstance(v, Far)]
    far_out = [i for i, o in enumerate(outs) if not o[2]]
    room = [pltpu.VMEM(ins[i].shape, ins[i].value.dtype) for i in far_in]
    room += [pltpu.VMEM(outs[i][0], outs[i][1]) for i in far_out]
    need = sum(math.prod(r.shape) * jnp.dtype(r.dtype).itemsize for r in room + list(scratch))

    def run(s, *refs):
        given, refs = list(refs[:n_in]), refs[n_in + n_after :]
        made, refs = list(refs[:n_out]), refs[n_out:]
        own, refs = refs[: len(scratch)], refs[len(scratch) :]
        rooms, sems = refs[:-1], refs[-1]
        for k, i in enumerate(far_in):
            copy = pltpu.make_async_copy(ins[i].cut(s, given[i]), rooms[k], sems.at[k])
            copy.start()
            given[i] = Loaded(rooms[k], copy)
        bringing = []
        for k in range(n_loads):
            copy = pltpu.make_async_copy(given[n_own + k], made[n_out - n_loads + k], sems.at[len(rooms) + k])
            copy.start()
            bringing.append(copy)
        leaving = []
        for k, i in enumerate(far_out, len(far_in)):
            made[i] = Leaving(rooms[k], pltpu.make_async_copy(rooms[k], made[i], sems.at[k]))
            leaving.append(made[i])
        kernel(s, *given[:n_own], *made[: n_out - n_loads], *own)
        for copy in bringing:
            copy.wait()
        for value in given:
            if isinstance(value, Loaded):
                value.get()
        for value in leaving:
            value.send()
        for value in leaving:
            value.copy.wait()

    near, far = pl.BlockSpec(memory_space=pltpu.VMEM), pl.BlockSpec(memory_space=pltpu.HBM)
    return pl.pallas_call(
        run,
        in_specs=[pl.BlockSpec(memory_space=pltpu.SMEM)]
        + [far if isinstance(v, Far) else near for v in ins]
        + [far if isinstance(v, Far) else near for v in after],
        out_specs=[near if stays else far for _, _, stays in outs],
        out_shape=[(pltpu.VMEM if stays else pltpu.HBM)(shape, dtype) for shape, dtype, stays in outs],
        scratch_shapes=list(scratch) + room + [pltpu.SemaphoreType.DMA((max(1, len(room) + n_loads),))],
        compiler_params=pltpu.CompilerParams(vmem_limit_bytes=need + SPILL),
        cost_estimate=pl.CostEstimate(flops=int(cost * COST), bytes_accessed=0, transcendentals=0),
        name=name,
    )(scalars, *[pin(v) for v in ins], *[pin(v) for v in after])


def pin(value):
    if isinstance(value, Far):
        return pltpu.with_memory_space_constraint(value.value, pltpu.HBM)
    return pltpu.with_memory_space_constraint(value, pltpu.VMEM)


def swap(value, axes, sizes, mask):
    count = 1
    for size in sizes:
        count *= size
    return lax.ppermute(value, axes, [(i, i ^ mask) for i in range(count)])


class Moves:
    def __init__(self, n_dp, n_tensor):
        self.n_dp, self.n_tensor = n_dp, n_tensor
        self.dp = lax.axis_index("dp")
        self.here = lax.axis_index("tensor")

    def along(self, value, mask):
        return swap(value, "dp", (self.n_dp,), mask)

    def core(self, value):
        return self.along(value, 1)

    def side(self, value):
        return self.along(value, 2)

    def over(self, value):
        return swap(value, "tensor", (self.n_tensor,), 1)

    def cross(self, value):
        return swap(value, ("dp", "tensor"), (self.n_dp, self.n_tensor), 5)


    def reduce_core(self, scalars, keep, sent, name, after=()):
        n = 2 * sent.shape[1]
        outs = [((n, 128), BF, True), ((n, 128), F32, True)]
        return call(core_kernel, scalars, [keep, self.core(sent)], outs, name=name, after=after, cost=FOLD)

    def reduce_over(self, scalars, low, rest, name, after=()):
        n = low.shape[0] // 2
        outs = [((n, 128), BF, True), ((n, 128), F32, True)]
        return call(over_kernel, scalars, [rest, self.over(low)], outs, name=name, after=after, cost=FOLD)

    def reduce_core_all(self, scalars, keep, sent, name, vectors=(), spare=0, after=()):
        n = sent.shape[1] + spare
        outs = [((n, 128), BF, True)] * 3 + [((n, 128), F32, True)]
        ins = [keep, self.core(sent), *vectors]
        return call(core_all_kernel, scalars, ins, outs, name=name, after=after, cost=FOLD)

    def sides(self, lows):
        return [self.side(lows[0]), self.over(lows[1]), self.cross(lows[2])]

    def total(self, scalars, values, name, after=()):
        shape = values[0].shape
        return call(total_kernel, scalars, values, [(shape, BF, True)], name=name, after=after, cost=FOLD)[0]

    def halves(self, scalars, values, name, after=()):
        n = values[0].shape[0]
        return call(
            halves_kernel,
            scalars,
            values,
            [((n // 2, 128), BF, True)] * 2,
            [pltpu.VMEM((n, 128), F32)],
            name=name,
            after=after,
            cost=FOLD,
        )

    def join(self, scalars, mine, got, name, after=()):
        shape = (mine.shape[0] * 2, 128)
        return call(join_kernel, scalars, [mine, got], [(shape, BF, True)], name=name, after=after, cost=FOLD)[0]

    def bits(self):
        return [1 << i for i in range(2, self.n_dp.bit_length() - 1)]

    def gather(self, total):
        near = self.side(total)
        return total, near, self.core(total), self.core(near)


def local(
    n_dp, n_tensor, frames, resets, first_gain, first_shift, qkv_weight, out_weight, out_bias, second_gain,
    second_shift, up_weight, up_bias, down_weight, down_bias, prior_gain, prior_shift, prior_weight,
    prior_bias, out_cotangent, logit_cotangent,
):
    move = Moves(n_dp, n_tensor)
    rows, half = frames.shape
    width = 2 * half
    mine = rows // 2
    blocks = mine // BLOCK
    hidden_width, n_logits = up_bias.shape[0], prior_bias.shape[0]
    row = lambda v: v.reshape(1, -1)
    core, side = move.dp & 1, (move.dp >> 1) & 1
    reset_rows = jnp.pad(resets.reshape(-1, BLOCK), ((0, -(2 * blocks) % 8), (0, -BLOCK % 128)))
    scalars = jnp.stack([move.here, core * 2 + side, (move.dp >> 2) & 1]).astype(jnp.int32)
    total_rows = blocks * PAD
    quarter = hidden_width // 4

    def near_rows(*entries):
        return [((total_rows, n), dtype, True) for n, dtype in entries]

    def pieces(n):
        return [((4, n, 128), F32, True), ((4, n, 128), BF, True)]

    def columns(value, size, which):
        cut = lambda s, ref: ref.at[..., pl.ds(pl.multiple_of(s[which] * size, 128), size)]
        return Far(value, (*value.shape[:-1], size), cut)

    def some_rows(value, size, which):
        cut = lambda s, ref: ref.at[pl.ds(pl.multiple_of(s[which] * size, 16), size), :]
        return Far(value, (size, value.shape[1]), cut)

    vectors = [first_gain, first_shift, out_bias, second_gain, second_shift, down_bias, prior_gain, prior_shift]
    vectors = [row(v) for v in vectors + [up_bias, prior_bias]]
    qkv_rows = 3 * (width // 4) * (half // 128)
    sent_first, sent_one, sent_two, frames_own, small, resets_near = call(
        first_kernel,
        scalars,
        [
            Far(frames),
            Far(
                qkv_weight,
                (3, width // 4, half),
                lambda s, ref: ref.at[:, pl.ds(pl.multiple_of(s[1] * (width // 4), 16), width // 4), :],
            ),
            columns(up_weight, quarter, 1),
            some_rows(out_weight, half // 4, 1),
            some_rows(down_weight, quarter, 1),
            columns(prior_weight, n_logits // 4, 1),
            Far(reset_rows),
            *[Far(v) for v in vectors],
        ],
        [((total_rows * (half // 128) + qkv_rows, 128), BF, True)]
        + [((width * 2 + half + 48, 128), BF, True), ((quarter * 4 + width, 128), BF, True)]
        + near_rows((half, BF))
        + [((16, hidden_width), F32, True), (reset_rows.shape, jnp.int32, True)],
        [pltpu.VMEM((rows + 16, half), F32), pltpu.VMEM((16, 128), F32), pltpu.VMEM((total_rows, half), BF)],
        "first_parts",
        cost=2.0,
    )

    def all_quarters(got):
        beside = move.side(got)
        return [got, beside, move.core(got), move.core(beside)]

    got_first = move.over(sent_first)
    (qkv_got,) = call(cut_kernel, scalars, [got_first], [((qkv_rows, 128), BF, True)], name="cut", cost=100.0)
    (sent_one,) = gate([sent_one], [got_first], "after_first")
    got_one = move.over(sent_one)
    cot_sent, logit_own, out_own, qkv_near, out_near, up_near, down_near, prior_near = call(
        cotangents_kernel,
        scalars,
        [Far(logit_cotangent), Far(out_cotangent)],
        near_rows((n_logits + half, BF), (n_logits, BF), (half, BF)),
        [pltpu.VMEM((rows + 16, n_logits), F32)]
        + [pltpu.VMEM((total_rows, n), BF) for n in (n_logits, half)],
        name="cotangents",
        after=(sent_first,),
        cost=2.3,
        loads=(qkv_weight, out_weight, up_weight, down_weight, prior_weight),
    )
    (sent_two,) = gate([sent_two], [qkv_got, sent_one, cot_sent], "after_cut")
    got_two = move.over(sent_two)
    first, triple, mixed, qkv_other, frames_other = call(
        attend_kernel,
        scalars,
        [frames_own, got_first, resets_near, small, *all_quarters(qkv_got), qkv_near],
        near_rows((width, BF), (3 * width, BF), (width, BF)) + [(qkv_weight.shape, BF, True)] + near_rows((half, BF)),
        name="attend",
        cost=5.5,
    )
    beside_one = move.side(got_one)
    got_two, cot_sent = gate([got_two, cot_sent], [mixed, beside_one], "after_attend")
    beside_two = move.side(got_two)
    packed = [got_one, beside_one, move.core(got_one), move.core(beside_one)]
    packed += [got_two, beside_two, move.core(got_two), move.core(beside_two)]
    cotangents = move.over(cot_sent)
    block_send, block_own, middle, second, act, slope, ending, prior_in, out_other, up_other, down_other = call(
        feed_kernel,
        scalars,
        [frames_own, frames_other, mixed, small, out_near, up_near, down_near, *packed],
        near_rows((half, BF), (half, BF))
        + near_rows((width, F32), (width, BF), (2 * hidden_width, BF), (2 * hidden_width, F32))
        + near_rows((width, F32), (width, BF))
        + [(v.shape, BF, True) for v in (out_weight, up_weight, down_weight)],
        [pltpu.VMEM((1, hidden_width), F32)],
        name="feed",
        cost=7.2,
    )
    grad_ending, ending_grad, vec_three, prior_bias_sum, prior_other, prior_bias_other = call(
        prior_kernel,
        scalars,
        [ending, small, logit_own, out_own, *packed, cotangents, prior_near],
        near_rows((width, F32), (width, BF))
        + [((3, width), F32, True), ((1, 2 * n_logits), F32, True)]
        + [(prior_weight.shape, BF, True), ((1, n_logits), F32, True)],
        name="prior",
        cost=2.5,
    )
    hidden_grad, grad_middle, middle_grad, vec_two, up_bias_sum = call(
        feed_back_kernel,
        scalars,
        [ending_grad, slope, middle, grad_ending, small, down_near, down_other, up_near, up_other],
        near_rows((2 * hidden_width, BF), (width, F32), (width, BF))
        + [((3, width), F32, True), ((1, 2 * hidden_width), F32, True)],
        name="feed_back",
        cost=6.5,
    )
    up_keep, up_send = call(
        up_grads_kernel,
        scalars,
        [second, hidden_grad, mixed, middle_grad, prior_in, logit_own, cotangents],
        pieces(width * hidden_width // 512 + half + width),
        [pltpu.VMEM((width, total_rows), BF), pltpu.VMEM((half, width), F32), pltpu.VMEM((width, n_logits), F32)],
        name="up_grads",
        cost=3.0,
    )
    late_keep, late_send = call(
        late_grads_kernel,
        scalars,
        [act, ending_grad],
        pieces(hidden_width),
        name="late_grads",
        after=(up_send,),
        cost=3.5,
    )
    *up_low, up_rest = move.reduce_core_all(scalars, up_keep, up_send, "up_core", after=(late_send,))
    def attend_back(half, out, after):
        return call(
            functools.partial(attend_back_kernel, half),
            scalars,
            [middle_grad, triple, out, resets_near],
            near_rows((3 * width // 2, BF)),
            [pltpu.VMEM((total_rows, width // 2), BF)],
            name=f"attend_back_{half}",
            after=after,
            cost=4.5,
        )[0]

    grad_own = attend_back(0, out_near, (up_low[0],))
    *late_low, late_rest = move.reduce_core_all(scalars, late_keep, late_send, "late_core", after=(grad_own,))
    grad_other = attend_back(1, out_other, (late_low[0],))
    keep, send = call(
        early_grads_kernel,
        scalars,
        [first, grad_own, grad_other],
        pieces(768),
        name="early_grads",
        cost=2.0,
    )
    frames_send, frames_grad, vec_one = call(
        frames_back_kernel,
        scalars,
        [grad_own, grad_other, grad_middle, frames_own, frames_other, qkv_other, small, qkv_near],
        near_rows((half, BF), (half, F32)) + [((2, width), F32, True)],
        name="frames_back",
        after=(send,),
        cost=2.5,
    )
    up, up_half = move.halves(scalars, [up_rest, *move.sides(up_low)], "up_1", (vec_one,))
    bits = move.bits()
    spare = 64
    vectors = [vec_one, vec_two, vec_three, up_bias_sum, prior_bias_sum]
    *early_low, early_rest = move.reduce_core_all(scalars, keep, send, "early_core", vectors, spare, (up,))
    done = up = move.total(scalars, [up, move.along(up_half, bits[0])], "up_2", (early_low[0],))
    done = late, late_half = move.halves(scalars, [late_rest, *move.sides(late_low)], "late_1", (done,))
    done = late
    for bit in bits[1:]:
        done = up = move.total(scalars, [up, move.along(up, bit)], "up_3", (done,))
    done = early = move.total(scalars, [early_rest, *move.sides(early_low)], "early_1", (done,))
    done = late = move.total(scalars, [late, move.along(late_half, bits[0])], "late_2", (done,))
    back_send, logits_own = call(
        logits_kernel,
        scalars,
        [prior_in, small, prior_near, prior_other, prior_bias_other, block_send, frames_send],
        near_rows((n_logits + 2 * half, BF), (n_logits, F32)),
        name="logits",
        after=(done,),
        cost=2.0,
    )
    done = up = move.join(scalars, up, move.along(up, bits[0]), "up_4", (back_send,))
    for bit in bits[:-1]:
        done = early = move.total(scalars, [early, move.along(early, bit)], "early_2", (done,))
    for bit in bits[1:]:
        done = late = move.total(scalars, [late, move.along(late, bit)], "late_3", (done,))
    done = early = move.total(scalars, [early, move.along(early, bits[-1])], "early_3", (done,))
    late = move.join(scalars, late, move.along(late, bits[0]), "late_4", (done,))
    up_grad, out_grad, prior_grad, up_done = call(
        up_place_kernel,
        scalars,
        list(move.gather(up)),
        [((width, hidden_width), F32, False), ((half, width), F32, False), ((width, n_logits), F32, False)]
        + [((8, 128), F32, True)],
        name="up_place",
        after=(late,),
        cost=FOLD,
    )
    back_got = move.over(back_send)
    (early_near,) = gate([move.side(early)], [up_done], "after_up")
    block_out, logits, grad_frames, rows_done = call(
        functools.partial(
            rows_kernel,
            [slice(n_logits, n_logits + half), slice(0, n_logits), slice(n_logits + half, n_logits + 2 * half)],
        ),
        scalars,
        [block_own, back_got, logits_own, back_got, frames_grad, back_got],
        [((rows, half), BF, False), ((rows, n_logits), F32, False), ((rows, half), F32, False)]
        + [((8, 128), F32, True)],
        [pltpu.VMEM((rows, n), F32) for n in (half, n_logits, half)],
        name="rows_back",
        after=(early_near,),
        cost=FOLD,
    )
    (late_near,) = gate([move.side(late)], [rows_done], "after_rows")
    early_pieces = [early, early_near, move.core(early), move.core(early_near)]
    late_pieces = [late, late_near, move.core(late), move.core(late_near)]
    qkv_grad, *named = call(
        early_place_kernel,
        scalars,
        early_pieces,
        [((3, width, half), F32, False)]
        + [((1, n), F32, False) for n in [width] * 8 + [hidden_width, n_logits]],
        [pltpu.VMEM((spare, 128), F32)],
        name="early_place",
        after=(rows_done,),
        cost=FOLD,
    )
    (down_grad,) = call(
        late_place_kernel,
        scalars,
        late_pieces,
        [((hidden_width, width), F32, False)],
        name="late_place",
        after=(Far(qkv_grad),),
        cost=FOLD,
    )
    named = [v.reshape(-1) for v in named]
    return (
        block_out,
        logits,
        grad_frames,
        named[0],
        named[1],
        qkv_grad,
        out_grad,
        named[4],
        named[2],
        named[3],
        up_grad,
        named[8],
        down_grad,
        named[7],
        named[5],
        named[6],
        prior_grad,
        named[9],
    )


def solution(mesh):
    rows, cols = P("dp", "tensor"), P(None, "tensor")
    placed = (
        rows, P("dp"), P(), P(), P(None, None, "tensor"), P("tensor", None), P(), P(), P(), cols, P("tensor"),
        P("tensor", None), P(), P(), P(), cols, P("tensor"), rows, rows,
    )
    given = (
        rows, rows, rows, P(), P(), P(None, None, "tensor"), P("tensor", None), P(), P(), P(), cols,
        P("tensor"), P("tensor", None), P(), P(), P(), cols, P("tensor"),
    )
    return jax.shard_map(
        functools.partial(local, mesh.shape["dp"], mesh.shape["tensor"]),
        mesh=mesh,
        in_specs=placed,
        out_specs=given,
        check_vma=False,
    )
```

```python
import functools
import math

import jax
import jax.numpy as jnp
from jax import lax
from jax.experimental import pallas as pl
from jax.experimental.pallas import tpu as pltpu
from jax.sharding import PartitionSpec as P

HEAD_DIM = 64
SEQ_LEN = 50
BLOCK = 4 * SEQ_LEN
PAD = -(-BLOCK // 16) * 16
EPS = 1e-05
NEG = -1e30
GELU_C = 0.7978845608028654
GELU_A = 0.044715
SPILL = 8 * 1024 * 1024
GROUP, GROUP_BACK = 4, 6
COST = 1e8
FOLD = 100.0
BF = jnp.bfloat16
F32 = jnp.float32
FIRST_GAIN, FIRST_SHIFT, OUT_BIAS, SECOND_GAIN, SECOND_SHIFT, DOWN_BIAS, PRIOR_GAIN, PRIOR_SHIFT, UP_BIAS, PRIOR_BIAS = range(10)


def mm(a, b):
    return lax.dot_general(a, b, (((1,), (0,)), ((), ())), preferred_element_type=F32)


def mm_bt(a, b):
    return lax.dot_general(a, b, (((1,), (1,)), ((), ())), preferred_element_type=F32)


def mm_at(a, b):
    return lax.dot_general(a, b, (((0,), (0,)), ((), ())), preferred_element_type=F32)


def norm_of(value):
    centre = value - jnp.mean(value, axis=-1, keepdims=True)
    factor = lax.rsqrt(jnp.mean(centre * centre, axis=-1, keepdims=True) + EPS)
    return centre * factor, factor


def norm_back(grad, unit, factor, gain):
    scaled = grad * gain
    first = jnp.mean(scaled, axis=-1, keepdims=True)
    second = jnp.mean(scaled * unit, axis=-1, keepdims=True)
    return factor * (scaled - first - unit * second)


def col_sum(value):
    return jnp.sum(value, axis=0, keepdims=True)


def whole_rows(here, own, other):
    low = jnp.where(here == 0, own[...], other[...])
    high = jnp.where(here == 0, other[...], own[...])
    return jnp.concatenate([low, high], axis=1).astype(F32)


def allowed_pairs(resets):
    place = lax.broadcasted_iota(jnp.int32, (1, PAD), 1)
    starts = jnp.where((resets == 1) | (lax.rem(place, SEQ_LEN) == 0) | (place >= BLOCK), place, 0)
    row = lax.broadcasted_iota(jnp.int32, (PAD, PAD), 0)
    col = lax.broadcasted_iota(jnp.int32, (PAD, PAD), 1)
    seg = jnp.max(jnp.where(col <= row, starts, 0).astype(F32), axis=-1, keepdims=True).astype(jnp.int32)
    seg2 = jnp.concatenate([seg, seg], axis=0)
    row = lax.broadcasted_iota(jnp.int32, (2 * PAD, PAD), 0)
    row = jnp.where(row >= PAD, row - PAD, row)
    col = lax.broadcasted_iota(jnp.int32, (2 * PAD, PAD), 1)
    return (col <= row) & (col >= seg2)


def two_heads(value):
    first = lax.broadcasted_iota(jnp.int32, value.shape, 1) < HEAD_DIM
    none = jnp.zeros_like(value)
    return jnp.concatenate([jnp.where(first, value, none), jnp.where(first, none, value)], axis=0)


def one_pair(value):
    first = lax.broadcasted_iota(jnp.int32, (PAD, 2 * HEAD_DIM), 1) < HEAD_DIM
    return jnp.where(first, value[:PAD], value[PAD:])


def softmax_of(scores, allowed):
    scores = jnp.where(allowed, scores, NEG)
    expo = jnp.exp(scores - jnp.max(scores, axis=-1, keepdims=True))
    return expo * (1.0 / jnp.sum(expo, axis=-1, keepdims=True))


def vector(small, index, n):
    return small[index : index + 1, :n]


def blocks_in(ref):
    return [slice(i * PAD, i * PAD + PAD) for i in range(ref.shape[0] // PAD)]


def add_up(sums, values):
    return [v if s is None else s + v for s, v in zip(sums, values, strict=True)]


def split_rows(half, source, own, sent, wide_rows):
    rows, n = source.shape
    wide_rows[0:rows, 0:n] = source[...].astype(F32)
    for which, target in ((half, own), (1 - half, sent)):
        for block, at in enumerate(blocks_in(target)):
            start = pl.multiple_of(which * (rows // 2) + block * BLOCK, 8)
            part = wide_rows[pl.ds(start, PAD), 0:n]
            inside = lax.broadcasted_iota(jnp.int32, part.shape, 0) < BLOCK
            target[at, :] = jnp.where(inside, part, 0.0).astype(BF)


def tiles_of(ref, start, n, count):
    return jnp.concatenate([ref[start + t * n : start + t * n + n, :] for t in range(count)], axis=1)


class Packed:
    def __init__(self, refs, n, q, o):
        self.one, self.two = refs
        self.n, self.q, self.o = n, q, o

    def up(self):
        return tiles_of(self.one, 0, self.n, 2)

    def out(self):
        return tiles_of(self.one, 2 * self.n, self.o, 4)

    def bias(self):
        start = 2 * self.n + 4 * self.o
        parts = [self.one[start + 16 * k : start + 16 * k + 16, :].astype(F32) for k in range(3)]
        return (parts[2] + parts[1] + parts[0])[:3]

    def down(self):
        return tiles_of(self.two, 0, self.q, 4)

    def prior(self):
        return self.two[4 * self.q : 4 * self.q + self.n, :]


def put_tiles(target, start, part):
    for t in range(part.shape[-1] // 128):
        target[start : start + part.shape[0], :] = part[:, t * 128 : t * 128 + 128]
        start += part.shape[0]
    return start


def first_kernel(s, frames, qkv, up, out, down, prior, resets, *refs):
    smalls, refs = refs[:-9], refs[-9:]
    qkv_ref, sent_ref, one_ref, two_ref, own_ref, small_ref, resets_ref, wide_rows, rows = refs
    start = 0
    for c in range(3):
        start = put_tiles(qkv_ref, start, qkv.get().at[c])
    split_rows(s[0], frames, own_ref, sent_ref, wide_rows)
    resets_ref[...] = jnp.zeros_like(resets_ref)
    line = resets[...].reshape(1, -1)
    for block in range(line.shape[1] // BLOCK):
        resets_ref[block : block + 1, :BLOCK] = line[:, block * BLOCK : block * BLOCK + BLOCK]
    start = put_tiles(one_ref, put_tiles(one_ref, 0, up), out)
    for i, ref in enumerate(smalls):
        small_ref[i : i + 1, : ref.shape[1]] = ref[...]
    rows[...] = jnp.zeros_like(rows)
    for t in range(2):
        rows[t : t + 1, :] = smalls[UP_BIAS][:, pl.ds(pl.multiple_of(s[1] * 256 + t * 128, 128), 128)]
    rows[2:3, :] = smalls[PRIOR_BIAS][:, pl.ds(pl.multiple_of(s[1] * 128, 128), 128)]
    left = rows[...]
    for k in range(3):
        term = left.astype(BF)
        one_ref[start : start + 16, :] = term
        left = left - term.astype(F32)
        start += 16
    put_tiles(two_ref, put_tiles(two_ref, 0, down), prior)


def cotangents_kernel(s, logit, out, sent, logit_own, out_own, wide_rows, logit_sent, out_sent):
    split_rows(s[0], logit, logit_own, logit_sent, wide_rows)
    split_rows(s[0], out, out_own, out_sent, wide_rows)
    n = logit_sent.shape[1]
    sent[:, :n] = logit_sent[...]
    sent[:, n:] = out_sent[...]


def gate(values, after, name=None):
    count, total = len(values), len(values) + len(after)

    def run(*refs):
        for source, target in zip(refs[:count], refs[total:], strict=True):
            target[...] = source[...]

    near = pl.BlockSpec(memory_space=pltpu.VMEM)
    return pl.pallas_call(
        run,
        in_specs=[near] * total,
        out_specs=[near] * count,
        out_shape=[pltpu.VMEM(v.shape, v.dtype) for v in values],
        compiler_params=pltpu.CompilerParams(vmem_limit_bytes=SPILL),
        cost_estimate=pl.CostEstimate(flops=0, bytes_accessed=0, transcendentals=0),
        name=name,
    )(*[pin(v) for v in values], *[pin(v) for v in after])


def attend_kernel(
    s, own, other, resets, small, q0, q1, q2, q3, qkv,
    first_ref, triple_ref, mixed_ref, qkv_other_ref,
):
    unit, _ = norm_of(whole_rows(s[0], own, other))
    n = first_ref.shape[1]
    first_ref[...] = (unit * vector(small, FIRST_GAIN, n) + vector(small, FIRST_SHIFT, n)).astype(BF)
    for j, piece in enumerate((q0, q1, q2, q3)):
        size = qkv.shape[1] // 4
        rows = pl.ds(pl.multiple_of((s[1] ^ j) * size, 16), size)
        for c in range(3):
            qkv_other_ref[c, rows, :] = tiles_of(piece, c * 2 * size, size, 2)
    for half, weight in enumerate((qkv, qkv_other_ref)):
        for c in range(3):
            value = mm(first_ref[...], weight[c]).astype(BF)
            triple_ref[:, (half * 3 + c) * 256 : (half * 3 + c + 1) * 256] = value
    units = []
    for block, at in enumerate(blocks_in(own)):
        allowed = allowed_pairs(resets[pl.ds(s[0] * len(blocks_in(own)) + block, 1), :PAD])
        units += [(at, allowed, pair, (pair // 2) * 768 + (pair % 2) * 128) for pair in range(4)]
    for group in range(0, len(units), GROUP):
        some = units[group : group + GROUP]
        scores = [
            mm_bt(two_heads(triple_ref[at, start : start + 128] * HEAD_DIM ** (-0.5)), triple_ref[at, start + 256 : start + 384])
            for at, _, _, start in some
        ]
        weights = [softmax_of(score, allowed).astype(BF) for score, (_, allowed, _, _) in zip(scores, some, strict=True)]
        for weight, (at, _, pair, start) in zip(weights, some, strict=True):
            mixed = one_pair(mm(weight, triple_ref[at, start + 512 : start + 640])).astype(BF)
            mixed_ref[at, pair * 128 : pair * 128 + 128] = mixed


def feed_kernel(
    s, own, other, mixed, small, out, up, down, a0, a1, a2, a3, b0, b1, b2, b3,
    block_other_ref, block_own_ref, middle_ref, second_ref, act_ref, slope_ref, ending_ref, prior_in_ref,
    out_other_ref, up_other_ref, down_other_ref, bias_other,
):
    n, half, wide = out.shape[0], up.shape[1], up.shape[0]
    for j, piece in enumerate(zip((a0, a1, a2, a3), (b0, b1, b2, b3))):
        piece = Packed(piece, wide, half // 4, n // 4)
        place = s[1] ^ j
        out_other_ref[pl.ds(pl.multiple_of(place * (n // 4), 16), n // 4), :] = piece.out()
        at = pl.ds(pl.multiple_of(place * 256, 256), 256)
        up_other_ref[:, at] = piece.up()
        down_other_ref[at, :] = piece.down()
        bias = piece.bias()
        bias_other[:, at] = jnp.concatenate([bias[0:1], bias[1:2]], axis=1)
    middle_ref[...] = (
        whole_rows(s[0], own, other)
        + vector(small, OUT_BIAS, wide)
        + mm(mixed[:, :n], out[...])
        + mm(mixed[:, n:], out_other_ref[...])
    )
    unit, _ = norm_of(middle_ref[...])
    second_ref[...] = (unit * vector(small, SECOND_GAIN, wide) + vector(small, SECOND_SHIFT, wide)).astype(BF)
    total = middle_ref[...] + vector(small, DOWN_BIAS, wide)
    for h, (w_up, w_down) in enumerate(((up, down), (up_other_ref, down_other_ref))):
        for i in range(half // 256):
            at = slice(i * 256, i * 256 + 256)
            to = slice(h * half + i * 256, h * half + i * 256 + 256)
            bias = bias_other[:, at] if h else small[UP_BIAS : UP_BIAS + 1, at]
            for rows in blocks_in(own):
                hidden = mm(second_ref[rows, :], w_up[:, at]) + bias
                square = hidden * hidden
                bent = jnp.tanh(GELU_C * (hidden + GELU_A * hidden * square))
                act_ref[rows, to] = (0.5 * hidden * (1.0 + bent)).astype(BF)
                slope_ref[rows, to] = 0.5 * (1.0 + bent) + (0.5 * GELU_C) * hidden * (1.0 - bent * bent) * (
                    1.0 + (3.0 * GELU_A) * square
                )
        total = total + mm(act_ref[:, h * half : h * half + half], w_down[...])
    ending_ref[...] = total
    unit, _ = norm_of(total)
    prior_in_ref[...] = (unit * vector(small, PRIOR_GAIN, wide) + vector(small, PRIOR_SHIFT, wide)).astype(BF)
    low, high = total[:, :256].astype(BF), total[:, 256:].astype(BF)
    block_own_ref[...] = jnp.where(s[0] == 0, low, high)
    block_other_ref[...] = jnp.where(s[0] == 0, high, low)


def prior_kernel(
    s, ending, small, logit_own, out_own, a0, a1, a2, a3, b0, b1, b2, b3, cotangents, prior,
    grad_ending_ref, ending_grad_ref, vec_ref, bias_ref, weight, bias,
):
    half, n = prior.shape[1], prior.shape[0]
    for j, piece in enumerate(zip((a0, a1, a2, a3), (b0, b1, b2, b3))):
        at = pl.ds(pl.multiple_of((s[1] ^ j) * 128, 128), 128)
        piece = Packed(piece, n, n // 2, n // 8)
        weight[:, at] = piece.prior()
        bias[:, at] = piece.bias()[2:3]
    logit_other = cotangents.at[:, :half]
    back = mm_bt(logit_own[...], prior[...]) + mm_bt(logit_other[...], weight[...])
    unit, factor = norm_of(ending[...])
    gain = vector(small, PRIOR_GAIN, unit.shape[1])
    grad = whole_rows(s[0], out_own, cotangents.at[:, half:]) + norm_back(back, unit, factor, gain)
    grad_ending_ref[...] = grad
    ending_grad_ref[...] = grad.astype(BF)
    vec_ref[...] = jnp.concatenate([col_sum(back * unit), col_sum(back), col_sum(grad)], axis=0)
    bias_ref[:, :half] = col_sum(logit_own[...].astype(F32))
    bias_ref[:, half:] = col_sum(logit_other[...].astype(F32))


def logits_kernel(s, prior_in, small, prior, weight, bias, block_other, frames_other, sent_ref, logits_ref):
    half, n = prior.shape[1], block_other.shape[1]
    sent_ref[:, :half] = (mm(prior_in[...], weight[...]) + bias[...]).astype(BF)
    sent_ref[:, half : half + n] = block_other[...]
    sent_ref[:, half + n :] = frames_other[...]
    logits_ref[...] = mm(prior_in[...], prior[...]) + vector(small, PRIOR_BIAS, half)


def store_piece(keep, send, h, j, start, value):
    at = slice(start, start + value.shape[0])
    if j < 2:
        keep[h * 2 + j, at, :] = value
    else:
        send[h * 2 + j - 2, at, :] = value.astype(BF)


def late_grads_kernel(s, act, ending_grad, keep, send):
    half = act.shape[1] // 2
    for h in range(2):
        for j in (2, 3, 0, 1):
            part = act[:, pl.ds(pl.multiple_of(h * half + (s[1] ^ j) * 256, 256), 256)]
            value = mm_at(part, ending_grad[...])
            for t in range(value.shape[1] // 128):
                store_piece(keep, send, h, j, t * 256, value[:, t * 128 : t * 128 + 128])


def up_grads_kernel(
    s, second, hidden_grad, mixed, middle_grad, prior_in, logit_own, cotangents, keep, send, turned, wide, tall,
):
    turned[...] = second[...].T
    half = hidden_grad.shape[1] // 2
    n, m = second.shape[1], mixed.shape[1] // 2
    logit_other = cotangents.at[:, : logit_own.shape[1]]
    for h in range(2):
        wide[...] = mm_at(mixed[:, h * m : h * m + m], middle_grad[...])
        tall[...] = mm_at(prior_in[...], (logit_own, logit_other)[h][...])
        for j in (2, 3, 0, 1):
            place = s[1] ^ j
            at = pl.ds(pl.multiple_of(place * 128, 128), 128)
            value = mm(turned[...], hidden_grad[:, pl.ds(pl.multiple_of(h * half + place * 256, 256), 256)])
            for t in range(2):
                store_piece(keep, send, h, j, t * n, value[:, t * 128 : t * 128 + 128])
            store_piece(keep, send, h, j, 2 * n, wide[:, at])
            store_piece(keep, send, h, j, 2 * n + m, tall[:, at])


def early_grads_kernel(s, first, grad_own, grad_other, keep, send):
    for h in range(2):
        for j in (2, 3, 0, 1):
            place = pl.multiple_of((s[1] ^ j) * 128, 128)
            value = mm_at(first[:, pl.ds(place, 128)], (grad_own, grad_other)[h][...])
            for c in range(3):
                for t in range(2):
                    at = slice(c * 256 + t * 128, c * 256 + t * 128 + 128)
                    store_piece(keep, send, h, j, (t * 3 + c) * 128, value[:, at])


def feed_back_kernel(
    s, ending_grad, slope, middle, grad_ending, small, down, down_other, up, up_other,
    hidden_grad_ref, grad_middle_ref, middle_grad_ref, vec_ref, bias_ref,
):
    half = up.shape[1]
    back = None
    for h, (w_up, w_down) in enumerate(((up, down), (up_other, down_other))):
        for i in range(half // 256):
            at = slice(i * 256, i * 256 + 256)
            to = slice(h * half + i * 256, h * half + i * 256 + 256)
            sums = [None]
            for rows in blocks_in(ending_grad):
                low = (mm_bt(ending_grad[rows, :], w_down[at, :]) * slope[rows, to]).astype(BF)
                hidden_grad_ref[rows, to] = low
                sums = add_up(sums, [col_sum(low.astype(F32))])
            bias_ref[:, to] = sums[0]
        value = mm_bt(hidden_grad_ref[:, h * half : h * half + half], w_up[...])
        back = value if back is None else back + value
    unit, factor = norm_of(middle[...])
    gain = vector(small, SECOND_GAIN, unit.shape[1])
    total = grad_ending[...] + norm_back(back, unit, factor, gain)
    grad_middle_ref[...] = total
    middle_grad_ref[...] = total.astype(BF)
    vec_ref[...] = jnp.concatenate([col_sum(back * unit), col_sum(back), col_sum(total)], axis=0)


def attend_back_kernel(
    half, s, middle_grad, triple, out, resets,
    triple_grad_ref, mixed_grad,
):
    mixed_grad[...] = mm_bt(middle_grad[...], out[...]).astype(BF)
    factor = HEAD_DIM ** (-0.5)
    units = []
    for block, at in enumerate(blocks_in(triple)):
        allowed = allowed_pairs(resets[pl.ds(s[0] * len(blocks_in(triple)) + block, 1), :PAD])
        units += [(at, allowed, pair) for pair in range(2)]
    for group in range(0, len(units), GROUP_BACK):
        some = units[group : group + GROUP_BACK]
        loaded = []
        for at, _, pair in some:
            start = half * 768 + pair * 128
            query, key, value = (triple[at, start + c * 256 : start + c * 256 + 128] for c in range(3))
            mixed2 = two_heads(mixed_grad[at, pair * 128 : pair * 128 + 128])
            loaded.append((two_heads(query * factor), key, value, mixed2))
        scores = [mm_bt(query2, key) for query2, key, _, _ in loaded]
        weight_grads = [mm_bt(mixed2, value) for _, _, value, mixed2 in loaded]
        inner = []
        for score, weight_grad, (_, allowed, _) in zip(scores, weight_grads, some, strict=True):
            again = softmax_of(score, allowed)
            both = again * weight_grad
            total = jnp.sum(both, axis=-1, keepdims=True)
            inner.append((again.astype(BF), (both - again * total).astype(BF)))
        for (again, score_grad), (query2, key, _, mixed2), (at, _, pair) in zip(inner, loaded, some, strict=True):
            thirds = (
                (one_pair(mm(score_grad, key)) * factor).astype(BF),
                mm_at(score_grad, query2).astype(BF),
                mm_at(again, mixed2).astype(BF),
            )
            for c in range(3):
                triple_grad_ref[at, c * 256 + pair * 128 : c * 256 + pair * 128 + 128] = thirds[c]


def frames_back_kernel(
    s, grad_own, grad_other, grad_middle, own, other, qkv_other, small, qkv,
    sent_ref, frames_own_ref, vec_ref,
):
    back = None
    for part, weight in ((grad_own, qkv), (grad_other, qkv_other)):
        for c in range(3):
            value = mm_bt(part[:, c * 256 : c * 256 + 256], weight[c])
            back = value if back is None else back + value
    unit, scale = norm_of(whole_rows(s[0], own, other))
    total = grad_middle[...] + norm_back(back, unit, scale, vector(small, FIRST_GAIN, unit.shape[1]))
    low, high = total[:, :256], total[:, 256:]
    frames_own_ref[...] = jnp.where(s[0] == 0, low, high)
    sent_ref[...] = jnp.where(s[0] == 0, high, low).astype(BF)
    vec_ref[...] = jnp.concatenate([col_sum(back * unit), col_sum(back)], axis=0)


def late_place_kernel(s, mine, near, far, farther, down_ref):
    q = down_ref.shape[0] // 4
    for j, piece in enumerate((mine, near, far, farther)):
        rows = pl.ds(pl.multiple_of((s[1] ^ j) * q, 8), q)
        for t in range(down_ref.shape[1] // 128):
            down_ref[rows, t * 128 : t * 128 + 128] = piece[t * q : t * q + q, :].astype(F32)


def up_place_kernel(s, mine, near, far, farther, up_ref, out_ref, prior_ref, token):
    token[...] = jnp.zeros_like(token)
    n, m = up_ref.shape[0], out_ref.shape[0]
    for j, piece in enumerate((mine, near, far, farther)):
        place = s[1] ^ j
        for t in range(2):
            columns = pl.ds(pl.multiple_of(place * 256 + t * 128, 128), 128)
            up_ref[:, columns] = piece[t * n : t * n + n, :].astype(F32)
        at = pl.ds(pl.multiple_of(place * 128, 128), 128)
        out_ref[:, at] = piece[2 * n : 2 * n + m, :].astype(F32)
        prior_ref[:, at] = piece[2 * n + m :, :].astype(F32)


def early_place_kernel(s, mine, near, far, farther, qkv_ref, *vecs):
    vecs, sums = vecs[:-1], vecs[-1]
    sums[...] = mine[6 * 128 :, :].astype(F32) + far[6 * 128 :, :].astype(F32)
    for j, piece in enumerate((mine, near, far, farther)):
        at = pl.ds(pl.multiple_of((s[1] ^ j) * 128, 128), 128)
        for c in range(3):
            for t in range(2):
                start = (t * 3 + c) * 128
                qkv_ref[c, at, t * 128 : t * 128 + 128] = piece[start : start + 128, :].astype(F32)
    qkv_ref.send()
    row = 0
    for ref in vecs[:8]:
        for t in range(ref.shape[1] // 128):
            ref[:, t * 128 : t * 128 + 128] = sums[row : row + 1, :]
            row += 1
    for ref in vecs[8:]:
        tiles = ref.shape[1] // 128
        for t in range(tiles):
            ref[:, t * 128 : t * 128 + 128] = sums[pl.ds(row + s[0] * tiles + t, 1), :]
        row += 2 * tiles


def core_kernel(s, keep, got, low, rest):
    n = keep.shape[1]
    for out, places, dtype in ((low, (2, 3), BF), (rest, (0, 1), F32)):
        for k, i in enumerate(places):
            out[k * n : k * n + n, :] = (keep[i] + got[i].astype(F32)).astype(dtype)


def core_all_kernel(s, keep, got, *refs):
    vectors, lows, rest = refs[:-4], refs[-4:-1], refs[-1]
    n = keep.shape[1]
    for i in (1, 2, 3):
        lows[i - 1][:n, :] = (keep[i] + got[i].astype(F32)).astype(BF)
    rest[:n, :] = keep[0] + got[0].astype(F32)
    if vectors:
        put_vectors(s, vectors, rest, n)
        for low in lows:
            low[n:, :] = rest[n:, :].astype(BF)


def put_vectors(s, vectors, rest, row):
    for ref in vectors[:3]:
        for i in range(ref.shape[0]):
            for t in range(ref.shape[1] // 128):
                rest[row : row + 1, :] = ref[i : i + 1, t * 128 : t * 128 + 128]
                row += 1
    for ref in vectors[3:]:
        tiles = ref.shape[1] // 128
        for t in range(tiles):
            place = row + lax.rem(t + s[0] * (tiles // 2), tiles)
            rest[pl.ds(place, 1), :] = ref[:, t * 128 : t * 128 + 128]
        row += tiles
    rest[row:, :] = jnp.zeros((rest.shape[0] - row, 128), F32)


def over_kernel(s, rest, got, low, mine):
    n = low.shape[0]
    low[...] = (rest[n:, :] + got[n:, :].astype(F32)).astype(BF)
    mine[...] = rest[:n, :] + got[:n, :].astype(F32)


def halves_kernel(s, *refs):
    total, (keep, send) = refs[-1], refs[-3:-1]
    total[...] = functools.reduce(lambda x, y: x + y, [r[...].astype(F32) for r in refs[:-3]])
    n = keep.shape[0]
    send[...] = total[pl.ds(pl.multiple_of((1 - s[2]) * n, 16), n), :].astype(BF)
    keep[...] = total[pl.ds(pl.multiple_of(s[2] * n, 16), n), :].astype(BF)


def join_kernel(s, mine, got, out):
    n = mine.shape[0]
    out[pl.ds(pl.multiple_of(s[2] * n, 16), n), :] = mine[...]
    out[pl.ds(pl.multiple_of((1 - s[2]) * n, 16), n), :] = got[...]


def total_kernel(s, *refs):
    refs[-1][...] = functools.reduce(lambda x, y: x + y, [r[...].astype(F32) for r in refs[:-1]]).astype(BF)


def rows_kernel(entries, s, *refs):
    count = len(entries)
    given, outs, token, rooms = refs[: 2 * count], refs[2 * count : 3 * count], refs[3 * count], refs[3 * count + 1 :]
    token[...] = jnp.zeros_like(token)
    for i, columns in enumerate(entries):
        own, got, out, room = given[2 * i], given[2 * i + 1], outs[i], rooms[i]
        rows = out.shape[0] // 2
        for block, at in enumerate(blocks_in(own)):
            for which, ref, cut in ((s[0], own, slice(None)), (1 - s[0], got, columns)):
                start = pl.multiple_of(which * rows + block * BLOCK, 8)
                room[pl.ds(start, BLOCK), :] = ref[at, cut].astype(F32)[:BLOCK]
        out[...] = room[...].astype(out.ref.dtype)
        out.send()


class Loaded:
    def __init__(self, ref, copy):
        self.ref, self.copy, self.shape = ref, copy, ref.shape

    def get(self):
        if self.copy is not None:
            self.copy.wait()
            self.copy = None
        return self.ref

    def __getitem__(self, index):
        return self.get()[index]


class Leaving:
    def __init__(self, ref, copy):
        self.ref, self.copy, self.shape, self.sent = ref, copy, ref.shape, False

    def __getitem__(self, index):
        return self.ref[index]

    def __setitem__(self, index, value):
        self.ref[index] = value

    def send(self):
        if not self.sent:
            self.copy.start()
            self.sent = True


class Far:
    def __init__(self, value, shape=None, cut=None):
        self.value, self.shape, self.cut = value, shape or value.shape, cut or (lambda s, ref: ref)


def call(kernel, scalars, ins, outs, scratch=(), name=None, after=(), cost=1.0, loads=()):
    n_own, n_loads = len(ins), len(loads)
    ins, outs = [*ins, *[Far(v) for v in loads]], [*outs, *[(v.shape, v.dtype, True) for v in loads]]
    n_in, n_out, n_after = len(ins), len(outs), len(after)
    far_in = [i for i, v in enumerate(ins[:n_own]) if isinstance(v, Far)]
    far_out = [i for i, o in enumerate(outs) if not o[2]]
    room = [pltpu.VMEM(ins[i].shape, ins[i].value.dtype) for i in far_in]
    room += [pltpu.VMEM(outs[i][0], outs[i][1]) for i in far_out]
    need = sum(math.prod(r.shape) * jnp.dtype(r.dtype).itemsize for r in room + list(scratch))

    def run(s, *refs):
        given, refs = list(refs[:n_in]), refs[n_in + n_after :]
        made, refs = list(refs[:n_out]), refs[n_out:]
        own, refs = refs[: len(scratch)], refs[len(scratch) :]
        rooms, sems = refs[:-1], refs[-1]
        for k, i in enumerate(far_in):
            copy = pltpu.make_async_copy(ins[i].cut(s, given[i]), rooms[k], sems.at[k])
            copy.start()
            given[i] = Loaded(rooms[k], copy)
        bringing = []
        for k in range(n_loads):
            copy = pltpu.make_async_copy(given[n_own + k], made[n_out - n_loads + k], sems.at[len(rooms) + k])
            copy.start()
            bringing.append(copy)
        leaving = []
        for k, i in enumerate(far_out, len(far_in)):
            made[i] = Leaving(rooms[k], pltpu.make_async_copy(rooms[k], made[i], sems.at[k]))
            leaving.append(made[i])
        kernel(s, *given[:n_own], *made[: n_out - n_loads], *own)
        for copy in bringing:
            copy.wait()
        for value in given:
            if isinstance(value, Loaded):
                value.get()
        for value in leaving:
            value.send()
        for value in leaving:
            value.copy.wait()

    near, far = pl.BlockSpec(memory_space=pltpu.VMEM), pl.BlockSpec(memory_space=pltpu.HBM)
    return pl.pallas_call(
        run,
        in_specs=[pl.BlockSpec(memory_space=pltpu.SMEM)]
        + [far if isinstance(v, Far) else near for v in ins]
        + [far if isinstance(v, Far) else near for v in after],
        out_specs=[near if stays else far for _, _, stays in outs],
        out_shape=[(pltpu.VMEM if stays else pltpu.HBM)(shape, dtype) for shape, dtype, stays in outs],
        scratch_shapes=list(scratch) + room + [pltpu.SemaphoreType.DMA((max(1, len(room) + n_loads),))],
        compiler_params=pltpu.CompilerParams(vmem_limit_bytes=need + SPILL),
        cost_estimate=pl.CostEstimate(flops=int(cost * COST), bytes_accessed=0, transcendentals=0),
        name=name,
    )(scalars, *[pin(v) for v in ins], *[pin(v) for v in after])


def pin(value):
    if isinstance(value, Far):
        return pltpu.with_memory_space_constraint(value.value, pltpu.HBM)
    return pltpu.with_memory_space_constraint(value, pltpu.VMEM)


def swap(value, axes, sizes, mask):
    count = 1
    for size in sizes:
        count *= size
    return lax.ppermute(value, axes, [(i, i ^ mask) for i in range(count)])


class Moves:
    def __init__(self, n_dp, n_tensor):
        self.n_dp, self.n_tensor = n_dp, n_tensor
        self.dp = lax.axis_index("dp")
        self.here = lax.axis_index("tensor")

    def along(self, value, mask):
        return swap(value, "dp", (self.n_dp,), mask)

    def core(self, value):
        return self.along(value, 1)

    def side(self, value):
        return self.along(value, 2)

    def over(self, value):
        return swap(value, "tensor", (self.n_tensor,), 1)

    def cross(self, value):
        return swap(value, ("dp", "tensor"), (self.n_dp, self.n_tensor), 5)


    def reduce_core(self, scalars, keep, sent, name, after=()):
        n = 2 * sent.shape[1]
        outs = [((n, 128), BF, True), ((n, 128), F32, True)]
        return call(core_kernel, scalars, [keep, self.core(sent)], outs, name=name, after=after, cost=FOLD)

    def reduce_over(self, scalars, low, rest, name, after=()):
        n = low.shape[0] // 2
        outs = [((n, 128), BF, True), ((n, 128), F32, True)]
        return call(over_kernel, scalars, [rest, self.over(low)], outs, name=name, after=after, cost=FOLD)

    def reduce_core_all(self, scalars, keep, sent, name, vectors=(), spare=0, after=()):
        n = sent.shape[1] + spare
        outs = [((n, 128), BF, True)] * 3 + [((n, 128), F32, True)]
        ins = [keep, self.core(sent), *vectors]
        return call(core_all_kernel, scalars, ins, outs, name=name, after=after, cost=FOLD)

    def sides(self, lows):
        return [self.side(lows[0]), self.over(lows[1]), self.cross(lows[2])]

    def total(self, scalars, values, name, after=()):
        shape = values[0].shape
        return call(total_kernel, scalars, values, [(shape, BF, True)], name=name, after=after, cost=FOLD)[0]

    def halves(self, scalars, values, name, after=()):
        n = values[0].shape[0]
        return call(
            halves_kernel,
            scalars,
            values,
            [((n // 2, 128), BF, True)] * 2,
            [pltpu.VMEM((n, 128), F32)],
            name=name,
            after=after,
            cost=FOLD,
        )

    def join(self, scalars, mine, got, name, after=()):
        shape = (mine.shape[0] * 2, 128)
        return call(join_kernel, scalars, [mine, got], [(shape, BF, True)], name=name, after=after, cost=FOLD)[0]

    def bits(self):
        return [1 << i for i in range(2, self.n_dp.bit_length() - 1)]

    def gather(self, total):
        near = self.side(total)
        return total, near, self.core(total), self.core(near)


def local(
    n_dp, n_tensor, frames, resets, first_gain, first_shift, qkv_weight, out_weight, out_bias, second_gain,
    second_shift, up_weight, up_bias, down_weight, down_bias, prior_gain, prior_shift, prior_weight,
    prior_bias, out_cotangent, logit_cotangent,
):
    move = Moves(n_dp, n_tensor)
    rows, half = frames.shape
    width = 2 * half
    mine = rows // 2
    blocks = mine // BLOCK
    hidden_width, n_logits = up_bias.shape[0], prior_bias.shape[0]
    row = lambda v: v.reshape(1, -1)
    core, side = move.dp & 1, (move.dp >> 1) & 1
    scalars = jnp.stack([move.here, core * 2 + side, (move.dp >> 2) & 1]).astype(jnp.int32)
    total_rows = blocks * PAD
    quarter = hidden_width // 4

    def near_rows(*entries):
        return [((total_rows, n), dtype, True) for n, dtype in entries]

    def pieces(n):
        return [((4, n, 128), F32, True), ((4, n, 128), BF, True)]

    def columns(value, size, which):
        cut = lambda s, ref: ref.at[..., pl.ds(pl.multiple_of(s[which] * size, 128), size)]
        return Far(value, (*value.shape[:-1], size), cut)

    def some_rows(value, size, which):
        cut = lambda s, ref: ref.at[pl.ds(pl.multiple_of(s[which] * size, 16), size), :]
        return Far(value, (size, value.shape[1]), cut)

    vectors = [first_gain, first_shift, out_bias, second_gain, second_shift, down_bias, prior_gain, prior_shift]
    vectors = [row(v) for v in vectors + [up_bias, prior_bias]]
    qkv_rows = 3 * (width // 4) * (half // 128)
    sent_qkv, sent_frames, sent_one, sent_two, frames_own, small, resets_near = call(
        first_kernel,
        scalars,
        [
            Far(frames),
            Far(
                qkv_weight,
                (3, width // 4, half),
                lambda s, ref: ref.at[:, pl.ds(pl.multiple_of(s[1] * (width // 4), 16), width // 4), :],
            ),
            columns(up_weight, quarter, 1),
            some_rows(out_weight, half // 4, 1),
            some_rows(down_weight, quarter, 1),
            columns(prior_weight, n_logits // 4, 1),
            Far(resets),
            *[Far(v) for v in vectors],
        ],
        [((qkv_rows, 128), BF, True)]
        + near_rows((half, BF))
        + [((width * 2 + half + 48, 128), BF, True), ((quarter * 4 + width, 128), BF, True)]
        + near_rows((half, BF))
        + [((16, hidden_width), F32, True), ((-(-2 * blocks // 8) * 8, -(-BLOCK // 128) * 128), jnp.int32, True)],
        [pltpu.VMEM((rows + 16, half), F32), pltpu.VMEM((16, 128), F32)],
        "first_parts",
        cost=2.0,
    )

    def all_quarters(got):
        beside = move.side(got)
        return [got, beside, move.core(got), move.core(beside)]

    qkv_got = move.over(sent_qkv)
    frames_other = move.over(sent_frames)
    qkv_pieces = all_quarters(qkv_got)
    cot_sent, logit_own, out_own, qkv_near, out_near, up_near, down_near, prior_near = call(
        cotangents_kernel,
        scalars,
        [Far(logit_cotangent), Far(out_cotangent)],
        near_rows((n_logits + half, BF), (n_logits, BF), (half, BF)),
        [pltpu.VMEM((rows + 16, n_logits), F32)]
        + [pltpu.VMEM((total_rows, n), BF) for n in (n_logits, half)],
        name="cotangents",
        after=(sent_frames,),
        cost=2.3,
        loads=(qkv_weight, out_weight, up_weight, down_weight, prior_weight),
    )
    (sent_one,) = gate([sent_one], [frames_other, cot_sent], "after_frames")
    got_one = move.over(sent_one)
    (sent_two,) = gate([sent_two], [sent_one, qkv_pieces[1]], "after_one")
    got_two = move.over(sent_two)
    first, triple, mixed, qkv_other = call(
        attend_kernel,
        scalars,
        [frames_own, frames_other, resets_near, small, *qkv_pieces, qkv_near],
        near_rows((width, BF), (3 * width, BF), (width, BF)) + [(qkv_weight.shape, BF, True)],
        name="attend",
        cost=5.5,
    )
    beside_one = move.side(got_one)
    (cot_sent,) = gate([cot_sent], [got_two, beside_one], "after_two")
    (beside_two,) = gate([move.side(got_two)], [mixed], "after_attend")
    packed = [got_one, beside_one, move.core(got_one), move.core(beside_one)]
    packed += [got_two, beside_two, move.core(got_two), move.core(beside_two)]
    cotangents = move.over(cot_sent)
    block_send, block_own, middle, second, act, slope, ending, prior_in, out_other, up_other, down_other = call(
        feed_kernel,
        scalars,
        [frames_own, frames_other, mixed, small, out_near, up_near, down_near, *packed],
        near_rows((half, BF), (half, BF))
        + near_rows((width, F32), (width, BF), (2 * hidden_width, BF), (2 * hidden_width, F32))
        + near_rows((width, F32), (width, BF))
        + [(v.shape, BF, True) for v in (out_weight, up_weight, down_weight)],
        [pltpu.VMEM((1, hidden_width), F32)],
        name="feed",
        cost=7.2,
    )
    grad_ending, ending_grad, vec_three, prior_bias_sum, prior_other, prior_bias_other = call(
        prior_kernel,
        scalars,
        [ending, small, logit_own, out_own, *packed, cotangents, prior_near],
        near_rows((width, F32), (width, BF))
        + [((3, width), F32, True), ((1, 2 * n_logits), F32, True)]
        + [(prior_weight.shape, BF, True), ((1, n_logits), F32, True)],
        name="prior",
        cost=2.5,
    )
    hidden_grad, grad_middle, middle_grad, vec_two, up_bias_sum = call(
        feed_back_kernel,
        scalars,
        [ending_grad, slope, middle, grad_ending, small, down_near, down_other, up_near, up_other],
        near_rows((2 * hidden_width, BF), (width, F32), (width, BF))
        + [((3, width), F32, True), ((1, 2 * hidden_width), F32, True)],
        name="feed_back",
        cost=6.5,
    )
    up_keep, up_send = call(
        up_grads_kernel,
        scalars,
        [second, hidden_grad, mixed, middle_grad, prior_in, logit_own, cotangents],
        pieces(width * hidden_width // 512 + half + width),
        [pltpu.VMEM((width, total_rows), BF), pltpu.VMEM((half, width), F32), pltpu.VMEM((width, n_logits), F32)],
        name="up_grads",
        cost=3.0,
    )
    late_keep, late_send = call(
        late_grads_kernel,
        scalars,
        [act, ending_grad],
        pieces(hidden_width),
        name="late_grads",
        after=(up_send,),
        cost=3.5,
    )
    *up_low, up_rest = move.reduce_core_all(scalars, up_keep, up_send, "up_core", after=(late_send,))
    def attend_back(half, out, after):
        return call(
            functools.partial(attend_back_kernel, half),
            scalars,
            [middle_grad, triple, out, resets_near],
            near_rows((3 * width // 2, BF)),
            [pltpu.VMEM((total_rows, width // 2), BF)],
            name=f"attend_back_{half}",
            after=after,
            cost=4.5,
        )[0]

    grad_own = attend_back(0, out_near, (up_low[0],))
    *late_low, late_rest = move.reduce_core_all(scalars, late_keep, late_send, "late_core", after=(grad_own,))
    grad_other = attend_back(1, out_other, (late_low[0],))
    keep, send = call(
        early_grads_kernel,
        scalars,
        [first, grad_own, grad_other],
        pieces(768),
        name="early_grads",
        cost=2.0,
    )
    frames_send, frames_grad, vec_one = call(
        frames_back_kernel,
        scalars,
        [grad_own, grad_other, grad_middle, frames_own, frames_other, qkv_other, small, qkv_near],
        near_rows((half, BF), (half, F32)) + [((2, width), F32, True)],
        name="frames_back",
        after=(send,),
        cost=2.5,
    )
    up, up_half = move.halves(scalars, [up_rest, *move.sides(up_low)], "up_1", (vec_one,))
    bits = move.bits()
    spare = 64
    vectors = [vec_one, vec_two, vec_three, up_bias_sum, prior_bias_sum]
    *early_low, early_rest = move.reduce_core_all(scalars, keep, send, "early_core", vectors, spare, (up,))
    done = up = move.total(scalars, [up, move.along(up_half, bits[0])], "up_2", (early_low[0],))
    done = late, late_half = move.halves(scalars, [late_rest, *move.sides(late_low)], "late_1", (done,))
    done = late
    for bit in bits[1:]:
        done = up = move.total(scalars, [up, move.along(up, bit)], "up_3", (done,))
    back_send, logits_own = call(
        logits_kernel,
        scalars,
        [prior_in, small, prior_near, prior_other, prior_bias_other, block_send, frames_send],
        near_rows((n_logits + 2 * half, BF), (n_logits, F32)),
        name="logits",
        after=(done,),
        cost=2.0,
    )
    done = back_send
    done = early = move.total(scalars, [early_rest, *move.sides(early_low)], "early_1", (done,))
    done = late = move.total(scalars, [late, move.along(late_half, bits[0])], "late_2", (done,))
    done = up = move.join(scalars, up, move.along(up, bits[0]), "up_4", (done,))
    for bit in bits[:-1]:
        done = early = move.total(scalars, [early, move.along(early, bit)], "early_2", (done,))
    for bit in bits[1:]:
        done = late = move.total(scalars, [late, move.along(late, bit)], "late_3", (done,))
    done = early = move.total(scalars, [early, move.along(early, bits[-1])], "early_3", (done,))
    late = move.join(scalars, late, move.along(late, bits[0]), "late_4", (done,))
    up_grad, out_grad, prior_grad, up_done = call(
        up_place_kernel,
        scalars,
        list(move.gather(up)),
        [((width, hidden_width), F32, False), ((half, width), F32, False), ((width, n_logits), F32, False)]
        + [((8, 128), F32, True)],
        name="up_place",
        after=(late,),
        cost=FOLD,
    )
    back_got = move.over(back_send)
    (early_near,) = gate([move.side(early)], [up_done], "after_up")
    block_out, logits, grad_frames, rows_done = call(
        functools.partial(
            rows_kernel,
            [slice(n_logits, n_logits + half), slice(0, n_logits), slice(n_logits + half, n_logits + 2 * half)],
        ),
        scalars,
        [block_own, back_got, logits_own, back_got, frames_grad, back_got],
        [((rows, half), BF, False), ((rows, n_logits), F32, False), ((rows, half), F32, False)]
        + [((8, 128), F32, True)],
        [pltpu.VMEM((rows, n), F32) for n in (half, n_logits, half)],
        name="rows_back",
        after=(early_near,),
        cost=FOLD,
    )
    (late_near,) = gate([move.side(late)], [rows_done], "after_rows")
    early_pieces = [early, early_near, move.core(early), move.core(early_near)]
    late_pieces = [late, late_near, move.core(late), move.core(late_near)]
    qkv_grad, *named = call(
        early_place_kernel,
        scalars,
        early_pieces,
        [((3, width, half), F32, False)]
        + [((1, n), F32, False) for n in [width] * 8 + [hidden_width, n_logits]],
        [pltpu.VMEM((spare, 128), F32)],
        name="early_place",
        after=(rows_done,),
        cost=FOLD,
    )
    (down_grad,) = call(
        late_place_kernel,
        scalars,
        late_pieces,
        [((hidden_width, width), F32, False)],
        name="late_place",
        after=(Far(qkv_grad),),
        cost=FOLD,
    )
    named = [v.reshape(-1) for v in named]
    return (
        block_out,
        logits,
        grad_frames,
        named[0],
        named[1],
        qkv_grad,
        out_grad,
        named[4],
        named[2],
        named[3],
        up_grad,
        named[8],
        down_grad,
        named[7],
        named[5],
        named[6],
        prior_grad,
        named[9],
    )


def solution(mesh):
    rows, cols = P("dp", "tensor"), P(None, "tensor")
    placed = (
        rows, P("dp"), P(), P(), P(None, None, "tensor"), P("tensor", None), P(), P(), P(), cols, P("tensor"),
        P("tensor", None), P(), P(), P(), cols, P("tensor"), rows, rows,
    )
    given = (
        rows, rows, rows, P(), P(), P(None, None, "tensor"), P("tensor", None), P(), P(), P(), cols,
        P("tensor"), P("tensor", None), P(), P(), P(), cols, P("tensor"),
    )
    return jax.shard_map(
        functools.partial(local, mesh.shape["dp"], mesh.shape["tensor"]),
        mesh=mesh,
        in_specs=placed,
        out_specs=given,
        check_vma=False,
    )
```

```python
import functools
import math

import jax
import jax.numpy as jnp
from jax import lax
from jax.experimental import pallas as pl
from jax.experimental.pallas import tpu as pltpu
from jax.sharding import PartitionSpec as P

HEAD_DIM = 64
SEQ_LEN = 50
BLOCK = 4 * SEQ_LEN
PAD = -(-BLOCK // 16) * 16
EPS = 1e-05
NEG = -1e30
GELU_C = 0.7978845608028654
GELU_A = 0.044715
SPILL = 8 * 1024 * 1024
GROUP, GROUP_BACK = 4, 6
COST = 1e8
FOLD = 100.0
BF = jnp.bfloat16
F32 = jnp.float32
FIRST_GAIN, FIRST_SHIFT, OUT_BIAS, SECOND_GAIN, SECOND_SHIFT, DOWN_BIAS, PRIOR_GAIN, PRIOR_SHIFT, UP_BIAS, PRIOR_BIAS = range(10)


def mm(a, b):
    return lax.dot_general(a, b, (((1,), (0,)), ((), ())), preferred_element_type=F32)


def mm_bt(a, b):
    return lax.dot_general(a, b, (((1,), (1,)), ((), ())), preferred_element_type=F32)


def mm_at(a, b):
    return lax.dot_general(a, b, (((0,), (0,)), ((), ())), preferred_element_type=F32)


def norm_of(value):
    centre = value - jnp.mean(value, axis=-1, keepdims=True)
    factor = lax.rsqrt(jnp.mean(centre * centre, axis=-1, keepdims=True) + EPS)
    return centre * factor, factor


def norm_back(grad, unit, factor, gain):
    scaled = grad * gain
    first = jnp.mean(scaled, axis=-1, keepdims=True)
    second = jnp.mean(scaled * unit, axis=-1, keepdims=True)
    return factor * (scaled - first - unit * second)


def col_sum(value):
    return jnp.sum(value, axis=0, keepdims=True)


def whole_rows(here, own, other):
    low = jnp.where(here == 0, own[...], other[...])
    high = jnp.where(here == 0, other[...], own[...])
    return jnp.concatenate([low, high], axis=1).astype(F32)


def allowed_pairs(resets):
    place = lax.broadcasted_iota(jnp.int32, (1, PAD), 1)
    starts = jnp.where((resets == 1) | (lax.rem(place, SEQ_LEN) == 0) | (place >= BLOCK), place, 0)
    row = lax.broadcasted_iota(jnp.int32, (PAD, PAD), 0)
    col = lax.broadcasted_iota(jnp.int32, (PAD, PAD), 1)
    seg = jnp.max(jnp.where(col <= row, starts, 0).astype(F32), axis=-1, keepdims=True).astype(jnp.int32)
    seg2 = jnp.concatenate([seg, seg], axis=0)
    row = lax.broadcasted_iota(jnp.int32, (2 * PAD, PAD), 0)
    row = jnp.where(row >= PAD, row - PAD, row)
    col = lax.broadcasted_iota(jnp.int32, (2 * PAD, PAD), 1)
    return (col <= row) & (col >= seg2)


def two_heads(value):
    first = lax.broadcasted_iota(jnp.int32, value.shape, 1) < HEAD_DIM
    none = jnp.zeros_like(value)
    return jnp.concatenate([jnp.where(first, value, none), jnp.where(first, none, value)], axis=0)


def one_pair(value):
    first = lax.broadcasted_iota(jnp.int32, (PAD, 2 * HEAD_DIM), 1) < HEAD_DIM
    return jnp.where(first, value[:PAD], value[PAD:])


def softmax_of(scores, allowed):
    scores = jnp.where(allowed, scores, NEG)
    expo = jnp.exp(scores - jnp.max(scores, axis=-1, keepdims=True))
    return expo * (1.0 / jnp.sum(expo, axis=-1, keepdims=True))


def vector(small, index, n):
    return small[index : index + 1, :n]


def blocks_in(ref):
    return [slice(i * PAD, i * PAD + PAD) for i in range(ref.shape[0] // PAD)]


def add_up(sums, values):
    return [v if s is None else s + v for s, v in zip(sums, values, strict=True)]


def split_rows(half, source, own, sent, wide_rows):
    rows, n = source.shape
    wide_rows[0:rows, 0:n] = source[...].astype(F32)
    for which, target in ((half, own), (1 - half, sent)):
        for block, at in enumerate(blocks_in(target)):
            start = pl.multiple_of(which * (rows // 2) + block * BLOCK, 8)
            part = wide_rows[pl.ds(start, PAD), 0:n]
            inside = lax.broadcasted_iota(jnp.int32, part.shape, 0) < BLOCK
            target[at, :] = jnp.where(inside, part, 0.0).astype(BF)


def tiles_of(ref, start, n, count):
    return jnp.concatenate([ref[start + t * n : start + t * n + n, :] for t in range(count)], axis=1)


class Packed:
    def __init__(self, refs, n, q, o):
        self.one, self.two = refs
        self.n, self.q, self.o = n, q, o

    def up(self):
        return tiles_of(self.one, 0, self.n, 2)

    def out(self):
        return tiles_of(self.one, 2 * self.n, self.o, 4)

    def bias(self):
        start = 2 * self.n + 4 * self.o
        parts = [self.one[start + 16 * k : start + 16 * k + 16, :].astype(F32) for k in range(3)]
        return (parts[2] + parts[1] + parts[0])[:3]

    def down(self):
        return tiles_of(self.two, 0, self.q, 4)

    def prior(self):
        return self.two[4 * self.q : 4 * self.q + self.n, :]


def put_tiles(target, start, part):
    for t in range(part.shape[-1] // 128):
        target[start : start + part.shape[0], :] = part[:, t * 128 : t * 128 + 128]
        start += part.shape[0]
    return start


def first_kernel(s, frames, qkv, up, out, down, prior, resets, *refs):
    smalls, refs = refs[:-9], refs[-9:]
    qkv_ref, sent_ref, one_ref, two_ref, own_ref, small_ref, resets_ref, wide_rows, rows = refs
    start = 0
    for c in range(3):
        start = put_tiles(qkv_ref, start, qkv.get().at[c])
    split_rows(s[0], frames, own_ref, sent_ref, wide_rows)
    resets_ref[...] = jnp.zeros_like(resets_ref)
    line = resets[...].reshape(1, -1)
    for block in range(line.shape[1] // BLOCK):
        resets_ref[block : block + 1, :BLOCK] = line[:, block * BLOCK : block * BLOCK + BLOCK]
    start = put_tiles(one_ref, put_tiles(one_ref, 0, up), out)
    for i, ref in enumerate(smalls):
        small_ref[i : i + 1, : ref.shape[1]] = ref[...]
    rows[...] = jnp.zeros_like(rows)
    for t in range(2):
        rows[t : t + 1, :] = smalls[UP_BIAS][:, pl.ds(pl.multiple_of(s[1] * 256 + t * 128, 128), 128)]
    rows[2:3, :] = smalls[PRIOR_BIAS][:, pl.ds(pl.multiple_of(s[1] * 128, 128), 128)]
    left = rows[...]
    for k in range(3):
        term = left.astype(BF)
        one_ref[start : start + 16, :] = term
        left = left - term.astype(F32)
        start += 16
    put_tiles(two_ref, put_tiles(two_ref, 0, down), prior)


def cotangents_kernel(s, logit, out, sent, logit_own, out_own, wide_rows, logit_sent, out_sent):
    split_rows(s[0], logit, logit_own, logit_sent, wide_rows)
    split_rows(s[0], out, out_own, out_sent, wide_rows)
    n = logit_sent.shape[1]
    sent[:, :n] = logit_sent[...]
    sent[:, n:] = out_sent[...]


def gate(values, after, name=None):
    count, total = len(values), len(values) + len(after)

    def run(*refs):
        for source, target in zip(refs[:count], refs[total:], strict=True):
            target[...] = source[...]

    near = pl.BlockSpec(memory_space=pltpu.VMEM)
    return pl.pallas_call(
        run,
        in_specs=[near] * total,
        out_specs=[near] * count,
        out_shape=[pltpu.VMEM(v.shape, v.dtype) for v in values],
        compiler_params=pltpu.CompilerParams(vmem_limit_bytes=SPILL),
        cost_estimate=pl.CostEstimate(flops=0, bytes_accessed=0, transcendentals=0),
        name=name,
    )(*[pin(v) for v in values], *[pin(v) for v in after])


def attend_kernel(
    s, own, other, resets, small, q0, q1, q2, q3, qkv,
    first_ref, triple_ref, mixed_ref, qkv_other_ref,
):
    unit, _ = norm_of(whole_rows(s[0], own, other))
    n = first_ref.shape[1]
    first_ref[...] = (unit * vector(small, FIRST_GAIN, n) + vector(small, FIRST_SHIFT, n)).astype(BF)
    for j, piece in enumerate((q0, q1, q2, q3)):
        size = qkv.shape[1] // 4
        rows = pl.ds(pl.multiple_of((s[1] ^ j) * size, 16), size)
        for c in range(3):
            qkv_other_ref[c, rows, :] = tiles_of(piece, c * 2 * size, size, 2)
    for half, weight in enumerate((qkv, qkv_other_ref)):
        for c in range(3):
            value = mm(first_ref[...], weight[c]).astype(BF)
            triple_ref[:, (half * 3 + c) * 256 : (half * 3 + c + 1) * 256] = value
    units = []
    for block, at in enumerate(blocks_in(own)):
        allowed = allowed_pairs(resets[pl.ds(s[0] * len(blocks_in(own)) + block, 1), :PAD])
        units += [(at, allowed, pair, (pair // 2) * 768 + (pair % 2) * 128) for pair in range(4)]
    for group in range(0, len(units), GROUP):
        some = units[group : group + GROUP]
        scores = [
            mm_bt(two_heads(triple_ref[at, start : start + 128] * HEAD_DIM ** (-0.5)), triple_ref[at, start + 256 : start + 384])
            for at, _, _, start in some
        ]
        weights = [softmax_of(score, allowed).astype(BF) for score, (_, allowed, _, _) in zip(scores, some, strict=True)]
        for weight, (at, _, pair, start) in zip(weights, some, strict=True):
            mixed = one_pair(mm(weight, triple_ref[at, start + 512 : start + 640])).astype(BF)
            mixed_ref[at, pair * 128 : pair * 128 + 128] = mixed


def feed_kernel(
    s, own, other, mixed, small, out, up, down, a0, a1, a2, a3, b0, b1, b2, b3,
    block_other_ref, block_own_ref, middle_ref, second_ref, act_ref, slope_ref, ending_ref, prior_in_ref,
    out_other_ref, up_other_ref, down_other_ref, bias_other,
):
    n, half, wide = out.shape[0], up.shape[1], up.shape[0]
    for j, piece in enumerate(zip((a0, a1, a2, a3), (b0, b1, b2, b3))):
        piece = Packed(piece, wide, half // 4, n // 4)
        place = s[1] ^ j
        out_other_ref[pl.ds(pl.multiple_of(place * (n // 4), 16), n // 4), :] = piece.out()
        at = pl.ds(pl.multiple_of(place * 256, 256), 256)
        up_other_ref[:, at] = piece.up()
        down_other_ref[at, :] = piece.down()
        bias = piece.bias()
        bias_other[:, at] = jnp.concatenate([bias[0:1], bias[1:2]], axis=1)
    middle_ref[...] = (
        whole_rows(s[0], own, other)
        + vector(small, OUT_BIAS, wide)
        + mm(mixed[:, :n], out[...])
        + mm(mixed[:, n:], out_other_ref[...])
    )
    unit, _ = norm_of(middle_ref[...])
    second_ref[...] = (unit * vector(small, SECOND_GAIN, wide) + vector(small, SECOND_SHIFT, wide)).astype(BF)
    total = middle_ref[...] + vector(small, DOWN_BIAS, wide)
    for h, (w_up, w_down) in enumerate(((up, down), (up_other_ref, down_other_ref))):
        for i in range(half // 256):
            at = slice(i * 256, i * 256 + 256)
            to = slice(h * half + i * 256, h * half + i * 256 + 256)
            bias = bias_other[:, at] if h else small[UP_BIAS : UP_BIAS + 1, at]
            for rows in blocks_in(own):
                hidden = mm(second_ref[rows, :], w_up[:, at]) + bias
                square = hidden * hidden
                bent = jnp.tanh(GELU_C * (hidden + GELU_A * hidden * square))
                act_ref[rows, to] = (0.5 * hidden * (1.0 + bent)).astype(BF)
                slope_ref[rows, to] = 0.5 * (1.0 + bent) + (0.5 * GELU_C) * hidden * (1.0 - bent * bent) * (
                    1.0 + (3.0 * GELU_A) * square
                )
        total = total + mm(act_ref[:, h * half : h * half + half], w_down[...])
    ending_ref[...] = total
    unit, _ = norm_of(total)
    prior_in_ref[...] = (unit * vector(small, PRIOR_GAIN, wide) + vector(small, PRIOR_SHIFT, wide)).astype(BF)
    low, high = total[:, :256].astype(BF), total[:, 256:].astype(BF)
    block_own_ref[...] = jnp.where(s[0] == 0, low, high)
    block_other_ref[...] = jnp.where(s[0] == 0, high, low)


def prior_kernel(
    s, ending, small, logit_own, out_own, a0, a1, a2, a3, b0, b1, b2, b3, cotangents, prior,
    grad_ending_ref, ending_grad_ref, vec_ref, bias_ref, weight, bias,
):
    half, n = prior.shape[1], prior.shape[0]
    for j, piece in enumerate(zip((a0, a1, a2, a3), (b0, b1, b2, b3))):
        at = pl.ds(pl.multiple_of((s[1] ^ j) * 128, 128), 128)
        piece = Packed(piece, n, n // 2, n // 8)
        weight[:, at] = piece.prior()
        bias[:, at] = piece.bias()[2:3]
    logit_other = cotangents.at[:, :half]
    back = mm_bt(logit_own[...], prior[...]) + mm_bt(logit_other[...], weight[...])
    unit, factor = norm_of(ending[...])
    gain = vector(small, PRIOR_GAIN, unit.shape[1])
    grad = whole_rows(s[0], out_own, cotangents.at[:, half:]) + norm_back(back, unit, factor, gain)
    grad_ending_ref[...] = grad
    ending_grad_ref[...] = grad.astype(BF)
    vec_ref[...] = jnp.concatenate([col_sum(back * unit), col_sum(back), col_sum(grad)], axis=0)
    bias_ref[:, :half] = col_sum(logit_own[...].astype(F32))
    bias_ref[:, half:] = col_sum(logit_other[...].astype(F32))


def logits_kernel(s, prior_in, small, prior, weight, bias, block_other, frames_other, sent_ref, logits_ref):
    half, n = prior.shape[1], block_other.shape[1]
    sent_ref[:, :half] = (mm(prior_in[...], weight[...]) + bias[...]).astype(BF)
    sent_ref[:, half : half + n] = block_other[...]
    sent_ref[:, half + n :] = frames_other[...]
    logits_ref[...] = mm(prior_in[...], prior[...]) + vector(small, PRIOR_BIAS, half)


def store_piece(keep, send, h, j, start, value):
    at = slice(start, start + value.shape[0])
    if j < 2:
        keep[h * 2 + j, at, :] = value
    else:
        send[h * 2 + j - 2, at, :] = value.astype(BF)


def late_grads_kernel(s, act, ending_grad, keep, send):
    half = act.shape[1] // 2
    for h in range(2):
        for j in (2, 3, 0, 1):
            part = act[:, pl.ds(pl.multiple_of(h * half + (s[1] ^ j) * 256, 256), 256)]
            value = mm_at(part, ending_grad[...])
            for t in range(value.shape[1] // 128):
                store_piece(keep, send, h, j, t * 256, value[:, t * 128 : t * 128 + 128])


def up_grads_kernel(
    s, second, hidden_grad, mixed, middle_grad, prior_in, logit_own, cotangents, keep, send, turned, wide, tall,
):
    turned[...] = second[...].T
    half = hidden_grad.shape[1] // 2
    n, m = second.shape[1], mixed.shape[1] // 2
    logit_other = cotangents.at[:, : logit_own.shape[1]]
    for h in range(2):
        wide[...] = mm_at(mixed[:, h * m : h * m + m], middle_grad[...])
        tall[...] = mm_at(prior_in[...], (logit_own, logit_other)[h][...])
        for j in (2, 3, 0, 1):
            place = s[1] ^ j
            at = pl.ds(pl.multiple_of(place * 128, 128), 128)
            value = mm(turned[...], hidden_grad[:, pl.ds(pl.multiple_of(h * half + place * 256, 256), 256)])
            for t in range(2):
                store_piece(keep, send, h, j, t * n, value[:, t * 128 : t * 128 + 128])
            store_piece(keep, send, h, j, 2 * n, wide[:, at])
            store_piece(keep, send, h, j, 2 * n + m, tall[:, at])


def early_grads_kernel(s, first, grad_own, grad_other, keep, send):
    for h in range(2):
        for j in (2, 3, 0, 1):
            place = pl.multiple_of((s[1] ^ j) * 128, 128)
            value = mm_at(first[:, pl.ds(place, 128)], (grad_own, grad_other)[h][...])
            for c in range(3):
                for t in range(2):
                    at = slice(c * 256 + t * 128, c * 256 + t * 128 + 128)
                    store_piece(keep, send, h, j, (t * 3 + c) * 128, value[:, at])


def feed_back_kernel(
    s, ending_grad, slope, middle, grad_ending, small, down, down_other, up, up_other,
    hidden_grad_ref, grad_middle_ref, middle_grad_ref, vec_ref, bias_ref,
):
    half = up.shape[1]
    back, steps = None, half // 256
    tasks = [(h, i) for h in range(2) for i in range(steps)]

    def product(h, i):
        return mm_bt(ending_grad[...], (down, down_other)[h][i * 256 : i * 256 + 256, :])

    ahead = product(*tasks[0])
    for k, (h, i) in enumerate(tasks):
        value, ahead = ahead, product(*tasks[k + 1]) if k + 1 < len(tasks) else None
        to = slice(h * half + i * 256, h * half + i * 256 + 256)
        low = (value * slope[:, to]).astype(BF)
        hidden_grad_ref[:, to] = low
        bias_ref[:, to] = col_sum(low.astype(F32))
        if i + 1 == steps:
            part = mm_bt(hidden_grad_ref[:, h * half : h * half + half], (up, up_other)[h][...])
            back = part if back is None else back + part
    unit, factor = norm_of(middle[...])
    gain = vector(small, SECOND_GAIN, unit.shape[1])
    total = grad_ending[...] + norm_back(back, unit, factor, gain)
    grad_middle_ref[...] = total
    middle_grad_ref[...] = total.astype(BF)
    vec_ref[...] = jnp.concatenate([col_sum(back * unit), col_sum(back), col_sum(total)], axis=0)


def attend_back_kernel(
    half, s, middle_grad, triple, out, resets,
    triple_grad_ref, mixed_grad,
):
    mixed_grad[...] = mm_bt(middle_grad[...], out[...]).astype(BF)
    factor = HEAD_DIM ** (-0.5)
    units = []
    for block, at in enumerate(blocks_in(triple)):
        allowed = allowed_pairs(resets[pl.ds(s[0] * len(blocks_in(triple)) + block, 1), :PAD])
        units += [(at, allowed, pair) for pair in range(2)]
    for group in range(0, len(units), GROUP_BACK):
        some = units[group : group + GROUP_BACK]
        loaded = []
        for at, _, pair in some:
            start = half * 768 + pair * 128
            query, key, value = (triple[at, start + c * 256 : start + c * 256 + 128] for c in range(3))
            mixed2 = two_heads(mixed_grad[at, pair * 128 : pair * 128 + 128])
            loaded.append((two_heads(query * factor), key, value, mixed2))
        scores = [mm_bt(query2, key) for query2, key, _, _ in loaded]
        weight_grads = [mm_bt(mixed2, value) for _, _, value, mixed2 in loaded]
        inner = []
        for score, weight_grad, (_, allowed, _) in zip(scores, weight_grads, some, strict=True):
            again = softmax_of(score, allowed)
            both = again * weight_grad
            total = jnp.sum(both, axis=-1, keepdims=True)
            inner.append((again.astype(BF), (both - again * total).astype(BF)))
        for (again, score_grad), (query2, key, _, mixed2), (at, _, pair) in zip(inner, loaded, some, strict=True):
            thirds = (
                (one_pair(mm(score_grad, key)) * factor).astype(BF),
                mm_at(score_grad, query2).astype(BF),
                mm_at(again, mixed2).astype(BF),
            )
            for c in range(3):
                triple_grad_ref[at, c * 256 + pair * 128 : c * 256 + pair * 128 + 128] = thirds[c]


def frames_back_kernel(
    s, grad_own, grad_other, grad_middle, own, other, qkv_other, small, qkv,
    sent_ref, frames_own_ref, vec_ref,
):
    back = None
    for part, weight in ((grad_own, qkv), (grad_other, qkv_other)):
        for c in range(3):
            value = mm_bt(part[:, c * 256 : c * 256 + 256], weight[c])
            back = value if back is None else back + value
    unit, scale = norm_of(whole_rows(s[0], own, other))
    total = grad_middle[...] + norm_back(back, unit, scale, vector(small, FIRST_GAIN, unit.shape[1]))
    low, high = total[:, :256], total[:, 256:]
    frames_own_ref[...] = jnp.where(s[0] == 0, low, high)
    sent_ref[...] = jnp.where(s[0] == 0, high, low).astype(BF)
    vec_ref[...] = jnp.concatenate([col_sum(back * unit), col_sum(back)], axis=0)


def late_place_kernel(s, mine, near, far, farther, down_ref):
    q = down_ref.shape[0] // 4
    for j, piece in enumerate((mine, near, far, farther)):
        rows = pl.ds(pl.multiple_of((s[1] ^ j) * q, 8), q)
        for t in range(down_ref.shape[1] // 128):
            down_ref[rows, t * 128 : t * 128 + 128] = piece[t * q : t * q + q, :].astype(F32)


def up_place_kernel(s, mine, near, far, farther, up_ref, out_ref, prior_ref, token):
    token[...] = jnp.zeros_like(token)
    n, m = up_ref.shape[0], out_ref.shape[0]
    for j, piece in enumerate((mine, near, far, farther)):
        place = s[1] ^ j
        for t in range(2):
            columns = pl.ds(pl.multiple_of(place * 256 + t * 128, 128), 128)
            up_ref[:, columns] = piece[t * n : t * n + n, :].astype(F32)
        at = pl.ds(pl.multiple_of(place * 128, 128), 128)
        out_ref[:, at] = piece[2 * n : 2 * n + m, :].astype(F32)
        prior_ref[:, at] = piece[2 * n + m :, :].astype(F32)


def last_place_kernel(s, mine, near, far, farther, l0, l1, l2, l3, qkv_ref, down_ref, *vecs):
    vecs, sums = vecs[:-1], vecs[-1]
    late_place_kernel(s, l0, l1, l2, l3, down_ref)
    down_ref.send()
    sums[...] = mine[6 * 128 :, :].astype(F32) + far[6 * 128 :, :].astype(F32)
    for j, piece in enumerate((mine, near, far, farther)):
        at = pl.ds(pl.multiple_of((s[1] ^ j) * 128, 128), 128)
        for c in range(3):
            for t in range(2):
                start = (t * 3 + c) * 128
                qkv_ref[c, at, t * 128 : t * 128 + 128] = piece[start : start + 128, :].astype(F32)
    qkv_ref.send()
    row = 0
    for ref in vecs[:8]:
        for t in range(ref.shape[1] // 128):
            ref[:, t * 128 : t * 128 + 128] = sums[row : row + 1, :]
            row += 1
    for ref in vecs[8:]:
        tiles = ref.shape[1] // 128
        for t in range(tiles):
            ref[:, t * 128 : t * 128 + 128] = sums[pl.ds(row + s[0] * tiles + t, 1), :]
        row += 2 * tiles


def core_kernel(s, keep, got, low, rest):
    n = keep.shape[1]
    for out, places, dtype in ((low, (2, 3), BF), (rest, (0, 1), F32)):
        for k, i in enumerate(places):
            out[k * n : k * n + n, :] = (keep[i] + got[i].astype(F32)).astype(dtype)


def core_all_kernel(s, keep, got, *refs):
    vectors, lows, rest = refs[:-4], refs[-4:-1], refs[-1]
    n = keep.shape[1]
    for i in (1, 2, 3):
        lows[i - 1][:n, :] = (keep[i] + got[i].astype(F32)).astype(BF)
    rest[:n, :] = keep[0] + got[0].astype(F32)
    if vectors:
        put_vectors(s, vectors, rest, n)
        for low in lows:
            low[n:, :] = rest[n:, :].astype(BF)


def put_vectors(s, vectors, rest, row):
    for ref in vectors[:3]:
        for i in range(ref.shape[0]):
            for t in range(ref.shape[1] // 128):
                rest[row : row + 1, :] = ref[i : i + 1, t * 128 : t * 128 + 128]
                row += 1
    for ref in vectors[3:]:
        tiles = ref.shape[1] // 128
        for t in range(tiles):
            place = row + lax.rem(t + s[0] * (tiles // 2), tiles)
            rest[pl.ds(place, 1), :] = ref[:, t * 128 : t * 128 + 128]
        row += tiles
    rest[row:, :] = jnp.zeros((rest.shape[0] - row, 128), F32)


def over_kernel(s, rest, got, low, mine):
    n = low.shape[0]
    low[...] = (rest[n:, :] + got[n:, :].astype(F32)).astype(BF)
    mine[...] = rest[:n, :] + got[:n, :].astype(F32)


def halves_kernel(s, *refs):
    total, (keep, send) = refs[-1], refs[-3:-1]
    total[...] = functools.reduce(lambda x, y: x + y, [r[...].astype(F32) for r in refs[:-3]])
    n = keep.shape[0]
    send[...] = total[pl.ds(pl.multiple_of((1 - s[2]) * n, 16), n), :].astype(BF)
    keep[...] = total[pl.ds(pl.multiple_of(s[2] * n, 16), n), :].astype(BF)


def join_kernel(s, mine, got, out):
    n = mine.shape[0]
    out[pl.ds(pl.multiple_of(s[2] * n, 16), n), :] = mine[...]
    out[pl.ds(pl.multiple_of((1 - s[2]) * n, 16), n), :] = got[...]


def total_kernel(s, *refs):
    refs[-1][...] = functools.reduce(lambda x, y: x + y, [r[...].astype(F32) for r in refs[:-1]]).astype(BF)


def rows_kernel(entries, s, *refs):
    count = len(entries)
    given, outs, token, rooms = refs[: 2 * count], refs[2 * count : 3 * count], refs[3 * count], refs[3 * count + 1 :]
    token[...] = jnp.zeros_like(token)
    for i, columns in enumerate(entries):
        own, got, out, room = given[2 * i], given[2 * i + 1], outs[i], rooms[i]
        rows = out.shape[0] // 2
        for block, at in enumerate(blocks_in(own)):
            for which, ref, cut in ((s[0], own, slice(None)), (1 - s[0], got, columns)):
                start = pl.multiple_of(which * rows + block * BLOCK, 8)
                room[pl.ds(start, BLOCK), :] = ref[at, cut].astype(F32)[:BLOCK]
        out[...] = room[...].astype(out.ref.dtype)
        out.send()


class Loaded:
    def __init__(self, ref, copy):
        self.ref, self.copy, self.shape = ref, copy, ref.shape

    def get(self):
        if self.copy is not None:
            self.copy.wait()
            self.copy = None
        return self.ref

    def __getitem__(self, index):
        return self.get()[index]


class Leaving:
    def __init__(self, ref, copy):
        self.ref, self.copy, self.shape, self.sent = ref, copy, ref.shape, False

    def __getitem__(self, index):
        return self.ref[index]

    def __setitem__(self, index, value):
        self.ref[index] = value

    def send(self):
        if not self.sent:
            self.copy.start()
            self.sent = True


class Far:
    def __init__(self, value, shape=None, cut=None):
        self.value, self.shape, self.cut = value, shape or value.shape, cut or (lambda s, ref: ref)


def call(kernel, scalars, ins, outs, scratch=(), name=None, after=(), cost=1.0, loads=()):
    n_own, n_loads = len(ins), len(loads)
    ins, outs = [*ins, *[Far(v) for v in loads]], [*outs, *[(v.shape, v.dtype, True) for v in loads]]
    n_in, n_out, n_after = len(ins), len(outs), len(after)
    far_in = [i for i, v in enumerate(ins[:n_own]) if isinstance(v, Far)]
    far_out = [i for i, o in enumerate(outs) if not o[2]]
    room = [pltpu.VMEM(ins[i].shape, ins[i].value.dtype) for i in far_in]
    room += [pltpu.VMEM(outs[i][0], outs[i][1]) for i in far_out]
    need = sum(math.prod(r.shape) * jnp.dtype(r.dtype).itemsize for r in room + list(scratch))

    def run(s, *refs):
        given, refs = list(refs[:n_in]), refs[n_in + n_after :]
        made, refs = list(refs[:n_out]), refs[n_out:]
        own, refs = refs[: len(scratch)], refs[len(scratch) :]
        rooms, sems = refs[:-1], refs[-1]
        for k, i in enumerate(far_in):
            copy = pltpu.make_async_copy(ins[i].cut(s, given[i]), rooms[k], sems.at[k])
            copy.start()
            given[i] = Loaded(rooms[k], copy)
        bringing = []
        for k in range(n_loads):
            copy = pltpu.make_async_copy(given[n_own + k], made[n_out - n_loads + k], sems.at[len(rooms) + k])
            copy.start()
            bringing.append(copy)
        leaving = []
        for k, i in enumerate(far_out, len(far_in)):
            made[i] = Leaving(rooms[k], pltpu.make_async_copy(rooms[k], made[i], sems.at[k]))
            leaving.append(made[i])
        kernel(s, *given[:n_own], *made[: n_out - n_loads], *own)
        for copy in bringing:
            copy.wait()
        for value in given:
            if isinstance(value, Loaded):
                value.get()
        for value in leaving:
            value.send()
        for value in leaving:
            value.copy.wait()

    near, far = pl.BlockSpec(memory_space=pltpu.VMEM), pl.BlockSpec(memory_space=pltpu.HBM)
    return pl.pallas_call(
        run,
        in_specs=[pl.BlockSpec(memory_space=pltpu.SMEM)]
        + [far if isinstance(v, Far) else near for v in ins]
        + [far if isinstance(v, Far) else near for v in after],
        out_specs=[near if stays else far for _, _, stays in outs],
        out_shape=[(pltpu.VMEM if stays else pltpu.HBM)(shape, dtype) for shape, dtype, stays in outs],
        scratch_shapes=list(scratch) + room + [pltpu.SemaphoreType.DMA((max(1, len(room) + n_loads),))],
        compiler_params=pltpu.CompilerParams(vmem_limit_bytes=need + SPILL),
        cost_estimate=pl.CostEstimate(flops=int(cost * COST), bytes_accessed=0, transcendentals=0),
        name=name,
    )(scalars, *[pin(v) for v in ins], *[pin(v) for v in after])


def pin(value):
    if isinstance(value, Far):
        return pltpu.with_memory_space_constraint(value.value, pltpu.HBM)
    return pltpu.with_memory_space_constraint(value, pltpu.VMEM)


def swap(value, axes, sizes, mask):
    count = 1
    for size in sizes:
        count *= size
    return lax.ppermute(value, axes, [(i, i ^ mask) for i in range(count)])


class Moves:
    def __init__(self, n_dp, n_tensor):
        self.n_dp, self.n_tensor = n_dp, n_tensor
        self.dp = lax.axis_index("dp")
        self.here = lax.axis_index("tensor")

    def along(self, value, mask):
        return swap(value, "dp", (self.n_dp,), mask)

    def core(self, value):
        return self.along(value, 1)

    def side(self, value):
        return self.along(value, 2)

    def over(self, value):
        return swap(value, "tensor", (self.n_tensor,), 1)

    def cross(self, value):
        return swap(value, ("dp", "tensor"), (self.n_dp, self.n_tensor), 5)


    def reduce_core(self, scalars, keep, sent, name, after=()):
        n = 2 * sent.shape[1]
        outs = [((n, 128), BF, True), ((n, 128), F32, True)]
        return call(core_kernel, scalars, [keep, self.core(sent)], outs, name=name, after=after, cost=FOLD)

    def reduce_over(self, scalars, low, rest, name, after=()):
        n = low.shape[0] // 2
        outs = [((n, 128), BF, True), ((n, 128), F32, True)]
        return call(over_kernel, scalars, [rest, self.over(low)], outs, name=name, after=after, cost=FOLD)

    def reduce_core_all(self, scalars, keep, sent, name, vectors=(), spare=0, after=()):
        n = sent.shape[1] + spare
        outs = [((n, 128), BF, True)] * 3 + [((n, 128), F32, True)]
        ins = [keep, self.core(sent), *vectors]
        return call(core_all_kernel, scalars, ins, outs, name=name, after=after, cost=FOLD)

    def sides(self, lows):
        return [self.side(lows[0]), self.over(lows[1]), self.cross(lows[2])]

    def total(self, scalars, values, name, after=()):
        shape = values[0].shape
        return call(total_kernel, scalars, values, [(shape, BF, True)], name=name, after=after, cost=FOLD)[0]

    def halves(self, scalars, values, name, after=()):
        n = values[0].shape[0]
        return call(
            halves_kernel,
            scalars,
            values,
            [((n // 2, 128), BF, True)] * 2,
            [pltpu.VMEM((n, 128), F32)],
            name=name,
            after=after,
            cost=FOLD,
        )

    def join(self, scalars, mine, got, name, after=()):
        shape = (mine.shape[0] * 2, 128)
        return call(join_kernel, scalars, [mine, got], [(shape, BF, True)], name=name, after=after, cost=FOLD)[0]

    def bits(self):
        return [1 << i for i in range(2, self.n_dp.bit_length() - 1)]

    def gather(self, total):
        near = self.side(total)
        return total, near, self.core(total), self.core(near)


def local(
    n_dp, n_tensor, frames, resets, first_gain, first_shift, qkv_weight, out_weight, out_bias, second_gain,
    second_shift, up_weight, up_bias, down_weight, down_bias, prior_gain, prior_shift, prior_weight,
    prior_bias, out_cotangent, logit_cotangent,
):
    move = Moves(n_dp, n_tensor)
    rows, half = frames.shape
    width = 2 * half
    mine = rows // 2
    blocks = mine // BLOCK
    hidden_width, n_logits = up_bias.shape[0], prior_bias.shape[0]
    row = lambda v: v.reshape(1, -1)
    core, side = move.dp & 1, (move.dp >> 1) & 1
    scalars = jnp.stack([move.here, core * 2 + side, (move.dp >> 2) & 1]).astype(jnp.int32)
    total_rows = blocks * PAD
    quarter = hidden_width // 4

    def near_rows(*entries):
        return [((total_rows, n), dtype, True) for n, dtype in entries]

    def pieces(n):
        return [((4, n, 128), F32, True), ((4, n, 128), BF, True)]

    def columns(value, size, which):
        cut = lambda s, ref: ref.at[..., pl.ds(pl.multiple_of(s[which] * size, 128), size)]
        return Far(value, (*value.shape[:-1], size), cut)

    def some_rows(value, size, which):
        cut = lambda s, ref: ref.at[pl.ds(pl.multiple_of(s[which] * size, 16), size), :]
        return Far(value, (size, value.shape[1]), cut)

    vectors = [first_gain, first_shift, out_bias, second_gain, second_shift, down_bias, prior_gain, prior_shift]
    vectors = [row(v) for v in vectors + [up_bias, prior_bias]]
    qkv_rows = 3 * (width // 4) * (half // 128)
    sent_qkv, sent_frames, sent_one, sent_two, frames_own, small, resets_near = call(
        first_kernel,
        scalars,
        [
            Far(frames),
            Far(
                qkv_weight,
                (3, width // 4, half),
                lambda s, ref: ref.at[:, pl.ds(pl.multiple_of(s[1] * (width // 4), 16), width // 4), :],
            ),
            columns(up_weight, quarter, 1),
            some_rows(out_weight, half // 4, 1),
            some_rows(down_weight, quarter, 1),
            columns(prior_weight, n_logits // 4, 1),
            Far(resets),
            *[Far(v) for v in vectors],
        ],
        [((qkv_rows, 128), BF, True)]
        + near_rows((half, BF))
        + [((width * 2 + half + 48, 128), BF, True), ((quarter * 4 + width, 128), BF, True)]
        + near_rows((half, BF))
        + [((16, hidden_width), F32, True), ((-(-2 * blocks // 8) * 8, -(-BLOCK // 128) * 128), jnp.int32, True)],
        [pltpu.VMEM((rows + 16, half), F32), pltpu.VMEM((16, 128), F32)],
        "first_parts",
        cost=2.0,
    )

    def all_quarters(got):
        beside = move.side(got)
        return [got, beside, move.core(got), move.core(beside)]

    qkv_got = move.over(sent_qkv)
    frames_other = move.over(sent_frames)
    qkv_pieces = all_quarters(qkv_got)
    cot_sent, logit_own, out_own, qkv_near, out_near, up_near, down_near, prior_near = call(
        cotangents_kernel,
        scalars,
        [Far(logit_cotangent), Far(out_cotangent)],
        near_rows((n_logits + half, BF), (n_logits, BF), (half, BF)),
        [pltpu.VMEM((rows + 16, n_logits), F32)]
        + [pltpu.VMEM((total_rows, n), BF) for n in (n_logits, half)],
        name="cotangents",
        after=(sent_frames,),
        cost=2.3,
        loads=(qkv_weight, out_weight, up_weight, down_weight, prior_weight),
    )
    (sent_one,) = gate([sent_one], [frames_other, cot_sent], "after_frames")
    got_one = move.over(sent_one)
    (sent_two,) = gate([sent_two], [sent_one, qkv_pieces[1]], "after_one")
    got_two = move.over(sent_two)
    first, triple, mixed, qkv_other = call(
        attend_kernel,
        scalars,
        [frames_own, frames_other, resets_near, small, *qkv_pieces, qkv_near],
        near_rows((width, BF), (3 * width, BF), (width, BF)) + [(qkv_weight.shape, BF, True)],
        name="attend",
        cost=5.5,
    )
    beside_one = move.side(got_one)
    (cot_sent,) = gate([cot_sent], [got_two, beside_one], "after_two")
    (beside_two,) = gate([move.side(got_two)], [mixed], "after_attend")
    packed = [got_one, beside_one, move.core(got_one), move.core(beside_one)]
    packed += [got_two, beside_two, move.core(got_two), move.core(beside_two)]
    cotangents = move.over(cot_sent)
    block_send, block_own, middle, second, act, slope, ending, prior_in, out_other, up_other, down_other = call(
        feed_kernel,
        scalars,
        [frames_own, frames_other, mixed, small, out_near, up_near, down_near, *packed],
        near_rows((half, BF), (half, BF))
        + near_rows((width, F32), (width, BF), (2 * hidden_width, BF), (2 * hidden_width, F32))
        + near_rows((width, F32), (width, BF))
        + [(v.shape, BF, True) for v in (out_weight, up_weight, down_weight)],
        [pltpu.VMEM((1, hidden_width), F32)],
        name="feed",
        cost=7.2,
    )
    grad_ending, ending_grad, vec_three, prior_bias_sum, prior_other, prior_bias_other = call(
        prior_kernel,
        scalars,
        [ending, small, logit_own, out_own, *packed, cotangents, prior_near],
        near_rows((width, F32), (width, BF))
        + [((3, width), F32, True), ((1, 2 * n_logits), F32, True)]
        + [(prior_weight.shape, BF, True), ((1, n_logits), F32, True)],
        name="prior",
        cost=2.5,
    )
    hidden_grad, grad_middle, middle_grad, vec_two, up_bias_sum = call(
        feed_back_kernel,
        scalars,
        [ending_grad, slope, middle, grad_ending, small, down_near, down_other, up_near, up_other],
        near_rows((2 * hidden_width, BF), (width, F32), (width, BF))
        + [((3, width), F32, True), ((1, 2 * hidden_width), F32, True)],
        name="feed_back",
        cost=6.5,
    )
    up_keep, up_send = call(
        up_grads_kernel,
        scalars,
        [second, hidden_grad, mixed, middle_grad, prior_in, logit_own, cotangents],
        pieces(width * hidden_width // 512 + half + width),
        [pltpu.VMEM((width, total_rows), BF), pltpu.VMEM((half, width), F32), pltpu.VMEM((width, n_logits), F32)],
        name="up_grads",
        cost=3.0,
    )
    late_keep, late_send = call(
        late_grads_kernel,
        scalars,
        [act, ending_grad],
        pieces(hidden_width),
        name="late_grads",
        after=(up_send,),
        cost=3.5,
    )
    *up_low, up_rest = move.reduce_core_all(scalars, up_keep, up_send, "up_core", after=(late_send,))
    def attend_back(half, out, after):
        return call(
            functools.partial(attend_back_kernel, half),
            scalars,
            [middle_grad, triple, out, resets_near],
            near_rows((3 * width // 2, BF)),
            [pltpu.VMEM((total_rows, width // 2), BF)],
            name=f"attend_back_{half}",
            after=after,
            cost=4.5,
        )[0]

    grad_own = attend_back(0, out_near, (up_low[0],))
    *late_low, late_rest = move.reduce_core_all(scalars, late_keep, late_send, "late_core", after=(grad_own,))
    grad_other = attend_back(1, out_other, (late_low[0],))
    keep, send = call(
        early_grads_kernel,
        scalars,
        [first, grad_own, grad_other],
        pieces(768),
        name="early_grads",
        cost=2.0,
    )
    frames_send, frames_grad, vec_one = call(
        frames_back_kernel,
        scalars,
        [grad_own, grad_other, grad_middle, frames_own, frames_other, qkv_other, small, qkv_near],
        near_rows((half, BF), (half, F32)) + [((2, width), F32, True)],
        name="frames_back",
        after=(send,),
        cost=2.5,
    )
    up, up_half = move.halves(scalars, [up_rest, *move.sides(up_low)], "up_1", (vec_one,))
    bits = move.bits()
    spare = 64
    vectors = [vec_one, vec_two, vec_three, up_bias_sum, prior_bias_sum]
    *early_low, early_rest = move.reduce_core_all(scalars, keep, send, "early_core", vectors, spare, (up,))
    done = up = move.total(scalars, [up, move.along(up_half, bits[0])], "up_2", (early_low[0],))
    done = late, late_half = move.halves(scalars, [late_rest, *move.sides(late_low)], "late_1", (done,))
    done = late
    for bit in bits[1:]:
        done = up = move.total(scalars, [up, move.along(up, bit)], "up_3", (done,))
    back_send, logits_own = call(
        logits_kernel,
        scalars,
        [prior_in, small, prior_near, prior_other, prior_bias_other, block_send, frames_send],
        near_rows((n_logits + 2 * half, BF), (n_logits, F32)),
        name="logits",
        after=(done,),
        cost=2.0,
    )
    done = back_send
    early, early_half = move.halves(scalars, [early_rest, *move.sides(early_low)], "early_1", (done,))
    done = early
    done = late = move.total(scalars, [late, move.along(late_half, bits[0])], "late_2", (done,))
    done = up = move.join(scalars, up, move.along(up, bits[0]), "up_4", (done,))
    done = early = move.total(scalars, [early, move.along(early_half, bits[0])], "early_2", (done,))
    for bit in bits[1:]:
        done = late = move.total(scalars, [late, move.along(late, bit)], "late_3", (done,))
    for bit in bits[1:]:
        done = early = move.total(scalars, [early, move.along(early, bit)], "early_3", (done,))
    up_pieces = list(move.gather(up))
    late = move.join(scalars, late, move.along(late, bits[0]), "late_4", (done, up_pieces[2]))
    early = move.join(scalars, early, move.along(early, bits[0]), "early_4", (late,))
    up_grad, out_grad, prior_grad, up_done = call(
        up_place_kernel,
        scalars,
        up_pieces,
        [((width, hidden_width), F32, False), ((half, width), F32, False), ((width, n_logits), F32, False)]
        + [((8, 128), F32, True)],
        name="up_place",
        after=(early,),
        cost=FOLD,
    )
    back_got = move.over(back_send)
    block_out, logits, grad_frames, rows_done = call(
        functools.partial(
            rows_kernel,
            [slice(n_logits, n_logits + half), slice(0, n_logits), slice(n_logits + half, n_logits + 2 * half)],
        ),
        scalars,
        [block_own, back_got, logits_own, back_got, frames_grad, back_got],
        [((rows, half), BF, False), ((rows, n_logits), F32, False), ((rows, half), F32, False)]
        + [((8, 128), F32, True)],
        [pltpu.VMEM((rows, n), F32) for n in (half, n_logits, half)],
        name="rows_back",
        after=(up_done,),
        cost=FOLD,
    )
    (early_near,) = gate([move.side(early)], [up_done], "after_up")
    (late_near,) = gate([move.side(late)], [rows_done], "after_rows")
    early_pieces = [early, early_near, move.core(early), move.core(early_near)]
    late_pieces = [late, late_near, move.core(late), move.core(late_near)]
    qkv_grad, down_grad, *named = call(
        last_place_kernel,
        scalars,
        early_pieces + late_pieces,
        [((3, width, half), F32, False), ((hidden_width, width), F32, False)]
        + [((1, n), F32, False) for n in [width] * 8 + [hidden_width, n_logits]],
        [pltpu.VMEM((spare, 128), F32)],
        name="last_place",
        after=(rows_done,),
        cost=FOLD,
    )
    named = [v.reshape(-1) for v in named]
    return (
        block_out,
        logits,
        grad_frames,
        named[0],
        named[1],
        qkv_grad,
        out_grad,
        named[4],
        named[2],
        named[3],
        up_grad,
        named[8],
        down_grad,
        named[7],
        named[5],
        named[6],
        prior_grad,
        named[9],
    )


def solution(mesh):
    rows, cols = P("dp", "tensor"), P(None, "tensor")
    placed = (
        rows, P("dp"), P(), P(), P(None, None, "tensor"), P("tensor", None), P(), P(), P(), cols, P("tensor"),
        P("tensor", None), P(), P(), P(), cols, P("tensor"), rows, rows,
    )
    given = (
        rows, rows, rows, P(), P(), P(None, None, "tensor"), P("tensor", None), P(), P(), P(), cols,
        P("tensor"), P("tensor", None), P(), P(), P(), cols, P("tensor"),
    )
    return jax.shard_map(
        functools.partial(local, mesh.shape["dp"], mesh.shape["tensor"]),
        mesh=mesh,
        in_specs=placed,
        out_specs=given,
        check_vma=False,
    )
```

```python
import functools
import math

import jax
import jax.numpy as jnp
from jax import lax
from jax.experimental import pallas as pl
from jax.experimental.pallas import tpu as pltpu
from jax.sharding import PartitionSpec as P

HEAD_DIM = 64
SEQ_LEN = 50
BLOCK = 4 * SEQ_LEN
PAD = -(-BLOCK // 16) * 16
EPS = 1e-05
NEG = -1e30
GELU_C = 0.7978845608028654
GELU_A = 0.044715
SPILL = 8 * 1024 * 1024
GROUP, GROUP_BACK = 4, 6
COST = 1e8
FOLD = 100.0
BF = jnp.bfloat16
F32 = jnp.float32
FIRST_GAIN, FIRST_SHIFT, OUT_BIAS, SECOND_GAIN, SECOND_SHIFT, DOWN_BIAS, PRIOR_GAIN, PRIOR_SHIFT, UP_BIAS, PRIOR_BIAS = range(10)


def mm(a, b):
    return lax.dot_general(a, b, (((1,), (0,)), ((), ())), preferred_element_type=F32)


def mm_bt(a, b):
    return lax.dot_general(a, b, (((1,), (1,)), ((), ())), preferred_element_type=F32)


def mm_at(a, b):
    return lax.dot_general(a, b, (((0,), (0,)), ((), ())), preferred_element_type=F32)


def norm_of(value):
    centre = value - jnp.mean(value, axis=-1, keepdims=True)
    factor = lax.rsqrt(jnp.mean(centre * centre, axis=-1, keepdims=True) + EPS)
    return centre * factor, factor


def norm_back(grad, unit, factor, gain):
    scaled = grad * gain
    first = jnp.mean(scaled, axis=-1, keepdims=True)
    second = jnp.mean(scaled * unit, axis=-1, keepdims=True)
    return factor * (scaled - first - unit * second)


def col_sum(value):
    return jnp.sum(value, axis=0, keepdims=True)


def whole_rows(here, own, other):
    low = jnp.where(here == 0, own[...], other[...])
    high = jnp.where(here == 0, other[...], own[...])
    return jnp.concatenate([low, high], axis=1).astype(F32)


def allowed_pairs(resets):
    place = lax.broadcasted_iota(jnp.int32, (1, PAD), 1)
    starts = jnp.where((resets == 1) | (lax.rem(place, SEQ_LEN) == 0) | (place >= BLOCK), place, 0)
    row = lax.broadcasted_iota(jnp.int32, (PAD, PAD), 0)
    col = lax.broadcasted_iota(jnp.int32, (PAD, PAD), 1)
    seg = jnp.max(jnp.where(col <= row, starts, 0).astype(F32), axis=-1, keepdims=True).astype(jnp.int32)
    seg2 = jnp.concatenate([seg, seg], axis=0)
    row = lax.broadcasted_iota(jnp.int32, (2 * PAD, PAD), 0)
    row = jnp.where(row >= PAD, row - PAD, row)
    col = lax.broadcasted_iota(jnp.int32, (2 * PAD, PAD), 1)
    return (col <= row) & (col >= seg2)


def two_heads(value):
    first = lax.broadcasted_iota(jnp.int32, value.shape, 1) < HEAD_DIM
    none = jnp.zeros_like(value)
    return jnp.concatenate([jnp.where(first, value, none), jnp.where(first, none, value)], axis=0)


def one_pair(value):
    first = lax.broadcasted_iota(jnp.int32, (PAD, 2 * HEAD_DIM), 1) < HEAD_DIM
    return jnp.where(first, value[:PAD], value[PAD:])


def softmax_of(scores, allowed):
    scores = jnp.where(allowed, scores, NEG)
    expo = jnp.exp(scores - jnp.max(scores, axis=-1, keepdims=True))
    return expo * (1.0 / jnp.sum(expo, axis=-1, keepdims=True))


def vector(small, index, n):
    return small[index : index + 1, :n]


def blocks_in(ref):
    return [slice(i * PAD, i * PAD + PAD) for i in range(ref.shape[0] // PAD)]


def add_up(sums, values):
    return [v if s is None else s + v for s, v in zip(sums, values, strict=True)]


def split_rows(half, source, own, sent, wide_rows):
    rows, n = source.shape
    wide_rows[0:rows, 0:n] = source[...].astype(F32)
    for which, target in ((half, own), (1 - half, sent)):
        for block, at in enumerate(blocks_in(target)):
            start = pl.multiple_of(which * (rows // 2) + block * BLOCK, 8)
            part = wide_rows[pl.ds(start, PAD), 0:n]
            inside = lax.broadcasted_iota(jnp.int32, part.shape, 0) < BLOCK
            target[at, :] = jnp.where(inside, part, 0.0).astype(BF)


def tiles_of(ref, start, n, count):
    return jnp.concatenate([ref[start + t * n : start + t * n + n, :] for t in range(count)], axis=1)


class Packed:
    def __init__(self, refs, n, q, o):
        self.one, self.two = refs
        self.n, self.q, self.o = n, q, o

    def up(self):
        return tiles_of(self.one, 0, self.n, 2)

    def out(self):
        return tiles_of(self.one, 2 * self.n, self.o, 4)

    def bias(self):
        start = 2 * self.n + 4 * self.o
        parts = [self.one[start + 16 * k : start + 16 * k + 16, :].astype(F32) for k in range(3)]
        return (parts[2] + parts[1] + parts[0])[:3]

    def down(self):
        return tiles_of(self.two, 0, self.q, 4)

    def prior(self):
        return self.two[4 * self.q : 4 * self.q + self.n, :]


def put_tiles(target, start, part):
    for t in range(part.shape[-1] // 128):
        target[start : start + part.shape[0], :] = part[:, t * 128 : t * 128 + 128]
        start += part.shape[0]
    return start


def first_kernel(s, frames, qkv, resets, qkv_ref, sent_ref, own_ref, resets_ref, wide_rows):
    start = 0
    for c in range(3):
        start = put_tiles(qkv_ref, start, qkv.get().at[c])
    split_rows(s[0], frames, own_ref, sent_ref, wide_rows)
    resets_ref[...] = jnp.zeros_like(resets_ref)
    line = resets[...].reshape(1, -1)
    for block in range(line.shape[1] // BLOCK):
        resets_ref[block : block + 1, :BLOCK] = line[:, block * BLOCK : block * BLOCK + BLOCK]


def packs_kernel(s, up, out, down, prior, *refs):
    smalls, (one_ref, two_ref, small_ref, rows) = refs[:-4], refs[-4:]
    start = put_tiles(one_ref, put_tiles(one_ref, 0, up), out)
    for i, ref in enumerate(smalls):
        small_ref[i : i + 1, : ref.shape[1]] = ref[...]
    rows[...] = jnp.zeros_like(rows)
    for t in range(2):
        rows[t : t + 1, :] = smalls[UP_BIAS][:, pl.ds(pl.multiple_of(s[1] * 256 + t * 128, 128), 128)]
    rows[2:3, :] = smalls[PRIOR_BIAS][:, pl.ds(pl.multiple_of(s[1] * 128, 128), 128)]
    left = rows[...]
    for k in range(3):
        term = left.astype(BF)
        one_ref[start : start + 16, :] = term
        left = left - term.astype(F32)
        start += 16
    put_tiles(two_ref, put_tiles(two_ref, 0, down), prior)


def cotangents_kernel(s, logit, out, sent, logit_own, out_own, wide_rows, logit_sent, out_sent):
    split_rows(s[0], logit, logit_own, logit_sent, wide_rows)
    split_rows(s[0], out, out_own, out_sent, wide_rows)
    n = logit_sent.shape[1]
    sent[:, :n] = logit_sent[...]
    sent[:, n:] = out_sent[...]


def gate(values, after, name=None):
    count, total = len(values), len(values) + len(after)

    def run(*refs):
        for source, target in zip(refs[:count], refs[total:], strict=True):
            target[...] = source[...]

    near = pl.BlockSpec(memory_space=pltpu.VMEM)
    return pl.pallas_call(
        run,
        in_specs=[near] * total,
        out_specs=[near] * count,
        out_shape=[pltpu.VMEM(v.shape, v.dtype) for v in values],
        compiler_params=pltpu.CompilerParams(vmem_limit_bytes=SPILL),
        cost_estimate=pl.CostEstimate(flops=0, bytes_accessed=0, transcendentals=0),
        name=name,
    )(*[pin(v) for v in values], *[pin(v) for v in after])


def attend_kernel(
    s, own, other, resets, small, q0, q1, q2, q3, qkv,
    first_ref, triple_ref, mixed_ref, qkv_other_ref,
):
    unit, _ = norm_of(whole_rows(s[0], own, other))
    n = first_ref.shape[1]
    first_ref[...] = (unit * vector(small, FIRST_GAIN, n) + vector(small, FIRST_SHIFT, n)).astype(BF)
    for j, piece in enumerate((q0, q1, q2, q3)):
        size = qkv.shape[1] // 4
        rows = pl.ds(pl.multiple_of((s[1] ^ j) * size, 16), size)
        for c in range(3):
            qkv_other_ref[c, rows, :] = tiles_of(piece, c * 2 * size, size, 2)
    for half, weight in enumerate((qkv, qkv_other_ref)):
        for c in range(3):
            value = mm(first_ref[...], weight[c]).astype(BF)
            triple_ref[:, (half * 3 + c) * 256 : (half * 3 + c + 1) * 256] = value
    units = []
    for block, at in enumerate(blocks_in(own)):
        allowed = allowed_pairs(resets[pl.ds(s[0] * len(blocks_in(own)) + block, 1), :PAD])
        units += [(at, allowed, pair, (pair // 2) * 768 + (pair % 2) * 128) for pair in range(4)]
    for group in range(0, len(units), GROUP):
        some = units[group : group + GROUP]
        scores = [
            mm_bt(two_heads(triple_ref[at, start : start + 128] * HEAD_DIM ** (-0.5)), triple_ref[at, start + 256 : start + 384])
            for at, _, _, start in some
        ]
        weights = [softmax_of(score, allowed).astype(BF) for score, (_, allowed, _, _) in zip(scores, some, strict=True)]
        for weight, (at, _, pair, start) in zip(weights, some, strict=True):
            mixed = one_pair(mm(weight, triple_ref[at, start + 512 : start + 640])).astype(BF)
            mixed_ref[at, pair * 128 : pair * 128 + 128] = mixed


def feed_kernel(
    s, own, other, mixed, small, out, up, down, a0, a1, a2, a3, b0, b1, b2, b3,
    block_other_ref, block_own_ref, middle_ref, second_ref, act_ref, slope_ref, ending_ref, prior_in_ref,
    out_other_ref, up_other_ref, down_other_ref, bias_other,
):
    n, half, wide = out.shape[0], up.shape[1], up.shape[0]
    for j, piece in enumerate(zip((a0, a1, a2, a3), (b0, b1, b2, b3))):
        piece = Packed(piece, wide, half // 4, n // 4)
        place = s[1] ^ j
        out_other_ref[pl.ds(pl.multiple_of(place * (n // 4), 16), n // 4), :] = piece.out()
        at = pl.ds(pl.multiple_of(place * 256, 256), 256)
        up_other_ref[:, at] = piece.up()
        down_other_ref[at, :] = piece.down()
        bias = piece.bias()
        bias_other[:, at] = jnp.concatenate([bias[0:1], bias[1:2]], axis=1)
    middle_ref[...] = (
        whole_rows(s[0], own, other)
        + vector(small, OUT_BIAS, wide)
        + mm(mixed[:, :n], out[...])
        + mm(mixed[:, n:], out_other_ref[...])
    )
    unit, _ = norm_of(middle_ref[...])
    second_ref[...] = (unit * vector(small, SECOND_GAIN, wide) + vector(small, SECOND_SHIFT, wide)).astype(BF)
    total = middle_ref[...] + vector(small, DOWN_BIAS, wide)
    for h, (w_up, w_down) in enumerate(((up, down), (up_other_ref, down_other_ref))):
        for i in range(half // 256):
            at = slice(i * 256, i * 256 + 256)
            to = slice(h * half + i * 256, h * half + i * 256 + 256)
            bias = bias_other[:, at] if h else small[UP_BIAS : UP_BIAS + 1, at]
            for rows in blocks_in(own):
                hidden = mm(second_ref[rows, :], w_up[:, at]) + bias
                square = hidden * hidden
                bent = jnp.tanh(GELU_C * (hidden + GELU_A * hidden * square))
                act_ref[rows, to] = (0.5 * hidden * (1.0 + bent)).astype(BF)
                slope_ref[rows, to] = 0.5 * (1.0 + bent) + (0.5 * GELU_C) * hidden * (1.0 - bent * bent) * (
                    1.0 + (3.0 * GELU_A) * square
                )
        total = total + mm(act_ref[:, h * half : h * half + half], w_down[...])
    ending_ref[...] = total
    unit, _ = norm_of(total)
    prior_in_ref[...] = (unit * vector(small, PRIOR_GAIN, wide) + vector(small, PRIOR_SHIFT, wide)).astype(BF)
    low, high = total[:, :256].astype(BF), total[:, 256:].astype(BF)
    block_own_ref[...] = jnp.where(s[0] == 0, low, high)
    block_other_ref[...] = jnp.where(s[0] == 0, high, low)


def prior_kernel(
    s, ending, small, logit_own, out_own, a0, a1, a2, a3, b0, b1, b2, b3, cotangents, prior,
    grad_ending_ref, ending_grad_ref, vec_ref, bias_ref, weight, bias,
):
    half, n = prior.shape[1], prior.shape[0]
    for j, piece in enumerate(zip((a0, a1, a2, a3), (b0, b1, b2, b3))):
        at = pl.ds(pl.multiple_of((s[1] ^ j) * 128, 128), 128)
        piece = Packed(piece, n, n // 2, n // 8)
        weight[:, at] = piece.prior()
        bias[:, at] = piece.bias()[2:3]
    logit_other = cotangents.at[:, :half]
    back = mm_bt(logit_own[...], prior[...]) + mm_bt(logit_other[...], weight[...])
    unit, factor = norm_of(ending[...])
    gain = vector(small, PRIOR_GAIN, unit.shape[1])
    grad = whole_rows(s[0], out_own, cotangents.at[:, half:]) + norm_back(back, unit, factor, gain)
    grad_ending_ref[...] = grad
    ending_grad_ref[...] = grad.astype(BF)
    vec_ref[...] = jnp.concatenate([col_sum(back * unit), col_sum(back), col_sum(grad)], axis=0)
    bias_ref[:, :half] = col_sum(logit_own[...].astype(F32))
    bias_ref[:, half:] = col_sum(logit_other[...].astype(F32))


def logits_kernel(s, prior_in, small, prior, weight, bias, block_other, frames_other, sent_ref, logits_ref):
    half, n = prior.shape[1], block_other.shape[1]
    sent_ref[:, :half] = (mm(prior_in[...], weight[...]) + bias[...]).astype(BF)
    sent_ref[:, half : half + n] = block_other[...]
    sent_ref[:, half + n :] = frames_other[...]
    logits_ref[...] = mm(prior_in[...], prior[...]) + vector(small, PRIOR_BIAS, half)


def store_piece(keep, send, h, j, start, value):
    at = slice(start, start + value.shape[0])
    if j < 2:
        keep[h * 2 + j, at, :] = value
    else:
        send[h * 2 + j - 2, at, :] = value.astype(BF)


def late_grads_kernel(s, act, ending_grad, keep, send):
    half = act.shape[1] // 2
    for h in range(2):
        for j in (2, 3, 0, 1):
            part = act[:, pl.ds(pl.multiple_of(h * half + (s[1] ^ j) * 256, 256), 256)]
            value = mm_at(part, ending_grad[...])
            for t in range(value.shape[1] // 128):
                store_piece(keep, send, h, j, t * 256, value[:, t * 128 : t * 128 + 128])


def up_grads_kernel(
    s, second, hidden_grad, mixed, middle_grad, prior_in, logit_own, cotangents, keep, send, turned, wide, tall,
):
    turned[...] = second[...].T
    half = hidden_grad.shape[1] // 2
    n, m = second.shape[1], mixed.shape[1] // 2
    logit_other = cotangents.at[:, : logit_own.shape[1]]
    for h in range(2):
        wide[...] = mm_at(mixed[:, h * m : h * m + m], middle_grad[...])
        tall[...] = mm_at(prior_in[...], (logit_own, logit_other)[h][...])
        for j in (2, 3, 0, 1):
            place = s[1] ^ j
            at = pl.ds(pl.multiple_of(place * 128, 128), 128)
            value = mm(turned[...], hidden_grad[:, pl.ds(pl.multiple_of(h * half + place * 256, 256), 256)])
            for t in range(2):
                store_piece(keep, send, h, j, t * n, value[:, t * 128 : t * 128 + 128])
            store_piece(keep, send, h, j, 2 * n, wide[:, at])
            store_piece(keep, send, h, j, 2 * n + m, tall[:, at])


def early_grads_kernel(s, first, grad_own, grad_other, keep, send):
    for h in range(2):
        for j in (2, 3, 0, 1):
            place = pl.multiple_of((s[1] ^ j) * 128, 128)
            value = mm_at(first[:, pl.ds(place, 128)], (grad_own, grad_other)[h][...])
            for c in range(3):
                for t in range(2):
                    at = slice(c * 256 + t * 128, c * 256 + t * 128 + 128)
                    store_piece(keep, send, h, j, (t * 3 + c) * 128, value[:, at])


def feed_back_kernel(
    s, ending_grad, slope, middle, grad_ending, small, down, down_other, up, up_other,
    hidden_grad_ref, grad_middle_ref, middle_grad_ref, vec_ref, bias_ref,
):
    half = up.shape[1]
    back, steps = None, half // 256
    tasks = [(h, i) for h in range(2) for i in range(steps)]

    def product(h, i):
        return mm_bt(ending_grad[...], (down, down_other)[h][i * 256 : i * 256 + 256, :])

    ahead = product(*tasks[0])
    for k, (h, i) in enumerate(tasks):
        value, ahead = ahead, product(*tasks[k + 1]) if k + 1 < len(tasks) else None
        to = slice(h * half + i * 256, h * half + i * 256 + 256)
        low = (value * slope[:, to]).astype(BF)
        hidden_grad_ref[:, to] = low
        bias_ref[:, to] = col_sum(low.astype(F32))
        if i + 1 == steps:
            part = mm_bt(hidden_grad_ref[:, h * half : h * half + half], (up, up_other)[h][...])
            back = part if back is None else back + part
    unit, factor = norm_of(middle[...])
    gain = vector(small, SECOND_GAIN, unit.shape[1])
    total = grad_ending[...] + norm_back(back, unit, factor, gain)
    grad_middle_ref[...] = total
    middle_grad_ref[...] = total.astype(BF)
    vec_ref[...] = jnp.concatenate([col_sum(back * unit), col_sum(back), col_sum(total)], axis=0)


def attend_back_kernel(
    half, s, middle_grad, triple, out, resets,
    triple_grad_ref, mixed_grad,
):
    mixed_grad[...] = mm_bt(middle_grad[...], out[...]).astype(BF)
    factor = HEAD_DIM ** (-0.5)
    units = []
    for block, at in enumerate(blocks_in(triple)):
        allowed = allowed_pairs(resets[pl.ds(s[0] * len(blocks_in(triple)) + block, 1), :PAD])
        units += [(at, allowed, pair) for pair in range(2)]
    for group in range(0, len(units), GROUP_BACK):
        some = units[group : group + GROUP_BACK]
        loaded = []
        for at, _, pair in some:
            start = half * 768 + pair * 128
            query, key, value = (triple[at, start + c * 256 : start + c * 256 + 128] for c in range(3))
            mixed2 = two_heads(mixed_grad[at, pair * 128 : pair * 128 + 128])
            loaded.append((two_heads(query * factor), key, value, mixed2))
        scores = [mm_bt(query2, key) for query2, key, _, _ in loaded]
        weight_grads = [mm_bt(mixed2, value) for _, _, value, mixed2 in loaded]
        inner = []
        for score, weight_grad, (_, allowed, _) in zip(scores, weight_grads, some, strict=True):
            again = softmax_of(score, allowed)
            both = again * weight_grad
            total = jnp.sum(both, axis=-1, keepdims=True)
            inner.append((again.astype(BF), (both - again * total).astype(BF)))
        for (again, score_grad), (query2, key, _, mixed2), (at, _, pair) in zip(inner, loaded, some, strict=True):
            thirds = (
                (one_pair(mm(score_grad, key)) * factor).astype(BF),
                mm_at(score_grad, query2).astype(BF),
                mm_at(again, mixed2).astype(BF),
            )
            for c in range(3):
                triple_grad_ref[at, c * 256 + pair * 128 : c * 256 + pair * 128 + 128] = thirds[c]


def frames_back_kernel(
    s, grad_own, grad_other, grad_middle, own, other, qkv_other, small, qkv,
    sent_ref, frames_own_ref, vec_ref,
):
    back = None
    for part, weight in ((grad_own, qkv), (grad_other, qkv_other)):
        for c in range(3):
            value = mm_bt(part[:, c * 256 : c * 256 + 256], weight[c])
            back = value if back is None else back + value
    unit, scale = norm_of(whole_rows(s[0], own, other))
    total = grad_middle[...] + norm_back(back, unit, scale, vector(small, FIRST_GAIN, unit.shape[1]))
    low, high = total[:, :256], total[:, 256:]
    frames_own_ref[...] = jnp.where(s[0] == 0, low, high)
    sent_ref[...] = jnp.where(s[0] == 0, high, low).astype(BF)
    vec_ref[...] = jnp.concatenate([col_sum(back * unit), col_sum(back)], axis=0)


def late_place_kernel(s, mine, near, far, farther, down_ref):
    q = down_ref.shape[0] // 4
    for j, piece in enumerate((mine, near, far, farther)):
        rows = pl.ds(pl.multiple_of((s[1] ^ j) * q, 8), q)
        for t in range(down_ref.shape[1] // 128):
            down_ref[rows, t * 128 : t * 128 + 128] = piece[t * q : t * q + q, :].astype(F32)


def up_place_kernel(s, mine, near, far, farther, up_ref, out_ref, prior_ref, token):
    token[...] = jnp.zeros_like(token)
    n, m = up_ref.shape[0], out_ref.shape[0]
    for j, piece in enumerate((mine, near, far, farther)):
        place = s[1] ^ j
        for t in range(2):
            columns = pl.ds(pl.multiple_of(place * 256 + t * 128, 128), 128)
            up_ref[:, columns] = piece[t * n : t * n + n, :].astype(F32)
        at = pl.ds(pl.multiple_of(place * 128, 128), 128)
        out_ref[:, at] = piece[2 * n : 2 * n + m, :].astype(F32)
        prior_ref[:, at] = piece[2 * n + m :, :].astype(F32)


def last_place_kernel(s, mine, near, far, farther, l0, l1, l2, l3, qkv_ref, down_ref, *vecs):
    vecs, sums = vecs[:-1], vecs[-1]
    late_place_kernel(s, l0, l1, l2, l3, down_ref)
    down_ref.send()
    sums[...] = mine[6 * 128 :, :].astype(F32) + far[6 * 128 :, :].astype(F32)
    for j, piece in enumerate((mine, near, far, farther)):
        at = pl.ds(pl.multiple_of((s[1] ^ j) * 128, 128), 128)
        for c in range(3):
            for t in range(2):
                start = (t * 3 + c) * 128
                qkv_ref[c, at, t * 128 : t * 128 + 128] = piece[start : start + 128, :].astype(F32)
    qkv_ref.send()
    row = 0
    for ref in vecs[:8]:
        for t in range(ref.shape[1] // 128):
            ref[:, t * 128 : t * 128 + 128] = sums[row : row + 1, :]
            row += 1
    for ref in vecs[8:]:
        tiles = ref.shape[1] // 128
        for t in range(tiles):
            ref[:, t * 128 : t * 128 + 128] = sums[pl.ds(row + s[0] * tiles + t, 1), :]
        row += 2 * tiles


def core_kernel(s, keep, got, low, rest):
    n = keep.shape[1]
    for out, places, dtype in ((low, (2, 3), BF), (rest, (0, 1), F32)):
        for k, i in enumerate(places):
            out[k * n : k * n + n, :] = (keep[i] + got[i].astype(F32)).astype(dtype)


def core_all_kernel(s, keep, got, *refs):
    vectors, lows, rest = refs[:-4], refs[-4:-1], refs[-1]
    n = keep.shape[1]
    for i in (1, 2, 3):
        lows[i - 1][:n, :] = (keep[i] + got[i].astype(F32)).astype(BF)
    rest[:n, :] = keep[0] + got[0].astype(F32)
    if vectors:
        put_vectors(s, vectors, rest, n)
        for low in lows:
            low[n:, :] = rest[n:, :].astype(BF)


def put_vectors(s, vectors, rest, row):
    for ref in vectors[:3]:
        for i in range(ref.shape[0]):
            for t in range(ref.shape[1] // 128):
                rest[row : row + 1, :] = ref[i : i + 1, t * 128 : t * 128 + 128]
                row += 1
    for ref in vectors[3:]:
        tiles = ref.shape[1] // 128
        for t in range(tiles):
            place = row + lax.rem(t + s[0] * (tiles // 2), tiles)
            rest[pl.ds(place, 1), :] = ref[:, t * 128 : t * 128 + 128]
        row += tiles
    rest[row:, :] = jnp.zeros((rest.shape[0] - row, 128), F32)


def over_kernel(s, rest, got, low, mine):
    n = low.shape[0]
    low[...] = (rest[n:, :] + got[n:, :].astype(F32)).astype(BF)
    mine[...] = rest[:n, :] + got[:n, :].astype(F32)


def halves_kernel(s, *refs):
    total, (keep, send) = refs[-1], refs[-3:-1]
    total[...] = functools.reduce(lambda x, y: x + y, [r[...].astype(F32) for r in refs[:-3]])
    n = keep.shape[0]
    send[...] = total[pl.ds(pl.multiple_of((1 - s[2]) * n, 16), n), :].astype(BF)
    keep[...] = total[pl.ds(pl.multiple_of(s[2] * n, 16), n), :].astype(BF)


def join_kernel(s, mine, got, out):
    n = mine.shape[0]
    out[pl.ds(pl.multiple_of(s[2] * n, 16), n), :] = mine[...]
    out[pl.ds(pl.multiple_of((1 - s[2]) * n, 16), n), :] = got[...]


def total_kernel(s, *refs):
    refs[-1][...] = functools.reduce(lambda x, y: x + y, [r[...].astype(F32) for r in refs[:-1]]).astype(BF)


def rows_kernel(entries, s, *refs):
    count = len(entries)
    given, outs, token, room = refs[: 2 * count], refs[2 * count : 3 * count], refs[3 * count], refs[-1]
    token[...] = jnp.zeros_like(token)
    for i, columns in enumerate(entries):
        own, got, out = given[2 * i], given[2 * i + 1], outs[i]
        whole = out.ref.dtype == F32
        target = out.ref if whole else room
        rows = out.shape[0] // 2
        for block, at in enumerate(blocks_in(own)):
            for which, ref, cut in ((s[0], own, slice(None)), (1 - s[0], got, columns)):
                start = pl.multiple_of(which * rows + block * BLOCK, 8)
                target[pl.ds(start, BLOCK), :] = ref[at, cut].astype(F32)[:BLOCK]
        if not whole:
            out[...] = room[...].astype(out.ref.dtype)
        out.send()


class Loaded:
    def __init__(self, ref, copy):
        self.ref, self.copy, self.shape = ref, copy, ref.shape

    def get(self):
        if self.copy is not None:
            self.copy.wait()
            self.copy = None
        return self.ref

    def __getitem__(self, index):
        return self.get()[index]


class Leaving:
    def __init__(self, ref, copy):
        self.ref, self.copy, self.shape, self.sent = ref, copy, ref.shape, False

    def __getitem__(self, index):
        return self.ref[index]

    def __setitem__(self, index, value):
        self.ref[index] = value

    def send(self):
        if not self.sent:
            self.copy.start()
            self.sent = True


class Far:
    def __init__(self, value, shape=None, cut=None):
        self.value, self.shape, self.cut = value, shape or value.shape, cut or (lambda s, ref: ref)


def call(kernel, scalars, ins, outs, scratch=(), name=None, after=(), cost=1.0, loads=()):
    n_own, n_loads = len(ins), len(loads)
    ins, outs = [*ins, *[Far(v) for v in loads]], [*outs, *[(v.shape, v.dtype, True) for v in loads]]
    n_in, n_out, n_after = len(ins), len(outs), len(after)
    far_in = [i for i, v in enumerate(ins[:n_own]) if isinstance(v, Far)]
    far_out = [i for i, o in enumerate(outs) if not o[2]]
    room = [pltpu.VMEM(ins[i].shape, ins[i].value.dtype) for i in far_in]
    room += [pltpu.VMEM(outs[i][0], outs[i][1]) for i in far_out]
    need = sum(math.prod(r.shape) * jnp.dtype(r.dtype).itemsize for r in room + list(scratch))

    def run(s, *refs):
        given, refs = list(refs[:n_in]), refs[n_in + n_after :]
        made, refs = list(refs[:n_out]), refs[n_out:]
        own, refs = refs[: len(scratch)], refs[len(scratch) :]
        rooms, sems = refs[:-1], refs[-1]
        for k, i in enumerate(far_in):
            copy = pltpu.make_async_copy(ins[i].cut(s, given[i]), rooms[k], sems.at[k])
            copy.start()
            given[i] = Loaded(rooms[k], copy)
        bringing = []
        for k in range(n_loads):
            copy = pltpu.make_async_copy(given[n_own + k], made[n_out - n_loads + k], sems.at[len(rooms) + k])
            copy.start()
            bringing.append(copy)
        leaving = []
        for k, i in enumerate(far_out, len(far_in)):
            made[i] = Leaving(rooms[k], pltpu.make_async_copy(rooms[k], made[i], sems.at[k]))
            leaving.append(made[i])
        kernel(s, *given[:n_own], *made[: n_out - n_loads], *own)
        for copy in bringing:
            copy.wait()
        for value in given:
            if isinstance(value, Loaded):
                value.get()
        for value in leaving:
            value.send()
        for value in leaving:
            value.copy.wait()

    near, far = pl.BlockSpec(memory_space=pltpu.VMEM), pl.BlockSpec(memory_space=pltpu.HBM)
    return pl.pallas_call(
        run,
        in_specs=[pl.BlockSpec(memory_space=pltpu.SMEM)]
        + [far if isinstance(v, Far) else near for v in ins]
        + [far if isinstance(v, Far) else near for v in after],
        out_specs=[near if stays else far for _, _, stays in outs],
        out_shape=[(pltpu.VMEM if stays else pltpu.HBM)(shape, dtype) for shape, dtype, stays in outs],
        scratch_shapes=list(scratch) + room + [pltpu.SemaphoreType.DMA((max(1, len(room) + n_loads),))],
        compiler_params=pltpu.CompilerParams(vmem_limit_bytes=need + SPILL),
        cost_estimate=pl.CostEstimate(flops=int(cost * COST), bytes_accessed=0, transcendentals=0),
        name=name,
    )(scalars, *[pin(v) for v in ins], *[pin(v) for v in after])


def pin(value):
    if isinstance(value, Far):
        return pltpu.with_memory_space_constraint(value.value, pltpu.HBM)
    return pltpu.with_memory_space_constraint(value, pltpu.VMEM)


def swap(value, axes, sizes, mask):
    count = 1
    for size in sizes:
        count *= size
    return lax.ppermute(value, axes, [(i, i ^ mask) for i in range(count)])


class Moves:
    def __init__(self, n_dp, n_tensor):
        self.n_dp, self.n_tensor = n_dp, n_tensor
        self.dp = lax.axis_index("dp")
        self.here = lax.axis_index("tensor")

    def along(self, value, mask):
        return swap(value, "dp", (self.n_dp,), mask)

    def core(self, value):
        return self.along(value, 1)

    def side(self, value):
        return self.along(value, 2)

    def over(self, value):
        return swap(value, "tensor", (self.n_tensor,), 1)

    def cross(self, value):
        return swap(value, ("dp", "tensor"), (self.n_dp, self.n_tensor), 5)


    def reduce_core(self, scalars, keep, sent, name, after=()):
        n = 2 * sent.shape[1]
        outs = [((n, 128), BF, True), ((n, 128), F32, True)]
        return call(core_kernel, scalars, [keep, self.core(sent)], outs, name=name, after=after, cost=FOLD)

    def reduce_over(self, scalars, low, rest, name, after=()):
        n = low.shape[0] // 2
        outs = [((n, 128), BF, True), ((n, 128), F32, True)]
        return call(over_kernel, scalars, [rest, self.over(low)], outs, name=name, after=after, cost=FOLD)

    def reduce_core_all(self, scalars, keep, sent, name, vectors=(), spare=0, after=()):
        n = sent.shape[1] + spare
        outs = [((n, 128), BF, True)] * 3 + [((n, 128), F32, True)]
        ins = [keep, self.core(sent), *vectors]
        return call(core_all_kernel, scalars, ins, outs, name=name, after=after, cost=FOLD)

    def sides(self, lows):
        return [self.side(lows[0]), self.over(lows[1]), self.cross(lows[2])]

    def total(self, scalars, values, name, after=()):
        shape = values[0].shape
        return call(total_kernel, scalars, values, [(shape, BF, True)], name=name, after=after, cost=FOLD)[0]

    def halves(self, scalars, values, name, after=()):
        n = values[0].shape[0]
        return call(
            halves_kernel,
            scalars,
            values,
            [((n // 2, 128), BF, True)] * 2,
            [pltpu.VMEM((n, 128), F32)],
            name=name,
            after=after,
            cost=FOLD,
        )

    def join(self, scalars, mine, got, name, after=()):
        shape = (mine.shape[0] * 2, 128)
        return call(join_kernel, scalars, [mine, got], [(shape, BF, True)], name=name, after=after, cost=FOLD)[0]

    def bits(self):
        return [1 << i for i in range(2, self.n_dp.bit_length() - 1)]

    def gather(self, total):
        near = self.side(total)
        return total, near, self.core(total), self.core(near)


def local(
    n_dp, n_tensor, frames, resets, first_gain, first_shift, qkv_weight, out_weight, out_bias, second_gain,
    second_shift, up_weight, up_bias, down_weight, down_bias, prior_gain, prior_shift, prior_weight,
    prior_bias, out_cotangent, logit_cotangent,
):
    move = Moves(n_dp, n_tensor)
    rows, half = frames.shape
    width = 2 * half
    mine = rows // 2
    blocks = mine // BLOCK
    hidden_width, n_logits = up_bias.shape[0], prior_bias.shape[0]
    row = lambda v: v.reshape(1, -1)
    core, side = move.dp & 1, (move.dp >> 1) & 1
    scalars = jnp.stack([move.here, core * 2 + side, (move.dp >> 2) & 1]).astype(jnp.int32)
    total_rows = blocks * PAD
    quarter = hidden_width // 4

    def near_rows(*entries):
        return [((total_rows, n), dtype, True) for n, dtype in entries]

    def pieces(n):
        return [((4, n, 128), F32, True), ((4, n, 128), BF, True)]

    def columns(value, size, which):
        cut = lambda s, ref: ref.at[..., pl.ds(pl.multiple_of(s[which] * size, 128), size)]
        return Far(value, (*value.shape[:-1], size), cut)

    def some_rows(value, size, which):
        cut = lambda s, ref: ref.at[pl.ds(pl.multiple_of(s[which] * size, 16), size), :]
        return Far(value, (size, value.shape[1]), cut)

    vectors = [first_gain, first_shift, out_bias, second_gain, second_shift, down_bias, prior_gain, prior_shift]
    vectors = [row(v) for v in vectors + [up_bias, prior_bias]]
    qkv_rows = 3 * (width // 4) * (half // 128)
    sent_qkv, sent_frames, frames_own, resets_near = call(
        first_kernel,
        scalars,
        [
            Far(frames),
            Far(
                qkv_weight,
                (3, width // 4, half),
                lambda s, ref: ref.at[:, pl.ds(pl.multiple_of(s[1] * (width // 4), 16), width // 4), :],
            ),
            Far(resets),
        ],
        [((qkv_rows, 128), BF, True)]
        + near_rows((half, BF), (half, BF))
        + [((-(-2 * blocks // 8) * 8, -(-BLOCK // 128) * 128), jnp.int32, True)],
        [pltpu.VMEM((rows + 16, half), F32)],
        "first_parts",
        cost=2.0,
    )
    sent_one, sent_two, small = call(
        packs_kernel,
        scalars,
        [
            columns(up_weight, quarter, 1),
            some_rows(out_weight, half // 4, 1),
            some_rows(down_weight, quarter, 1),
            columns(prior_weight, n_logits // 4, 1),
            *[Far(v) for v in vectors],
        ],
        [((width * 2 + half + 48, 128), BF, True), ((quarter * 4 + width, 128), BF, True)]
        + [((16, hidden_width), F32, True)],
        [pltpu.VMEM((16, 128), F32)],
        "packs",
        after=(sent_frames,),
        cost=2.0,
    )

    def all_quarters(got):
        beside = move.side(got)
        return [got, beside, move.core(got), move.core(beside)]

    qkv_got = move.over(sent_qkv)
    frames_other = move.over(sent_frames)
    qkv_pieces = all_quarters(qkv_got)
    cot_sent, logit_own, out_own, qkv_near, out_near, up_near, down_near, prior_near = call(
        cotangents_kernel,
        scalars,
        [Far(logit_cotangent), Far(out_cotangent)],
        near_rows((n_logits + half, BF), (n_logits, BF), (half, BF)),
        [pltpu.VMEM((rows + 16, n_logits), F32)]
        + [pltpu.VMEM((total_rows, n), BF) for n in (n_logits, half)],
        name="cotangents",
        after=(sent_frames,),
        cost=2.3,
        loads=(qkv_weight, out_weight, up_weight, down_weight, prior_weight),
    )
    (sent_one,) = gate([sent_one], [frames_other, cot_sent], "after_frames")
    got_one = move.over(sent_one)
    (sent_two,) = gate([sent_two], [sent_one, qkv_pieces[1]], "after_one")
    got_two = move.over(sent_two)
    first, triple, mixed, qkv_other = call(
        attend_kernel,
        scalars,
        [frames_own, frames_other, resets_near, small, *qkv_pieces, qkv_near],
        near_rows((width, BF), (3 * width, BF), (width, BF)) + [(qkv_weight.shape, BF, True)],
        name="attend",
        cost=5.5,
    )
    beside_one = move.side(got_one)
    (cot_sent,) = gate([cot_sent], [got_two, beside_one], "after_two")
    (beside_two,) = gate([move.side(got_two)], [mixed], "after_attend")
    packed = [got_one, beside_one, move.core(got_one), move.core(beside_one)]
    packed += [got_two, beside_two, move.core(got_two), move.core(beside_two)]
    cotangents = move.over(cot_sent)
    block_send, block_own, middle, second, act, slope, ending, prior_in, out_other, up_other, down_other = call(
        feed_kernel,
        scalars,
        [frames_own, frames_other, mixed, small, out_near, up_near, down_near, *packed],
        near_rows((half, BF), (half, BF))
        + near_rows((width, F32), (width, BF), (2 * hidden_width, BF), (2 * hidden_width, F32))
        + near_rows((width, F32), (width, BF))
        + [(v.shape, BF, True) for v in (out_weight, up_weight, down_weight)],
        [pltpu.VMEM((1, hidden_width), F32)],
        name="feed",
        cost=7.2,
    )
    grad_ending, ending_grad, vec_three, prior_bias_sum, prior_other, prior_bias_other = call(
        prior_kernel,
        scalars,
        [ending, small, logit_own, out_own, *packed, cotangents, prior_near],
        near_rows((width, F32), (width, BF))
        + [((3, width), F32, True), ((1, 2 * n_logits), F32, True)]
        + [(prior_weight.shape, BF, True), ((1, n_logits), F32, True)],
        name="prior",
        cost=2.5,
    )
    hidden_grad, grad_middle, middle_grad, vec_two, up_bias_sum = call(
        feed_back_kernel,
        scalars,
        [ending_grad, slope, middle, grad_ending, small, down_near, down_other, up_near, up_other],
        near_rows((2 * hidden_width, BF), (width, F32), (width, BF))
        + [((3, width), F32, True), ((1, 2 * hidden_width), F32, True)],
        name="feed_back",
        cost=6.5,
    )
    up_keep, up_send = call(
        up_grads_kernel,
        scalars,
        [second, hidden_grad, mixed, middle_grad, prior_in, logit_own, cotangents],
        pieces(width * hidden_width // 512 + half + width),
        [pltpu.VMEM((width, total_rows), BF), pltpu.VMEM((half, width), F32), pltpu.VMEM((width, n_logits), F32)],
        name="up_grads",
        cost=3.0,
    )
    late_keep, late_send = call(
        late_grads_kernel,
        scalars,
        [act, ending_grad],
        pieces(hidden_width),
        name="late_grads",
        after=(up_send,),
        cost=3.5,
    )
    *up_low, up_rest = move.reduce_core_all(scalars, up_keep, up_send, "up_core", after=(late_send,))
    def attend_back(half, out, after):
        return call(
            functools.partial(attend_back_kernel, half),
            scalars,
            [middle_grad, triple, out, resets_near],
            near_rows((3 * width // 2, BF)),
            [pltpu.VMEM((total_rows, width // 2), BF)],
            name=f"attend_back_{half}",
            after=after,
            cost=4.5,
        )[0]

    grad_own = attend_back(0, out_near, (up_low[0],))
    *late_low, late_rest = move.reduce_core_all(scalars, late_keep, late_send, "late_core", after=(grad_own,))
    grad_other = attend_back(1, out_other, (late_low[0],))
    keep, send = call(
        early_grads_kernel,
        scalars,
        [first, grad_own, grad_other],
        pieces(768),
        name="early_grads",
        cost=2.0,
    )
    frames_send, frames_grad, vec_one = call(
        frames_back_kernel,
        scalars,
        [grad_own, grad_other, grad_middle, frames_own, frames_other, qkv_other, small, qkv_near],
        near_rows((half, BF), (half, F32)) + [((2, width), F32, True)],
        name="frames_back",
        after=(send,),
        cost=2.5,
    )
    up, up_half = move.halves(scalars, [up_rest, *move.sides(up_low)], "up_1", (vec_one,))
    bits = move.bits()
    spare = 64
    vectors = [vec_one, vec_two, vec_three, up_bias_sum, prior_bias_sum]
    *early_low, early_rest = move.reduce_core_all(scalars, keep, send, "early_core", vectors, spare, (up,))
    done = up = move.total(scalars, [up, move.along(up_half, bits[0])], "up_2", (early_low[0],))
    done = late, late_half = move.halves(scalars, [late_rest, *move.sides(late_low)], "late_1", (done,))
    done = late
    for bit in bits[1:]:
        done = up = move.total(scalars, [up, move.along(up, bit)], "up_3", (done,))
    back_send, logits_own = call(
        logits_kernel,
        scalars,
        [prior_in, small, prior_near, prior_other, prior_bias_other, block_send, frames_send],
        near_rows((n_logits + 2 * half, BF), (n_logits, F32)),
        name="logits",
        after=(done,),
        cost=2.0,
    )
    done = back_send
    early, early_half = move.halves(scalars, [early_rest, *move.sides(early_low)], "early_1", (done,))
    done = early
    done = late = move.total(scalars, [late, move.along(late_half, bits[0])], "late_2", (done,))
    done = up = move.join(scalars, up, move.along(up, bits[0]), "up_4", (done,))
    done = early = move.total(scalars, [early, move.along(early_half, bits[0])], "early_2", (done,))
    for bit in bits[1:]:
        done = late = move.total(scalars, [late, move.along(late, bit)], "late_3", (done,))
    for bit in bits[1:]:
        done = early = move.total(scalars, [early, move.along(early, bit)], "early_3", (done,))
    up_pieces = list(move.gather(up))
    late = move.join(scalars, late, move.along(late, bits[0]), "late_4", (done, up_pieces[2]))
    early = move.join(scalars, early, move.along(early, bits[0]), "early_4", (late,))
    up_grad, out_grad, prior_grad, up_done = call(
        up_place_kernel,
        scalars,
        up_pieces,
        [((width, hidden_width), F32, False), ((half, width), F32, False), ((width, n_logits), F32, False)]
        + [((8, 128), F32, True)],
        name="up_place",
        after=(early,),
        cost=FOLD,
    )
    back_got = move.over(back_send)
    logits, grad_frames, block_out, rows_done = call(
        functools.partial(
            rows_kernel,
            [slice(0, n_logits), slice(n_logits + half, n_logits + 2 * half), slice(n_logits, n_logits + half)],
        ),
        scalars,
        [logits_own, back_got, frames_grad, back_got, block_own, back_got],
        [((rows, n_logits), F32, False), ((rows, half), F32, False), ((rows, half), BF, False)]
        + [((8, 128), F32, True)],
        [pltpu.VMEM((rows, half), F32)],
        name="rows_back",
        after=(up_done,),
        cost=FOLD,
    )
    (early_near,) = gate([move.side(early)], [up_done], "after_up")
    (late_near,) = gate([move.side(late)], [rows_done], "after_rows")
    early_pieces = [early, early_near, move.core(early), move.core(early_near)]
    late_pieces = [late, late_near, move.core(late), move.core(late_near)]
    qkv_grad, down_grad, *named = call(
        last_place_kernel,
        scalars,
        early_pieces + late_pieces,
        [((3, width, half), F32, False), ((hidden_width, width), F32, False)]
        + [((1, n), F32, False) for n in [width] * 8 + [hidden_width, n_logits]],
        [pltpu.VMEM((spare, 128), F32)],
        name="last_place",
        after=(rows_done,),
        cost=FOLD,
    )
    named = [v.reshape(-1) for v in named]
    return (
        block_out,
        logits,
        grad_frames,
        named[0],
        named[1],
        qkv_grad,
        out_grad,
        named[4],
        named[2],
        named[3],
        up_grad,
        named[8],
        down_grad,
        named[7],
        named[5],
        named[6],
        prior_grad,
        named[9],
    )


def solution(mesh):
    rows, cols = P("dp", "tensor"), P(None, "tensor")
    placed = (
        rows, P("dp"), P(), P(), P(None, None, "tensor"), P("tensor", None), P(), P(), P(), cols, P("tensor"),
        P("tensor", None), P(), P(), P(), cols, P("tensor"), rows, rows,
    )
    given = (
        rows, rows, rows, P(), P(), P(None, None, "tensor"), P("tensor", None), P(), P(), P(), cols,
        P("tensor"), P("tensor", None), P(), P(), P(), cols, P("tensor"),
    )
    return jax.shard_map(
        functools.partial(local, mesh.shape["dp"], mesh.shape["tensor"]),
        mesh=mesh,
        in_specs=placed,
        out_specs=given,
        check_vma=False,
    )
```

```python
import functools
import math

import jax
import jax.numpy as jnp
from jax import lax
from jax.experimental import pallas as pl
from jax.experimental.pallas import tpu as pltpu
from jax.sharding import PartitionSpec as P

HEAD_DIM = 64
SEQ_LEN = 50
BLOCK = 4 * SEQ_LEN
PAD = -(-BLOCK // 16) * 16
EPS = 1e-05
NEG = -1e30
GELU_C = 0.7978845608028654
GELU_A = 0.044715
SPILL = 8 * 1024 * 1024
GROUP, GROUP_BACK = 4, 6
COST = 1e8
FOLD = 100.0
BF = jnp.bfloat16
F32 = jnp.float32
FIRST_GAIN, FIRST_SHIFT, OUT_BIAS, SECOND_GAIN, SECOND_SHIFT, DOWN_BIAS, PRIOR_GAIN, PRIOR_SHIFT, UP_BIAS, PRIOR_BIAS = range(10)


def mm(a, b):
    return lax.dot_general(a, b, (((1,), (0,)), ((), ())), preferred_element_type=F32)


def mm_bt(a, b):
    return lax.dot_general(a, b, (((1,), (1,)), ((), ())), preferred_element_type=F32)


def mm_at(a, b):
    return lax.dot_general(a, b, (((0,), (0,)), ((), ())), preferred_element_type=F32)


def norm_of(value):
    centre = value - jnp.mean(value, axis=-1, keepdims=True)
    factor = lax.rsqrt(jnp.mean(centre * centre, axis=-1, keepdims=True) + EPS)
    return centre * factor, factor


def norm_back(grad, unit, factor, gain):
    scaled = grad * gain
    first = jnp.mean(scaled, axis=-1, keepdims=True)
    second = jnp.mean(scaled * unit, axis=-1, keepdims=True)
    return factor * (scaled - first - unit * second)


def col_sum(value):
    return jnp.sum(value, axis=0, keepdims=True)


def whole_rows(here, own, other):
    low = jnp.where(here == 0, own[...], other[...])
    high = jnp.where(here == 0, other[...], own[...])
    return jnp.concatenate([low, high], axis=1).astype(F32)


def allowed_pairs(resets):
    place = lax.broadcasted_iota(jnp.int32, (1, PAD), 1)
    starts = jnp.where((resets == 1) | (lax.rem(place, SEQ_LEN) == 0) | (place >= BLOCK), place, 0)
    row = lax.broadcasted_iota(jnp.int32, (PAD, PAD), 0)
    col = lax.broadcasted_iota(jnp.int32, (PAD, PAD), 1)
    seg = jnp.max(jnp.where(col <= row, starts, 0).astype(F32), axis=-1, keepdims=True).astype(jnp.int32)
    seg2 = jnp.concatenate([seg, seg], axis=0)
    row = lax.broadcasted_iota(jnp.int32, (2 * PAD, PAD), 0)
    row = jnp.where(row >= PAD, row - PAD, row)
    col = lax.broadcasted_iota(jnp.int32, (2 * PAD, PAD), 1)
    return (col <= row) & (col >= seg2)


def two_heads(value):
    first = lax.broadcasted_iota(jnp.int32, value.shape, 1) < HEAD_DIM
    none = jnp.zeros_like(value)
    return jnp.concatenate([jnp.where(first, value, none), jnp.where(first, none, value)], axis=0)


def one_pair(value):
    first = lax.broadcasted_iota(jnp.int32, (PAD, 2 * HEAD_DIM), 1) < HEAD_DIM
    return jnp.where(first, value[:PAD], value[PAD:])


def softmax_of(scores, allowed):
    scores = jnp.where(allowed, scores, NEG)
    expo = jnp.exp(scores - jnp.max(scores, axis=-1, keepdims=True))
    return expo * (1.0 / jnp.sum(expo, axis=-1, keepdims=True))


def vector(small, index, n):
    return small[index : index + 1, :n]


def blocks_in(ref):
    return [slice(i * PAD, i * PAD + PAD) for i in range(ref.shape[0] // PAD)]


def add_up(sums, values):
    return [v if s is None else s + v for s, v in zip(sums, values, strict=True)]


def split_rows(half, source, own, sent, wide_rows):
    rows, n = source.shape
    wide_rows[0:rows, 0:n] = source[...].astype(F32)
    for which, target in ((half, own), (1 - half, sent)):
        for block, at in enumerate(blocks_in(target)):
            start = pl.multiple_of(which * (rows // 2) + block * BLOCK, 8)
            part = wide_rows[pl.ds(start, PAD), 0:n]
            inside = lax.broadcasted_iota(jnp.int32, part.shape, 0) < BLOCK
            target[at, :] = jnp.where(inside, part, 0.0).astype(BF)


def tiles_of(ref, start, n, count):
    return jnp.concatenate([ref[start + t * n : start + t * n + n, :] for t in range(count)], axis=1)


class Packed:
    def __init__(self, refs, n, q, o):
        self.one, self.two = refs
        self.n, self.q, self.o = n, q, o

    def up(self):
        return tiles_of(self.one, 0, self.n, 2)

    def out(self):
        return tiles_of(self.one, 2 * self.n, self.o, 4)

    def bias(self):
        start = 2 * self.n + 4 * self.o
        parts = [self.one[start + 16 * k : start + 16 * k + 16, :].astype(F32) for k in range(3)]
        return (parts[2] + parts[1] + parts[0])[:3]

    def down(self):
        return tiles_of(self.two, 0, self.q, 4)

    def prior(self):
        return self.two[4 * self.q : 4 * self.q + self.n, :]


def put_tiles(target, start, part):
    for t in range(part.shape[-1] // 128):
        target[start : start + part.shape[0], :] = part[:, t * 128 : t * 128 + 128]
        start += part.shape[0]
    return start


def first_kernel(s, frames, qkv, resets, qkv_ref, sent_ref, own_ref, resets_ref, wide_rows):
    start = 0
    for c in range(3):
        start = put_tiles(qkv_ref, start, qkv.get().at[c])
    split_rows(s[0], frames, own_ref, sent_ref, wide_rows)
    resets_ref[...] = jnp.zeros_like(resets_ref)
    line = resets[...].reshape(1, -1)
    for block in range(line.shape[1] // BLOCK):
        resets_ref[block : block + 1, :BLOCK] = line[:, block * BLOCK : block * BLOCK + BLOCK]


def packs_kernel(s, up, out, down, prior, *refs):
    smalls, (one_ref, two_ref, small_ref, rows) = refs[:-4], refs[-4:]
    start = put_tiles(one_ref, put_tiles(one_ref, 0, up), out)
    for i, ref in enumerate(smalls):
        small_ref[i : i + 1, : ref.shape[1]] = ref[...]
    rows[...] = jnp.zeros_like(rows)
    for t in range(2):
        rows[t : t + 1, :] = smalls[UP_BIAS][:, pl.ds(pl.multiple_of(s[1] * 256 + t * 128, 128), 128)]
    rows[2:3, :] = smalls[PRIOR_BIAS][:, pl.ds(pl.multiple_of(s[1] * 128, 128), 128)]
    left = rows[...]
    for k in range(3):
        term = left.astype(BF)
        one_ref[start : start + 16, :] = term
        left = left - term.astype(F32)
        start += 16
    put_tiles(two_ref, put_tiles(two_ref, 0, down), prior)


def cotangents_kernel(s, logit, out, sent, logit_own, out_own, wide_rows, logit_sent, out_sent):
    split_rows(s[0], logit, logit_own, logit_sent, wide_rows)
    split_rows(s[0], out, out_own, out_sent, wide_rows)
    n = logit_sent.shape[1]
    sent[:, :n] = logit_sent[...]
    sent[:, n:] = out_sent[...]


def gate(values, after, name=None):
    count, total = len(values), len(values) + len(after)

    def run(*refs):
        for source, target in zip(refs[:count], refs[total:], strict=True):
            target[...] = source[...]

    near = pl.BlockSpec(memory_space=pltpu.VMEM)
    return pl.pallas_call(
        run,
        in_specs=[near] * total,
        out_specs=[near] * count,
        out_shape=[pltpu.VMEM(v.shape, v.dtype) for v in values],
        compiler_params=pltpu.CompilerParams(vmem_limit_bytes=SPILL),
        cost_estimate=pl.CostEstimate(flops=0, bytes_accessed=0, transcendentals=0),
        name=name,
    )(*[pin(v) for v in values], *[pin(v) for v in after])


def attend_kernel(
    s, own, other, resets, small, q0, q1, q2, q3, qkv,
    first_ref, triple_ref, mixed_ref, qkv_other_ref,
):
    unit, _ = norm_of(whole_rows(s[0], own, other))
    n = first_ref.shape[1]
    first_ref[...] = (unit * vector(small, FIRST_GAIN, n) + vector(small, FIRST_SHIFT, n)).astype(BF)
    for j, piece in enumerate((q0, q1, q2, q3)):
        size = qkv.shape[1] // 4
        rows = pl.ds(pl.multiple_of((s[1] ^ j) * size, 16), size)
        for c in range(3):
            qkv_other_ref[c, rows, :] = tiles_of(piece, c * 2 * size, size, 2)
    for half, weight in enumerate((qkv, qkv_other_ref)):
        for c in range(3):
            value = mm(first_ref[...], weight[c]).astype(BF)
            triple_ref[:, (half * 3 + c) * 256 : (half * 3 + c + 1) * 256] = value
    units = []
    for block, at in enumerate(blocks_in(own)):
        allowed = allowed_pairs(resets[pl.ds(s[0] * len(blocks_in(own)) + block, 1), :PAD])
        units += [(at, allowed, pair, (pair // 2) * 768 + (pair % 2) * 128) for pair in range(4)]
    for group in range(0, len(units), GROUP):
        some = units[group : group + GROUP]
        scores = [
            mm_bt(two_heads(triple_ref[at, start : start + 128] * HEAD_DIM ** (-0.5)), triple_ref[at, start + 256 : start + 384])
            for at, _, _, start in some
        ]
        weights = [softmax_of(score, allowed).astype(BF) for score, (_, allowed, _, _) in zip(scores, some, strict=True)]
        for weight, (at, _, pair, start) in zip(weights, some, strict=True):
            mixed = one_pair(mm(weight, triple_ref[at, start + 512 : start + 640])).astype(BF)
            mixed_ref[at, pair * 128 : pair * 128 + 128] = mixed


def feed_kernel(
    s, own, other, mixed, small, out, up, down, a0, a1, a2, a3, b0, b1, b2, b3,
    block_other_ref, block_own_ref, middle_ref, second_ref, act_ref, slope_ref, ending_ref, prior_in_ref,
    out_other_ref, up_other_ref, down_other_ref, bias_other,
):
    n, half, wide = out.shape[0], up.shape[1], up.shape[0]
    for j, piece in enumerate(zip((a0, a1, a2, a3), (b0, b1, b2, b3))):
        piece = Packed(piece, wide, half // 4, n // 4)
        place = s[1] ^ j
        out_other_ref[pl.ds(pl.multiple_of(place * (n // 4), 16), n // 4), :] = piece.out()
        at = pl.ds(pl.multiple_of(place * 256, 256), 256)
        up_other_ref[:, at] = piece.up()
        down_other_ref[at, :] = piece.down()
        bias = piece.bias()
        bias_other[:, at] = jnp.concatenate([bias[0:1], bias[1:2]], axis=1)
    middle_ref[...] = (
        whole_rows(s[0], own, other)
        + vector(small, OUT_BIAS, wide)
        + mm(mixed[:, :n], out[...])
        + mm(mixed[:, n:], out_other_ref[...])
    )
    unit, _ = norm_of(middle_ref[...])
    second_ref[...] = (unit * vector(small, SECOND_GAIN, wide) + vector(small, SECOND_SHIFT, wide)).astype(BF)
    total = middle_ref[...] + vector(small, DOWN_BIAS, wide)
    for h, (w_up, w_down) in enumerate(((up, down), (up_other_ref, down_other_ref))):
        for i in range(half // 256):
            at = slice(i * 256, i * 256 + 256)
            to = slice(h * half + i * 256, h * half + i * 256 + 256)
            bias = bias_other[:, at] if h else small[UP_BIAS : UP_BIAS + 1, at]
            for rows in blocks_in(own):
                hidden = mm(second_ref[rows, :], w_up[:, at]) + bias
                square = hidden * hidden
                bent = jnp.tanh(GELU_C * (hidden + GELU_A * hidden * square))
                act_ref[rows, to] = (0.5 * hidden * (1.0 + bent)).astype(BF)
                slope_ref[rows, to] = 0.5 * (1.0 + bent) + (0.5 * GELU_C) * hidden * (1.0 - bent * bent) * (
                    1.0 + (3.0 * GELU_A) * square
                )
        total = total + mm(act_ref[:, h * half : h * half + half], w_down[...])
    ending_ref[...] = total
    unit, _ = norm_of(total)
    prior_in_ref[...] = (unit * vector(small, PRIOR_GAIN, wide) + vector(small, PRIOR_SHIFT, wide)).astype(BF)
    low, high = total[:, :256].astype(BF), total[:, 256:].astype(BF)
    block_own_ref[...] = jnp.where(s[0] == 0, low, high)
    block_other_ref[...] = jnp.where(s[0] == 0, high, low)


def prior_kernel(
    s, ending, small, logit_own, out_own, a0, a1, a2, a3, b0, b1, b2, b3, cotangents, prior,
    grad_ending_ref, ending_grad_ref, vec_ref, bias_ref, weight, bias,
):
    half, n = prior.shape[1], prior.shape[0]
    for j, piece in enumerate(zip((a0, a1, a2, a3), (b0, b1, b2, b3))):
        at = pl.ds(pl.multiple_of((s[1] ^ j) * 128, 128), 128)
        piece = Packed(piece, n, n // 2, n // 8)
        weight[:, at] = piece.prior()
        bias[:, at] = piece.bias()[2:3]
    logit_other = cotangents.at[:, :half]
    back = mm_bt(logit_own[...], prior[...]) + mm_bt(logit_other[...], weight[...])
    unit, factor = norm_of(ending[...])
    gain = vector(small, PRIOR_GAIN, unit.shape[1])
    grad = whole_rows(s[0], out_own, cotangents.at[:, half:]) + norm_back(back, unit, factor, gain)
    grad_ending_ref[...] = grad
    ending_grad_ref[...] = grad.astype(BF)
    vec_ref[...] = jnp.concatenate([col_sum(back * unit), col_sum(back), col_sum(grad)], axis=0)
    bias_ref[:, :half] = col_sum(logit_own[...].astype(F32))
    bias_ref[:, half:] = col_sum(logit_other[...].astype(F32))


def logits_kernel(s, prior_in, small, prior, weight, bias, block_other, frames_other, sent_ref, logits_ref):
    half, n = prior.shape[1], block_other.shape[1]
    sent_ref[:, :half] = (mm(prior_in[...], weight[...]) + bias[...]).astype(BF)
    sent_ref[:, half : half + n] = block_other[...]
    sent_ref[:, half + n :] = frames_other[...]
    logits_ref[...] = mm(prior_in[...], prior[...]) + vector(small, PRIOR_BIAS, half)


def store_piece(keep, send, h, j, start, value):
    at = slice(start, start + value.shape[0])
    if j < 2:
        keep[h * 2 + j, at, :] = value
    else:
        send[h * 2 + j - 2, at, :] = value.astype(BF)


def late_grads_kernel(s, act, ending_grad, keep, send):
    half = act.shape[1] // 2
    for h in range(2):
        for j in (2, 3, 0, 1):
            part = act[:, pl.ds(pl.multiple_of(h * half + (s[1] ^ j) * 256, 256), 256)]
            value = mm_at(part, ending_grad[...])
            for t in range(value.shape[1] // 128):
                store_piece(keep, send, h, j, t * 256, value[:, t * 128 : t * 128 + 128])


def up_grads_kernel(
    s, second, hidden_grad, mixed, middle_grad, prior_in, logit_own, cotangents, keep, send, turned, wide, tall, turned_in,
):
    turned[...] = second[...].T
    turned_in[...] = prior_in[...].T
    half = hidden_grad.shape[1] // 2
    n, m = second.shape[1], mixed.shape[1] // 2
    logit_other = cotangents.at[:, : logit_own.shape[1]]
    for h in range(2):
        wide[...] = mm_at(mixed[:, h * m : h * m + m], middle_grad[...])
        tall[...] = mm(turned_in[...], (logit_own, logit_other)[h][...])
        for j in (2, 3, 0, 1):
            place = s[1] ^ j
            at = pl.ds(pl.multiple_of(place * 128, 128), 128)
            value = mm(turned[...], hidden_grad[:, pl.ds(pl.multiple_of(h * half + place * 256, 256), 256)])
            for t in range(2):
                store_piece(keep, send, h, j, t * n, value[:, t * 128 : t * 128 + 128])
            store_piece(keep, send, h, j, 2 * n, wide[:, at])
            store_piece(keep, send, h, j, 2 * n + m, tall[:, at])


def early_grads_kernel(s, first, grad_own, grad_other, keep, send):
    for h in range(2):
        for j in (2, 3, 0, 1):
            place = pl.multiple_of((s[1] ^ j) * 128, 128)
            value = mm_at(first[:, pl.ds(place, 128)], (grad_own, grad_other)[h][...])
            for c in range(3):
                for t in range(2):
                    at = slice(c * 256 + t * 128, c * 256 + t * 128 + 128)
                    store_piece(keep, send, h, j, (t * 3 + c) * 128, value[:, at])


def feed_back_kernel(
    s, ending_grad, slope, middle, grad_ending, small, down, down_other, up, up_other,
    hidden_grad_ref, grad_middle_ref, middle_grad_ref, vec_ref, bias_ref,
):
    half = up.shape[1]
    back, steps = None, half // 256
    tasks = [(h, i) for h in range(2) for i in range(steps)]

    def product(h, i):
        return mm_bt(ending_grad[...], (down, down_other)[h][i * 256 : i * 256 + 256, :])

    ahead = product(*tasks[0])
    for k, (h, i) in enumerate(tasks):
        value, ahead = ahead, product(*tasks[k + 1]) if k + 1 < len(tasks) else None
        to = slice(h * half + i * 256, h * half + i * 256 + 256)
        low = (value * slope[:, to]).astype(BF)
        hidden_grad_ref[:, to] = low
        bias_ref[:, to] = col_sum(low.astype(F32))
        if i + 1 == steps:
            part = mm_bt(hidden_grad_ref[:, h * half : h * half + half], (up, up_other)[h][...])
            back = part if back is None else back + part
    unit, factor = norm_of(middle[...])
    gain = vector(small, SECOND_GAIN, unit.shape[1])
    total = grad_ending[...] + norm_back(back, unit, factor, gain)
    grad_middle_ref[...] = total
    middle_grad_ref[...] = total.astype(BF)
    vec_ref[...] = jnp.concatenate([col_sum(back * unit), col_sum(back), col_sum(total)], axis=0)


def attend_back_kernel(
    half, s, middle_grad, triple, out, resets,
    triple_grad_ref, mixed_grad,
):
    mixed_grad[...] = mm_bt(middle_grad[...], out[...]).astype(BF)
    factor = HEAD_DIM ** (-0.5)
    units = []
    for block, at in enumerate(blocks_in(triple)):
        allowed = allowed_pairs(resets[pl.ds(s[0] * len(blocks_in(triple)) + block, 1), :PAD])
        units += [(at, allowed, pair) for pair in range(2)]
    for group in range(0, len(units), GROUP_BACK):
        some = units[group : group + GROUP_BACK]
        loaded = []
        for at, _, pair in some:
            start = half * 768 + pair * 128
            query, key, value = (triple[at, start + c * 256 : start + c * 256 + 128] for c in range(3))
            mixed2 = two_heads(mixed_grad[at, pair * 128 : pair * 128 + 128])
            loaded.append((two_heads(query * factor), key, value, mixed2))
        scores = [mm_bt(query2, key) for query2, key, _, _ in loaded]
        weight_grads = [mm_bt(mixed2, value) for _, _, value, mixed2 in loaded]
        inner = []
        for score, weight_grad, (_, allowed, _) in zip(scores, weight_grads, some, strict=True):
            again = softmax_of(score, allowed)
            both = again * weight_grad
            total = jnp.sum(both, axis=-1, keepdims=True)
            inner.append((again.astype(BF), (both - again * total).astype(BF)))
        for (again, score_grad), (query2, key, _, mixed2), (at, _, pair) in zip(inner, loaded, some, strict=True):
            thirds = (
                (one_pair(mm(score_grad, key)) * factor).astype(BF),
                mm_at(score_grad, query2).astype(BF),
                mm_at(again, mixed2).astype(BF),
            )
            for c in range(3):
                triple_grad_ref[at, c * 256 + pair * 128 : c * 256 + pair * 128 + 128] = thirds[c]


def frames_back_kernel(
    s, grad_own, grad_other, grad_middle, own, other, qkv_other, small, qkv,
    sent_ref, frames_own_ref, vec_ref,
):
    back = None
    for part, weight in ((grad_own, qkv), (grad_other, qkv_other)):
        for c in range(3):
            value = mm_bt(part[:, c * 256 : c * 256 + 256], weight[c])
            back = value if back is None else back + value
    unit, scale = norm_of(whole_rows(s[0], own, other))
    total = grad_middle[...] + norm_back(back, unit, scale, vector(small, FIRST_GAIN, unit.shape[1]))
    low, high = total[:, :256], total[:, 256:]
    frames_own_ref[...] = jnp.where(s[0] == 0, low, high)
    sent_ref[...] = jnp.where(s[0] == 0, high, low).astype(BF)
    vec_ref[...] = jnp.concatenate([col_sum(back * unit), col_sum(back)], axis=0)


def late_place_kernel(s, mine, near, far, farther, down_ref):
    q = down_ref.shape[0] // 4
    for j, piece in enumerate((mine, near, far, farther)):
        rows = pl.ds(pl.multiple_of((s[1] ^ j) * q, 8), q)
        for t in range(down_ref.shape[1] // 128):
            down_ref[rows, t * 128 : t * 128 + 128] = piece[t * q : t * q + q, :].astype(F32)


def up_place_kernel(s, mine, near, far, farther, up_ref, out_ref, prior_ref, token):
    token[...] = jnp.zeros_like(token)
    n, m = up_ref.shape[0], out_ref.shape[0]
    for j, piece in enumerate((mine, near, far, farther)):
        place = s[1] ^ j
        for t in range(2):
            columns = pl.ds(pl.multiple_of(place * 256 + t * 128, 128), 128)
            up_ref[:, columns] = piece[t * n : t * n + n, :].astype(F32)
        at = pl.ds(pl.multiple_of(place * 128, 128), 128)
        out_ref[:, at] = piece[2 * n : 2 * n + m, :].astype(F32)
        prior_ref[:, at] = piece[2 * n + m :, :].astype(F32)


def last_place_kernel(s, mine, near, far, farther, l0, l1, l2, l3, qkv_ref, down_ref, *vecs):
    vecs, sums = vecs[:-1], vecs[-1]
    late_place_kernel(s, l0, l1, l2, l3, down_ref)
    down_ref.send()
    sums[...] = mine[6 * 128 :, :].astype(F32) + far[6 * 128 :, :].astype(F32)
    for j, piece in enumerate((mine, near, far, farther)):
        at = pl.ds(pl.multiple_of((s[1] ^ j) * 128, 128), 128)
        for c in range(3):
            for t in range(2):
                start = (t * 3 + c) * 128
                qkv_ref[c, at, t * 128 : t * 128 + 128] = piece[start : start + 128, :].astype(F32)
    qkv_ref.send()
    row = 0
    for ref in vecs[:8]:
        for t in range(ref.shape[1] // 128):
            ref[:, t * 128 : t * 128 + 128] = sums[row : row + 1, :]
            row += 1
    for ref in vecs[8:]:
        tiles = ref.shape[1] // 128
        for t in range(tiles):
            ref[:, t * 128 : t * 128 + 128] = sums[pl.ds(row + s[0] * tiles + t, 1), :]
        row += 2 * tiles


def core_kernel(s, keep, got, low, rest):
    n = keep.shape[1]
    for out, places, dtype in ((low, (2, 3), BF), (rest, (0, 1), F32)):
        for k, i in enumerate(places):
            out[k * n : k * n + n, :] = (keep[i] + got[i].astype(F32)).astype(dtype)


def core_all_kernel(s, keep, got, *refs):
    vectors, lows, rest = refs[:-4], refs[-4:-1], refs[-1]
    n = keep.shape[1]
    for i in (1, 2, 3):
        lows[i - 1][:n, :] = (keep[i] + got[i].astype(F32)).astype(BF)
    rest[:n, :] = keep[0] + got[0].astype(F32)
    if vectors:
        put_vectors(s, vectors, rest, n)
        for low in lows:
            low[n:, :] = rest[n:, :].astype(BF)


def put_vectors(s, vectors, rest, row):
    for ref in vectors[:3]:
        for i in range(ref.shape[0]):
            for t in range(ref.shape[1] // 128):
                rest[row : row + 1, :] = ref[i : i + 1, t * 128 : t * 128 + 128]
                row += 1
    for ref in vectors[3:]:
        tiles = ref.shape[1] // 128
        for t in range(tiles):
            place = row + lax.rem(t + s[0] * (tiles // 2), tiles)
            rest[pl.ds(place, 1), :] = ref[:, t * 128 : t * 128 + 128]
        row += tiles
    rest[row:, :] = jnp.zeros((rest.shape[0] - row, 128), F32)


def over_kernel(s, rest, got, low, mine):
    n = low.shape[0]
    low[...] = (rest[n:, :] + got[n:, :].astype(F32)).astype(BF)
    mine[...] = rest[:n, :] + got[:n, :].astype(F32)


def halves_kernel(s, *refs):
    total, (keep, send) = refs[-1], refs[-3:-1]
    total[...] = functools.reduce(lambda x, y: x + y, [r[...].astype(F32) for r in refs[:-3]])
    n = keep.shape[0]
    send[...] = total[pl.ds(pl.multiple_of((1 - s[2]) * n, 16), n), :].astype(BF)
    keep[...] = total[pl.ds(pl.multiple_of(s[2] * n, 16), n), :].astype(BF)


def join_kernel(s, mine, got, out):
    n = mine.shape[0]
    out[pl.ds(pl.multiple_of(s[2] * n, 16), n), :] = mine[...]
    out[pl.ds(pl.multiple_of((1 - s[2]) * n, 16), n), :] = got[...]


def total_kernel(s, *refs):
    refs[-1][...] = functools.reduce(lambda x, y: x + y, [r[...].astype(F32) for r in refs[:-1]]).astype(BF)


def rows_kernel(entries, s, *refs):
    count = len(entries)
    given, outs, token, room = refs[: 2 * count], refs[2 * count : 3 * count], refs[3 * count], refs[-1]
    token[...] = jnp.zeros_like(token)
    for i, columns in enumerate(entries):
        own, got, out = given[2 * i], given[2 * i + 1], outs[i]
        whole = out.ref.dtype == F32
        target = out.ref if whole else room
        rows = out.shape[0] // 2
        for block, at in enumerate(blocks_in(own)):
            for which, ref, cut in ((s[0], own, slice(None)), (1 - s[0], got, columns)):
                start = pl.multiple_of(which * rows + block * BLOCK, 8)
                target[pl.ds(start, BLOCK), :] = ref[at, cut].astype(F32)[:BLOCK]
        if not whole:
            out[...] = room[...].astype(out.ref.dtype)
        out.send()


class Loaded:
    def __init__(self, ref, copy):
        self.ref, self.copy, self.shape = ref, copy, ref.shape

    def get(self):
        if self.copy is not None:
            self.copy.wait()
            self.copy = None
        return self.ref

    def __getitem__(self, index):
        return self.get()[index]


class Leaving:
    def __init__(self, ref, copy):
        self.ref, self.copy, self.shape, self.sent = ref, copy, ref.shape, False

    def __getitem__(self, index):
        return self.ref[index]

    def __setitem__(self, index, value):
        self.ref[index] = value

    def send(self):
        if not self.sent:
            self.copy.start()
            self.sent = True


class Far:
    def __init__(self, value, shape=None, cut=None):
        self.value, self.shape, self.cut = value, shape or value.shape, cut or (lambda s, ref: ref)


def call(kernel, scalars, ins, outs, scratch=(), name=None, after=(), cost=1.0, loads=()):
    n_own, n_loads = len(ins), len(loads)
    ins, outs = [*ins, *[Far(v) for v in loads]], [*outs, *[(v.shape, v.dtype, True) for v in loads]]
    n_in, n_out, n_after = len(ins), len(outs), len(after)
    far_in = [i for i, v in enumerate(ins[:n_own]) if isinstance(v, Far)]
    far_out = [i for i, o in enumerate(outs) if not o[2]]
    room = [pltpu.VMEM(ins[i].shape, ins[i].value.dtype) for i in far_in]
    room += [pltpu.VMEM(outs[i][0], outs[i][1]) for i in far_out]
    need = sum(math.prod(r.shape) * jnp.dtype(r.dtype).itemsize for r in room + list(scratch))

    def run(s, *refs):
        given, refs = list(refs[:n_in]), refs[n_in + n_after :]
        made, refs = list(refs[:n_out]), refs[n_out:]
        own, refs = refs[: len(scratch)], refs[len(scratch) :]
        rooms, sems = refs[:-1], refs[-1]
        for k, i in enumerate(far_in):
            copy = pltpu.make_async_copy(ins[i].cut(s, given[i]), rooms[k], sems.at[k])
            copy.start()
            given[i] = Loaded(rooms[k], copy)
        bringing = []
        for k in range(n_loads):
            copy = pltpu.make_async_copy(given[n_own + k], made[n_out - n_loads + k], sems.at[len(rooms) + k])
            copy.start()
            bringing.append(copy)
        leaving = []
        for k, i in enumerate(far_out, len(far_in)):
            made[i] = Leaving(rooms[k], pltpu.make_async_copy(rooms[k], made[i], sems.at[k]))
            leaving.append(made[i])
        kernel(s, *given[:n_own], *made[: n_out - n_loads], *own)
        for copy in bringing:
            copy.wait()
        for value in given:
            if isinstance(value, Loaded):
                value.get()
        for value in leaving:
            value.send()
        for value in leaving:
            value.copy.wait()

    near, far = pl.BlockSpec(memory_space=pltpu.VMEM), pl.BlockSpec(memory_space=pltpu.HBM)
    return pl.pallas_call(
        run,
        in_specs=[pl.BlockSpec(memory_space=pltpu.SMEM)]
        + [far if isinstance(v, Far) else near for v in ins]
        + [far if isinstance(v, Far) else near for v in after],
        out_specs=[near if stays else far for _, _, stays in outs],
        out_shape=[(pltpu.VMEM if stays else pltpu.HBM)(shape, dtype) for shape, dtype, stays in outs],
        scratch_shapes=list(scratch) + room + [pltpu.SemaphoreType.DMA((max(1, len(room) + n_loads),))],
        compiler_params=pltpu.CompilerParams(vmem_limit_bytes=need + SPILL),
        cost_estimate=pl.CostEstimate(flops=int(cost * COST), bytes_accessed=0, transcendentals=0),
        name=name,
    )(scalars, *[pin(v) for v in ins], *[pin(v) for v in after])


def pin(value):
    if isinstance(value, Far):
        return pltpu.with_memory_space_constraint(value.value, pltpu.HBM)
    return pltpu.with_memory_space_constraint(value, pltpu.VMEM)


def swap(value, axes, sizes, mask):
    count = 1
    for size in sizes:
        count *= size
    return lax.ppermute(value, axes, [(i, i ^ mask) for i in range(count)])


class Moves:
    def __init__(self, n_dp, n_tensor):
        self.n_dp, self.n_tensor = n_dp, n_tensor
        self.dp = lax.axis_index("dp")
        self.here = lax.axis_index("tensor")

    def along(self, value, mask):
        return swap(value, "dp", (self.n_dp,), mask)

    def core(self, value):
        return self.along(value, 1)

    def side(self, value):
        return self.along(value, 2)

    def over(self, value):
        return swap(value, "tensor", (self.n_tensor,), 1)

    def cross(self, value):
        return swap(value, ("dp", "tensor"), (self.n_dp, self.n_tensor), 5)


    def reduce_core(self, scalars, keep, sent, name, after=()):
        n = 2 * sent.shape[1]
        outs = [((n, 128), BF, True), ((n, 128), F32, True)]
        return call(core_kernel, scalars, [keep, self.core(sent)], outs, name=name, after=after, cost=FOLD)

    def reduce_over(self, scalars, low, rest, name, after=()):
        n = low.shape[0] // 2
        outs = [((n, 128), BF, True), ((n, 128), F32, True)]
        return call(over_kernel, scalars, [rest, self.over(low)], outs, name=name, after=after, cost=FOLD)

    def reduce_core_all(self, scalars, keep, sent, name, vectors=(), spare=0, after=()):
        n = sent.shape[1] + spare
        outs = [((n, 128), BF, True)] * 3 + [((n, 128), F32, True)]
        ins = [keep, self.core(sent), *vectors]
        return call(core_all_kernel, scalars, ins, outs, name=name, after=after, cost=FOLD)

    def sides(self, lows):
        return [self.side(lows[0]), self.over(lows[1]), self.cross(lows[2])]

    def total(self, scalars, values, name, after=()):
        shape = values[0].shape
        return call(total_kernel, scalars, values, [(shape, BF, True)], name=name, after=after, cost=FOLD)[0]

    def halves(self, scalars, values, name, after=()):
        n = values[0].shape[0]
        return call(
            halves_kernel,
            scalars,
            values,
            [((n // 2, 128), BF, True)] * 2,
            [pltpu.VMEM((n, 128), F32)],
            name=name,
            after=after,
            cost=FOLD,
        )

    def join(self, scalars, mine, got, name, after=()):
        shape = (mine.shape[0] * 2, 128)
        return call(join_kernel, scalars, [mine, got], [(shape, BF, True)], name=name, after=after, cost=FOLD)[0]

    def bits(self):
        return [1 << i for i in range(2, self.n_dp.bit_length() - 1)]

    def gather(self, total):
        near = self.side(total)
        return total, near, self.core(total), self.core(near)


def local(
    n_dp, n_tensor, frames, resets, first_gain, first_shift, qkv_weight, out_weight, out_bias, second_gain,
    second_shift, up_weight, up_bias, down_weight, down_bias, prior_gain, prior_shift, prior_weight,
    prior_bias, out_cotangent, logit_cotangent,
):
    move = Moves(n_dp, n_tensor)
    rows, half = frames.shape
    width = 2 * half
    mine = rows // 2
    blocks = mine // BLOCK
    hidden_width, n_logits = up_bias.shape[0], prior_bias.shape[0]
    row = lambda v: v.reshape(1, -1)
    core, side = move.dp & 1, (move.dp >> 1) & 1
    scalars = jnp.stack([move.here, core * 2 + side, (move.dp >> 2) & 1]).astype(jnp.int32)
    total_rows = blocks * PAD
    quarter = hidden_width // 4

    def near_rows(*entries):
        return [((total_rows, n), dtype, True) for n, dtype in entries]

    def pieces(n):
        return [((4, n, 128), F32, True), ((4, n, 128), BF, True)]

    def columns(value, size, which):
        cut = lambda s, ref: ref.at[..., pl.ds(pl.multiple_of(s[which] * size, 128), size)]
        return Far(value, (*value.shape[:-1], size), cut)

    def some_rows(value, size, which):
        cut = lambda s, ref: ref.at[pl.ds(pl.multiple_of(s[which] * size, 16), size), :]
        return Far(value, (size, value.shape[1]), cut)

    vectors = [first_gain, first_shift, out_bias, second_gain, second_shift, down_bias, prior_gain, prior_shift]
    vectors = [row(v) for v in vectors + [up_bias, prior_bias]]
    qkv_rows = 3 * (width // 4) * (half // 128)
    sent_qkv, sent_frames, frames_own, resets_near = call(
        first_kernel,
        scalars,
        [
            Far(frames),
            Far(
                qkv_weight,
                (3, width // 4, half),
                lambda s, ref: ref.at[:, pl.ds(pl.multiple_of(s[1] * (width // 4), 16), width // 4), :],
            ),
            Far(resets),
        ],
        [((qkv_rows, 128), BF, True)]
        + near_rows((half, BF), (half, BF))
        + [((-(-2 * blocks // 8) * 8, -(-BLOCK // 128) * 128), jnp.int32, True)],
        [pltpu.VMEM((rows + 16, half), F32)],
        "first_parts",
        cost=2.0,
    )
    sent_one, sent_two, small = call(
        packs_kernel,
        scalars,
        [
            columns(up_weight, quarter, 1),
            some_rows(out_weight, half // 4, 1),
            some_rows(down_weight, quarter, 1),
            columns(prior_weight, n_logits // 4, 1),
            *[Far(v) for v in vectors],
        ],
        [((width * 2 + half + 48, 128), BF, True), ((quarter * 4 + width, 128), BF, True)]
        + [((16, hidden_width), F32, True)],
        [pltpu.VMEM((16, 128), F32)],
        "packs",
        after=(sent_frames,),
        cost=2.0,
    )

    def all_quarters(got):
        beside = move.side(got)
        return [got, beside, move.core(got), move.core(beside)]

    qkv_got = move.over(sent_qkv)
    frames_other = move.over(sent_frames)
    qkv_pieces = all_quarters(qkv_got)
    cot_sent, logit_own, out_own, qkv_near, out_near, up_near, down_near, prior_near = call(
        cotangents_kernel,
        scalars,
        [Far(logit_cotangent), Far(out_cotangent)],
        near_rows((n_logits + half, BF), (n_logits, BF), (half, BF)),
        [pltpu.VMEM((rows + 16, n_logits), F32)]
        + [pltpu.VMEM((total_rows, n), BF) for n in (n_logits, half)],
        name="cotangents",
        after=(sent_frames,),
        cost=2.3,
        loads=(qkv_weight, out_weight, up_weight, down_weight, prior_weight),
    )
    (sent_one,) = gate([sent_one], [frames_other, cot_sent], "after_frames")
    got_one = move.over(sent_one)
    (sent_two,) = gate([sent_two], [sent_one, qkv_pieces[1]], "after_one")
    got_two = move.over(sent_two)
    first, triple, mixed, qkv_other = call(
        attend_kernel,
        scalars,
        [frames_own, frames_other, resets_near, small, *qkv_pieces, qkv_near],
        near_rows((width, BF), (3 * width, BF), (width, BF)) + [(qkv_weight.shape, BF, True)],
        name="attend",
        cost=5.5,
    )
    beside_one = move.side(got_one)
    (cot_sent,) = gate([cot_sent], [got_two, beside_one], "after_two")
    (beside_two,) = gate([move.side(got_two)], [mixed], "after_attend")
    packed = [got_one, beside_one, move.core(got_one), move.core(beside_one)]
    packed += [got_two, beside_two, move.core(got_two), move.core(beside_two)]
    cotangents = move.over(cot_sent)
    block_send, block_own, middle, second, act, slope, ending, prior_in, out_other, up_other, down_other = call(
        feed_kernel,
        scalars,
        [frames_own, frames_other, mixed, small, out_near, up_near, down_near, *packed],
        near_rows((half, BF), (half, BF))
        + near_rows((width, F32), (width, BF), (2 * hidden_width, BF), (2 * hidden_width, F32))
        + near_rows((width, F32), (width, BF))
        + [(v.shape, BF, True) for v in (out_weight, up_weight, down_weight)],
        [pltpu.VMEM((1, hidden_width), F32)],
        name="feed",
        cost=7.2,
    )
    grad_ending, ending_grad, vec_three, prior_bias_sum, prior_other, prior_bias_other = call(
        prior_kernel,
        scalars,
        [ending, small, logit_own, out_own, *packed, cotangents, prior_near],
        near_rows((width, F32), (width, BF))
        + [((3, width), F32, True), ((1, 2 * n_logits), F32, True)]
        + [(prior_weight.shape, BF, True), ((1, n_logits), F32, True)],
        name="prior",
        cost=2.5,
    )
    hidden_grad, grad_middle, middle_grad, vec_two, up_bias_sum = call(
        feed_back_kernel,
        scalars,
        [ending_grad, slope, middle, grad_ending, small, down_near, down_other, up_near, up_other],
        near_rows((2 * hidden_width, BF), (width, F32), (width, BF))
        + [((3, width), F32, True), ((1, 2 * hidden_width), F32, True)],
        name="feed_back",
        cost=6.5,
    )
    up_keep, up_send = call(
        up_grads_kernel,
        scalars,
        [second, hidden_grad, mixed, middle_grad, prior_in, logit_own, cotangents],
        pieces(width * hidden_width // 512 + half + width),
        [pltpu.VMEM((width, total_rows), BF), pltpu.VMEM((half, width), F32), pltpu.VMEM((width, n_logits), F32)]
        + [pltpu.VMEM((width, total_rows), BF)],
        name="up_grads",
        cost=3.0,
    )
    late_keep, late_send = call(
        late_grads_kernel,
        scalars,
        [act, ending_grad],
        pieces(hidden_width),
        name="late_grads",
        after=(up_send,),
        cost=3.5,
    )
    *up_low, up_rest = move.reduce_core_all(scalars, up_keep, up_send, "up_core", after=(late_send,))
    def attend_back(half, out, after):
        return call(
            functools.partial(attend_back_kernel, half),
            scalars,
            [middle_grad, triple, out, resets_near],
            near_rows((3 * width // 2, BF)),
            [pltpu.VMEM((total_rows, width // 2), BF)],
            name=f"attend_back_{half}",
            after=after,
            cost=4.5,
        )[0]

    grad_own = attend_back(0, out_near, (up_low[0],))
    *late_low, late_rest = move.reduce_core_all(scalars, late_keep, late_send, "late_core", after=(grad_own,))
    grad_other = attend_back(1, out_other, (late_low[0],))
    keep, send = call(
        early_grads_kernel,
        scalars,
        [first, grad_own, grad_other],
        pieces(768),
        name="early_grads",
        cost=2.0,
    )
    frames_send, frames_grad, vec_one = call(
        frames_back_kernel,
        scalars,
        [grad_own, grad_other, grad_middle, frames_own, frames_other, qkv_other, small, qkv_near],
        near_rows((half, BF), (half, F32)) + [((2, width), F32, True)],
        name="frames_back",
        after=(send,),
        cost=2.5,
    )
    up, up_half = move.halves(scalars, [up_rest, *move.sides(up_low)], "up_1", (vec_one,))
    bits = move.bits()
    spare = 64
    vectors = [vec_one, vec_two, vec_three, up_bias_sum, prior_bias_sum]
    *early_low, early_rest = move.reduce_core_all(scalars, keep, send, "early_core", vectors, spare, (up,))
    done = up = move.total(scalars, [up, move.along(up_half, bits[0])], "up_2", (early_low[0],))
    done = late, late_half = move.halves(scalars, [late_rest, *move.sides(late_low)], "late_1", (done,))
    done = late
    for bit in bits[1:]:
        done = up = move.total(scalars, [up, move.along(up, bit)], "up_3", (done,))
    back_send, logits_own = call(
        logits_kernel,
        scalars,
        [prior_in, small, prior_near, prior_other, prior_bias_other, block_send, frames_send],
        near_rows((n_logits + 2 * half, BF), (n_logits, F32)),
        name="logits",
        after=(done,),
        cost=2.0,
    )
    done = back_send
    early, early_half = move.halves(scalars, [early_rest, *move.sides(early_low)], "early_1", (done,))
    done = early
    done = late = move.total(scalars, [late, move.along(late_half, bits[0])], "late_2", (done,))
    done = up = move.join(scalars, up, move.along(up, bits[0]), "up_4", (done,))
    done = early = move.total(scalars, [early, move.along(early_half, bits[0])], "early_2", (done,))
    for bit in bits[1:]:
        done = late = move.total(scalars, [late, move.along(late, bit)], "late_3", (done,))
    for bit in bits[1:]:
        done = early = move.total(scalars, [early, move.along(early, bit)], "early_3", (done,))
    up_pieces = list(move.gather(up))
    late = move.join(scalars, late, move.along(late, bits[0]), "late_4", (done, up_pieces[2]))
    early = move.join(scalars, early, move.along(early, bits[0]), "early_4", (late,))
    up_grad, out_grad, prior_grad, up_done = call(
        up_place_kernel,
        scalars,
        up_pieces,
        [((width, hidden_width), F32, False), ((half, width), F32, False), ((width, n_logits), F32, False)]
        + [((8, 128), F32, True)],
        name="up_place",
        after=(early,),
        cost=FOLD,
    )
    back_got = move.over(back_send)
    logits, grad_frames, block_out, rows_done = call(
        functools.partial(
            rows_kernel,
            [slice(0, n_logits), slice(n_logits + half, n_logits + 2 * half), slice(n_logits, n_logits + half)],
        ),
        scalars,
        [logits_own, back_got, frames_grad, back_got, block_own, back_got],
        [((rows, n_logits), F32, False), ((rows, half), F32, False), ((rows, half), BF, False)]
        + [((8, 128), F32, True)],
        [pltpu.VMEM((rows, half), F32)],
        name="rows_back",
        after=(up_done,),
        cost=FOLD,
    )
    (early_near,) = gate([move.side(early)], [up_done], "after_up")
    (late_near,) = gate([move.side(late)], [rows_done], "after_rows")
    early_pieces = [early, early_near, move.core(early), move.core(early_near)]
    late_pieces = [late, late_near, move.core(late), move.core(late_near)]
    qkv_grad, down_grad, *named = call(
        last_place_kernel,
        scalars,
        early_pieces + late_pieces,
        [((3, width, half), F32, False), ((hidden_width, width), F32, False)]
        + [((1, n), F32, False) for n in [width] * 8 + [hidden_width, n_logits]],
        [pltpu.VMEM((spare, 128), F32)],
        name="last_place",
        after=(rows_done,),
        cost=FOLD,
    )
    named = [v.reshape(-1) for v in named]
    return (
        block_out,
        logits,
        grad_frames,
        named[0],
        named[1],
        qkv_grad,
        out_grad,
        named[4],
        named[2],
        named[3],
        up_grad,
        named[8],
        down_grad,
        named[7],
        named[5],
        named[6],
        prior_grad,
        named[9],
    )


def solution(mesh):
    rows, cols = P("dp", "tensor"), P(None, "tensor")
    placed = (
        rows, P("dp"), P(), P(), P(None, None, "tensor"), P("tensor", None), P(), P(), P(), cols, P("tensor"),
        P("tensor", None), P(), P(), P(), cols, P("tensor"), rows, rows,
    )
    given = (
        rows, rows, rows, P(), P(), P(None, None, "tensor"), P("tensor", None), P(), P(), P(), cols,
        P("tensor"), P("tensor", None), P(), P(), P(), cols, P("tensor"),
    )
    return jax.shard_map(
        functools.partial(local, mesh.shape["dp"], mesh.shape["tensor"]),
        mesh=mesh,
        in_specs=placed,
        out_specs=given,
        check_vma=False,
    )
```
